32 devices in a mesh: dp: 2 (over x), context: 8 (over z, core), tensor: 2 (over y).
Axes of the slice: x: 2, y: 2, z: 4, core: 2. Of those that a mesh axis runs over, the one named last changes fastest.
Arguments:
- block_input: bfloat16 [2, 2048, 1600], P('dp', ('context', 'tensor')), may hold values from -6 to 6
- segment_ids: int32 [2, 2048], P('dp'), may hold values from 0 to 7, as said below
- slot_order: int32 [2, 16], P('dp'), may hold values from 0 to 15, as said below
- first_gain: bfloat16 [1600], P(('dp', 'context')), may hold values from 0.5 to 1.5
- first_shift: bfloat16 [1600], P(('dp', 'context')), may hold values from -3 to 3
- qkv_weight: bfloat16 [1600, 4800], P(('dp', 'context')), may hold values from -0.5 to 0.5
- qv_bias: bfloat16 [3200], P(('dp', 'context')), may hold values from -3 to 3
- out_weight: bfloat16 [1600, 1600], P(('dp', 'context')), may hold values from -0.3125 to 0.3125
- out_bias: bfloat16 [1600], P(('dp', 'context')), may hold values from -3 to 3
- second_gain: bfloat16 [1600], P(('dp', 'context')), may hold values from 0.5 to 1.5
- second_shift: bfloat16 [1600], P(('dp', 'context')), may hold values from -3 to 3
- fc_weight: bfloat16 [1600, 6400], P(('dp', 'context'), 'tensor'), may hold values from -0.15625 to 0.15625
- fc_bias: bfloat16 [6400], P('tensor'), may hold values from -3 to 3
- proj_weight: bfloat16 [6400, 1600], P('tensor', ('dp', 'context')), may hold values from -0.078125 to 0.078125
- proj_bias: bfloat16 [1600], P(('dp', 'context')), may hold values from -3 to 3
- out_grad: bfloat16 [2, 2048, 1600], P('dp', ('context', 'tensor')), may hold values from -6 to 6
Outputs:
- block_output: float32 [2, 2048, 1600], P('dp', ('context', 'tensor'))
- input_grad: float32 [2, 2048, 1600], P('dp', ('context', 'tensor'))
- qkv_weight_grad: float32 [1600, 4800], P(('dp', 'context'))
- qv_bias_grad: float32 [3200], P(('dp', 'context'))
- out_weight_grad: float32 [1600, 1600], P(('dp', 'context'))
- out_bias_grad: float32 [1600], P(('dp', 'context'))
- first_gain_grad: float32 [1600], P(('dp', 'context'))
- first_shift_grad: float32 [1600], P(('dp', 'context'))
- second_gain_grad: float32 [1600], P(('dp', 'context'))
- second_shift_grad: float32 [1600], P(('dp', 'context'))
- fc_weight_grad: float32 [1600, 6400], P(('dp', 'context'), 'tensor')
- fc_bias_grad: float32 [6400], P('tensor')
- proj_weight_grad: float32 [6400, 1600], P('tensor', ('dp', 'context'))
- proj_bias_grad: float32 [1600], P(('dp', 'context'))
The draws below stay inside these ranges and needn't reach their ends.
Inputs may be any that keep to these rules, and one draw needn't show every extreme that they name: `segment_ids`: ids of the 8 documents of a row, not falling along position (not along slot order); every id appears in every row; one document of each row holds half of the row's positions or more, the others share the rest unevenly. `slot_order`: each row is a permutation of the slot numbers.
All inputs are finite; a program needn't handle non-finite values.
Results may differ from the reference program's by a relative error of at most 0.02.
Values may be sent and summed in bfloat16 or wider, within the bound.
A program may use at most 384 MiB of HBM per device.

```python
import math
import jax
import jax.numpy as jnp
from jax import lax

D = 1600
HEADS = 25
HEAD_DIM = 64
FF = 6400
TOK_SLOT = 128
DOCS = 8
SLOTS = 16
ROW_LEN = 2048
ROWS = 2


def row_layout(key):
    cut_key, order_key, long_key, where_key = jax.random.split(key, 4)
    span = TOK_SLOT * SLOTS
    long_len = span // 2 + jax.random.randint(long_key, (), 0, span // 4 + 1, dtype=jnp.int32)
    rest = span - long_len
    shuffled = jax.random.permutation(cut_key, span - 1).astype(jnp.int32)
    ranks = jnp.where(shuffled < rest - 1, jnp.arange(span - 1, dtype=jnp.int32), span).astype(jnp.int32)
    unused, picked = lax.top_k(-ranks, DOCS - 2)
    cuts = jnp.sort(jnp.take(shuffled, picked) + 1).astype(jnp.int32)
    bounds = jnp.concatenate([jnp.zeros((1,), jnp.int32), cuts, jnp.reshape(rest, (1,)).astype(jnp.int32)])
    long_place = jax.random.randint(where_key, (), 0, DOCS, dtype=jnp.int32)
    start = jnp.take(bounds, long_place)
    places = jnp.arange(span, dtype=jnp.int32)
    shifted = jnp.where(places < start, places, places - long_len)
    short_ids = jnp.sum((shifted[:, None] >= cuts[None, :]).astype(jnp.int32), axis=1).astype(jnp.int32)
    true_ids = jnp.where(places < start, short_ids, jnp.where(places < start + long_len, long_place, short_ids + 1)).astype(jnp.int32)
    order = jax.random.permutation(order_key, SLOTS).astype(jnp.int32)
    dealt = true_ids.reshape(SLOTS, TOK_SLOT)[order].reshape(span)
    return (dealt, order)


def both_layouts(key):
    row_keys = jax.random.split(jax.random.fold_in(key, 5), ROWS)
    return jax.vmap(row_layout)(row_keys)


def draw_segment_ids(key, part):
    dealt, order = both_layouts(key)
    return dealt


def draw_slot_order(key, part):
    dealt, order = both_layouts(key)
    return order


def draw_qkv_weight(key, part):
    base_key = jax.random.fold_in(jax.random.fold_in(key, 29), 0)
    base = jax.random.truncated_normal(base_key, -4.0, 4.0, (D, 3 * D), jnp.float32) * D ** (-0.5)
    query_part = 1.5 * base[:, :D]
    key_part = 1.5 * base[:, D:2 * D]
    return jnp.clip(jnp.concatenate([query_part, key_part, base[:, 2 * D:]], axis=1), -0.5, 0.5).astype(jnp.bfloat16)


def with_spikes(array, stream_key, source, target, blocks, factor):
    def block_of(axis_at):
        return (jnp.arange(array.shape[axis_at]) // (array.shape[axis_at] // blocks)).reshape((-1,) + (1,) * (array.ndim - 1 - axis_at))

    one_side = jax.random.permutation(stream_key, blocks)[block_of(target)]
    second = (block_of(target) + blocks // 2) % blocks
    return jnp.where((block_of(source) == one_side) | (block_of(source) == second), factor * array, array)


def level_of(own_key, dims, shards, smallest, high):
    gain, own = 1.0, jax.random.fold_in(own_key, 6)
    for position, shards_of in shards:
        draws = jnp.exp(jax.random.uniform(jax.random.fold_in(own, position), (shards_of,), jnp.float32, smallest / len(shards), high / len(shards)))
        gain = gain * jnp.repeat(draws, dims[position] // shards_of).reshape([-1 if axis == position else 1 for axis in range(len(dims))])
    return gain


def centred(stream_key, dims, spread, most, pieces=(), kind=jnp.bfloat16):
    values = spread * jax.random.normal(stream_key, dims, jnp.float32)
    if pieces:
        values = values * level_of(stream_key, dims, pieces, -0.22, 0.18)
    return jnp.clip(values, -most, most).astype(kind)


def bell_draw_with(own_key, dims, scale, most, cuts, heavy, held_as=jnp.bfloat16):
    values = scale * jax.random.normal(own_key, dims, jnp.float32)
    if cuts:
        values = values * level_of(own_key, dims, cuts, -0.22, 0.18)
    return jnp.clip(with_spikes(values, jax.random.fold_in(own_key, 3), *heavy), -most, most).astype(held_as)


def setup_inputs(seed: int = 0) -> dict:
    splits = jax.random.split(jax.random.key(seed), 17)
    return {
        "block_input": bell_draw_with(splits[0], (ROWS, ROW_LEN, D), 1.0, 6.0, ((0, 2), (1, 16)), (1, 2, 16, 2.0)),
        "segment_ids": draw_segment_ids(jax.random.fold_in(splits[16], 71), 0),
        "slot_order": draw_slot_order(jax.random.fold_in(splits[16], 71), 0),
        "first_gain": jnp.clip(1.0 + 0.1 * jax.random.normal(splits[3], (D,), jnp.float32), 0.5, 1.5).astype(jnp.bfloat16),
        "first_shift": centred(splits[4], (D,), 0.5, 3.0, ((0, 16),)),
        "qkv_weight": draw_qkv_weight(jax.random.fold_in(splits[16], 71), 0),
        "qv_bias": centred(splits[6], (2 * D,), 0.5, 3.0, ((0, 16),)),
        "out_weight": centred(splits[7], (D, D), (D // 4) ** -0.5, 0.3125, ((0, 16),)),
        "out_bias": centred(splits[8], (D,), 0.5, 3.0, ((0, 16),)),
        "second_gain": jnp.clip(1.0 + 0.1 * jax.random.normal(splits[9], (D,), jnp.float32), 0.5, 1.5).astype(jnp.bfloat16),
        "second_shift": centred(splits[10], (D,), 0.5, 3.0, ((0, 16),)),
        "fc_weight": centred(splits[11], (D, FF), D ** -0.5, 0.15625, ((0, 16), (1, 2))),
        "fc_bias": centred(splits[12], (FF,), 0.5, 3.0, ((0, 2),)),
        "proj_weight": centred(splits[13], (FF, D), FF ** -0.5, 0.078125, ((0, 2), (1, 16))),
        "proj_bias": centred(splits[14], (D,), 0.5, 3.0, ((0, 16),)),
        "out_grad": bell_draw_with(splits[15], (ROWS, ROW_LEN, D), 1.0, 6.0, ((0, 2), (1, 16)), (1, 2, 16, 2.0)),
    }


NORM_EPS = 1e-05
GELU_SCALE = 0.7978845608028654
GELU_CUBE = 0.044715
MASK_FLOOR = -1e+30

def gelu_parts(values):
    inner_arg = GELU_SCALE * (values + GELU_CUBE * values * values * values)
    tanh_value = jnp.tanh(inner_arg)
    result = 0.5 * values * (1.0 + tanh_value)
    derivative = 0.5 * (1.0 + tanh_value) + 0.5 * values * (1.0 - tanh_value * tanh_value) * GELU_SCALE * (1.0 + 3.0 * GELU_CUBE * values * values)
    return (result, derivative)

def norm_forward(values, norm_gain, norm_shift):
    mean_value = lax.optimization_barrier(jnp.mean(values, axis=-1, keepdims=True))
    centered = values - mean_value
    inv_sigma = lax.rsqrt(lax.optimization_barrier(jnp.mean(centered * centered, axis=-1, keepdims=True)) + NORM_EPS)
    normed = centered * inv_sigma
    return (normed, inv_sigma, normed * norm_gain + norm_shift)

def norm_backward(upstream, normed, inv_sigma, norm_gain):
    scaled = upstream * norm_gain
    return inv_sigma * (scaled - lax.optimization_barrier(jnp.mean(scaled, axis=-1, keepdims=True)) - normed * lax.optimization_barrier(jnp.mean(scaled * normed, axis=-1, keepdims=True)))

def contract(left_side, right_side, left_dim, right_dim):
    return lax.dot_general(left_side, right_side, (((left_dim,), (right_dim,)), ((), ())), preferred_element_type=jnp.float32)

def widen(values):
    return lax.optimization_barrier(values).astype(jnp.float32)

def permit(query_seg, query_place, key_seg, key_place):
    same_doc = key_seg[None, :] == query_seg[:, None]
    earlier = key_place[None, :] <= query_place[:, None]
    return jnp.logical_and(same_doc, earlier)

def reference(block_input, segment_ids, slot_order, first_gain, first_shift, qkv_weight, qv_bias, out_weight, out_bias, second_gain, second_shift, fc_weight, fc_bias, proj_weight, proj_bias, out_grad):
    features = D
    span = TOK_SLOT * SLOTS
    scale = 1.0 / math.sqrt(HEAD_DIM)
    query_block = math.gcd(span, 1024)
    block_total = span // query_block
    offsets = jnp.arange(TOK_SLOT, dtype=jnp.int32)
    gain_one = first_gain.astype(jnp.float32)
    shift_one = first_shift.astype(jnp.float32)
    gain_two = second_gain.astype(jnp.float32)
    shift_two = second_shift.astype(jnp.float32)
    bias_qv = qv_bias.astype(jnp.float32)
    bias_out = out_bias.astype(jnp.float32)
    bias_fc = fc_bias.astype(jnp.float32)
    bias_proj = proj_bias.astype(jnp.float32)
    outputs = []
    input_grads = []
    grad_sums = None
    for row_index in range(ROWS):
        row_input = block_input[row_index].astype(jnp.float32)
        places = (slot_order[row_index][:, None] * TOK_SLOT + offsets[None, :]).reshape(span).astype(jnp.int32)
        row_segments = segment_ids[row_index]
        normed_one, inv_one, pre_one = norm_forward(row_input, gain_one, shift_one)
        norm_one = pre_one.astype(jnp.bfloat16)
        projected = jnp.dot(norm_one, qkv_weight, preferred_element_type=jnp.float32)
        queries = (projected[:, :features] + bias_qv[:features]).astype(jnp.bfloat16)
        keys_row = projected[:, features:2 * features].astype(jnp.bfloat16)
        values_row = (projected[:, 2 * features:] + bias_qv[features:]).astype(jnp.bfloat16)
        query_wide = widen(queries).reshape(span, HEADS, HEAD_DIM)
        key_wide = widen(keys_row).reshape(span, HEADS, HEAD_DIM)
        value_wide = widen(values_row).reshape(span, HEADS, HEAD_DIM)

        def block_mask(begin_row):
            return permit(lax.dynamic_slice_in_dim(row_segments, begin_row, query_block, 0), lax.dynamic_slice_in_dim(places, begin_row, query_block, 0), row_segments, places)

        def forward_block(block_index):
            begin_row = block_index * query_block
            query_part = lax.dynamic_slice_in_dim(query_wide, begin_row, query_block, 0)
            allowed = block_mask(begin_row)
            scores = jnp.einsum('qhd,khd->hqk', query_part, key_wide) * scale
            scores = jnp.where(allowed[None], scores, MASK_FLOOR)
            row_max = lax.optimization_barrier(jnp.max(scores, axis=-1))
            row_total = lax.optimization_barrier(jnp.sum(jnp.where(allowed[None], jnp.exp(scores - row_max[..., None]), 0.0), axis=-1))
            log_total = row_max + jnp.log(row_total)
            weights = widen(jnp.where(allowed[None], jnp.exp(scores - log_total[..., None]), 0.0).astype(jnp.bfloat16))
            attended = jnp.einsum('hqk,khd->qhd', weights, value_wide)
            return (attended, log_total)
        attended, log_totals = lax.map(forward_block, jnp.arange(block_total, dtype=jnp.int32))
        attention = attended.reshape(span, features).astype(jnp.bfloat16)
        hidden = row_input + jnp.dot(attention, out_weight, preferred_element_type=jnp.float32) + bias_out
        normed_two, inv_two, pre_two = norm_forward(hidden, gain_two, shift_two)
        norm_two = pre_two.astype(jnp.bfloat16)
        preact = jnp.dot(norm_two, fc_weight, preferred_element_type=jnp.float32) + bias_fc
        activated, derivative = gelu_parts(preact)
        activation = activated.astype(jnp.bfloat16)
        row_output = hidden + jnp.dot(activation, proj_weight, preferred_element_type=jnp.float32) + bias_proj
        outputs.append(row_output)
        row_grad = out_grad[row_index]
        grad_wide = row_grad.astype(jnp.float32)
        proj_bias_term = lax.optimization_barrier(jnp.sum(grad_wide, axis=0))
        proj_weight_term = contract(activation, row_grad, 0, 0)
        dpreact = contract(row_grad, proj_weight, 1, 1) * derivative
        fc_bias_term = lax.optimization_barrier(jnp.sum(dpreact, axis=0))
        dpreact_b = dpreact.astype(jnp.bfloat16)
        fc_weight_term = contract(norm_two, dpreact_b, 0, 0)
        dnorm_two = contract(dpreact_b, fc_weight, 1, 1)
        second_gain_term = lax.optimization_barrier(jnp.sum(dnorm_two * normed_two, axis=0))
        second_shift_term = lax.optimization_barrier(jnp.sum(dnorm_two, axis=0))
        dhidden = grad_wide + norm_backward(dnorm_two, normed_two, inv_two, gain_two)
        out_bias_term = lax.optimization_barrier(jnp.sum(dhidden, axis=0))
        dhidden_b = dhidden.astype(jnp.bfloat16)
        out_weight_term = contract(attention, dhidden_b, 0, 0)
        dattention = contract(dhidden_b, out_weight, 1, 1).astype(jnp.bfloat16)
        dattention_wide = widen(dattention).reshape(span, HEADS, HEAD_DIM)
        delta = lax.optimization_barrier(jnp.sum(dattention_wide * widen(attention).reshape(span, HEADS, HEAD_DIM), axis=-1))

        def backward_block(carried, block_index):
            key_total, value_total = carried
            begin_row = block_index * query_block
            query_part = lax.dynamic_slice_in_dim(query_wide, begin_row, query_block, 0)
            grad_part = lax.dynamic_slice_in_dim(dattention_wide, begin_row, query_block, 0)
            delta_part = jnp.transpose(lax.dynamic_slice_in_dim(delta, begin_row, query_block, 0), (1, 0))
            log_part = log_totals[block_index]
            allowed = block_mask(begin_row)
            scores = jnp.einsum('qhd,khd->hqk', query_part, key_wide) * scale
            weights = jnp.where(allowed[None], jnp.exp(scores - log_part[..., None]), 0.0)
            dprob = jnp.einsum('qhd,khd->hqk', grad_part, value_wide)
            dscore = widen((weights * (dprob - delta_part[..., None]) * scale).astype(jnp.bfloat16))
            dquery = jnp.einsum('hqk,khd->qhd', dscore, key_wide)
            key_total = key_total + jnp.einsum('hqk,qhd->khd', dscore, query_part)
            value_total = value_total + jnp.einsum('hqk,qhd->khd', widen(weights.astype(jnp.bfloat16)), grad_part)
            return ((key_total, value_total), dquery)
        zeros_keys = jnp.zeros((span, HEADS, HEAD_DIM), jnp.float32)
        (key_total, value_total), dquery_blocks = lax.scan(backward_block, (zeros_keys, zeros_keys), jnp.arange(block_total, dtype=jnp.int32))
        dquery = dquery_blocks.reshape(span, features)
        dkey = key_total.reshape(span, features)
        dvalue = value_total.reshape(span, features)
        dprojected = jnp.concatenate([dquery, dkey, dvalue], axis=1)
        qv_bias_term = jnp.concatenate([lax.optimization_barrier(jnp.sum(dquery, axis=0)), lax.optimization_barrier(jnp.sum(dvalue, axis=0))])
        dprojected_b = dprojected.astype(jnp.bfloat16)
        qkv_weight_term = contract(norm_one, dprojected_b, 0, 0)
        dnorm_one = contract(dprojected_b, qkv_weight, 1, 1)
        first_gain_term = lax.optimization_barrier(jnp.sum(dnorm_one * normed_one, axis=0))
        first_shift_term = lax.optimization_barrier(jnp.sum(dnorm_one, axis=0))
        input_grads.append(dhidden + norm_backward(dnorm_one, normed_one, inv_one, gain_one))
        terms = [qkv_weight_term, qv_bias_term, out_weight_term, out_bias_term, first_gain_term, first_shift_term, second_gain_term, second_shift_term, fc_weight_term, fc_bias_term, proj_weight_term, proj_bias_term]
        if grad_sums is None:
            grad_sums = terms
        else:
            grad_sums = [older + newer for older, newer in zip(grad_sums, terms)]
    return (jnp.stack(outputs), jnp.stack(input_grads), grad_sums[0], grad_sums[1], grad_sums[2], grad_sums[3], grad_sums[4], grad_sums[5], grad_sums[6], grad_sums[7], grad_sums[8], grad_sums[9], grad_sums[10], grad_sums[11])
```

```python
import functools
import math

import jax
import jax.numpy as jnp
import numpy as np
from jax import lax
from jax.experimental import pallas as pl
from jax.experimental.pallas import tpu as pltpu
from jax.sharding import Mesh
from jax.sharding import PartitionSpec as P

HEADS = 25
DOCS = 8
NORM_EPS = 1e-05
GELU_SCALE = 0.7978845608028654
GELU_CUBE = 0.044715
MASK_FLOOR = -1e30

F32 = jnp.float32
B16 = jnp.bfloat16
BLK = 256
VMEM_LIMIT = 60 * 1024 * 1024

ROW = ("h", "l", "c", "y")
CTX = ("h", "l", "c")
SHARD = ("x", "h", "l", "c")
FFG = ("l", "c", "y")


def gelu_parts(values):
    inner_arg = GELU_SCALE * (values + GELU_CUBE * values * values * values)
    tanh_value = jnp.tanh(inner_arg)
    result = 0.5 * values * (1.0 + tanh_value)
    derivative = 0.5 * (1.0 + tanh_value) + 0.5 * values * (
        1.0 - tanh_value * tanh_value
    ) * GELU_SCALE * (1.0 + 3.0 * GELU_CUBE * values * values)
    return (result, derivative)


def norm_forward(values):
    mean_value = jnp.mean(values, axis=-1, keepdims=True)
    centered = values - mean_value
    inv_sigma = lax.rsqrt(jnp.mean(centered * centered, axis=-1, keepdims=True) + NORM_EPS)
    return (centered * inv_sigma, inv_sigma)


def norm_backward(upstream, normed, inv_sigma, norm_gain):
    scaled = upstream * norm_gain
    return inv_sigma * (
        scaled
        - jnp.mean(scaled, axis=-1, keepdims=True)
        - normed * jnp.mean(scaled * normed, axis=-1, keepdims=True)
    )


def dot(left, right, left_dim, right_dim):
    return lax.dot_general(
        left, right, (((left_dim,), (right_dim,)), ((), ())), preferred_element_type=F32
    )


def sort_slots(inv_ref, src_ref, dst_ref, slot_len, start=0, width=None, factor=None):
    width = src_ref.shape[1] if width is None else width

    def body(piece, carry):
        slot = inv_ref[piece]
        rows = src_ref[pl.ds(pl.multiple_of(slot * slot_len, slot_len), slot_len), start : start + width]
        if factor is not None:
            rows = rows * jnp.asarray(factor, rows.dtype)
        dst_ref[pl.ds(pl.multiple_of(piece * slot_len, slot_len), slot_len), :] = rows
        return carry

    lax.fori_loop(0, src_ref.shape[0] // slot_len, body, 0)


def unsort_block(inv_ref, dst_ref, value, block, slot_len):
    for part in range(BLK // slot_len):
        slot = inv_ref[block * (BLK // slot_len) + part]
        dst_ref[pl.ds(pl.multiple_of(slot * slot_len, slot_len), slot_len), :] = value[
            part * slot_len : (part + 1) * slot_len
        ].astype(dst_ref.dtype)


def block_rows(block):
    return pl.ds(pl.multiple_of(block * BLK, BLK), BLK)


def mask_of(start_row, key_block, query_block, diagonal):
    key_at = key_block * BLK + lax.broadcasted_iota(jnp.int32, (BLK, BLK), 0)
    allowed = key_at >= start_row
    if diagonal:
        query_at = query_block * BLK + lax.broadcasted_iota(jnp.int32, (BLK, BLK), 1)
        allowed = jnp.logical_and(allowed, key_at <= query_at)
    return allowed


def attend_kernel(slot_len, head, inv_ref, low_ref, qkv_ref, start_ref, out_ref, lse_ref, q_s, k_s, vt_s):
    total = qkv_ref.shape[0]
    pair = 2 * head
    sort_slots(inv_ref, qkv_ref, q_s, slot_len, 0, pair, 1.0 / math.sqrt(head))
    sort_slots(inv_ref, qkv_ref, k_s, slot_len, pair, pair)

    def fill(piece, carry):
        slot = inv_ref[piece]
        rows = qkv_ref[pl.ds(pl.multiple_of(slot * slot_len, slot_len), slot_len), 2 * pair :]
        vt_s[:, pl.ds(pl.multiple_of(piece * slot_len, slot_len), slot_len)] = rows.astype(F32).T.astype(B16)
        return carry

    lax.fori_loop(0, total // slot_len, fill, 0)

    def per_query(block, carry):
        queries = q_s[block_rows(block), :]
        start_row = start_ref[block]

        def step(key_block, state, diagonal):
            allowed = mask_of(start_row, key_block, block, diagonal)
            keys = k_s[block_rows(key_block), :]
            values = vt_s[:, block_rows(key_block)]
            fresh = []
            for part in range(2):
                old_max, old_sum, old_acc = state[part]
                cols = slice(part * head, (part + 1) * head)
                scores = dot(keys[:, cols], queries[:, cols], 1, 1)
                scores = jnp.where(allowed, scores, MASK_FLOOR)
                new_max = jnp.maximum(old_max, jnp.max(scores, axis=0, keepdims=True))
                weights = jnp.where(allowed, jnp.exp(scores - new_max), 0.0)
                shrink = jnp.exp(old_max - new_max)
                new_sum = old_sum * shrink + jnp.sum(weights, axis=0, keepdims=True)
                new_acc = old_acc * shrink + dot(values[cols, :], weights.astype(B16), 1, 0)
                fresh.append((new_max, new_sum, new_acc))
            return tuple(fresh)

        first = tuple(
            (
                jnp.full((1, BLK), MASK_FLOOR, F32),
                jnp.zeros((1, BLK), F32),
                jnp.zeros((head, BLK), F32),
            )
            for part in range(2)
        )
        state = lax.fori_loop(low_ref[block], block, lambda j, s: step(j, s, False), first)
        state = step(block, state, True)
        lse_ref[block] = jnp.concatenate([s[0] + jnp.log(s[1]) for s in state], axis=0)
        result = jnp.concatenate([s[2] / s[1] for s in state], axis=0)
        unsort_block(inv_ref, out_ref, result.T, block, slot_len)
        return carry

    lax.fori_loop(0, total // BLK, per_query, 0)


def attend(inv, low, qkv, start3, slot_len, head):
    total = qkv.shape[0]
    vmem = pl.BlockSpec(memory_space=pltpu.VMEM)
    smem = pl.BlockSpec(memory_space=pltpu.SMEM)
    return pl.pallas_call(
        functools.partial(attend_kernel, slot_len, head),
        out_shape=(
            jax.ShapeDtypeStruct((total, 2 * head), B16),
            jax.ShapeDtypeStruct((total // BLK, 2, BLK), F32),
        ),
        in_specs=[smem, smem, vmem, vmem],
        out_specs=(vmem, vmem),
        scratch_shapes=[
            pltpu.VMEM((total, 2 * head), B16),
            pltpu.VMEM((total, 2 * head), B16),
            pltpu.VMEM((2 * head, total), B16),
        ],
        compiler_params=pltpu.CompilerParams(vmem_limit_bytes=VMEM_LIMIT),
        cost_estimate=pl.CostEstimate(
            flops=4 * total * total * head, bytes_accessed=8 * total * head * 2, transcendentals=total * total
        ),
        name="attend",
    )(inv, low, qkv, start3)


def attend_back_kernel(
    slot_len, head, inv_ref, low_ref, qkv_ref, out_ref, grad_ref, lse_ref, start_ref,
    dqkv_ref, q_s, k_s, v_s, kt_s, o_s, g_s, dk_s, dv_s,
):
    total = qkv_ref.shape[0]
    pair = 2 * head
    scale = 1.0 / math.sqrt(head)
    sort_slots(inv_ref, qkv_ref, q_s, slot_len, 0, pair, scale)
    sort_slots(inv_ref, qkv_ref, k_s, slot_len, pair, pair)
    sort_slots(inv_ref, qkv_ref, v_s, slot_len, 2 * pair, pair)
    sort_slots(inv_ref, out_ref, o_s, slot_len)
    sort_slots(inv_ref, grad_ref, g_s, slot_len)

    def fill(block, carry):
        kt_s[:, block_rows(block)] = k_s[block_rows(block), :].astype(F32).T.astype(B16)
        return carry

    lax.fori_loop(0, total // BLK, fill, 0)
    dk_s[...] = jnp.zeros_like(dk_s)
    dv_s[...] = jnp.zeros_like(dv_s)

    def per_query(block, carry):
        queries = q_s[block_rows(block), :]
        grads = g_s[block_rows(block), :]
        start_row = start_ref[block]
        lse = lse_ref[block]
        prod = (grads.astype(F32) * o_s[block_rows(block), :].astype(F32)).T
        delta = [jnp.sum(prod[part * head : (part + 1) * head], axis=0, keepdims=True) for part in range(2)]

        def step(key_block, state, diagonal):
            allowed = mask_of(start_row, key_block, block, diagonal)
            rows = block_rows(key_block)
            keys = k_s[rows, :]
            values = v_s[rows, :]
            flipped = kt_s[:, rows]
            fresh, dks, dvs = [], [], []
            for part in range(2):
                cols = slice(part * head, (part + 1) * head)
                scores = dot(keys[:, cols], queries[:, cols], 1, 1)
                weights = jnp.where(allowed, jnp.exp(scores - lse[part : part + 1]), 0.0)
                dprob = dot(values[:, cols], grads[:, cols], 1, 1)
                dscore = (weights * (dprob - delta[part])).astype(B16)
                dvs.append(dot(weights.astype(B16), grads[:, cols], 1, 0))
                dks.append(dot(dscore, queries[:, cols], 1, 0))
                fresh.append(state[part] + dot(flipped[cols, :], dscore, 1, 0))
            dk_s[rows, :] += jnp.concatenate(dks, axis=1)
            dv_s[rows, :] += jnp.concatenate(dvs, axis=1)
            return tuple(fresh)

        state = (jnp.zeros((head, BLK), F32), jnp.zeros((head, BLK), F32))
        state = lax.fori_loop(low_ref[block], block, lambda j, s: step(j, s, False), state)
        state = step(block, state, True)
        dq = jnp.concatenate(state, axis=0).T * scale
        for part in range(BLK // slot_len):
            slot = inv_ref[block * (BLK // slot_len) + part]
            dqkv_ref[pl.ds(pl.multiple_of(slot * slot_len, slot_len), slot_len), 0:pair] = dq[
                part * slot_len : (part + 1) * slot_len
            ]
        return carry

    lax.fori_loop(0, total // BLK, per_query, 0)

    def give(piece, carry):
        slot = inv_ref[piece]
        rows = pl.ds(pl.multiple_of(slot * slot_len, slot_len), slot_len)
        held = pl.ds(pl.multiple_of(piece * slot_len, slot_len), slot_len)
        dqkv_ref[rows, pair : 2 * pair] = dk_s[held, :]
        dqkv_ref[rows, 2 * pair :] = dv_s[held, :]
        return carry

    lax.fori_loop(0, total // slot_len, give, 0)


def attend_back(inv, low, qkv, out, grad, lse, start3, slot_len, head):
    total = qkv.shape[0]
    pair = 2 * head
    vmem = pl.BlockSpec(memory_space=pltpu.VMEM)
    smem = pl.BlockSpec(memory_space=pltpu.SMEM)
    held = pltpu.VMEM((total, pair), B16)
    return pl.pallas_call(
        functools.partial(attend_back_kernel, slot_len, head),
        out_shape=jax.ShapeDtypeStruct((total, 3 * pair), F32),
        in_specs=[smem, smem] + [vmem] * 5,
        out_specs=vmem,
        scratch_shapes=[
            held, held, held, pltpu.VMEM((pair, total), B16), held, held,
            pltpu.VMEM((total, pair), F32), pltpu.VMEM((total, pair), F32),
        ],
        compiler_params=pltpu.CompilerParams(vmem_limit_bytes=VMEM_LIMIT),
        cost_estimate=pl.CostEstimate(
            flops=10 * total * total * head, bytes_accessed=30 * total * head * 2, transcendentals=total * total
        ),
        name="attend_back",
    )(inv, low, qkv, out, grad, lse, start3)


def on_device(
    sizes, block_input, segment_ids, slot_order, first_gain, first_shift, qkv_weight, qv_bias, out_weight, out_bias,
    second_gain, second_shift, fc_weight, fc_bias, proj_weight, proj_bias, out_grad,
):
    n_x, n_ctx, n_y = sizes
    n_slot = n_ctx * n_y
    n_shard = n_x * n_ctx
    n_h = n_ctx // 4
    slot_len, feats = block_input.shape[1:]
    head = feats // HEADS
    pair = 2 * head
    rows = qkv_weight.shape[0]
    ff_own = fc_weight.shape[1] // 4
    padded = n_slot * pair
    y_at = lax.axis_index("y")
    ctx_at = lax.axis_index(CTX)
    slot_at = lax.axis_index(ROW)
    lc_at = lax.axis_index(("l", "c"))

    def gather(value, axes):
        return lax.all_gather(value, axes, axis=0, tiled=True)

    small = jnp.concatenate(
        [
            first_gain, first_shift, out_bias, second_gain, second_shift, proj_bias, qv_bias,
        ]
    )
    smalls = lax.all_gather(small, SHARD, axis=0, tiled=False).astype(F32)
    gain_one, shift_one, bias_out, gain_two, shift_two, bias_proj = [
        smalls[:, i * rows : (i + 1) * rows].reshape(feats) for i in range(6)
    ]
    bias_qv = smalls[:, 6 * rows :].reshape(2, feats)
    bias_pair = lax.dynamic_slice_in_dim(
        jnp.pad(bias_qv, ((0, 0), (0, padded - feats))), slot_at * pair, pair, 1
    )
    bias_qkv = jnp.concatenate([bias_pair[0], jnp.zeros((pair,), F32), bias_pair[1]])

    packed = jnp.pad(qkv_weight.reshape(rows, 3, feats), ((0, 0), (0, 0), (0, padded - feats)))
    packed = lax.dynamic_index_in_dim(packed.reshape(rows, 3, n_ctx, n_y, pair), y_at, 3, False)
    packed = packed.transpose(2, 0, 1, 3).reshape(n_ctx, rows, 3 * pair)
    packed = lax.all_to_all(packed, CTX, 0, 0, tiled=True)
    w_qkv = lax.all_gather(packed, "x", axis=0, tiled=False).reshape(feats, 3 * pair)

    ffn = jnp.concatenate(
        [
            fc_weight.reshape(rows, 4, ff_own).transpose(1, 0, 2),
            proj_weight.reshape(4, ff_own, rows).transpose(0, 2, 1),
        ],
        axis=2,
    )
    ffn = lax.all_to_all(ffn, ("l", "c"), 0, 0, tiled=True)
    ffn = gather(ffn.reshape(4 * rows, 2 * ff_own), ("x", "h"))
    w_fc, w_proj = ffn[:, :ff_own], ffn[:, ff_own:]
    w_out = gather(out_weight, SHARD)
    b_fc = lax.dynamic_slice_in_dim(fc_bias, lc_at * ff_own, ff_own, 0).astype(F32)

    order = slot_order[0]
    pieces = jnp.arange(n_slot, dtype=jnp.int32)
    inv = jnp.sum(jnp.where(order[None, :] == pieces[:, None], pieces[None, :], 0), axis=1).astype(jnp.int32)
    segs = jnp.take(segment_ids[0].reshape(n_slot, slot_len), inv, axis=0).reshape(-1)
    docs = jnp.arange(DOCS, dtype=jnp.int32)
    counts = jnp.sum((segs[None, :] == docs[:, None]).astype(jnp.int32), axis=1)
    starts = jnp.sum(jnp.where(segs[None, :] > docs[:, None], counts[:, None], 0), axis=0).astype(jnp.int32)
    start3 = starts.reshape(-1, 1, BLK)
    low = start3[:, 0, 0] // BLK

    own_input = block_input[0]
    own_wide = own_input.astype(F32)
    all_input = gather(own_input, ROW)
    normed_all, unused = norm_forward(all_input.astype(F32))
    norm_one = (normed_all * gain_one + shift_one).astype(B16)
    qkv = (dot(norm_one, w_qkv, 1, 0) + bias_qkv).astype(B16)
    heads_out, lse = attend(inv, low, qkv, start3, slot_len, head)
    attention = lax.all_to_all(heads_out.reshape(n_slot, slot_len, pair), ROW, 0, 0, tiled=True)
    attention = attention.transpose(1, 0, 2).reshape(slot_len, padded)[:, :feats]
    hidden = own_wide + dot(attention, w_out, 1, 0) + bias_out
    normed_two, inv_two = norm_forward(hidden)
    norm_two = (normed_two * gain_two + shift_two).astype(B16)
    grad_own = out_grad[0]
    grad_wide = grad_own.astype(F32)
    grad_all = gather(grad_own, FFG)
    norm_all = gather(norm_two, FFG)
    preact = dot(norm_all, w_fc, 1, 0) + b_fc
    activated, derivative = gelu_parts(preact)
    activation = activated.astype(B16)
    mlp_part = dot(activation, w_proj, 1, 1).astype(B16)
    mlp = lax.psum_scatter(mlp_part, FFG, scatter_dimension=0, tiled=True).astype(F32)
    block_output = hidden + mlp + bias_proj

    dpreact = dot(grad_all, w_proj, 1, 0) * derivative
    dpreact_b = dpreact.astype(B16)
    dnorm_part = dot(dpreact_b, w_fc, 1, 1).astype(B16)
    dnorm_two = lax.psum_scatter(dnorm_part, FFG, scatter_dimension=0, tiled=True).astype(F32)
    ffn_grad = jnp.concatenate([dot(norm_all, dpreact_b, 0, 0), dot(grad_all, activation, 0, 0)], axis=1).astype(B16)
    ffn_grad = lax.psum_scatter(ffn_grad, ("x", "h"), scatter_dimension=0, tiled=True)
    ffn_grad = lax.all_to_all(ffn_grad.reshape(4, rows, 2 * ff_own), ("l", "c"), 0, 0, tiled=True).astype(F32)
    fc_grad = ffn_grad[:, :, :ff_own].transpose(1, 0, 2).reshape(rows, 4 * ff_own)
    proj_grad = ffn_grad[:, :, ff_own:].transpose(0, 2, 1).reshape(4 * ff_own, rows)

    dhidden = grad_wide + norm_backward(dnorm_two, normed_two, inv_two, gain_two)
    dhidden_b = dhidden.astype(B16)
    out_part = dot(attention, dhidden_b, 0, 0).astype(B16).reshape(n_shard, rows, feats)
    row_pad = -rows % 16
    out_part = jnp.pad(out_part, ((0, 0), (0, row_pad), (0, 0))).reshape(-1, feats)
    out_grad_w = lax.psum_scatter(out_part, SHARD, scatter_dimension=0, tiled=True)[:rows]
    out_grad_w = lax.psum(out_grad_w, "y").astype(F32)

    dattention = dot(dhidden_b, w_out, 1, 1).astype(B16)
    dattention = jnp.pad(dattention, ((0, 0), (0, padded - feats))).reshape(slot_len, n_slot, pair).transpose(1, 0, 2)
    dattention = lax.all_to_all(dattention, ROW, 0, 0, tiled=True).reshape(n_slot * slot_len, pair)
    dqkv = attend_back(inv, low, qkv, heads_out, dattention, lse, start3, slot_len, head)
    dqkv_b = dqkv.astype(B16)
    dnorm_one_part = dot(dqkv_b, w_qkv, 1, 1).astype(B16)
    dnorm_one = lax.psum_scatter(dnorm_one_part, ROW, scatter_dimension=0, tiled=True).astype(F32)
    qkv_part = dot(norm_one, dqkv_b, 0, 0).astype(B16)
    qkv_part = lax.psum_scatter(qkv_part, "x", scatter_dimension=0, tiled=True).reshape(n_ctx, rows, 3 * pair)
    qkv_part = lax.all_to_all(qkv_part, CTX, 0, 0, tiled=True)
    qkv_all = lax.all_gather(qkv_part, "y", axis=0, tiled=False)
    qkv_grad = qkv_all.reshape(n_y, n_ctx, rows, 3, pair).transpose(2, 3, 1, 0, 4).reshape(rows, 3, padded)
    qkv_grad = qkv_grad[:, :, :feats].reshape(rows, 3 * feats).astype(F32)

    normed_one, inv_one = norm_forward(own_wide)
    input_grad = dhidden + norm_backward(dnorm_one, normed_one, inv_one, gain_one)

    dq_sum, dv_sum = jnp.sum(dqkv[:, :pair], axis=0), jnp.sum(dqkv[:, 2 * pair :], axis=0)

    def placed(value, width, at):
        return lax.dynamic_update_slice(jnp.zeros((width,), F32), value, (at,))

    vectors = jnp.concatenate(
        [
            jnp.sum(dhidden, axis=0),
            jnp.sum(dnorm_one * normed_one, axis=0),
            jnp.sum(dnorm_one, axis=0),
            jnp.sum(dnorm_two * normed_two, axis=0),
            jnp.sum(dnorm_two, axis=0),
            jnp.sum(grad_wide, axis=0),
            placed(dq_sum, padded, slot_at * pair)[:feats],
            placed(dv_sum, padded, slot_at * pair)[:feats],
            placed(jnp.sum(dpreact, axis=0), n_y * 4 * ff_own, (y_at * 4 + lc_at) * ff_own),
        ]
    )
    vectors = lax.psum(vectors, SHARD + ("y",))
    shard_at = lax.axis_index(SHARD)

    def own(index):
        return lax.dynamic_slice_in_dim(vectors, index * feats + shard_at * rows, rows, 0)

    qv_grad = lax.dynamic_slice_in_dim(vectors, 6 * feats + shard_at * 2 * rows, 2 * rows, 0)
    fc_bias_grad = lax.dynamic_slice_in_dim(vectors, 8 * feats + y_at * 4 * ff_own, 4 * ff_own, 0)
    return (
        block_output[None],
        input_grad[None],
        qkv_grad,
        qv_grad,
        out_grad_w,
        own(0),
        own(1),
        own(2),
        own(3),
        own(4),
        fc_grad,
        fc_bias_grad,
        proj_grad,
        own(5),
    )


def solution(mesh):
    n_x, n_ctx, n_y = (mesh.shape[axis] for axis in ("dp", "context", "tensor"))
    inner = Mesh(mesh.devices.reshape(n_x, n_ctx // 4, 2, 2, n_y), ("x", "h", "l", "c", "y"))
    tokens = P("x", ROW, None)
    shard = P(SHARD)
    shard_rows = P(SHARD, None)
    return jax.shard_map(
        functools.partial(on_device, (n_x, n_ctx, n_y)),
        mesh=inner,
        in_specs=(
            tokens, P("x", None), P("x", None), shard, shard, shard_rows, shard, shard_rows, shard, shard, shard,
            P(SHARD, "y"), P("y"), P("y", SHARD), shard, tokens,
        ),
        out_specs=(
            tokens, tokens, shard_rows, shard, shard_rows, shard, shard, shard, shard, shard,
            P(SHARD, "y"), P("y"), P("y", SHARD), shard,
        ),
        check_vma=False,
    )
```

```python
import functools
import math

import jax
import jax.numpy as jnp
import numpy as np
from jax import lax
from jax.experimental import pallas as pl
from jax.experimental.pallas import tpu as pltpu
from jax.sharding import Mesh
from jax.sharding import PartitionSpec as P

HEADS = 25
DOCS = 8
NORM_EPS = 1e-05
GELU_SCALE = 0.7978845608028654
GELU_CUBE = 0.044715
MASK_FLOOR = -1e30

F32 = jnp.float32
B16 = jnp.bfloat16
BLK = 256
VMEM_LIMIT = 60 * 1024 * 1024

ROW = ("h", "l", "c", "y")
CTX = ("h", "l", "c")
SHARD = ("x", "h", "l", "c")
FFG = ("l", "c", "y")


def gelu_parts(values):
    inner_arg = GELU_SCALE * (values + GELU_CUBE * values * values * values)
    tanh_value = jnp.tanh(inner_arg)
    result = 0.5 * values * (1.0 + tanh_value)
    derivative = 0.5 * (1.0 + tanh_value) + 0.5 * values * (
        1.0 - tanh_value * tanh_value
    ) * GELU_SCALE * (1.0 + 3.0 * GELU_CUBE * values * values)
    return (result, derivative)


def norm_forward(values):
    mean_value = jnp.mean(values, axis=-1, keepdims=True)
    centered = values - mean_value
    inv_sigma = lax.rsqrt(jnp.mean(centered * centered, axis=-1, keepdims=True) + NORM_EPS)
    return (centered * inv_sigma, inv_sigma)


def norm_backward(upstream, normed, inv_sigma, norm_gain):
    scaled = upstream * norm_gain
    return inv_sigma * (
        scaled
        - jnp.mean(scaled, axis=-1, keepdims=True)
        - normed * jnp.mean(scaled * normed, axis=-1, keepdims=True)
    )


def dot(left, right, left_dim, right_dim):
    return lax.dot_general(
        left, right, (((left_dim,), (right_dim,)), ((), ())), preferred_element_type=F32
    )


def sort_slots(inv_ref, src_ref, dst_ref, slot_len, start=0, width=None, factor=None):
    width = src_ref.shape[1] if width is None else width

    def body(piece, carry):
        slot = inv_ref[piece]
        rows = src_ref[pl.ds(pl.multiple_of(slot * slot_len, slot_len), slot_len), start : start + width]
        if factor is not None:
            rows = rows * jnp.asarray(factor, rows.dtype)
        dst_ref[pl.ds(pl.multiple_of(piece * slot_len, slot_len), slot_len), :] = rows
        return carry

    lax.fori_loop(0, src_ref.shape[0] // slot_len, body, 0)


def unsort_block(inv_ref, dst_ref, value, block, slot_len):
    for part in range(BLK // slot_len):
        slot = inv_ref[block * (BLK // slot_len) + part]
        dst_ref[pl.ds(pl.multiple_of(slot * slot_len, slot_len), slot_len), :] = value[
            part * slot_len : (part + 1) * slot_len
        ].astype(dst_ref.dtype)


def block_rows(block):
    return pl.ds(pl.multiple_of(block * BLK, BLK), BLK)


def mask_of(start_row, key_block, query_block, diagonal):
    key_at = key_block * BLK + lax.broadcasted_iota(jnp.int32, (BLK, BLK), 0)
    allowed = key_at >= start_row
    if diagonal:
        query_at = query_block * BLK + lax.broadcasted_iota(jnp.int32, (BLK, BLK), 1)
        allowed = jnp.logical_and(allowed, key_at <= query_at)
    return allowed


def attend_kernel(slot_len, head, inv_ref, low_ref, qkv_ref, start_ref, out_ref, lse_ref, q_s, k_s, vt_s):
    total = qkv_ref.shape[0]
    pair = 2 * head
    sort_slots(inv_ref, qkv_ref, q_s, slot_len, 0, pair, 1.0 / math.sqrt(head))
    sort_slots(inv_ref, qkv_ref, k_s, slot_len, pair, pair)

    def fill(piece, carry):
        slot = inv_ref[piece]
        rows = qkv_ref[pl.ds(pl.multiple_of(slot * slot_len, slot_len), slot_len), 2 * pair :]
        vt_s[:, pl.ds(pl.multiple_of(piece * slot_len, slot_len), slot_len)] = rows.astype(F32).T.astype(B16)
        return carry

    lax.fori_loop(0, total // slot_len, fill, 0)

    def per_query(block, carry):
        queries = q_s[block_rows(block), :]
        start_row = start_ref[block]

        def step(key_block, state, diagonal):
            allowed = mask_of(start_row, key_block, block, diagonal)
            keys = k_s[block_rows(key_block), :]
            values = vt_s[:, block_rows(key_block)]
            fresh = []
            for part in range(2):
                old_max, old_sum, old_acc = state[part]
                cols = slice(part * head, (part + 1) * head)
                scores = dot(keys[:, cols], queries[:, cols], 1, 1)
                scores = jnp.where(allowed, scores, MASK_FLOOR)
                new_max = jnp.maximum(old_max, jnp.max(scores, axis=0, keepdims=True))
                weights = jnp.where(allowed, jnp.exp(scores - new_max), 0.0)
                shrink = jnp.exp(old_max - new_max)
                new_sum = old_sum * shrink + jnp.sum(weights, axis=0, keepdims=True)
                new_acc = old_acc * shrink + dot(values[cols, :], weights.astype(B16), 1, 0)
                fresh.append((new_max, new_sum, new_acc))
            return tuple(fresh)

        first = tuple(
            (
                jnp.full((1, BLK), MASK_FLOOR, F32),
                jnp.zeros((1, BLK), F32),
                jnp.zeros((head, BLK), F32),
            )
            for part in range(2)
        )
        state = lax.fori_loop(low_ref[block], block, lambda j, s: step(j, s, False), first)
        state = step(block, state, True)
        lse_ref[block] = jnp.concatenate([s[0] + jnp.log(s[1]) for s in state], axis=0)
        result = jnp.concatenate([s[2] / s[1] for s in state], axis=0)
        unsort_block(inv_ref, out_ref, result.T, block, slot_len)
        return carry

    lax.fori_loop(0, total // BLK, per_query, 0)


def attend(inv, low, qkv, start3, slot_len, head):
    total = qkv.shape[0]
    vmem = pl.BlockSpec(memory_space=pltpu.VMEM)
    smem = pl.BlockSpec(memory_space=pltpu.SMEM)
    return pl.pallas_call(
        functools.partial(attend_kernel, slot_len, head),
        out_shape=(
            jax.ShapeDtypeStruct((total, 2 * head), B16),
            jax.ShapeDtypeStruct((total // BLK, 2, BLK), F32),
        ),
        in_specs=[smem, smem, vmem, vmem],
        out_specs=(vmem, vmem),
        scratch_shapes=[
            pltpu.VMEM((total, 2 * head), B16),
            pltpu.VMEM((total, 2 * head), B16),
            pltpu.VMEM((2 * head, total), B16),
        ],
        compiler_params=pltpu.CompilerParams(vmem_limit_bytes=VMEM_LIMIT),
        cost_estimate=pl.CostEstimate(
            flops=4 * total * total * head, bytes_accessed=8 * total * head * 2, transcendentals=total * total
        ),
        name="attend",
    )(inv, low, qkv, start3)


def attend_back_kernel(
    slot_len, head, inv_ref, low_ref, qkv_ref, out_ref, grad_ref, lse_ref, start_ref,
    dqkv_ref, q_s, k_s, v_s, kt_s, o_s, g_s, dk_s, dv_s,
):
    total = qkv_ref.shape[0]
    pair = 2 * head
    scale = 1.0 / math.sqrt(head)
    sort_slots(inv_ref, qkv_ref, q_s, slot_len, 0, pair, scale)
    sort_slots(inv_ref, qkv_ref, k_s, slot_len, pair, pair)
    sort_slots(inv_ref, qkv_ref, v_s, slot_len, 2 * pair, pair)
    sort_slots(inv_ref, out_ref, o_s, slot_len)
    sort_slots(inv_ref, grad_ref, g_s, slot_len)

    def fill(block, carry):
        kt_s[:, block_rows(block)] = k_s[block_rows(block), :].astype(F32).T.astype(B16)
        return carry

    lax.fori_loop(0, total // BLK, fill, 0)
    dk_s[...] = jnp.zeros_like(dk_s)
    dv_s[...] = jnp.zeros_like(dv_s)

    def per_query(block, carry):
        queries = q_s[block_rows(block), :]
        grads = g_s[block_rows(block), :]
        start_row = start_ref[block]
        lse = lse_ref[block]
        prod = (grads.astype(F32) * o_s[block_rows(block), :].astype(F32)).T
        delta = [jnp.sum(prod[part * head : (part + 1) * head], axis=0, keepdims=True) for part in range(2)]

        def step(key_block, state, diagonal):
            allowed = mask_of(start_row, key_block, block, diagonal)
            rows = block_rows(key_block)
            keys = k_s[rows, :]
            values = v_s[rows, :]
            flipped = kt_s[:, rows]
            fresh, dks, dvs = [], [], []
            for part in range(2):
                cols = slice(part * head, (part + 1) * head)
                scores = dot(keys[:, cols], queries[:, cols], 1, 1)
                weights = jnp.where(allowed, jnp.exp(scores - lse[part : part + 1]), 0.0)
                dprob = dot(values[:, cols], grads[:, cols], 1, 1)
                dscore = (weights * (dprob - delta[part])).astype(B16)
                dvs.append(dot(weights.astype(B16), grads[:, cols], 1, 0))
                dks.append(dot(dscore, queries[:, cols], 1, 0))
                fresh.append(state[part] + dot(flipped[cols, :], dscore, 1, 0))
            dk_s[rows, :] += jnp.concatenate(dks, axis=1)
            dv_s[rows, :] += jnp.concatenate(dvs, axis=1)
            return tuple(fresh)

        state = (jnp.zeros((head, BLK), F32), jnp.zeros((head, BLK), F32))
        state = lax.fori_loop(low_ref[block], block, lambda j, s: step(j, s, False), state)
        state = step(block, state, True)
        dq = jnp.concatenate(state, axis=0).T * scale
        for part in range(BLK // slot_len):
            slot = inv_ref[block * (BLK // slot_len) + part]
            dqkv_ref[pl.ds(pl.multiple_of(slot * slot_len, slot_len), slot_len), 0:pair] = dq[
                part * slot_len : (part + 1) * slot_len
            ]
        return carry

    lax.fori_loop(0, total // BLK, per_query, 0)

    def give(piece, carry):
        slot = inv_ref[piece]
        rows = pl.ds(pl.multiple_of(slot * slot_len, slot_len), slot_len)
        held = pl.ds(pl.multiple_of(piece * slot_len, slot_len), slot_len)
        dqkv_ref[rows, pair : 2 * pair] = dk_s[held, :]
        dqkv_ref[rows, 2 * pair :] = dv_s[held, :]
        return carry

    lax.fori_loop(0, total // slot_len, give, 0)


def attend_back(inv, low, qkv, out, grad, lse, start3, slot_len, head):
    total = qkv.shape[0]
    pair = 2 * head
    vmem = pl.BlockSpec(memory_space=pltpu.VMEM)
    smem = pl.BlockSpec(memory_space=pltpu.SMEM)
    held = pltpu.VMEM((total, pair), B16)
    return pl.pallas_call(
        functools.partial(attend_back_kernel, slot_len, head),
        out_shape=jax.ShapeDtypeStruct((total, 3 * pair), F32),
        in_specs=[smem, smem] + [vmem] * 5,
        out_specs=vmem,
        scratch_shapes=[
            held, held, held, pltpu.VMEM((pair, total), B16), held, held,
            pltpu.VMEM((total, pair), F32), pltpu.VMEM((total, pair), F32),
        ],
        compiler_params=pltpu.CompilerParams(vmem_limit_bytes=VMEM_LIMIT),
        cost_estimate=pl.CostEstimate(
            flops=10 * total * total * head, bytes_accessed=30 * total * head * 2, transcendentals=total * total
        ),
        name="attend_back",
    )(inv, low, qkv, out, grad, lse, start3)


class Place:
    def __init__(self, whole_line):
        self.x, self.h, self.l, self.c, self.y = (lax.axis_index(a) for a in ("x", "h", "l", "c", "y"))
        self.whole_line = whole_line
        self.n_z = 2 * lax.axis_size("h") if whole_line else 2
        self.z = self.h * 2 + self.l if whole_line else self.l
        self.ctx = self.z * 2 + self.c
        self.slot = self.ctx * 2 + self.y

    def at_z(self, z):
        return {"h": z // 2, "l": lax.rem(z, 2)} if self.whole_line else {"l": z}

    def at_ctx(self, k):
        return dict(self.at_z(k // 2), c=lax.rem(k, 2))

    def at_slot(self, s):
        return dict(self.at_ctx(s // 2), y=lax.rem(s, 2))

    def far_z(self):
        order = []
        for step in range(1, self.n_z // 2 + 1):
            order += [step] if 2 * step == self.n_z else [step, self.n_z - step]
        return [lax.rem(self.z + step, self.n_z) for step in order]

    def slot_of(self, z, c, y):
        return (z * 2 + c) * 2 + y


class Copies:
    def __init__(self, sems):
        self.sems = sems
        self.begun = []

    def send(self, src, dst, recv, peer):
        at = len(self.begun)
        copy = pltpu.make_async_remote_copy(
            src_ref=src,
            dst_ref=dst,
            send_sem=self.sems.at[at],
            recv_sem=recv,
            device_id=peer,
            device_id_type=pl.DeviceIdType.MESH,
        )
        copy.start()
        self.begun.append(copy.wait_send)

    def local(self, src, dst, sem=None):
        copy = pltpu.make_async_copy(src, dst, self.sems.at[len(self.begun)] if sem is None else sem)
        copy.start()
        self.begun.append(copy.wait if sem is None else (lambda: None))
        return copy

    def arrived(self, dst, recv, peer):
        pltpu.make_async_remote_copy(
            src_ref=dst,
            dst_ref=dst,
            send_sem=self.sems.at[0],
            recv_sem=recv,
            device_id=peer,
            device_id_type=pl.DeviceIdType.MESH,
        ).wait_recv()

    def finish(self):
        for wait in self.begun:
            wait()


def meet(peers):
    barrier = pltpu.get_barrier_semaphore()
    for peer in peers:
        pl.semaphore_signal(barrier, inc=1, device_id=peer, device_id_type=pl.DeviceIdType.MESH)
    pl.semaphore_wait(barrier, len(peers))


def others(me, count):
    return [lax.rem(me + step, count) for step in range(1, count)]


ANY = pl.BlockSpec(memory_space=pl.ANY)
IN_VMEM = pl.BlockSpec(memory_space=pltpu.VMEM)


def dma_sems(*counts):
    return [pltpu.SemaphoreType.DMA((count,)) for count in counts]


def comm_params(collective_id):
    return pltpu.CompilerParams(
        collective_id=collective_id, has_side_effects=True, vmem_limit_bytes=VMEM_LIMIT
    )


def gather_begin(place, own, out, copies, recv):
    peer_y, peer_c = {"y": 1 - place.y}, {"c": 1 - place.c}
    copies.local(own, out.at[place.slot])
    for z in place.far_z():
        copies.send(own, out.at[place.slot], recv.at[place.slot], place.at_z(z))
    copies.send(own, out.at[place.slot], recv.at[place.slot], peer_y)
    copies.send(own, out.at[place.slot], recv.at[place.slot], peer_c)


def gather_middle(place, out, copies, recv):
    peer_y, peer_c = {"y": 1 - place.y}, {"c": 1 - place.c}
    for z in place.far_z():
        at = place.slot_of(z, place.c, place.y)
        copies.arrived(out.at[at], recv.at[at], place.at_z(z))
        copies.send(out.at[at], out.at[at], recv.at[at], peer_y)
        copies.send(out.at[at], out.at[at], recv.at[at], peer_c)
    for z in [place.z] + place.far_z():
        at = place.slot_of(z, place.c, 1 - place.y)
        copies.arrived(out.at[at], recv.at[at], peer_y)
        copies.send(out.at[at], out.at[at], recv.at[at], peer_c)


def gather_end(place, out, copies, recv):
    for z in [place.z] + place.far_z():
        for y in (place.y, 1 - place.y):
            at = place.slot_of(z, 1 - place.c, y)
            copies.arrived(out.at[at], recv.at[at], {"c": 1 - place.c})


def gather_copies(n_z):
    return 4 * n_z


def group_gather_kernel(own, out, send, recv):
    place = Place(False)
    copies = Copies(send)
    meet([place.at_z(1 - place.z), {"y": 1 - place.y}, {"c": 1 - place.c}])
    gather_begin(place, own, out, copies, recv)
    gather_middle(place, out, copies, recv)
    gather_end(place, out, copies, recv)
    copies.finish()


def group_gather(value, collective_id):
    return pl.pallas_call(
        group_gather_kernel,
        out_shape=jax.ShapeDtypeStruct((8,) + value.shape, value.dtype),
        in_specs=[ANY],
        out_specs=ANY,
        scratch_shapes=dma_sems(gather_copies(2), 8),
        compiler_params=comm_params(collective_id),
        name="group_gather",
    )(value)


def opening_kernel(own, blocks, out, blocks_all, send, recv, recv_w):
    place = Place(True)
    n_ctx = blocks.shape[0]
    copies = Copies(send)
    peer_x = {"x": 1 - place.x}
    far_ctx = others(place.ctx, n_ctx)
    meet([place.at_ctx(k) for k in far_ctx] + [{"y": 1 - place.y}, peer_x])
    mine = blocks_all.at[place.x, place.ctx]

    def sem_w(x, k):
        return recv_w.at[x * n_ctx + k]

    gather_begin(place, own, out, copies, recv)
    for k in far_ctx:
        copies.send(blocks.at[k], mine, sem_w(place.x, place.ctx), place.at_ctx(k))
    copies.local(blocks.at[place.ctx], mine)
    copies.send(blocks.at[place.ctx], mine, sem_w(place.x, place.ctx), peer_x)
    gather_middle(place, out, copies, recv)
    for k in far_ctx:
        block = blocks_all.at[place.x, k]
        copies.arrived(block, sem_w(place.x, k), place.at_ctx(k))
        copies.send(block, block, sem_w(place.x, k), peer_x)
    gather_end(place, out, copies, recv)
    for k in [place.ctx] + far_ctx:
        copies.arrived(blocks_all.at[1 - place.x, k], sem_w(1 - place.x, k), peer_x)
    copies.finish()


def opening(own, blocks):
    n_ctx = blocks.shape[0]
    return pl.pallas_call(
        opening_kernel,
        out_shape=(
            jax.ShapeDtypeStruct((2 * n_ctx,) + own.shape, own.dtype),
            jax.ShapeDtypeStruct((2,) + blocks.shape, blocks.dtype),
        ),
        in_specs=[ANY, ANY],
        out_specs=(ANY, ANY),
        scratch_shapes=dma_sems(gather_copies(n_ctx // 2) + 2 * n_ctx, 2 * n_ctx, 2 * n_ctx),
        compiler_params=comm_params(1),
        name="opening",
    )(own, blocks)


def to_tokens_kernel(src, dst, send, recv):
    place = Place(True)
    copies = Copies(send)
    count, width = src.shape[0], src.shape[2]
    far = others(place.slot, count)
    meet([place.at_slot(s) for s in far])

    def columns(s):
        return dst.at[:, pl.ds(pl.multiple_of(s * width, width), width)]

    for s in far:
        copies.send(src.at[s], columns(place.slot), recv.at[place.slot], place.at_slot(s))
    copies.local(src.at[place.slot], columns(place.slot))
    for s in far:
        copies.arrived(columns(s), recv.at[s], place.at_slot(s))
    copies.finish()


def to_tokens(value):
    count, tokens, width = value.shape
    return pl.pallas_call(
        to_tokens_kernel,
        out_shape=jax.ShapeDtypeStruct((tokens, count * width), value.dtype),
        in_specs=[ANY],
        out_specs=ANY,
        scratch_shapes=dma_sems(count, count),
        compiler_params=comm_params(2),
        name="to_tokens",
    )(value)


def to_heads_kernel(src, dst, send, recv):
    place = Place(True)
    copies = Copies(send)
    count, width = dst.shape[0], dst.shape[2]
    far = others(place.slot, count)
    meet([place.at_slot(s) for s in far])

    def columns(s):
        return src.at[:, pl.ds(pl.multiple_of(s * width, width), width)]

    for s in far:
        copies.send(columns(s), dst.at[place.slot], recv.at[place.slot], place.at_slot(s))
    copies.local(columns(place.slot), dst.at[place.slot])
    for s in far:
        copies.arrived(dst.at[s], recv.at[s], place.at_slot(s))
    copies.finish()


def to_heads(value, count):
    tokens, width = value.shape[0], value.shape[1] // count
    return pl.pallas_call(
        to_heads_kernel,
        out_shape=jax.ShapeDtypeStruct((count, tokens, width), value.dtype),
        in_specs=[ANY],
        out_specs=ANY,
        scratch_shapes=dma_sems(count, count),
        compiler_params=comm_params(3),
        name="to_heads",
    )(value)


class Scatter:
    def __init__(self, place, part, held, from_c, from_y, from_z, out, copies, loads, rc, ry, rz):
        self.__dict__.update(locals())

    def order(self):
        return self.place.far_z() + [self.place.z]

    def begin(self):
        p = self.place
        for y in (1 - p.y, p.y):
            for z in self.order():
                at = z * 2 + y
                self.copies.send(
                    self.part.at[p.slot_of(z, 1 - p.c, y)], self.from_c.at[at], self.rc.at[at], {"c": 1 - p.c}
                )
                self.copies.local(self.part.at[p.slot_of(z, p.c, y)], self.held.at[at], self.loads.at[at])

    def add_c(self, z, y):
        at = z * 2 + y
        self.copies.arrived(self.from_c.at[at], self.rc.at[at], {"c": 1 - self.place.c})
        pltpu.make_async_copy(self.held.at[at], self.held.at[at], self.loads.at[at]).wait()
        self.from_c[at] = self.from_c[at] + self.held[at]

    def over_c_far(self):
        p = self.place
        for z in self.order():
            self.add_c(z, 1 - p.y)
            self.copies.send(self.from_c.at[z * 2 + 1 - p.y], self.from_y.at[z], self.ry.at[z], {"y": 1 - p.y})

    def over_c_near(self):
        for z in self.order():
            self.add_c(z, self.place.y)

    def over_y(self):
        p = self.place
        for z in self.order():
            self.copies.arrived(self.from_y.at[z], self.ry.at[z], {"y": 1 - p.y})
            self.from_y[z] = self.from_y[z] + self.from_c[z * 2 + p.y]
            if z is not p.z:
                self.copies.send(self.from_y.at[z], self.from_z.at[p.z], self.rz.at[p.z], p.at_z(z))

    def over_z(self):
        p = self.place
        total = self.from_y[p.z].astype(F32)
        for z in p.far_z():
            self.copies.arrived(self.from_z.at[z], self.rz.at[z], p.at_z(z))
            total = total + self.from_z[z].astype(F32)
        self.out[...] = total


def scatter_scratch(n_z, block):
    return [
        pltpu.VMEM((2 * n_z,) + block, B16),
        pltpu.VMEM((2 * n_z,) + block, B16),
        pltpu.VMEM((n_z,) + block, B16),
        pltpu.VMEM((n_z,) + block, B16),
    ]


def scatter_sems(n_z, more=0):
    return dma_sems(6 * n_z + more, 2 * n_z, 2 * n_z, n_z, n_z)


def group_scatter_kernel(part, out, held, from_c, from_y, from_z, send, loads, rc, ry, rz):
    place = Place(False)
    copies = Copies(send)
    meet([place.at_z(1 - place.z), {"y": 1 - place.y}, {"c": 1 - place.c}])
    sums = Scatter(place, part, held, from_c, from_y, from_z, out, copies, loads, rc, ry, rz)
    sums.begin()
    sums.over_c_far()
    sums.over_c_near()
    sums.over_y()
    sums.over_z()
    copies.finish()


def group_scatter(part, collective_id):
    block = part.shape[1:]
    return pl.pallas_call(
        group_scatter_kernel,
        out_shape=jax.ShapeDtypeStruct(block, F32),
        in_specs=[ANY],
        out_specs=IN_VMEM,
        scratch_shapes=scatter_scratch(2, block) + scatter_sems(2),
        compiler_params=comm_params(collective_id),
        name="group_scatter",
    )(part)


def closing_kernel(
    part, grads, out, grads_out, held, from_c, from_y, from_z, own_x, from_x,
    send, loads, rc, ry, rz, load_x, rx, rk, rg,
):
    place = Place(True)
    n_ctx = grads.shape[1]
    copies = Copies(send)
    far_ctx = others(place.ctx, n_ctx)
    peer_x, peer_y = {"x": 1 - place.x}, {"y": 1 - place.y}
    meet([place.at_ctx(k) for k in far_ctx] + [peer_y, peer_x])
    sums = Scatter(place, part, held, from_c, from_y, from_z, out, copies, loads, rc, ry, rz)
    sums.begin()
    for k in far_ctx + [place.ctx]:
        copies.send(grads.at[1 - place.x, k], from_x.at[k], rx.at[k], peer_x)
        copies.local(grads.at[place.x, k], own_x.at[k], load_x.at[k])
    sums.over_c_far()
    mine = grads_out.at[place.y, place.ctx]
    for k in far_ctx + [place.ctx]:
        copies.arrived(from_x.at[k], rx.at[k], peer_x)
        pltpu.make_async_copy(own_x.at[k], own_x.at[k], load_x.at[k]).wait()
        from_x[k] = from_x[k] + own_x[k]
        if k is not place.ctx:
            copies.send(from_x.at[k], mine, rk.at[place.ctx], place.at_ctx(k))
    copies.local(from_x.at[place.ctx], mine)
    copies.send(from_x.at[place.ctx], mine, rg.at[place.ctx], peer_y)
    sums.over_c_near()
    sums.over_y()
    for k in far_ctx:
        block = grads_out.at[place.y, k]
        copies.arrived(block, rk.at[k], place.at_ctx(k))
        copies.send(block, block, rg.at[k], peer_y)
    sums.over_z()
    for k in [place.ctx] + far_ctx:
        copies.arrived(grads_out.at[1 - place.y, k], rg.at[k], peer_y)
    copies.finish()


def closing(part, grads):
    block = part.shape[1:]
    n_ctx = grads.shape[1]
    n_z = n_ctx // 2
    piece = grads.shape[1:]
    return pl.pallas_call(
        closing_kernel,
        out_shape=(jax.ShapeDtypeStruct(block, F32), jax.ShapeDtypeStruct((2,) + piece, B16)),
        in_specs=[ANY, ANY],
        out_specs=(IN_VMEM, ANY),
        scratch_shapes=scatter_scratch(n_z, block)
        + [pltpu.VMEM(piece, B16), pltpu.VMEM(piece, B16)]
        + scatter_sems(n_z, 5 * n_ctx)
        + dma_sems(n_ctx, n_ctx, n_ctx, n_ctx),
        compiler_params=comm_params(4),
        name="closing",
    )(part, grads)


def vectors_kernel(src, own_out, ff_out, from_all, half, from_y, send, recv, ry):
    place = Place(True)
    count = src.shape[0]
    n_ctx = count // 2
    copies = Copies(send)
    me = place.x * n_ctx + place.ctx
    far = others(me, count)
    peer_y = {"y": 1 - place.y}

    def peer(k):
        return dict(place.at_ctx(lax.rem(k, n_ctx)), x=k // n_ctx)

    meet([peer(k) for k in far] + [peer_y])
    for k in far:
        copies.send(src.at[k], from_all.at[me], recv.at[me], peer(k))
    from_all[me] = src[me]
    for k in far:
        copies.arrived(from_all.at[k], recv.at[k], peer(k))
    total = from_all[0, 0:8, :]
    for k in range(1, count):
        total = total + from_all[k, 0:8, :]
    half[...] = total
    copies.send(half, from_y, ry.at[0], peer_y)
    for part in range(4):
        total = from_all[part, 8:16, :]
        for k in range(part + 4, count, 4):
            total = total + from_all[k, 8:16, :]
        ff_out[part] = total
    copies.arrived(from_y, ry.at[0], peer_y)
    own_out[...] = half[...] + from_y[...]
    copies.finish()


def vectors_sum(value):
    count = value.shape[0]
    flat = jax.ShapeDtypeStruct((8, 128), F32)
    return pl.pallas_call(
        vectors_kernel,
        out_shape=(flat, jax.ShapeDtypeStruct((4, 8, 128), F32)),
        in_specs=[IN_VMEM],
        out_specs=(IN_VMEM, IN_VMEM),
        scratch_shapes=[
            pltpu.VMEM(value.shape, F32),
            pltpu.VMEM((8, 128), F32),
            pltpu.VMEM((8, 128), F32),
        ]
        + dma_sems(count + 1, count, 1),
        compiler_params=comm_params(5),
        name="vectors_sum",
    )(value)


def shift_perm(count, step):
    return [(i, (i + step) % count) for i in range(count)]


def spread(blocks, n_h):
    lc, h, x = lax.axis_index(("l", "c")), lax.axis_index("h"), lax.axis_index("x")

    def pick(value, at):
        return lax.dynamic_index_in_dim(value, at, 0, False)

    whole = jnp.zeros((2, n_h) + blocks.shape, blocks.dtype)
    mine = jnp.zeros(blocks.shape, blocks.dtype)
    mine = lax.dynamic_update_index_in_dim(mine, pick(blocks, lc), lc, 0)
    for step in range(1, 4):
        got = lax.ppermute(pick(blocks, lc ^ step), ("l", "c"), [(i, i ^ step) for i in range(4)])
        mine = lax.dynamic_update_index_in_dim(mine, got, lc ^ step, 0)
    line = jnp.zeros((n_h,) + blocks.shape, blocks.dtype)
    line = lax.dynamic_update_index_in_dim(line, mine, h, 0)
    for step in range(1, n_h):
        got = lax.ppermute(mine, "h", shift_perm(n_h, step))
        line = lax.dynamic_update_index_in_dim(line, got, lax.rem(h + n_h - step, n_h), 0)
    whole = lax.dynamic_update_index_in_dim(whole, line, x, 0)
    got = lax.ppermute(line, "x", shift_perm(2, 1))
    return lax.dynamic_update_index_in_dim(whole, got, 1 - x, 0)


def unspread(grad, n_h):
    lc, h, x = lax.axis_index(("l", "c")), lax.axis_index("h"), lax.axis_index("x")

    def pick(value, at):
        return lax.dynamic_index_in_dim(value, at, 0, False)

    line = pick(grad, x) + lax.ppermute(pick(grad, 1 - x), "x", shift_perm(2, 1))
    mine = pick(line, h)
    for step in range(1, n_h):
        mine = mine + lax.ppermute(pick(line, lax.rem(h + step, n_h)), "h", shift_perm(n_h, step))
    out = lax.dynamic_update_index_in_dim(jnp.zeros_like(mine), pick(mine, lc), lc, 0)
    for step in range(1, 4):
        got = lax.ppermute(pick(mine, lc ^ step), ("l", "c"), [(i, i ^ step) for i in range(4)])
        out = lax.dynamic_update_index_in_dim(out, got, lc ^ step, 0)
    return out


def on_device(
    sizes, block_input, segment_ids, slot_order, first_gain, first_shift, qkv_weight, qv_bias, out_weight, out_bias,
    second_gain, second_shift, fc_weight, fc_bias, proj_weight, proj_bias, out_grad,
):
    n_x, n_ctx, n_y = sizes
    n_slot = n_ctx * n_y
    n_shard = n_x * n_ctx
    n_h = n_ctx // 4
    slot_len, feats = block_input.shape[1:]
    head = feats // HEADS
    pair = 2 * head
    rows = qkv_weight.shape[0]
    ff_own = fc_weight.shape[1] // 4
    padded = n_slot * pair
    y_at = lax.axis_index("y")
    ctx_at = lax.axis_index(CTX)
    slot_at = lax.axis_index(ROW)
    lc_at = lax.axis_index(("l", "c"))

    def gather(value, axes):
        return lax.all_gather(value, axes, axis=0, tiled=True)

    small = jnp.concatenate(
        [
            first_gain, first_shift, out_bias, second_gain, second_shift, proj_bias, qv_bias,
        ]
    )
    row_pad = -rows % 16
    packed = jnp.pad(qkv_weight.reshape(rows, 3, feats), ((0, 0), (0, 0), (0, padded - feats)))
    packed = lax.dynamic_index_in_dim(packed.reshape(rows, 3, n_ctx, n_y, pair), y_at, 3, False)
    packed = packed.transpose(2, 0, 1, 3).reshape(n_ctx, rows, 3 * pair)
    small = jnp.pad(small, (0, row_pad * 3 * pair - small.shape[0])).reshape(1, row_pad, 3 * pair)
    packed = jnp.concatenate([packed, jnp.broadcast_to(small, (n_ctx, row_pad, 3 * pair))], axis=1)
    all_input, packed = opening(block_input[0], packed)
    all_input = all_input.reshape(n_slot * slot_len, feats)
    packed = packed.reshape(n_shard, rows + row_pad, 3 * pair)
    w_qkv = packed[:, :rows].reshape(feats, 3 * pair)
    smalls = packed[:, rows:].reshape(n_shard, -1)[:, : 8 * rows].astype(F32)
    gain_one, shift_one, bias_out, gain_two, shift_two, bias_proj = [
        smalls[:, i * rows : (i + 1) * rows].reshape(feats) for i in range(6)
    ]
    bias_qv = smalls[:, 6 * rows :].reshape(2, feats)
    bias_pair = lax.dynamic_slice_in_dim(
        jnp.pad(bias_qv, ((0, 0), (0, padded - feats))), slot_at * pair, pair, 1
    )
    bias_qkv = jnp.concatenate([bias_pair[0], jnp.zeros((pair,), F32), bias_pair[1]])

    w_fc = spread(fc_weight.reshape(rows, 4, ff_own).transpose(1, 0, 2), n_h).reshape(feats, ff_own)
    w_proj = spread(proj_weight.reshape(4, ff_own, rows).transpose(0, 2, 1), n_h).reshape(feats, ff_own)
    w_out = gather(out_weight, SHARD)
    b_fc = lax.dynamic_slice_in_dim(fc_bias, lc_at * ff_own, ff_own, 0).astype(F32)

    order = slot_order[0]
    pieces = jnp.arange(n_slot, dtype=jnp.int32)
    inv = jnp.sum(jnp.where(order[None, :] == pieces[:, None], pieces[None, :], 0), axis=1).astype(jnp.int32)
    segs = jnp.take(segment_ids[0].reshape(n_slot, slot_len), inv, axis=0).reshape(-1)
    docs = jnp.arange(DOCS, dtype=jnp.int32)
    counts = jnp.sum((segs[None, :] == docs[:, None]).astype(jnp.int32), axis=1)
    starts = jnp.sum(jnp.where(segs[None, :] > docs[:, None], counts[:, None], 0), axis=0).astype(jnp.int32)
    start3 = starts.reshape(-1, 1, BLK)
    low = start3[:, 0, 0] // BLK

    own_input = block_input[0]
    own_wide = own_input.astype(F32)
    normed_all, unused = norm_forward(all_input.astype(F32))
    norm_one = (normed_all * gain_one + shift_one).astype(B16)
    qkv = (dot(norm_one, w_qkv, 1, 0) + bias_qkv).astype(B16)
    heads_out, lse = attend(inv, low, qkv, start3, slot_len, head)
    attention = to_tokens(heads_out.reshape(n_slot, slot_len, pair))[:, :feats]
    hidden = own_wide + dot(attention, w_out, 1, 0) + bias_out
    normed_two, inv_two = norm_forward(hidden)
    norm_two = (normed_two * gain_two + shift_two).astype(B16)
    grad_own = out_grad[0]
    grad_wide = grad_own.astype(F32)
    grad_all = gather(grad_own, FFG)
    norm_all = group_gather(norm_two, 6).reshape(-1, feats)
    preact = dot(norm_all, w_fc, 1, 0) + b_fc
    activated, derivative = gelu_parts(preact)
    activation = activated.astype(B16)
    mlp_part = dot(activation, w_proj, 1, 1).astype(B16)
    mlp = lax.psum_scatter(mlp_part, FFG, scatter_dimension=0, tiled=True).astype(F32)
    block_output = hidden + mlp + bias_proj

    dpreact = dot(grad_all, w_proj, 1, 0) * derivative
    dpreact_b = dpreact.astype(B16)
    dnorm_part = dot(dpreact_b, w_fc, 1, 1).astype(B16)
    dnorm_two = group_scatter(dnorm_part.reshape(8, slot_len, feats), 7)
    ffn_shape = (n_x, n_h, 4, rows, ff_own)
    proj_grad = unspread(dot(grad_all, activation, 0, 0).astype(B16).reshape(ffn_shape), n_h)
    proj_grad = proj_grad.transpose(0, 2, 1).reshape(4 * ff_own, rows).astype(F32)
    fc_grad = unspread(dot(norm_all, dpreact_b, 0, 0).astype(B16).reshape(ffn_shape), n_h)
    fc_grad = fc_grad.transpose(1, 0, 2).reshape(rows, 4 * ff_own).astype(F32)

    dhidden = grad_wide + norm_backward(dnorm_two, normed_two, inv_two, gain_two)
    dhidden_b = dhidden.astype(B16)
    out_part = dot(attention, dhidden_b, 0, 0).astype(B16).reshape(n_shard, rows, feats)
    out_part = jnp.pad(out_part, ((0, 0), (0, row_pad), (0, 0))).reshape(-1, feats)
    out_grad_w = lax.psum_scatter(out_part, SHARD, scatter_dimension=0, tiled=True)[:rows]
    out_grad_w = lax.psum(out_grad_w, "y").astype(F32)

    dattention = dot(dhidden_b, w_out, 1, 1).astype(B16)
    dattention = jnp.pad(dattention, ((0, 0), (0, padded - feats)))
    dattention = to_heads(dattention, n_slot).reshape(n_slot * slot_len, pair)
    dqkv = attend_back(inv, low, qkv, heads_out, dattention, lse, start3, slot_len, head)
    dqkv_b = dqkv.astype(B16)
    dnorm_one_part = dot(dqkv_b, w_qkv, 1, 1).astype(B16)
    qkv_part = dot(norm_one, dqkv_b, 0, 0).astype(B16).reshape(n_x, n_ctx, rows, 3 * pair)
    qkv_part = jnp.pad(qkv_part, ((0, 0), (0, 0), (0, row_pad), (0, 0)))
    dnorm_one, qkv_all = closing(dnorm_one_part.reshape(n_slot, slot_len, feats), qkv_part)
    qkv_all = qkv_all[:, :, :rows].reshape(n_y, n_ctx, rows, 3, pair)
    qkv_grad = qkv_all.transpose(2, 3, 1, 0, 4).reshape(rows, 3, padded)
    qkv_grad = qkv_grad[:, :, :feats].reshape(rows, 3 * feats).astype(F32)

    normed_one, inv_one = norm_forward(own_wide)
    input_grad = dhidden + norm_backward(dnorm_one, normed_one, inv_one, gain_one)

    dq_sum, dv_sum = jnp.sum(dqkv[:, :pair], axis=0), jnp.sum(dqkv[:, 2 * pair :], axis=0)

    def placed(value, width, at):
        return lax.dynamic_update_slice(jnp.zeros((width,), F32), value, (at,))

    vectors = jnp.concatenate(
        [
            jnp.sum(dhidden, axis=0),
            jnp.sum(dnorm_one * normed_one, axis=0),
            jnp.sum(dnorm_one, axis=0),
            jnp.sum(dnorm_two * normed_two, axis=0),
            jnp.sum(dnorm_two, axis=0),
            jnp.sum(grad_wide, axis=0),
        ]
    )
    qv_sums = jnp.concatenate(
        [placed(dq_sum, padded, slot_at * pair)[:feats], placed(dv_sum, padded, slot_at * pair)[:feats]]
    )
    vectors = jnp.concatenate(
        [
            vectors.reshape(6, n_shard, rows).transpose(1, 0, 2).reshape(n_shard, 6 * rows),
            qv_sums.reshape(n_shard, 2 * rows),
            jnp.zeros((n_shard, 1024 - 8 * rows), F32),
            jnp.broadcast_to(jnp.sum(dpreact, axis=0)[None], (n_shard, ff_own)),
            jnp.zeros((n_shard, 1024 - ff_own), F32),
        ],
        axis=1,
    )
    owned, ff_sums = vectors_sum(vectors.reshape(n_shard, 16, 128))
    owned = owned.reshape(1024)
    fc_bias_grad = ff_sums.reshape(4, 1024)[:, :ff_own].reshape(4 * ff_own)
    qv_grad = owned[6 * rows : 8 * rows]

    def own(index):
        return owned[index * rows : (index + 1) * rows]

    return (
        block_output[None],
        input_grad[None],
        qkv_grad,
        qv_grad,
        out_grad_w,
        own(0),
        own(1),
        own(2),
        own(3),
        own(4),
        fc_grad,
        fc_bias_grad,
        proj_grad,
        own(5),
    )


def solution(mesh):
    n_x, n_ctx, n_y = (mesh.shape[axis] for axis in ("dp", "context", "tensor"))
    inner = Mesh(mesh.devices.reshape(n_x, n_ctx // 4, 2, 2, n_y), ("x", "h", "l", "c", "y"))
    tokens = P("x", ROW, None)
    shard = P(SHARD)
    shard_rows = P(SHARD, None)
    return jax.shard_map(
        functools.partial(on_device, (n_x, n_ctx, n_y)),
        mesh=inner,
        in_specs=(
            tokens, P("x", None), P("x", None), shard, shard, shard_rows, shard, shard_rows, shard, shard, shard,
            P(SHARD, "y"), P("y"), P("y", SHARD), shard, tokens,
        ),
        out_specs=(
            tokens, tokens, shard_rows, shard, shard_rows, shard, shard, shard, shard, shard,
            P(SHARD, "y"), P("y"), P("y", SHARD), shard,
        ),
        check_vma=False,
    )
```

```python
import functools
import math

import jax
import jax.numpy as jnp
import numpy as np
from jax import lax
from jax.experimental import pallas as pl
from jax.experimental.pallas import tpu as pltpu
from jax.sharding import Mesh
from jax.sharding import PartitionSpec as P

HEADS = 25
DOCS = 8
NORM_EPS = 1e-05
GELU_SCALE = 0.7978845608028654
GELU_CUBE = 0.044715
MASK_FLOOR = -1e30

F32 = jnp.float32
B16 = jnp.bfloat16
BLK = 256
VMEM_LIMIT = 60 * 1024 * 1024

ROW = ("h", "l", "c", "y")
CTX = ("h", "l", "c")
SHARD = ("x", "h", "l", "c")
FFG = ("l", "c", "y")


def gelu_parts(values):
    inner_arg = GELU_SCALE * (values + GELU_CUBE * values * values * values)
    tanh_value = jnp.tanh(inner_arg)
    result = 0.5 * values * (1.0 + tanh_value)
    derivative = 0.5 * (1.0 + tanh_value) + 0.5 * values * (
        1.0 - tanh_value * tanh_value
    ) * GELU_SCALE * (1.0 + 3.0 * GELU_CUBE * values * values)
    return (result, derivative)


def norm_forward(values, mask, feats):
    mean_value = jnp.sum(values, axis=-1, keepdims=True) / feats
    centered = (values - mean_value) * mask
    inv_sigma = lax.rsqrt(jnp.sum(centered * centered, axis=-1, keepdims=True) / feats + NORM_EPS)
    return (centered * inv_sigma, inv_sigma)


def norm_backward(upstream, normed, inv_sigma, norm_gain, feats):
    scaled = upstream * norm_gain
    return inv_sigma * (
        scaled
        - jnp.sum(scaled, axis=-1, keepdims=True) / feats
        - normed * (jnp.sum(scaled * normed, axis=-1, keepdims=True) / feats)
    )


def dot(left, right, left_dim, right_dim):
    return lax.dot_general(
        left, right, (((left_dim,), (right_dim,)), ((), ())), preferred_element_type=F32
    )


def sort_slots(inv_ref, src_ref, dst_ref, slot_len, start=0, width=None, factor=None):
    width = src_ref.shape[1] if width is None else width

    def body(piece, carry):
        slot = inv_ref[piece]
        rows = src_ref[pl.ds(pl.multiple_of(slot * slot_len, slot_len), slot_len), start : start + width]
        if factor is not None:
            rows = rows * jnp.asarray(factor, rows.dtype)
        dst_ref[pl.ds(pl.multiple_of(piece * slot_len, slot_len), slot_len), :] = rows
        return carry

    lax.fori_loop(0, src_ref.shape[0] // slot_len, body, 0)


def unsort_block(inv_ref, dst_ref, value, block, slot_len):
    for part in range(BLK // slot_len):
        slot = inv_ref[block * (BLK // slot_len) + part]
        dst_ref[pl.ds(pl.multiple_of(slot * slot_len, slot_len), slot_len), :] = value[
            part * slot_len : (part + 1) * slot_len
        ].astype(dst_ref.dtype)


def block_rows(block):
    return pl.ds(pl.multiple_of(block * BLK, BLK), BLK)


def mask_of(start_row, key_block, query_block, diagonal):
    key_at = key_block * BLK + lax.broadcasted_iota(jnp.int32, (BLK, BLK), 0)
    allowed = key_at >= start_row
    if diagonal:
        query_at = query_block * BLK + lax.broadcasted_iota(jnp.int32, (BLK, BLK), 1)
        allowed = jnp.logical_and(allowed, key_at <= query_at)
    return allowed


def attend_kernel(slot_len, head, inv_ref, low_ref, qkv_ref, start_ref, out_ref, lse_ref, q_s, k_s, vt_s):
    total = qkv_ref.shape[0]
    pair = 2 * head
    sort_slots(inv_ref, qkv_ref, q_s, slot_len, 0, pair, 1.0 / math.sqrt(head))
    sort_slots(inv_ref, qkv_ref, k_s, slot_len, pair, pair)

    def fill(piece, carry):
        slot = inv_ref[piece]
        rows = qkv_ref[pl.ds(pl.multiple_of(slot * slot_len, slot_len), slot_len), 2 * pair :]
        vt_s[:, pl.ds(pl.multiple_of(piece * slot_len, slot_len), slot_len)] = rows.astype(F32).T.astype(B16)
        return carry

    lax.fori_loop(0, total // slot_len, fill, 0)

    def per_query(block, carry):
        queries = q_s[block_rows(block), :]
        start_row = start_ref[block]

        def step(key_block, state, diagonal):
            allowed = mask_of(start_row, key_block, block, diagonal)
            keys = k_s[block_rows(key_block), :]
            values = vt_s[:, block_rows(key_block)]
            fresh = []
            for part in range(2):
                old_max, old_sum, old_acc = state[part]
                cols = slice(part * head, (part + 1) * head)
                scores = dot(keys[:, cols], queries[:, cols], 1, 1)
                scores = jnp.where(allowed, scores, MASK_FLOOR)
                new_max = jnp.maximum(old_max, jnp.max(scores, axis=0, keepdims=True))
                weights = jnp.where(allowed, jnp.exp(scores - new_max), 0.0)
                shrink = jnp.exp(old_max - new_max)
                new_sum = old_sum * shrink + jnp.sum(weights, axis=0, keepdims=True)
                new_acc = old_acc * shrink + dot(values[cols, :], weights.astype(B16), 1, 0)
                fresh.append((new_max, new_sum, new_acc))
            return tuple(fresh)

        first = tuple(
            (
                jnp.full((1, BLK), MASK_FLOOR, F32),
                jnp.zeros((1, BLK), F32),
                jnp.zeros((head, BLK), F32),
            )
            for part in range(2)
        )
        state = lax.fori_loop(low_ref[block], block, lambda j, s: step(j, s, False), first)
        state = step(block, state, True)
        lse_ref[block] = jnp.concatenate([s[0] + jnp.log(s[1]) for s in state], axis=0)
        result = jnp.concatenate([s[2] / s[1] for s in state], axis=0)
        unsort_block(inv_ref, out_ref, result.T, block, slot_len)
        return carry

    lax.fori_loop(0, total // BLK, per_query, 0)


def attend(inv, low, qkv, start3, slot_len, head):
    total = qkv.shape[0]
    vmem = pl.BlockSpec(memory_space=pltpu.VMEM)
    smem = pl.BlockSpec(memory_space=pltpu.SMEM)
    return pl.pallas_call(
        functools.partial(attend_kernel, slot_len, head),
        out_shape=(
            jax.ShapeDtypeStruct((total, 2 * head), B16),
            jax.ShapeDtypeStruct((total // BLK, 2, BLK), F32),
        ),
        in_specs=[smem, smem, vmem, vmem],
        out_specs=(vmem, vmem),
        scratch_shapes=[
            pltpu.VMEM((total, 2 * head), B16),
            pltpu.VMEM((total, 2 * head), B16),
            pltpu.VMEM((2 * head, total), B16),
        ],
        compiler_params=pltpu.CompilerParams(vmem_limit_bytes=VMEM_LIMIT),
        cost_estimate=pl.CostEstimate(
            flops=4 * total * total * head, bytes_accessed=8 * total * head * 2, transcendentals=total * total
        ),
        name="attend",
    )(inv, low, qkv, start3)


def attend_back_kernel(
    slot_len, head, inv_ref, low_ref, qkv_ref, out_ref, grad_ref, lse_ref, start_ref,
    dqkv_ref, q_s, k_s, v_s, kt_s, o_s, g_s, dk_s, dv_s,
):
    total = qkv_ref.shape[0]
    pair = 2 * head
    scale = 1.0 / math.sqrt(head)
    sort_slots(inv_ref, qkv_ref, q_s, slot_len, 0, pair, scale)
    sort_slots(inv_ref, qkv_ref, k_s, slot_len, pair, pair)
    sort_slots(inv_ref, qkv_ref, v_s, slot_len, 2 * pair, pair)
    sort_slots(inv_ref, out_ref, o_s, slot_len)
    sort_slots(inv_ref, grad_ref, g_s, slot_len)

    def fill(block, carry):
        kt_s[:, block_rows(block)] = k_s[block_rows(block), :].astype(F32).T.astype(B16)
        return carry

    lax.fori_loop(0, total // BLK, fill, 0)
    dk_s[...] = jnp.zeros_like(dk_s)
    dv_s[...] = jnp.zeros_like(dv_s)

    def per_query(block, carry):
        queries = q_s[block_rows(block), :]
        grads = g_s[block_rows(block), :]
        start_row = start_ref[block]
        lse = lse_ref[block]
        prod = (grads.astype(F32) * o_s[block_rows(block), :].astype(F32)).T
        delta = [jnp.sum(prod[part * head : (part + 1) * head], axis=0, keepdims=True) for part in range(2)]

        def step(key_block, state, diagonal):
            allowed = mask_of(start_row, key_block, block, diagonal)
            rows = block_rows(key_block)
            keys = k_s[rows, :]
            values = v_s[rows, :]
            flipped = kt_s[:, rows]
            fresh, dks, dvs = [], [], []
            for part in range(2):
                cols = slice(part * head, (part + 1) * head)
                scores = dot(keys[:, cols], queries[:, cols], 1, 1)
                weights = jnp.where(allowed, jnp.exp(scores - lse[part : part + 1]), 0.0)
                dprob = dot(values[:, cols], grads[:, cols], 1, 1)
                dscore = (weights * (dprob - delta[part])).astype(B16)
                dvs.append(dot(weights.astype(B16), grads[:, cols], 1, 0))
                dks.append(dot(dscore, queries[:, cols], 1, 0))
                fresh.append(state[part] + dot(flipped[cols, :], dscore, 1, 0))
            dk_s[rows, :] += jnp.concatenate(dks, axis=1)
            dv_s[rows, :] += jnp.concatenate(dvs, axis=1)
            return tuple(fresh)

        state = (jnp.zeros((head, BLK), F32), jnp.zeros((head, BLK), F32))
        state = lax.fori_loop(low_ref[block], block, lambda j, s: step(j, s, False), state)
        state = step(block, state, True)
        dq = jnp.concatenate(state, axis=0).T * scale
        for part in range(BLK // slot_len):
            slot = inv_ref[block * (BLK // slot_len) + part]
            dqkv_ref[pl.ds(pl.multiple_of(slot * slot_len, slot_len), slot_len), 0:pair] = dq[
                part * slot_len : (part + 1) * slot_len
            ]
        return carry

    lax.fori_loop(0, total // BLK, per_query, 0)

    def give(piece, carry):
        slot = inv_ref[piece]
        rows = pl.ds(pl.multiple_of(slot * slot_len, slot_len), slot_len)
        held = pl.ds(pl.multiple_of(piece * slot_len, slot_len), slot_len)
        dqkv_ref[rows, pair : 2 * pair] = dk_s[held, :]
        dqkv_ref[rows, 2 * pair :] = dv_s[held, :]
        return carry

    lax.fori_loop(0, total // slot_len, give, 0)


def attend_back(inv, low, qkv, out, grad, lse, start3, slot_len, head):
    total = qkv.shape[0]
    pair = 2 * head
    vmem = pl.BlockSpec(memory_space=pltpu.VMEM)
    smem = pl.BlockSpec(memory_space=pltpu.SMEM)
    held = pltpu.VMEM((total, pair), B16)
    return pl.pallas_call(
        functools.partial(attend_back_kernel, slot_len, head),
        out_shape=jax.ShapeDtypeStruct((total, 3 * pair), F32),
        in_specs=[smem, smem] + [vmem] * 5,
        out_specs=vmem,
        scratch_shapes=[
            held, held, held, pltpu.VMEM((pair, total), B16), held, held,
            pltpu.VMEM((total, pair), F32), pltpu.VMEM((total, pair), F32),
        ],
        compiler_params=pltpu.CompilerParams(vmem_limit_bytes=VMEM_LIMIT),
        cost_estimate=pl.CostEstimate(
            flops=10 * total * total * head, bytes_accessed=30 * total * head * 2, transcendentals=total * total
        ),
        name="attend_back",
    )(inv, low, qkv, out, grad, lse, start3)


class Place:
    def __init__(self, whole_line):
        self.x, self.h, self.l, self.c, self.y = (lax.axis_index(a) for a in ("x", "h", "l", "c", "y"))
        self.whole_line = whole_line
        self.n_z = 2 * lax.axis_size("h") if whole_line else 2
        self.z = self.h * 2 + self.l if whole_line else self.l
        self.ctx = self.z * 2 + self.c
        self.slot = self.ctx * 2 + self.y

    def at_z(self, z):
        return {"h": z // 2, "l": lax.rem(z, 2)} if self.whole_line else {"l": z}

    def at_ctx(self, k):
        return dict(self.at_z(k // 2), c=lax.rem(k, 2))

    def at_slot(self, s):
        return dict(self.at_ctx(s // 2), y=lax.rem(s, 2))

    def far_z(self):
        order = []
        for step in range(1, self.n_z // 2 + 1):
            order += [step] if 2 * step == self.n_z else [step, self.n_z - step]
        return [lax.rem(self.z + step, self.n_z) for step in order]

    def slot_of(self, z, c, y):
        return (z * 2 + c) * 2 + y


class Copies:
    def __init__(self, sems):
        self.sems = sems
        self.begun = []

    def send(self, src, dst, recv, peer):
        at = len(self.begun)
        copy = pltpu.make_async_remote_copy(
            src_ref=src,
            dst_ref=dst,
            send_sem=self.sems.at[at],
            recv_sem=recv,
            device_id=peer,
            device_id_type=pl.DeviceIdType.MESH,
        )
        copy.start()
        self.begun.append(copy.wait_send)

    def local(self, src, dst, sem=None):
        copy = pltpu.make_async_copy(src, dst, self.sems.at[len(self.begun)] if sem is None else sem)
        copy.start()
        if sem is None:
            self.begun.append(copy.wait)
        return copy

    def arrived(self, dst, recv, peer):
        pltpu.make_async_remote_copy(
            src_ref=dst,
            dst_ref=dst,
            send_sem=self.sems.at[0],
            recv_sem=recv,
            device_id=peer,
            device_id_type=pl.DeviceIdType.MESH,
        ).wait_recv()

    def finish(self):
        for wait in self.begun:
            wait()


def meet(peers):
    barrier = pltpu.get_barrier_semaphore()
    for peer in peers:
        pl.semaphore_signal(barrier, inc=1, device_id=peer, device_id_type=pl.DeviceIdType.MESH)
    pl.semaphore_wait(barrier, len(peers))


def others(me, count):
    return [lax.rem(me + step, count) for step in range(1, count)]


ANY = pl.BlockSpec(memory_space=pl.ANY)
IN_VMEM = pl.BlockSpec(memory_space=pltpu.VMEM)


def dma_sems(*counts):
    return [pltpu.SemaphoreType.DMA((count,)) for count in counts]


def comm_params(collective_id):
    return pltpu.CompilerParams(
        collective_id=collective_id, has_side_effects=True, vmem_limit_bytes=VMEM_LIMIT
    )


def gather_begin(place, own, out, copies, recv):
    peer_y, peer_c = {"y": 1 - place.y}, {"c": 1 - place.c}
    copies.local(own, out.at[place.slot])
    for z in place.far_z():
        copies.send(own, out.at[place.slot], recv.at[place.slot], place.at_z(z))
    copies.send(own, out.at[place.slot], recv.at[place.slot], peer_y)
    copies.send(own, out.at[place.slot], recv.at[place.slot], peer_c)


def gather_middle(place, out, copies, recv):
    peer_y, peer_c = {"y": 1 - place.y}, {"c": 1 - place.c}
    for z in place.far_z():
        at = place.slot_of(z, place.c, place.y)
        copies.arrived(out.at[at], recv.at[at], place.at_z(z))
        copies.send(out.at[at], out.at[at], recv.at[at], peer_y)
        copies.send(out.at[at], out.at[at], recv.at[at], peer_c)
    for z in [place.z] + place.far_z():
        at = place.slot_of(z, place.c, 1 - place.y)
        copies.arrived(out.at[at], recv.at[at], peer_y)
        copies.send(out.at[at], out.at[at], recv.at[at], peer_c)


def gather_end(place, out, copies, recv):
    for z in [place.z] + place.far_z():
        for y in (place.y, 1 - place.y):
            at = place.slot_of(z, 1 - place.c, y)
            copies.arrived(out.at[at], recv.at[at], {"c": 1 - place.c})


def gather_copies(n_z):
    return 4 * n_z


def group_gather_kernel(own, out, send, recv):
    place = Place(False)
    copies = Copies(send)
    meet([place.at_z(1 - place.z), {"y": 1 - place.y}, {"c": 1 - place.c}])
    gather_begin(place, own, out, copies, recv)
    gather_middle(place, out, copies, recv)
    gather_end(place, out, copies, recv)
    copies.finish()


def group_gather(value, collective_id):
    return pl.pallas_call(
        group_gather_kernel,
        out_shape=jax.ShapeDtypeStruct((8,) + value.shape, value.dtype),
        in_specs=[ANY],
        out_specs=ANY,
        scratch_shapes=dma_sems(gather_copies(2), 8),
        compiler_params=comm_params(collective_id),
        name="group_gather",
    )(value)


def opening_kernel(
    own, blocks, fc, proj, out_w, out, blocks_all, fc_all, proj_all, out_w_all, send, recv, recv_w, recv_f, recv_o, recv_p
):
    place, group = Place(True), Place(False)
    n_ctx = blocks.shape[0]
    copies = Copies(send)
    peer_x, peer_y, peer_c = {"x": 1 - place.x}, {"y": 1 - place.y}, {"c": 1 - place.c}
    far_ctx = others(place.ctx, n_ctx)
    meet([place.at_ctx(k) for k in far_ctx] + [peer_y, peer_x])
    mine = blocks_all.at[place.x, place.ctx]
    half = out_w.shape[1] // 2

    def sem_w(x, k):
        return recv_w.at[x * n_ctx + k]

    def out_block(x, z, c, y):
        at = (x * place.n_z + z) * 2 + c
        ref = out_w_all.at[at, :, pl.ds(pl.multiple_of(y * half, half), half)]
        return ref, recv_o.at[at * 2 + y]

    def give_out(x, z, c, y, peer):
        ref, sem = out_block(x, z, c, y)
        copies.send(ref, ref, sem, peer)

    def got_out(x, z, c, y, peer):
        ref, sem = out_block(x, z, c, y)
        copies.arrived(ref, sem, peer)

    gather_begin(place, own, out, copies, recv)
    for k in others(group.ctx, 4):
        copies.send(fc.at[k], fc_all.at[group.ctx], recv_f.at[group.ctx], group.at_ctx(k))
        copies.send(proj.at[k], proj_all.at[group.ctx], recv_p.at[group.ctx], group.at_ctx(k))
    copies.local(fc.at[group.ctx], fc_all.at[group.ctx])
    copies.local(proj.at[group.ctx], proj_all.at[group.ctx])
    for k in far_ctx:
        copies.send(blocks.at[k], mine, sem_w(place.x, place.ctx), place.at_ctx(k))
    copies.local(blocks.at[place.ctx], mine)
    copies.send(blocks.at[place.ctx], mine, sem_w(place.x, place.ctx), peer_x)
    own_out, own_sem = out_block(place.x, place.z, place.c, place.y)
    own_half = out_w.at[:, pl.ds(pl.multiple_of(place.y * half, half), half)]
    copies.local(own_half, own_out)
    for z in place.far_z():
        copies.send(own_half, own_out, own_sem, place.at_z(z))
    for peer in (peer_x, peer_y, peer_c):
        copies.send(own_half, own_out, own_sem, peer)
    gather_middle(place, out, copies, recv)
    for k in far_ctx:
        block = blocks_all.at[place.x, k]
        copies.arrived(block, sem_w(place.x, k), place.at_ctx(k))
        copies.send(block, block, sem_w(place.x, k), peer_x)
    for z in place.far_z():
        got_out(place.x, z, place.c, place.y, place.at_z(z))
        for peer in (peer_x, peer_y, peer_c):
            give_out(place.x, z, place.c, place.y, peer)
    for z in [place.z] + place.far_z():
        got_out(1 - place.x, z, place.c, place.y, peer_x)
        for peer in (peer_y, peer_c):
            give_out(1 - place.x, z, place.c, place.y, peer)
    gather_end(place, out, copies, recv)
    for x in (place.x, 1 - place.x):
        for z in [place.z] + place.far_z():
            got_out(x, z, place.c, 1 - place.y, peer_y)
            give_out(x, z, place.c, 1 - place.y, peer_c)
    for k in [place.ctx] + far_ctx:
        copies.arrived(blocks_all.at[1 - place.x, k], sem_w(1 - place.x, k), peer_x)
    for k in others(group.ctx, 4):
        copies.arrived(fc_all.at[k], recv_f.at[k], group.at_ctx(k))
        copies.arrived(proj_all.at[k], recv_p.at[k], group.at_ctx(k))
    for x in (place.x, 1 - place.x):
        for z in [place.z] + place.far_z():
            for y in (place.y, 1 - place.y):
                got_out(x, z, 1 - place.c, y, peer_c)
    copies.finish()


def opening(own, blocks, fc, proj, out_w):
    n_ctx = blocks.shape[0]
    n_z = n_ctx // 2
    sends = gather_copies(n_z) + 2 * n_ctx + 8 + (n_z - 1) + 4 + 3 * n_z + 2 * n_z + 2 * n_z
    return pl.pallas_call(
        opening_kernel,
        out_shape=(
            jax.ShapeDtypeStruct((2 * n_ctx,) + own.shape, own.dtype),
            jax.ShapeDtypeStruct((2,) + blocks.shape, blocks.dtype),
            jax.ShapeDtypeStruct(fc.shape, fc.dtype),
            jax.ShapeDtypeStruct(proj.shape, proj.dtype),
            jax.ShapeDtypeStruct((2 * n_ctx,) + out_w.shape, out_w.dtype),
        ),
        in_specs=[ANY] * 5,
        out_specs=(ANY,) * 5,
        scratch_shapes=dma_sems(sends, 2 * n_ctx, 2 * n_ctx, 4, 4 * n_ctx, 4),
        compiler_params=comm_params(1),
        name="opening",
    )(own, blocks, fc, proj, out_w)


def to_tokens_kernel(src, dst, send, recv):
    place = Place(True)
    copies = Copies(send)
    count, width = src.shape[0], src.shape[2]
    far = others(place.slot, count)
    meet([place.at_slot(s) for s in far])

    def columns(s):
        return dst.at[:, pl.ds(pl.multiple_of(s * width, width), width)]

    for s in far:
        copies.send(src.at[s], columns(place.slot), recv.at[place.slot], place.at_slot(s))
    copies.local(src.at[place.slot], columns(place.slot))
    for s in far:
        copies.arrived(columns(s), recv.at[s], place.at_slot(s))
    copies.finish()


def to_tokens(value):
    count, tokens, width = value.shape
    return pl.pallas_call(
        to_tokens_kernel,
        out_shape=jax.ShapeDtypeStruct((tokens, count * width), value.dtype),
        in_specs=[ANY],
        out_specs=ANY,
        scratch_shapes=dma_sems(count, count),
        compiler_params=comm_params(2),
        name="to_tokens",
    )(value)


def to_heads_kernel(src, dst, send, recv):
    place = Place(True)
    copies = Copies(send)
    count, width = dst.shape[0], dst.shape[2]
    far = others(place.slot, count)
    meet([place.at_slot(s) for s in far])

    def columns(s):
        return src.at[:, pl.ds(pl.multiple_of(s * width, width), width)]

    for s in far:
        copies.send(columns(s), dst.at[place.slot], recv.at[place.slot], place.at_slot(s))
    copies.local(columns(place.slot), dst.at[place.slot])
    for s in far:
        copies.arrived(dst.at[s], recv.at[s], place.at_slot(s))
    copies.finish()


def to_heads(value, count):
    tokens, width = value.shape[0], value.shape[1] // count
    return pl.pallas_call(
        to_heads_kernel,
        out_shape=jax.ShapeDtypeStruct((count, tokens, width), value.dtype),
        in_specs=[ANY],
        out_specs=ANY,
        scratch_shapes=dma_sems(count, count),
        compiler_params=comm_params(3),
        name="to_heads",
    )(value)


class Scatter:
    def __init__(self, place, part, held, from_c, from_y, from_z, out, copies, loads, rc, ry, rz):
        self.__dict__.update(locals())

    def order(self):
        return self.place.far_z() + [self.place.z]

    def begin(self):
        p = self.place
        for y in (1 - p.y, p.y):
            for z in self.order():
                at = z * 2 + y
                self.copies.send(
                    self.part.at[p.slot_of(z, 1 - p.c, y)], self.from_c.at[at], self.rc.at[at], {"c": 1 - p.c}
                )
        self.queue = [(z, y) for y in (1 - p.y, p.y) for z in self.order()]
        for at in range(min(self.held.shape[0], len(self.queue))):
            self.load(at)

    def load(self, at):
        p = self.place
        z, y = self.queue[at]
        at = at % self.held.shape[0]
        self.copies.local(self.part.at[p.slot_of(z, p.c, y)], self.held.at[at], self.loads.at[at])

    def add_c(self, step):
        z, y = self.queue[step]
        at, depth = z * 2 + y, self.held.shape[0]
        own = step % depth
        self.copies.arrived(self.from_c.at[at], self.rc.at[at], {"c": 1 - self.place.c})
        pltpu.make_async_copy(self.held.at[own], self.held.at[own], self.loads.at[own]).wait()
        self.from_c[at] = self.from_c[at] + self.held[own]
        if step + depth < len(self.queue):
            self.load(step + depth)

    def over_c_far(self):
        p = self.place
        for step, z in enumerate(self.order()):
            self.add_c(step)
            self.copies.send(self.from_c.at[z * 2 + 1 - p.y], self.from_y.at[z], self.ry.at[z], {"y": 1 - p.y})

    def over_c_near(self):
        for step in range(self.place.n_z):
            self.add_c(self.place.n_z + step)

    def over_y(self):
        p = self.place
        for z in self.order():
            self.copies.arrived(self.from_y.at[z], self.ry.at[z], {"y": 1 - p.y})
            self.from_y[z] = self.from_y[z] + self.from_c[z * 2 + p.y]
            if z is not p.z:
                self.copies.send(self.from_y.at[z], self.from_z.at[p.z], self.rz.at[p.z], p.at_z(z))

    def over_z(self):
        p = self.place
        total = self.from_y[p.z].astype(F32)
        for z in p.far_z():
            self.copies.arrived(self.from_z.at[z], self.rz.at[z], p.at_z(z))
            total = total + self.from_z[z].astype(F32)
        self.out[...] = total


def scatter_scratch(n_z, block):
    return [
        pltpu.VMEM((min(8, 2 * n_z),) + block, B16),
        pltpu.VMEM((2 * n_z,) + block, B16),
        pltpu.VMEM((n_z,) + block, B16),
        pltpu.VMEM((n_z,) + block, B16),
    ]


def scatter_sems(n_z, more=0):
    return dma_sems(4 * n_z + more, min(8, 2 * n_z), 2 * n_z, n_z, n_z)


def group_scatter_kernel(part, out, held, from_c, from_y, from_z, send, loads, rc, ry, rz):
    place = Place(False)
    copies = Copies(send)
    meet([place.at_z(1 - place.z), {"y": 1 - place.y}, {"c": 1 - place.c}])
    sums = Scatter(place, part, held, from_c, from_y, from_z, out, copies, loads, rc, ry, rz)
    sums.begin()
    sums.over_c_far()
    sums.over_c_near()
    sums.over_y()
    sums.over_z()
    copies.finish()


def group_scatter(part, collective_id):
    block = part.shape[1:]
    return pl.pallas_call(
        group_scatter_kernel,
        out_shape=jax.ShapeDtypeStruct(block, F32),
        in_specs=[ANY],
        out_specs=IN_VMEM,
        scratch_shapes=scatter_scratch(2, block) + scatter_sems(2),
        compiler_params=comm_params(collective_id),
        name="group_scatter",
    )(part)


class OutScatter:
    def __init__(self, place, part, held, from_c, from_x, from_y, from_z, out, copies, loads, rc, rx, ry, rz, rg):
        self.__dict__.update(locals())
        self.half = out.shape[2]

    def order(self):
        return self.place.far_z() + [self.place.z]

    def columns(self, y):
        return pl.ds(pl.multiple_of(y * self.half, self.half), self.half)

    def begin(self):
        p = self.place
        for x in (1 - p.x, p.x):
            for z in self.order():
                at = x * p.n_z + z
                self.copies.send(self.part.at[at * 2 + 1 - p.c], self.from_c.at[at], self.rc.at[at], {"c": 1 - p.c})
                self.copies.local(self.part.at[at * 2 + p.c], self.held.at[at], self.loads.at[at])

    def add_c(self, x, z):
        at = x * self.place.n_z + z
        self.copies.arrived(self.from_c.at[at], self.rc.at[at], {"c": 1 - self.place.c})
        pltpu.make_async_copy(self.held.at[at], self.held.at[at], self.loads.at[at]).wait()
        self.from_c[at] = self.from_c[at] + self.held[at]

    def over_c_far(self):
        p = self.place
        for z in self.order():
            self.add_c(1 - p.x, z)
            self.copies.send(
                self.from_c.at[(1 - p.x) * p.n_z + z], self.from_x.at[z], self.rx.at[z], {"x": 1 - p.x}
            )

    def over_c_near(self):
        for z in self.order():
            self.add_c(self.place.x, z)

    def over_x(self):
        p = self.place
        for z in self.order():
            self.copies.arrived(self.from_x.at[z], self.rx.at[z], {"x": 1 - p.x})
            self.from_x[z] = self.from_x[z] + self.from_c[p.x * p.n_z + z]
            self.copies.send(
                self.from_x.at[z, :, self.columns(1 - p.y)], self.from_y.at[z], self.ry.at[z], {"y": 1 - p.y}
            )

    def over_y(self):
        p = self.place
        for z in self.order():
            self.copies.arrived(self.from_y.at[z], self.ry.at[z], {"y": 1 - p.y})
            self.from_y[z] = self.from_y[z] + self.from_x[z, :, self.columns(p.y)]
            if z is not p.z:
                self.copies.send(self.from_y.at[z], self.from_z.at[p.z], self.rz.at[p.z], p.at_z(z))

    def over_z(self):
        p = self.place
        total = self.from_y[p.z].astype(F32)
        for z in p.far_z():
            self.copies.arrived(self.from_z.at[z], self.rz.at[z], p.at_z(z))
            total = total + self.from_z[z].astype(F32)
        self.out[p.y] = total.astype(B16)
        self.copies.send(self.out.at[p.y], self.out.at[p.y], self.rg.at[p.y], {"y": 1 - p.y})

    def end(self):
        p = self.place
        self.copies.arrived(self.out.at[1 - p.y], self.rg.at[1 - p.y], {"y": 1 - p.y})


def closing_kernel(
    part, grads, out_part, out, grads_out, out_w_out,
    held, from_c, from_y, from_z, own_x, from_x, o_held, o_c, o_x, o_y, o_z,
    send, loads, rc, ry, rz, load_x, rx, rk, rg, o_loads, orc, orx, ory, orz, org,
):
    place = Place(True)
    n_ctx = grads.shape[1]
    copies = Copies(send)
    far_ctx = others(place.ctx, n_ctx)
    peer_x, peer_y = {"x": 1 - place.x}, {"y": 1 - place.y}
    meet([place.at_ctx(k) for k in far_ctx] + [peer_y, peer_x])
    sums = Scatter(place, part, held, from_c, from_y, from_z, out, copies, loads, rc, ry, rz)
    outs = OutScatter(place, out_part, o_held, o_c, o_x, o_y, o_z, out_w_out, copies, o_loads, orc, orx, ory, orz, org)
    sums.begin()
    for k in far_ctx + [place.ctx]:
        copies.send(grads.at[1 - place.x, k], from_x.at[k], rx.at[k], peer_x)
        copies.local(grads.at[place.x, k], own_x.at[k], load_x.at[k])
    outs.begin()
    sums.over_c_far()
    mine = grads_out.at[place.y, place.ctx]
    for k in far_ctx + [place.ctx]:
        copies.arrived(from_x.at[k], rx.at[k], peer_x)
        pltpu.make_async_copy(own_x.at[k], own_x.at[k], load_x.at[k]).wait()
        from_x[k] = from_x[k] + own_x[k]
        if k is not place.ctx:
            copies.send(from_x.at[k], mine, rk.at[place.ctx], place.at_ctx(k))
    copies.local(from_x.at[place.ctx], mine)
    copies.send(from_x.at[place.ctx], mine, rg.at[place.ctx], peer_y)
    sums.over_c_near()
    outs.over_c_far()
    outs.over_c_near()
    sums.over_y()
    outs.over_x()
    for k in far_ctx:
        block = grads_out.at[place.y, k]
        copies.arrived(block, rk.at[k], place.at_ctx(k))
        copies.send(block, block, rg.at[k], peer_y)
    outs.over_y()
    sums.over_z()
    outs.over_z()
    for k in [place.ctx] + far_ctx:
        copies.arrived(grads_out.at[1 - place.y, k], rg.at[k], peer_y)
    outs.end()
    copies.finish()


def closing(part, grads, out_part):
    block = part.shape[1:]
    n_ctx = grads.shape[1]
    n_z = n_ctx // 2
    piece = grads.shape[1:]
    rows, width = out_part.shape[1:]
    half = (rows, width // 2)
    return pl.pallas_call(
        closing_kernel,
        out_shape=(
            jax.ShapeDtypeStruct(block, F32),
            jax.ShapeDtypeStruct((2,) + piece, B16),
            jax.ShapeDtypeStruct((2,) + half, B16),
        ),
        in_specs=[ANY] * 3,
        out_specs=(IN_VMEM, ANY, IN_VMEM),
        scratch_shapes=scatter_scratch(n_z, block)
        + [pltpu.VMEM(piece, B16), pltpu.VMEM(piece, B16)]
        + [pltpu.VMEM((2 * n_z, rows, width), B16), pltpu.VMEM((2 * n_z, rows, width), B16)]
        + [pltpu.VMEM((n_z, rows, width), B16), pltpu.VMEM((n_z,) + half, B16), pltpu.VMEM((n_z,) + half, B16)]
        + scatter_sems(n_z, 3 * n_ctx + 6 * n_z)
        + dma_sems(n_ctx, n_ctx, n_ctx, n_ctx)
        + dma_sems(2 * n_z, 2 * n_z, n_z, n_z, n_z, 2),
        compiler_params=comm_params(4),
        name="closing",
    )(part, grads, out_part)


def vectors_kernel(src, own_out, ff_out, from_all, half, from_y, send, recv, ry):
    place = Place(True)
    count = src.shape[0]
    n_ctx = count // 2
    copies = Copies(send)
    me = place.x * n_ctx + place.ctx
    far = others(me, count)
    peer_y = {"y": 1 - place.y}

    def peer(k):
        return dict(place.at_ctx(lax.rem(k, n_ctx)), x=k // n_ctx)

    meet([peer(k) for k in far] + [peer_y])
    for k in far:
        copies.send(src.at[k], from_all.at[me], recv.at[me], peer(k))
    from_all[me] = src[me]
    for k in far:
        copies.arrived(from_all.at[k], recv.at[k], peer(k))
    total = from_all[0, 0:8, :]
    for k in range(1, count):
        total = total + from_all[k, 0:8, :]
    half[...] = total
    copies.send(half, from_y, ry.at[0], peer_y)
    for part in range(4):
        total = from_all[part, 8:16, :]
        for k in range(part + 4, count, 4):
            total = total + from_all[k, 8:16, :]
        ff_out[part] = total
    copies.arrived(from_y, ry.at[0], peer_y)
    own_out[...] = half[...] + from_y[...]
    copies.finish()


def vectors_sum(value):
    count = value.shape[0]
    flat = jax.ShapeDtypeStruct((8, 128), F32)
    return pl.pallas_call(
        vectors_kernel,
        out_shape=(flat, jax.ShapeDtypeStruct((4, 8, 128), F32)),
        in_specs=[IN_VMEM],
        out_specs=(IN_VMEM, IN_VMEM),
        scratch_shapes=[
            pltpu.VMEM(value.shape, F32),
            pltpu.VMEM((8, 128), F32),
            pltpu.VMEM((8, 128), F32),
        ]
        + dma_sems(count + 1, count, 1),
        compiler_params=comm_params(5),
        name="vectors_sum",
    )(value)


def project_kernel(feats, x_ref, gain_ref, shift_ref, mask_ref, w_ref, bias_ref, norm_ref, qkv_ref):
    x = x_ref[...].astype(F32)
    mean = jnp.sum(x, axis=1, keepdims=True) * (1.0 / feats)
    centered = (x - mean) * mask_ref[...]
    inv = lax.rsqrt(jnp.sum(centered * centered, axis=1, keepdims=True) * (1.0 / feats) + NORM_EPS)
    norm = (centered * inv * gain_ref[...] + shift_ref[...]).astype(B16)
    norm_ref[...] = norm
    qkv_ref[...] = (dot(norm, w_ref[...], 1, 0) + bias_ref[...]).astype(B16)


def project(x, gain, shift, mask, weight, bias, feats):
    total, wide = x.shape
    cols = weight.shape[1]
    step = min(256, total)

    def fixed(shape):
        return pl.BlockSpec(shape, lambda i: (0, 0))

    return pl.pallas_call(
        functools.partial(project_kernel, feats),
        grid=(total // step,),
        in_specs=[pl.BlockSpec((step, wide), lambda i: (i, 0))]
        + [fixed((1, wide))] * 3
        + [fixed((wide, cols)), fixed((1, cols))],
        out_specs=(pl.BlockSpec((step, wide), lambda i: (i, 0)), pl.BlockSpec((step, cols), lambda i: (i, 0))),
        out_shape=(jax.ShapeDtypeStruct((total, wide), B16), jax.ShapeDtypeStruct((total, cols), B16)),
        compiler_params=pltpu.CompilerParams(vmem_limit_bytes=VMEM_LIMIT),
        cost_estimate=pl.CostEstimate(
            flops=2 * total * wide * cols, bytes_accessed=4 * total * wide, transcendentals=total
        ),
        name="project",
    )(x, gain[None], shift[None], mask[None], weight, bias[None])


def on_device(
    sizes, block_input, segment_ids, slot_order, first_gain, first_shift, qkv_weight, qv_bias, out_weight, out_bias,
    second_gain, second_shift, fc_weight, fc_bias, proj_weight, proj_bias, out_grad,
):
    n_x, n_ctx, n_y = sizes
    n_slot = n_ctx * n_y
    n_shard = n_x * n_ctx
    n_h = n_ctx // 4
    slot_len, feats = block_input.shape[1:]
    head = feats // HEADS
    pair = 2 * head
    rows = qkv_weight.shape[0]
    ff_own = fc_weight.shape[1] // 4
    padded = n_slot * pair
    y_at = lax.axis_index("y")
    ctx_at = lax.axis_index(CTX)
    slot_at = lax.axis_index(ROW)
    lc_at = lax.axis_index(("l", "c"))

    def gather(value, axes):
        return lax.all_gather(value, axes, axis=0, tiled=True)

    tall = rows + (-rows % 16)
    wide = n_shard * tall
    row_pad = tall - rows

    def widened(value):
        lead = value.shape[:-1]
        value = value.reshape(lead + (n_shard, rows))
        return jnp.pad(value, [(0, 0)] * (len(lead) + 1) + [(0, row_pad)]).reshape(lead + (wide,))

    def narrowed(value):
        lead = value.shape[:-1]
        return value.reshape(lead + (n_shard, tall))[..., :rows].reshape(lead + (feats,))

    mask = jnp.asarray((np.arange(wide) % tall < rows).astype(np.float32))

    small = jnp.concatenate([first_gain, first_shift, out_bias, second_gain, second_shift, proj_bias, qv_bias])
    packed = jnp.pad(qkv_weight.reshape(rows, 3, feats), ((0, 0), (0, 0), (0, padded - feats)))
    packed = lax.dynamic_index_in_dim(packed.reshape(rows, 3, n_ctx, n_y, pair), y_at, 3, False)
    packed = packed.transpose(2, 0, 1, 3).reshape(n_ctx, rows, 3 * pair)
    small = jnp.pad(small, (0, row_pad * 3 * pair - small.shape[0])).reshape(1, row_pad, 3 * pair)
    packed = jnp.concatenate([packed, jnp.broadcast_to(small, (n_ctx, row_pad, 3 * pair))], axis=1)
    fc_blocks = jnp.pad(fc_weight, ((0, row_pad), (0, 0))).reshape(tall, 4, ff_own).transpose(1, 0, 2)
    proj_blocks = jnp.pad(proj_weight.T, ((0, row_pad), (0, 0))).reshape(tall, 4, ff_own).transpose(1, 0, 2)
    own_input = widened(block_input[0])
    grad_own = widened(out_grad[0])
    grad_all = gather(grad_own, FFG)
    all_input, packed, fc_blocks, proj_blocks, w_out = opening(
        own_input, packed, fc_blocks, proj_blocks, widened(jnp.pad(out_weight, ((0, row_pad), (0, 0))))
    )
    w_fc = gather(fc_blocks.reshape(4 * tall, ff_own), ("x", "h"))
    w_proj = gather(proj_blocks.reshape(4 * tall, ff_own), ("x", "h"))
    w_out = w_out.reshape(wide, wide)
    packed = packed.reshape(n_shard, tall, 3 * pair)
    w_qkv = packed.reshape(wide, 3 * pair)
    smalls = packed[:, rows:].reshape(n_shard, -1)[:, : 8 * rows].astype(F32)
    singles = jnp.pad(smalls[:, : 6 * rows].reshape(n_shard, 6, rows), ((0, 0), (0, 0), (0, row_pad)))
    gain_one, shift_one, bias_out, gain_two, shift_two, bias_proj = singles.transpose(1, 0, 2).reshape(6, wide)
    bias_qv = smalls[:, 6 * rows :].reshape(2, feats)
    bias_pair = lax.dynamic_slice_in_dim(
        jnp.pad(bias_qv, ((0, 0), (0, padded - feats))), slot_at * pair, pair, 1
    )
    bias_qkv = jnp.concatenate([bias_pair[0], jnp.zeros((pair,), F32), bias_pair[1]])
    b_fc = lax.dynamic_slice_in_dim(fc_bias, lc_at * ff_own, ff_own, 0).astype(F32)

    order = slot_order[0]
    pieces = jnp.arange(n_slot, dtype=jnp.int32)
    inv = jnp.sum(jnp.where(order[None, :] == pieces[:, None], pieces[None, :], 0), axis=1).astype(jnp.int32)
    segs = jnp.take(segment_ids[0].reshape(n_slot, slot_len), inv, axis=0).reshape(-1)
    docs = jnp.arange(DOCS, dtype=jnp.int32)
    counts = jnp.sum((segs[None, :] == docs[:, None]).astype(jnp.int32), axis=1)
    starts = jnp.sum(jnp.where(segs[None, :] > docs[:, None], counts[:, None], 0), axis=0).astype(jnp.int32)
    start3 = starts.reshape(-1, 1, BLK)
    low = start3[:, 0, 0] // BLK

    own_wide = own_input.astype(F32)
    norm_one, qkv = project(
        all_input.reshape(n_slot * slot_len, wide), gain_one, shift_one, mask, w_qkv, bias_qkv, feats
    )
    heads_out, lse = attend(inv, low, qkv, start3, slot_len, head)
    attention = widened(to_tokens(heads_out.reshape(n_slot, slot_len, pair))[:, :feats])
    hidden = own_wide + dot(attention, w_out, 1, 0) + bias_out
    normed_two, inv_two = norm_forward(hidden, mask, feats)
    norm_two = (normed_two * gain_two + shift_two).astype(B16)
    grad_wide = grad_own.astype(F32)
    norm_all = group_gather(norm_two, 6).reshape(-1, wide)
    preact = dot(norm_all, w_fc, 1, 0) + b_fc
    activated, derivative = gelu_parts(preact)
    activation = activated.astype(B16)
    mlp_part = dot(activation, w_proj, 1, 1).astype(B16)
    mlp = lax.psum_scatter(mlp_part, FFG, scatter_dimension=0, tiled=True).astype(F32)
    block_output = narrowed(hidden + mlp + bias_proj)

    dpreact = dot(grad_all, w_proj, 1, 0) * derivative
    dpreact_b = dpreact.astype(B16)
    dnorm_part = dot(dpreact_b, w_fc, 1, 1).astype(B16)
    dnorm_two = group_scatter(dnorm_part.reshape(8, slot_len, wide), 7)

    def owner_sum(value):
        value = lax.psum_scatter(value.astype(B16), ("x", "h"), scatter_dimension=0, tiled=True)
        value = lax.all_to_all(value.reshape(4, tall, ff_own), ("l", "c"), 0, 0, tiled=True)
        return value[:, :rows].astype(F32)

    proj_grad = owner_sum(dot(grad_all, activation, 0, 0)).transpose(0, 2, 1).reshape(4 * ff_own, rows)
    fc_grad = owner_sum(dot(norm_all, dpreact_b, 0, 0)).transpose(1, 0, 2).reshape(rows, 4 * ff_own)

    dhidden = grad_wide + norm_backward(dnorm_two, normed_two, inv_two, gain_two, feats)
    dhidden_b = dhidden.astype(B16)
    out_part = dot(attention, dhidden_b, 0, 0).astype(B16).reshape(n_shard, tall, wide)
    dattention = narrowed(dot(dhidden_b, w_out, 1, 1).astype(B16))
    dattention = jnp.pad(dattention, ((0, 0), (0, padded - feats)))
    dattention = to_heads(dattention, n_slot).reshape(n_slot * slot_len, pair)
    dqkv = attend_back(inv, low, qkv, heads_out, dattention, lse, start3, slot_len, head)
    dqkv_b = dqkv.astype(B16)
    dnorm_one_part = dot(dqkv_b, w_qkv, 1, 1).astype(B16)
    qkv_part = dot(norm_one, dqkv_b, 0, 0).astype(B16).reshape(n_x, n_ctx, tall, 3 * pair)
    dnorm_one, qkv_all, out_all = closing(dnorm_one_part.reshape(n_slot, slot_len, wide), qkv_part, out_part)
    qkv_all = qkv_all[:, :, :rows].reshape(n_y, n_ctx, rows, 3, pair)
    qkv_grad = qkv_all.transpose(2, 3, 1, 0, 4).reshape(rows, 3, padded)
    qkv_grad = qkv_grad[:, :, :feats].reshape(rows, 3 * feats).astype(F32)
    out_grad_w = narrowed(out_all[:, :rows].transpose(1, 0, 2).reshape(rows, wide)).astype(F32)

    normed_one, inv_one = norm_forward(own_wide, mask, feats)
    input_grad = narrowed(dhidden + norm_backward(dnorm_one, normed_one, inv_one, gain_one, feats))

    dq_sum, dv_sum = jnp.sum(dqkv[:, :pair], axis=0), jnp.sum(dqkv[:, 2 * pair :], axis=0)

    def placed(value, width, at):
        return lax.dynamic_update_slice(jnp.zeros((width,), F32), value, (at,))[:feats]

    vectors = jnp.stack(
        [
            jnp.sum(dhidden, axis=0),
            jnp.sum(dnorm_one * normed_one, axis=0),
            jnp.sum(dnorm_one, axis=0),
            jnp.sum(dnorm_two * normed_two, axis=0),
            jnp.sum(dnorm_two, axis=0),
            jnp.sum(grad_wide, axis=0),
        ]
    )
    qv_sums = jnp.concatenate([placed(dq_sum, padded, slot_at * pair), placed(dv_sum, padded, slot_at * pair)])
    vectors = jnp.concatenate(
        [
            vectors.reshape(6, n_shard, tall).transpose(1, 0, 2).reshape(n_shard, 6 * tall),
            qv_sums.reshape(n_shard, 2 * rows),
            jnp.zeros((n_shard, 1024 - 6 * tall - 2 * rows), F32),
            jnp.broadcast_to(jnp.sum(dpreact, axis=0)[None], (n_shard, ff_own)),
            jnp.zeros((n_shard, 1024 - ff_own), F32),
        ],
        axis=1,
    )
    owned, ff_sums = vectors_sum(vectors.reshape(n_shard, 16, 128))
    owned = owned.reshape(1024)
    fc_bias_grad = ff_sums.reshape(4, 1024)[:, :ff_own].reshape(4 * ff_own)
    qv_grad = owned[6 * tall : 6 * tall + 2 * rows]

    def own(index):
        return owned[index * tall : index * tall + rows]

    return (
        block_output[None],
        input_grad[None],
        qkv_grad,
        qv_grad,
        out_grad_w,
        own(0),
        own(1),
        own(2),
        own(3),
        own(4),
        fc_grad,
        fc_bias_grad,
        proj_grad,
        own(5),
    )


def solution(mesh):
    n_x, n_ctx, n_y = (mesh.shape[axis] for axis in ("dp", "context", "tensor"))
    inner = Mesh(mesh.devices.reshape(n_x, n_ctx // 4, 2, 2, n_y), ("x", "h", "l", "c", "y"))
    tokens = P("x", ROW, None)
    shard = P(SHARD)
    shard_rows = P(SHARD, None)
    return jax.shard_map(
        functools.partial(on_device, (n_x, n_ctx, n_y)),
        mesh=inner,
        in_specs=(
            tokens, P("x", None), P("x", None), shard, shard, shard_rows, shard, shard_rows, shard, shard, shard,
            P(SHARD, "y"), P("y"), P("y", SHARD), shard, tokens,
        ),
        out_specs=(
            tokens, tokens, shard_rows, shard, shard_rows, shard, shard, shard, shard, shard,
            P(SHARD, "y"), P("y"), P("y", SHARD), shard,
        ),
        check_vma=False,
    )
```

```python
import functools
import math

import jax
import jax.numpy as jnp
import numpy as np
from jax import lax
from jax.experimental import pallas as pl
from jax.experimental.pallas import tpu as pltpu
from jax.sharding import Mesh
from jax.sharding import PartitionSpec as P

HEADS = 25
DOCS = 8
NORM_EPS = 1e-05
GELU_SCALE = 0.7978845608028654
GELU_CUBE = 0.044715
MASK_FLOOR = -1e30

F32 = jnp.float32
B16 = jnp.bfloat16
BLK = 256
VMEM_LIMIT = 60 * 1024 * 1024

ROW = ("h", "l", "c", "y")
CTX = ("h", "l", "c")
SHARD = ("x", "h", "l", "c")
FFG = ("l", "c", "y")


def gelu_parts(values):
    inner_arg = GELU_SCALE * (values + GELU_CUBE * values * values * values)
    tanh_value = jnp.tanh(inner_arg)
    result = 0.5 * values * (1.0 + tanh_value)
    derivative = 0.5 * (1.0 + tanh_value) + 0.5 * values * (
        1.0 - tanh_value * tanh_value
    ) * GELU_SCALE * (1.0 + 3.0 * GELU_CUBE * values * values)
    return (result, derivative)


def norm_forward(values, mask, feats):
    mean_value = jnp.sum(values, axis=-1, keepdims=True) / feats
    centered = (values - mean_value) * mask
    inv_sigma = lax.rsqrt(jnp.sum(centered * centered, axis=-1, keepdims=True) / feats + NORM_EPS)
    return (centered * inv_sigma, inv_sigma)


def norm_backward(upstream, normed, inv_sigma, norm_gain, feats):
    scaled = upstream * norm_gain
    return inv_sigma * (
        scaled
        - jnp.sum(scaled, axis=-1, keepdims=True) / feats
        - normed * (jnp.sum(scaled * normed, axis=-1, keepdims=True) / feats)
    )


def dot(left, right, left_dim, right_dim):
    return lax.dot_general(
        left, right, (((left_dim,), (right_dim,)), ((), ())), preferred_element_type=F32
    )


def sort_slots(inv_ref, src_ref, dst_ref, slot_len, start=0, width=None, factor=None):
    width = src_ref.shape[1] if width is None else width

    def body(piece, carry):
        slot = inv_ref[piece]
        rows = src_ref[pl.ds(pl.multiple_of(slot * slot_len, slot_len), slot_len), start : start + width]
        if factor is not None:
            rows = rows * jnp.asarray(factor, rows.dtype)
        dst_ref[pl.ds(pl.multiple_of(piece * slot_len, slot_len), slot_len), :] = rows
        return carry

    lax.fori_loop(0, src_ref.shape[0] // slot_len, body, 0)


def unsort_block(inv_ref, dst_ref, value, block, slot_len):
    for part in range(BLK // slot_len):
        slot = inv_ref[block * (BLK // slot_len) + part]
        dst_ref[pl.ds(pl.multiple_of(slot * slot_len, slot_len), slot_len), :] = value[
            part * slot_len : (part + 1) * slot_len
        ].astype(dst_ref.dtype)


def block_rows(block):
    return pl.ds(pl.multiple_of(block * BLK, BLK), BLK)


def mask_of(start_row, key_block, query_block, diagonal):
    key_at = key_block * BLK + lax.broadcasted_iota(jnp.int32, (BLK, BLK), 0)
    allowed = key_at >= start_row
    if diagonal:
        query_at = query_block * BLK + lax.broadcasted_iota(jnp.int32, (BLK, BLK), 1)
        allowed = jnp.logical_and(allowed, key_at <= query_at)
    return allowed


def attend_kernel(slot_len, head, inv_ref, low_ref, qkv_ref, start_ref, out_ref, lse_ref, q_s, k_s, vt_s):
    total = qkv_ref.shape[0]
    pair = 2 * head
    sort_slots(inv_ref, qkv_ref, q_s, slot_len, 0, pair, 1.0 / math.sqrt(head))
    sort_slots(inv_ref, qkv_ref, k_s, slot_len, pair, pair)

    def fill(piece, carry):
        slot = inv_ref[piece]
        rows = qkv_ref[pl.ds(pl.multiple_of(slot * slot_len, slot_len), slot_len), 2 * pair :]
        vt_s[:, pl.ds(pl.multiple_of(piece * slot_len, slot_len), slot_len)] = rows.astype(F32).T.astype(B16)
        return carry

    lax.fori_loop(0, total // slot_len, fill, 0)

    def per_query(block, carry):
        queries = q_s[block_rows(block), :]
        start_row = start_ref[block]

        def step(key_block, state, diagonal):
            allowed = mask_of(start_row, key_block, block, diagonal)
            keys = k_s[block_rows(key_block), :]
            values = vt_s[:, block_rows(key_block)]
            fresh = []
            for part in range(2):
                old_max, old_sum, old_acc = state[part]
                cols = slice(part * head, (part + 1) * head)
                scores = dot(keys[:, cols], queries[:, cols], 1, 1)
                scores = jnp.where(allowed, scores, MASK_FLOOR)
                new_max = jnp.maximum(old_max, jnp.max(scores, axis=0, keepdims=True))
                weights = jnp.where(allowed, jnp.exp(scores - new_max), 0.0)
                shrink = jnp.exp(old_max - new_max)
                new_sum = old_sum * shrink + jnp.sum(weights, axis=0, keepdims=True)
                new_acc = old_acc * shrink + dot(values[cols, :], weights.astype(B16), 1, 0)
                fresh.append((new_max, new_sum, new_acc))
            return tuple(fresh)

        first = tuple(
            (
                jnp.full((1, BLK), MASK_FLOOR, F32),
                jnp.zeros((1, BLK), F32),
                jnp.zeros((head, BLK), F32),
            )
            for part in range(2)
        )
        state = lax.fori_loop(low_ref[block], block, lambda j, s: step(j, s, False), first)
        state = step(block, state, True)
        lse_ref[block] = jnp.concatenate([s[0] + jnp.log(s[1]) for s in state], axis=0)
        result = jnp.concatenate([s[2] / s[1] for s in state], axis=0)
        unsort_block(inv_ref, out_ref, result.T, block, slot_len)
        return carry

    lax.fori_loop(0, total // BLK, per_query, 0)


def attend(inv, low, qkv, start3, slot_len, head):
    total = qkv.shape[0]
    vmem = pl.BlockSpec(memory_space=pltpu.VMEM)
    smem = pl.BlockSpec(memory_space=pltpu.SMEM)
    return pl.pallas_call(
        functools.partial(attend_kernel, slot_len, head),
        out_shape=(
            jax.ShapeDtypeStruct((total, 2 * head), B16),
            jax.ShapeDtypeStruct((total // BLK, 2, BLK), F32),
        ),
        in_specs=[smem, smem, vmem, vmem],
        out_specs=(vmem, vmem),
        scratch_shapes=[
            pltpu.VMEM((total, 2 * head), B16),
            pltpu.VMEM((total, 2 * head), B16),
            pltpu.VMEM((2 * head, total), B16),
        ],
        compiler_params=pltpu.CompilerParams(vmem_limit_bytes=VMEM_LIMIT),
        cost_estimate=pl.CostEstimate(
            flops=4 * total * total * head, bytes_accessed=8 * total * head * 2, transcendentals=total * total
        ),
        name="attend",
    )(inv, low, qkv, start3)


def attend_back_kernel(
    slot_len, head, inv_ref, low_ref, qkv_ref, out_ref, grad_ref, lse_ref, start_ref,
    dqkv_ref, q_s, k_s, v_s, kt_s, o_s, g_s, dk_s, dv_s,
):
    total = qkv_ref.shape[0]
    pair = 2 * head
    scale = 1.0 / math.sqrt(head)
    sort_slots(inv_ref, qkv_ref, q_s, slot_len, 0, pair, scale)
    sort_slots(inv_ref, qkv_ref, k_s, slot_len, pair, pair)
    sort_slots(inv_ref, qkv_ref, v_s, slot_len, 2 * pair, pair)
    sort_slots(inv_ref, out_ref, o_s, slot_len)
    sort_slots(inv_ref, grad_ref, g_s, slot_len)

    def fill(block, carry):
        kt_s[:, block_rows(block)] = k_s[block_rows(block), :].astype(F32).T.astype(B16)
        return carry

    lax.fori_loop(0, total // BLK, fill, 0)
    dk_s[...] = jnp.zeros_like(dk_s)
    dv_s[...] = jnp.zeros_like(dv_s)

    def per_query(block, carry):
        queries = q_s[block_rows(block), :]
        grads = g_s[block_rows(block), :]
        start_row = start_ref[block]
        lse = lse_ref[block]
        prod = (grads.astype(F32) * o_s[block_rows(block), :].astype(F32)).T
        delta = [jnp.sum(prod[part * head : (part + 1) * head], axis=0, keepdims=True) for part in range(2)]

        def step(key_block, state, diagonal):
            allowed = mask_of(start_row, key_block, block, diagonal)
            rows = block_rows(key_block)
            keys = k_s[rows, :]
            values = v_s[rows, :]
            flipped = kt_s[:, rows]
            fresh, dks, dvs = [], [], []
            for part in range(2):
                cols = slice(part * head, (part + 1) * head)
                scores = dot(keys[:, cols], queries[:, cols], 1, 1)
                weights = jnp.where(allowed, jnp.exp(scores - lse[part : part + 1]), 0.0)
                dprob = dot(values[:, cols], grads[:, cols], 1, 1)
                dscore = (weights * (dprob - delta[part])).astype(B16)
                dvs.append(dot(weights.astype(B16), grads[:, cols], 1, 0))
                dks.append(dot(dscore, queries[:, cols], 1, 0))
                fresh.append(state[part] + dot(flipped[cols, :], dscore, 1, 0))
            dk_s[rows, :] += jnp.concatenate(dks, axis=1)
            dv_s[rows, :] += jnp.concatenate(dvs, axis=1)
            return tuple(fresh)

        state = (jnp.zeros((head, BLK), F32), jnp.zeros((head, BLK), F32))
        state = lax.fori_loop(low_ref[block], block, lambda j, s: step(j, s, False), state)
        state = step(block, state, True)
        dq = jnp.concatenate(state, axis=0).T * scale
        for part in range(BLK // slot_len):
            slot = inv_ref[block * (BLK // slot_len) + part]
            dqkv_ref[pl.ds(pl.multiple_of(slot * slot_len, slot_len), slot_len), 0:pair] = dq[
                part * slot_len : (part + 1) * slot_len
            ]
        return carry

    lax.fori_loop(0, total // BLK, per_query, 0)

    def give(piece, carry):
        slot = inv_ref[piece]
        rows = pl.ds(pl.multiple_of(slot * slot_len, slot_len), slot_len)
        held = pl.ds(pl.multiple_of(piece * slot_len, slot_len), slot_len)
        dqkv_ref[rows, pair : 2 * pair] = dk_s[held, :]
        dqkv_ref[rows, 2 * pair :] = dv_s[held, :]
        return carry

    lax.fori_loop(0, total // slot_len, give, 0)


def attend_back(inv, low, qkv, out, grad, lse, start3, slot_len, head):
    total = qkv.shape[0]
    pair = 2 * head
    vmem = pl.BlockSpec(memory_space=pltpu.VMEM)
    smem = pl.BlockSpec(memory_space=pltpu.SMEM)
    held = pltpu.VMEM((total, pair), B16)
    return pl.pallas_call(
        functools.partial(attend_back_kernel, slot_len, head),
        out_shape=jax.ShapeDtypeStruct((total, 3 * pair), F32),
        in_specs=[smem, smem] + [vmem] * 5,
        out_specs=vmem,
        scratch_shapes=[
            held, held, held, pltpu.VMEM((pair, total), B16), held, held,
            pltpu.VMEM((total, pair), F32), pltpu.VMEM((total, pair), F32),
        ],
        compiler_params=pltpu.CompilerParams(vmem_limit_bytes=VMEM_LIMIT),
        cost_estimate=pl.CostEstimate(
            flops=10 * total * total * head, bytes_accessed=30 * total * head * 2, transcendentals=total * total
        ),
        name="attend_back",
    )(inv, low, qkv, out, grad, lse, start3)


class Place:
    def __init__(self, whole_line):
        self.x, self.h, self.l, self.c, self.y = (lax.axis_index(a) for a in ("x", "h", "l", "c", "y"))
        self.whole_line = whole_line
        self.n_z = 2 * lax.axis_size("h") if whole_line else 2
        self.z = self.h * 2 + self.l if whole_line else self.l
        self.ctx = self.z * 2 + self.c
        self.slot = self.ctx * 2 + self.y

    def at_z(self, z):
        return {"h": z // 2, "l": lax.rem(z, 2)} if self.whole_line else {"l": z}

    def at_ctx(self, k):
        return dict(self.at_z(k // 2), c=lax.rem(k, 2))

    def at_slot(self, s):
        return dict(self.at_ctx(s // 2), y=lax.rem(s, 2))

    def far_z(self):
        order = []
        for step in range(1, self.n_z // 2 + 1):
            order += [step] if 2 * step == self.n_z else [step, self.n_z - step]
        return [lax.rem(self.z + step, self.n_z) for step in order]

    def slot_of(self, z, c, y):
        return (z * 2 + c) * 2 + y


class Copies:
    def __init__(self, sems):
        self.sems = sems
        self.begun = []

    def send(self, src, dst, recv, peer):
        at = len(self.begun)
        copy = pltpu.make_async_remote_copy(
            src_ref=src,
            dst_ref=dst,
            send_sem=self.sems.at[at],
            recv_sem=recv,
            device_id=peer,
            device_id_type=pl.DeviceIdType.MESH,
        )
        copy.start()
        self.begun.append(copy.wait_send)

    def local(self, src, dst, sem=None):
        copy = pltpu.make_async_copy(src, dst, self.sems.at[len(self.begun)] if sem is None else sem)
        copy.start()
        if sem is None:
            self.begun.append(copy.wait)
        return copy

    def arrived(self, dst, recv, peer):
        pltpu.make_async_remote_copy(
            src_ref=dst,
            dst_ref=dst,
            send_sem=self.sems.at[0],
            recv_sem=recv,
            device_id=peer,
            device_id_type=pl.DeviceIdType.MESH,
        ).wait_recv()

    def finish(self):
        for wait in self.begun:
            wait()


def meet(peers):
    barrier = pltpu.get_barrier_semaphore()
    for peer in peers:
        pl.semaphore_signal(barrier, inc=1, device_id=peer, device_id_type=pl.DeviceIdType.MESH)
    pl.semaphore_wait(barrier, len(peers))


def others(me, count):
    return [lax.rem(me + step, count) for step in range(1, count)]


ANY = pl.BlockSpec(memory_space=pl.ANY)
IN_VMEM = pl.BlockSpec(memory_space=pltpu.VMEM)


def dma_sems(*counts):
    return [pltpu.SemaphoreType.DMA((count,)) for count in counts]


def comm_params(collective_id):
    return pltpu.CompilerParams(
        collective_id=collective_id, has_side_effects=True, vmem_limit_bytes=VMEM_LIMIT
    )


def gather_begin(place, own, out, copies, recv):
    peer_y, peer_c = {"y": 1 - place.y}, {"c": 1 - place.c}
    copies.local(own, out.at[place.slot])
    for z in place.far_z():
        copies.send(own, out.at[place.slot], recv.at[place.slot], place.at_z(z))
    copies.send(own, out.at[place.slot], recv.at[place.slot], peer_y)
    copies.send(own, out.at[place.slot], recv.at[place.slot], peer_c)


def gather_middle(place, out, copies, recv):
    peer_y, peer_c = {"y": 1 - place.y}, {"c": 1 - place.c}
    for z in place.far_z():
        at = place.slot_of(z, place.c, place.y)
        copies.arrived(out.at[at], recv.at[at], place.at_z(z))
        copies.send(out.at[at], out.at[at], recv.at[at], peer_y)
        copies.send(out.at[at], out.at[at], recv.at[at], peer_c)
    for z in [place.z] + place.far_z():
        at = place.slot_of(z, place.c, 1 - place.y)
        copies.arrived(out.at[at], recv.at[at], peer_y)
        copies.send(out.at[at], out.at[at], recv.at[at], peer_c)


def gather_end(place, out, copies, recv):
    for z in [place.z] + place.far_z():
        for y in (place.y, 1 - place.y):
            at = place.slot_of(z, 1 - place.c, y)
            copies.arrived(out.at[at], recv.at[at], {"c": 1 - place.c})


def gather_copies(n_z):
    return 4 * n_z


def group_gather_kernel(own, out, send, recv):
    place = Place(False)
    copies = Copies(send)
    meet([place.at_z(1 - place.z), {"y": 1 - place.y}, {"c": 1 - place.c}])
    gather_begin(place, own, out, copies, recv)
    gather_middle(place, out, copies, recv)
    gather_end(place, out, copies, recv)
    copies.finish()


def group_gather(value, collective_id):
    return pl.pallas_call(
        group_gather_kernel,
        out_shape=jax.ShapeDtypeStruct((8,) + value.shape, value.dtype),
        in_specs=[ANY],
        out_specs=ANY,
        scratch_shapes=dma_sems(gather_copies(2), 8),
        compiler_params=comm_params(collective_id),
        name="group_gather",
    )(value)


def opening_kernel(
    own, blocks, ffn, out_w, out, blocks_all, ffn_all, out_w_all, send, recv, recv_w, recv_f, recv_o
):
    place, group = Place(True), Place(False)
    n_ctx = blocks.shape[0]
    copies = Copies(send)
    peer_x, peer_y, peer_c = {"x": 1 - place.x}, {"y": 1 - place.y}, {"c": 1 - place.c}
    far_ctx = others(place.ctx, n_ctx)
    meet([place.at_ctx(k) for k in far_ctx] + [peer_y, peer_x])
    mine = blocks_all.at[place.x, place.ctx]
    half = out_w.shape[1] // 2

    def sem_w(x, k):
        return recv_w.at[x * n_ctx + k]

    def out_block(x, z, c, y):
        at = (x * place.n_z + z) * 2 + c
        ref = out_w_all.at[at, :, pl.ds(pl.multiple_of(y * half, half), half)]
        return ref, recv_o.at[at * 2 + y]

    def give_out(x, z, c, y, peer):
        ref, sem = out_block(x, z, c, y)
        copies.send(ref, ref, sem, peer)

    def got_out(x, z, c, y, peer):
        ref, sem = out_block(x, z, c, y)
        copies.arrived(ref, sem, peer)

    gather_begin(place, own, out, copies, recv)
    for k in others(group.ctx, 4):
        copies.send(ffn.at[:, k], ffn_all.at[:, group.ctx], recv_f.at[group.ctx], group.at_ctx(k))
    copies.local(ffn.at[:, group.ctx], ffn_all.at[:, group.ctx])
    for k in far_ctx:
        copies.send(blocks.at[k], mine, sem_w(place.x, place.ctx), place.at_ctx(k))
    copies.local(blocks.at[place.ctx], mine)
    copies.send(blocks.at[place.ctx], mine, sem_w(place.x, place.ctx), peer_x)
    own_out, own_sem = out_block(place.x, place.z, place.c, place.y)
    own_half = out_w.at[:, pl.ds(pl.multiple_of(place.y * half, half), half)]
    copies.local(own_half, own_out)
    for z in place.far_z():
        copies.send(own_half, own_out, own_sem, place.at_z(z))
    for peer in (peer_x, peer_y, peer_c):
        copies.send(own_half, own_out, own_sem, peer)
    gather_middle(place, out, copies, recv)
    for k in far_ctx:
        block = blocks_all.at[place.x, k]
        copies.arrived(block, sem_w(place.x, k), place.at_ctx(k))
        copies.send(block, block, sem_w(place.x, k), peer_x)
    for z in place.far_z():
        got_out(place.x, z, place.c, place.y, place.at_z(z))
        for peer in (peer_x, peer_y, peer_c):
            give_out(place.x, z, place.c, place.y, peer)
    for z in [place.z] + place.far_z():
        got_out(1 - place.x, z, place.c, place.y, peer_x)
        for peer in (peer_y, peer_c):
            give_out(1 - place.x, z, place.c, place.y, peer)
    gather_end(place, out, copies, recv)
    for x in (place.x, 1 - place.x):
        for z in [place.z] + place.far_z():
            got_out(x, z, place.c, 1 - place.y, peer_y)
            give_out(x, z, place.c, 1 - place.y, peer_c)
    for k in [place.ctx] + far_ctx:
        copies.arrived(blocks_all.at[1 - place.x, k], sem_w(1 - place.x, k), peer_x)
    for k in others(group.ctx, 4):
        copies.arrived(ffn_all.at[:, k], recv_f.at[k], group.at_ctx(k))
    for x in (place.x, 1 - place.x):
        for z in [place.z] + place.far_z():
            for y in (place.y, 1 - place.y):
                got_out(x, z, 1 - place.c, y, peer_c)
    copies.finish()


def opening(own, blocks, ffn, out_w):
    n_ctx = blocks.shape[0]
    n_z = n_ctx // 2
    sends = gather_copies(n_z) + 2 * n_ctx + 8 + (n_z - 1) + 4 + 3 * n_z + 2 * n_z + 2 * n_z
    return pl.pallas_call(
        opening_kernel,
        out_shape=(
            jax.ShapeDtypeStruct((2 * n_ctx,) + own.shape, own.dtype),
            jax.ShapeDtypeStruct((2,) + blocks.shape, blocks.dtype),
            jax.ShapeDtypeStruct(ffn.shape, ffn.dtype),
            jax.ShapeDtypeStruct((2 * n_ctx,) + out_w.shape, out_w.dtype),
        ),
        in_specs=[ANY] * 4,
        out_specs=(ANY,) * 4,
        scratch_shapes=dma_sems(sends, 2 * n_ctx, 2 * n_ctx, 4, 4 * n_ctx),
        compiler_params=comm_params(1),
        name="opening",
    )(own, blocks, ffn, out_w)


def to_tokens_kernel(src, dst, send, recv):
    place = Place(True)
    copies = Copies(send)
    count, width = src.shape[0], src.shape[2]
    far = others(place.slot, count)
    meet([place.at_slot(s) for s in far])

    def columns(s):
        return dst.at[:, pl.ds(pl.multiple_of(s * width, width), width)]

    for s in far:
        copies.send(src.at[s], columns(place.slot), recv.at[place.slot], place.at_slot(s))
    copies.local(src.at[place.slot], columns(place.slot))
    for s in far:
        copies.arrived(columns(s), recv.at[s], place.at_slot(s))
    copies.finish()


def to_tokens(value):
    count, tokens, width = value.shape
    return pl.pallas_call(
        to_tokens_kernel,
        out_shape=jax.ShapeDtypeStruct((tokens, count * width), value.dtype),
        in_specs=[ANY],
        out_specs=ANY,
        scratch_shapes=dma_sems(count, count),
        compiler_params=comm_params(2),
        name="to_tokens",
    )(value)


def to_heads_kernel(src, dst, send, recv):
    place = Place(True)
    copies = Copies(send)
    count, width = dst.shape[0], dst.shape[2]
    far = others(place.slot, count)
    meet([place.at_slot(s) for s in far])

    def columns(s):
        return src.at[:, pl.ds(pl.multiple_of(s * width, width), width)]

    for s in far:
        copies.send(columns(s), dst.at[place.slot], recv.at[place.slot], place.at_slot(s))
    copies.local(columns(place.slot), dst.at[place.slot])
    for s in far:
        copies.arrived(dst.at[s], recv.at[s], place.at_slot(s))
    copies.finish()


def to_heads(value, count):
    tokens, width = value.shape[0], value.shape[1] // count
    return pl.pallas_call(
        to_heads_kernel,
        out_shape=jax.ShapeDtypeStruct((count, tokens, width), value.dtype),
        in_specs=[ANY],
        out_specs=ANY,
        scratch_shapes=dma_sems(count, count),
        compiler_params=comm_params(3),
        name="to_heads",
    )(value)


class Scatter:
    def __init__(self, place, part, held, from_c, from_y, from_z, out, copies, loads, rc, ry, rz):
        self.__dict__.update(locals())

    def order(self):
        return self.place.far_z() + [self.place.z]

    def begin(self):
        p = self.place
        for y in (1 - p.y, p.y):
            for z in self.order():
                at = z * 2 + y
                self.copies.send(
                    self.part.at[p.slot_of(z, 1 - p.c, y)], self.from_c.at[at], self.rc.at[at], {"c": 1 - p.c}
                )
        self.queue = [(z, y) for y in (1 - p.y, p.y) for z in self.order()]
        for at in range(min(self.held.shape[0], len(self.queue))):
            self.load(at)

    def load(self, at):
        p = self.place
        z, y = self.queue[at]
        at = at % self.held.shape[0]
        self.copies.local(self.part.at[p.slot_of(z, p.c, y)], self.held.at[at], self.loads.at[at])

    def add_c(self, step):
        z, y = self.queue[step]
        at, depth = z * 2 + y, self.held.shape[0]
        own = step % depth
        self.copies.arrived(self.from_c.at[at], self.rc.at[at], {"c": 1 - self.place.c})
        pltpu.make_async_copy(self.held.at[own], self.held.at[own], self.loads.at[own]).wait()
        self.from_c[at] = self.from_c[at] + self.held[own]
        if step + depth < len(self.queue):
            self.load(step + depth)

    def over_c_far(self):
        p = self.place
        for step, z in enumerate(self.order()):
            self.add_c(step)
            self.copies.send(self.from_c.at[z * 2 + 1 - p.y], self.from_y.at[z], self.ry.at[z], {"y": 1 - p.y})

    def over_c_near(self):
        for step in range(self.place.n_z):
            self.add_c(self.place.n_z + step)

    def over_y(self):
        p = self.place
        for z in self.order():
            self.copies.arrived(self.from_y.at[z], self.ry.at[z], {"y": 1 - p.y})
            self.from_y[z] = self.from_y[z] + self.from_c[z * 2 + p.y]
            if z is not p.z:
                self.copies.send(self.from_y.at[z], self.from_z.at[p.z], self.rz.at[p.z], p.at_z(z))

    def over_z(self):
        p = self.place
        total = self.from_y[p.z].astype(F32)
        for z in p.far_z():
            self.copies.arrived(self.from_z.at[z], self.rz.at[z], p.at_z(z))
            total = total + self.from_z[z].astype(F32)
        self.out[...] = total


def scatter_scratch(n_z, block):
    return [
        pltpu.VMEM((min(8, 2 * n_z),) + block, B16),
        pltpu.VMEM((2 * n_z,) + block, B16),
        pltpu.VMEM((n_z,) + block, B16),
        pltpu.VMEM((n_z,) + block, B16),
    ]


def scatter_sems(n_z, more=0):
    return dma_sems(4 * n_z + more, min(8, 2 * n_z), 2 * n_z, n_z, n_z)


def group_scatter_kernel(part, out, held, from_c, from_y, from_z, send, loads, rc, ry, rz):
    place = Place(False)
    copies = Copies(send)
    meet([place.at_z(1 - place.z), {"y": 1 - place.y}, {"c": 1 - place.c}])
    sums = Scatter(place, part, held, from_c, from_y, from_z, out, copies, loads, rc, ry, rz)
    sums.begin()
    sums.over_c_far()
    sums.over_c_near()
    sums.over_y()
    sums.over_z()
    copies.finish()


def group_scatter(part, collective_id):
    block = part.shape[1:]
    return pl.pallas_call(
        group_scatter_kernel,
        out_shape=jax.ShapeDtypeStruct(block, F32),
        in_specs=[ANY],
        out_specs=IN_VMEM,
        scratch_shapes=scatter_scratch(2, block) + scatter_sems(2),
        compiler_params=comm_params(collective_id),
        name="group_scatter",
    )(part)


class OutScatter:
    def __init__(self, place, part, held, from_c, from_x, from_y, from_z, out, copies, loads, rc, rx, ry, rz, rg):
        self.__dict__.update(locals())
        self.half = out.shape[2]

    def order(self):
        return self.place.far_z() + [self.place.z]

    def columns(self, y):
        return pl.ds(pl.multiple_of(y * self.half, self.half), self.half)

    def begin(self):
        p = self.place
        for x in (1 - p.x, p.x):
            for z in self.order():
                at = x * p.n_z + z
                self.copies.send(self.part.at[at * 2 + 1 - p.c], self.from_c.at[at], self.rc.at[at], {"c": 1 - p.c})
                self.copies.local(self.part.at[at * 2 + p.c], self.held.at[at], self.loads.at[at])

    def add_c(self, x, z):
        at = x * self.place.n_z + z
        self.copies.arrived(self.from_c.at[at], self.rc.at[at], {"c": 1 - self.place.c})
        pltpu.make_async_copy(self.held.at[at], self.held.at[at], self.loads.at[at]).wait()
        self.from_c[at] = self.from_c[at] + self.held[at]

    def over_c_far(self):
        p = self.place
        for z in self.order():
            self.add_c(1 - p.x, z)
            self.copies.send(
                self.from_c.at[(1 - p.x) * p.n_z + z], self.from_x.at[z], self.rx.at[z], {"x": 1 - p.x}
            )

    def over_c_near(self):
        for z in self.order():
            self.add_c(self.place.x, z)

    def over_x(self):
        p = self.place
        for z in self.order():
            self.copies.arrived(self.from_x.at[z], self.rx.at[z], {"x": 1 - p.x})
            self.from_x[z] = self.from_x[z] + self.from_c[p.x * p.n_z + z]
            self.copies.send(
                self.from_x.at[z, :, self.columns(1 - p.y)], self.from_y.at[z], self.ry.at[z], {"y": 1 - p.y}
            )

    def over_y(self):
        p = self.place
        for z in self.order():
            self.copies.arrived(self.from_y.at[z], self.ry.at[z], {"y": 1 - p.y})
            self.from_y[z] = self.from_y[z] + self.from_x[z, :, self.columns(p.y)]
            if z is not p.z:
                self.copies.send(self.from_y.at[z], self.from_z.at[p.z], self.rz.at[p.z], p.at_z(z))

    def over_z(self):
        p = self.place
        total = self.from_y[p.z].astype(F32)
        for z in p.far_z():
            self.copies.arrived(self.from_z.at[z], self.rz.at[z], p.at_z(z))
            total = total + self.from_z[z].astype(F32)
        self.out[p.y] = total.astype(B16)
        self.copies.send(self.out.at[p.y], self.out.at[p.y], self.rg.at[p.y], {"y": 1 - p.y})

    def end(self):
        p = self.place
        self.copies.arrived(self.out.at[1 - p.y], self.rg.at[1 - p.y], {"y": 1 - p.y})


def closing_kernel(
    part, grads, out_part, fc, proj, out, grads_out, out_w_out, fc_out, proj_out,
    held, from_c, from_y, from_z, own_x, from_x, o_held, o_c, o_x, o_y, o_z,
    send, loads, rc, ry, rz, load_x, rx, rk, rg, o_loads, orc, orx, ory, orz, org, rfc, rproj,
):
    place, group = Place(True), Place(False)
    n_ctx = grads.shape[1]
    copies = Copies(send)
    far_ctx = others(place.ctx, n_ctx)
    peer_x, peer_y = {"x": 1 - place.x}, {"y": 1 - place.y}
    meet([place.at_ctx(k) for k in far_ctx] + [peer_y, peer_x])
    sums = Scatter(place, part, held, from_c, from_y, from_z, out, copies, loads, rc, ry, rz)
    outs = OutScatter(place, out_part, o_held, o_c, o_x, o_y, o_z, out_w_out, copies, o_loads, orc, orx, ory, orz, org)
    sums.begin()
    for k in far_ctx + [place.ctx]:
        copies.send(grads.at[1 - place.x, k], from_x.at[k], rx.at[k], peer_x)
        copies.local(grads.at[place.x, k], own_x.at[k], load_x.at[k])
    outs.begin()
    for k in others(group.ctx, 4):
        copies.send(fc.at[k], fc_out.at[group.ctx], rfc.at[group.ctx], group.at_ctx(k))
        copies.send(proj.at[k], proj_out.at[group.ctx], rproj.at[group.ctx], group.at_ctx(k))
    copies.local(fc.at[group.ctx], fc_out.at[group.ctx])
    copies.local(proj.at[group.ctx], proj_out.at[group.ctx])
    sums.over_c_far()
    mine = grads_out.at[place.y, place.ctx]
    for k in far_ctx + [place.ctx]:
        copies.arrived(from_x.at[k], rx.at[k], peer_x)
        pltpu.make_async_copy(own_x.at[k], own_x.at[k], load_x.at[k]).wait()
        from_x[k] = from_x[k] + own_x[k]
        if k is not place.ctx:
            copies.send(from_x.at[k], mine, rk.at[place.ctx], place.at_ctx(k))
    copies.local(from_x.at[place.ctx], mine)
    copies.send(from_x.at[place.ctx], mine, rg.at[place.ctx], peer_y)
    sums.over_c_near()
    outs.over_c_far()
    outs.over_c_near()
    sums.over_y()
    outs.over_x()
    for k in far_ctx:
        block = grads_out.at[place.y, k]
        copies.arrived(block, rk.at[k], place.at_ctx(k))
        copies.send(block, block, rg.at[k], peer_y)
    outs.over_y()
    sums.over_z()
    outs.over_z()
    for k in [place.ctx] + far_ctx:
        copies.arrived(grads_out.at[1 - place.y, k], rg.at[k], peer_y)
    outs.end()
    for k in others(group.ctx, 4):
        copies.arrived(fc_out.at[k], rfc.at[k], group.at_ctx(k))
        copies.arrived(proj_out.at[k], rproj.at[k], group.at_ctx(k))
    copies.finish()


def closing(part, grads, out_part, fc, proj):
    block = part.shape[1:]
    n_ctx = grads.shape[1]
    n_z = n_ctx // 2
    piece = grads.shape[1:]
    rows, width = out_part.shape[1:]
    half = (rows, width // 2)
    return pl.pallas_call(
        closing_kernel,
        out_shape=(
            jax.ShapeDtypeStruct(block, F32),
            jax.ShapeDtypeStruct((2,) + piece, B16),
            jax.ShapeDtypeStruct((2,) + half, B16),
            jax.ShapeDtypeStruct(fc.shape, fc.dtype),
            jax.ShapeDtypeStruct(proj.shape, proj.dtype),
        ),
        in_specs=[ANY] * 5,
        out_specs=(IN_VMEM, ANY, IN_VMEM, ANY, ANY),
        scratch_shapes=scatter_scratch(n_z, block)
        + [pltpu.VMEM(piece, B16), pltpu.VMEM(piece, B16)]
        + [pltpu.VMEM((2 * n_z, rows, width), B16), pltpu.VMEM((2 * n_z, rows, width), B16)]
        + [pltpu.VMEM((n_z, rows, width), B16), pltpu.VMEM((n_z,) + half, B16), pltpu.VMEM((n_z,) + half, B16)]
        + scatter_sems(n_z, 3 * n_ctx + 6 * n_z + 8)
        + dma_sems(n_ctx, n_ctx, n_ctx, n_ctx)
        + dma_sems(2 * n_z, 2 * n_z, n_z, n_z, n_z, 2, 4, 4),
        compiler_params=comm_params(4),
        name="closing",
    )(part, grads, out_part, fc, proj)


def vectors_kernel(src, own_out, ff_out, from_all, half, from_y, send, recv, ry):
    place = Place(True)
    count = src.shape[0]
    n_ctx = count // 2
    copies = Copies(send)
    me = place.x * n_ctx + place.ctx
    far = others(me, count)
    peer_y = {"y": 1 - place.y}

    def peer(k):
        return dict(place.at_ctx(lax.rem(k, n_ctx)), x=k // n_ctx)

    meet([peer(k) for k in far] + [peer_y])
    for k in far:
        copies.send(src.at[k], from_all.at[me], recv.at[me], peer(k))
    from_all[me] = src[me]
    for k in far:
        copies.arrived(from_all.at[k], recv.at[k], peer(k))
    total = from_all[0, 0:8, :]
    for k in range(1, count):
        total = total + from_all[k, 0:8, :]
    half[...] = total
    copies.send(half, from_y, ry.at[0], peer_y)
    for part in range(4):
        total = from_all[part, 8:16, :]
        for k in range(part + 4, count, 4):
            total = total + from_all[k, 8:16, :]
        ff_out[part] = total
    copies.arrived(from_y, ry.at[0], peer_y)
    own_out[...] = half[...] + from_y[...]
    copies.finish()


def vectors_sum(value):
    count = value.shape[0]
    flat = jax.ShapeDtypeStruct((8, 128), F32)
    return pl.pallas_call(
        vectors_kernel,
        out_shape=(flat, jax.ShapeDtypeStruct((4, 8, 128), F32)),
        in_specs=[IN_VMEM],
        out_specs=(IN_VMEM, IN_VMEM),
        scratch_shapes=[
            pltpu.VMEM(value.shape, F32),
            pltpu.VMEM((8, 128), F32),
            pltpu.VMEM((8, 128), F32),
        ]
        + dma_sems(count + 1, count, 1),
        compiler_params=comm_params(5),
        name="vectors_sum",
    )(value)


def project_kernel(feats, x_ref, gain_ref, shift_ref, mask_ref, w_ref, bias_ref, norm_ref, qkv_ref):
    x = x_ref[...].astype(F32)
    mean = jnp.sum(x, axis=1, keepdims=True) * (1.0 / feats)
    centered = (x - mean) * mask_ref[...]
    inv = lax.rsqrt(jnp.sum(centered * centered, axis=1, keepdims=True) * (1.0 / feats) + NORM_EPS)
    norm = (centered * inv * gain_ref[...] + shift_ref[...]).astype(B16)
    norm_ref[...] = norm
    qkv_ref[...] = (dot(norm, w_ref[...], 1, 0) + bias_ref[...]).astype(B16)


def project(x, gain, shift, mask, weight, bias, feats):
    total, wide = x.shape
    cols = weight.shape[1]
    step = min(256, total)

    def fixed(shape):
        return pl.BlockSpec(shape, lambda i: (0, 0))

    return pl.pallas_call(
        functools.partial(project_kernel, feats),
        grid=(total // step,),
        in_specs=[pl.BlockSpec((step, wide), lambda i: (i, 0))]
        + [fixed((1, wide))] * 3
        + [fixed((wide, cols)), fixed((1, cols))],
        out_specs=(pl.BlockSpec((step, wide), lambda i: (i, 0)), pl.BlockSpec((step, cols), lambda i: (i, 0))),
        out_shape=(jax.ShapeDtypeStruct((total, wide), B16), jax.ShapeDtypeStruct((total, cols), B16)),
        compiler_params=pltpu.CompilerParams(vmem_limit_bytes=VMEM_LIMIT),
        cost_estimate=pl.CostEstimate(
            flops=2 * total * wide * cols, bytes_accessed=4 * total * wide, transcendentals=total
        ),
        name="project",
    )(x, gain[None], shift[None], mask[None], weight, bias[None])


def after(value, other, unpack=False):
    value, other = lax.optimization_barrier((value, other))
    return (*value, other) if unpack else (value, other)


def shift_perm(count, step):
    return [(i, (i + step) % count) for i in range(count)]


def on_device(
    sizes, block_input, segment_ids, slot_order, first_gain, first_shift, qkv_weight, qv_bias, out_weight, out_bias,
    second_gain, second_shift, fc_weight, fc_bias, proj_weight, proj_bias, out_grad,
):
    n_x, n_ctx, n_y = sizes
    n_slot = n_ctx * n_y
    n_shard = n_x * n_ctx
    n_h = n_ctx // 4
    slot_len, feats = block_input.shape[1:]
    head = feats // HEADS
    pair = 2 * head
    rows = qkv_weight.shape[0]
    ff_own = fc_weight.shape[1] // 4
    padded = n_slot * pair
    y_at = lax.axis_index("y")
    ctx_at = lax.axis_index(CTX)
    slot_at = lax.axis_index(ROW)
    lc_at = lax.axis_index(("l", "c"))
    x_at, h_at = lax.axis_index("x"), lax.axis_index("h")

    def gather(value, axes):
        return lax.all_gather(value, axes, axis=0, tiled=True)

    tall = rows + (-rows % 16)
    wide = n_shard * tall
    row_pad = tall - rows

    def widened(value):
        lead = value.shape[:-1]
        value = value.reshape(lead + (n_shard, rows))
        return jnp.pad(value, [(0, 0)] * (len(lead) + 1) + [(0, row_pad)]).reshape(lead + (wide,))

    def narrowed(value):
        lead = value.shape[:-1]
        return value.reshape(lead + (n_shard, tall))[..., :rows].reshape(lead + (feats,))

    mask = jnp.asarray((np.arange(wide) % tall < rows).astype(np.float32))

    small = jnp.concatenate([first_gain, first_shift, out_bias, second_gain, second_shift, proj_bias, qv_bias])
    packed = jnp.pad(qkv_weight.reshape(rows, 3, feats), ((0, 0), (0, 0), (0, padded - feats)))
    packed = lax.dynamic_index_in_dim(packed.reshape(rows, 3, n_ctx, n_y, pair), y_at, 3, False)
    packed = packed.transpose(2, 0, 1, 3).reshape(n_ctx, rows, 3 * pair)
    small = jnp.pad(small, (0, row_pad * 3 * pair - small.shape[0])).reshape(1, row_pad, 3 * pair)
    packed = jnp.concatenate([packed, jnp.broadcast_to(small, (n_ctx, row_pad, 3 * pair))], axis=1)
    ffn_blocks = jnp.stack([fc_weight, proj_weight.T])
    ffn_blocks = jnp.pad(ffn_blocks, ((0, 0), (0, row_pad), (0, 0))).reshape(2, tall, 4, ff_own).transpose(0, 2, 1, 3)
    own_input = widened(block_input[0])
    grad_own = widened(out_grad[0])
    all_input, packed, ffn_blocks, w_out = opening(
        own_input, packed, ffn_blocks, widened(jnp.pad(out_weight, ((0, row_pad), (0, 0))))
    )
    grad_late, all_input = after(grad_own, all_input)
    grad_all = gather(grad_late, FFG)
    ffn_blocks = ffn_blocks.reshape(2, 4 * tall, ff_own)
    along_h = [lax.ppermute(ffn_blocks, "h", shift_perm(n_h, step)) for step in range(1, n_h)]
    along_x = lax.ppermute(ffn_blocks, "x", shift_perm(n_x, 1))
    w_out = w_out.reshape(wide, wide)
    packed = packed.reshape(n_shard, tall, 3 * pair)
    w_qkv = packed.reshape(wide, 3 * pair)
    smalls = packed[:, rows:].reshape(n_shard, -1)[:, : 8 * rows].astype(F32)
    singles = jnp.pad(smalls[:, : 6 * rows].reshape(n_shard, 6, rows), ((0, 0), (0, 0), (0, row_pad)))
    gain_one, shift_one, bias_out, gain_two, shift_two, bias_proj = singles.transpose(1, 0, 2).reshape(6, wide)
    bias_qv = smalls[:, 6 * rows :].reshape(2, feats)
    bias_pair = lax.dynamic_slice_in_dim(
        jnp.pad(bias_qv, ((0, 0), (0, padded - feats))), slot_at * pair, pair, 1
    )
    bias_qkv = jnp.concatenate([bias_pair[0], jnp.zeros((pair,), F32), bias_pair[1]])
    b_fc = lax.dynamic_slice_in_dim(fc_bias, lc_at * ff_own, ff_own, 0).astype(F32)

    order = slot_order[0]
    pieces = jnp.arange(n_slot, dtype=jnp.int32)
    inv = jnp.sum(jnp.where(order[None, :] == pieces[:, None], pieces[None, :], 0), axis=1).astype(jnp.int32)
    segs = jnp.take(segment_ids[0].reshape(n_slot, slot_len), inv, axis=0).reshape(-1)
    docs = jnp.arange(DOCS, dtype=jnp.int32)
    counts = jnp.sum((segs[None, :] == docs[:, None]).astype(jnp.int32), axis=1)
    starts = jnp.sum(jnp.where(segs[None, :] > docs[:, None], counts[:, None], 0), axis=0).astype(jnp.int32)
    start3 = starts.reshape(-1, 1, BLK)
    low = start3[:, 0, 0] // BLK

    own_wide = own_input.astype(F32)
    norm_one, qkv = project(
        all_input.reshape(n_slot * slot_len, wide), gain_one, shift_one, mask, w_qkv, bias_qkv, feats
    )
    heads_out, lse = attend(inv, low, qkv, start3, slot_len, head)
    attention = widened(to_tokens(heads_out.reshape(n_slot, slot_len, pair))[:, :feats])
    hidden = own_wide + dot(attention, w_out, 1, 0) + bias_out
    normed_two, inv_two = norm_forward(hidden, mask, feats)
    norm_two = (normed_two * gain_two + shift_two).astype(B16)
    grad_wide = grad_own.astype(F32)
    along_h, grad_all, norm_two = after((along_h, grad_all), norm_two, True)
    along_both = [lax.ppermute(value, "x", shift_perm(n_x, 1)) for value in along_h]
    norm_all = group_gather(norm_two, 6).reshape(-1, wide)
    w_ffn = jnp.zeros((2, n_x, n_h, 4 * tall, ff_own), B16)

    def put(whole, value, x, h):
        return lax.dynamic_update_slice(whole, value[:, None, None], (0, x, h, 0, 0))

    w_ffn = put(put(w_ffn, ffn_blocks, x_at, h_at), along_x, 1 - x_at, h_at)
    for step in range(1, n_h):
        h_from = lax.rem(h_at + n_h - step, n_h)
        w_ffn = put(put(w_ffn, along_h[step - 1], x_at, h_from), along_both[step - 1], 1 - x_at, h_from)
    w_fc, w_proj = w_ffn[0].reshape(wide, ff_own), w_ffn[1].reshape(wide, ff_own)
    preact = dot(norm_all, w_fc, 1, 0) + b_fc
    activated, derivative = gelu_parts(preact)
    activation = activated.astype(B16)
    mlp_part = dot(activation, w_proj, 1, 1).astype(B16)

    dpreact = dot(grad_all, w_proj, 1, 0) * derivative
    dpreact_b = dpreact.astype(B16)
    dnorm_part = dot(dpreact_b, w_fc, 1, 1).astype(B16)
    dnorm_two = group_scatter(dnorm_part.reshape(8, slot_len, wide), 7)

    def pick(value, at):
        return lax.dynamic_index_in_dim(value, at, 0, False)

    def by_owner(value):
        return value.astype(B16).reshape(n_x, n_h, 4 * tall, ff_own)

    proj_part = by_owner(dot(grad_all, activation, 0, 0))
    proj_x = lax.ppermute(pick(proj_part, 1 - x_at), "x", shift_perm(n_x, 1))
    fc_part = by_owner(dot(norm_all, dpreact_b, 0, 0))
    fc_x = lax.ppermute(pick(fc_part, 1 - x_at), "x", shift_perm(n_x, 1))

    def over_h(value):
        gives = [pick(value, lax.rem(h_at + step, n_h)) for step in range(1, n_h)]
        return [lax.ppermute(give, "h", shift_perm(n_h, step + 1)) for step, give in enumerate(gives)]

    def total(value, received):
        value = pick(value, h_at).astype(F32)
        for other in received:
            value = value + other
        return value.astype(B16).reshape(4, tall, ff_own)

    proj_x, mlp_part, dnorm_two = after((proj_x, mlp_part), dnorm_two, True)
    proj_line = pick(proj_part, x_at) + proj_x
    proj_h = over_h(proj_line)
    mlp = lax.psum_scatter(mlp_part, FFG, scatter_dimension=0, tiled=True)
    dhidden = grad_wide + norm_backward(dnorm_two, normed_two, inv_two, gain_two, feats)
    dhidden_b = dhidden.astype(B16)
    out_part = dot(attention, dhidden_b, 0, 0).astype(B16).reshape(n_shard, tall, wide)
    dattention = narrowed(dot(dhidden_b, w_out, 1, 1).astype(B16))
    dattention = jnp.pad(dattention, ((0, 0), (0, padded - feats)))
    dattention = to_heads(dattention, n_slot).reshape(n_slot * slot_len, pair)
    fc_x, dattention = after(fc_x, dattention)
    fc_line = pick(fc_part, x_at) + fc_x
    fc_h = over_h(fc_line)
    dqkv = attend_back(inv, low, qkv, heads_out, dattention, lse, start3, slot_len, head)
    dqkv_b = dqkv.astype(B16)
    dnorm_one_part = dot(dqkv_b, w_qkv, 1, 1).astype(B16)
    qkv_part = dot(norm_one, dqkv_b, 0, 0).astype(B16).reshape(n_x, n_ctx, tall, 3 * pair)
    proj_h, fc_h, dnorm_one_part = after((proj_h, fc_h), dnorm_one_part, True)
    dnorm_one, qkv_all, out_all, fc_all, proj_all = closing(
        dnorm_one_part.reshape(n_slot, slot_len, wide), qkv_part, out_part, total(fc_line, fc_h), total(proj_line, proj_h)
    )
    mlp, dnorm_one = after(mlp, dnorm_one)
    block_output = narrowed(hidden + mlp.astype(F32) + bias_proj)
    proj_grad = proj_all[:, :rows].astype(F32).transpose(0, 2, 1).reshape(4 * ff_own, rows)
    fc_grad = fc_all[:, :rows].astype(F32).transpose(1, 0, 2).reshape(rows, 4 * ff_own)
    qkv_all = qkv_all[:, :, :rows].reshape(n_y, n_ctx, rows, 3, pair)
    qkv_grad = qkv_all.transpose(2, 3, 1, 0, 4).reshape(rows, 3, padded)
    qkv_grad = qkv_grad[:, :, :feats].reshape(rows, 3 * feats).astype(F32)
    out_grad_w = narrowed(out_all[:, :rows].transpose(1, 0, 2).reshape(rows, wide)).astype(F32)

    normed_one, inv_one = norm_forward(own_wide, mask, feats)
    input_grad = narrowed(dhidden + norm_backward(dnorm_one, normed_one, inv_one, gain_one, feats))

    dq_sum, dv_sum = jnp.sum(dqkv[:, :pair], axis=0), jnp.sum(dqkv[:, 2 * pair :], axis=0)

    def placed(value, width, at):
        return lax.dynamic_update_slice(jnp.zeros((width,), F32), value, (at,))[:feats]

    vectors = jnp.stack(
        [
            jnp.sum(dhidden, axis=0),
            jnp.sum(dnorm_one * normed_one, axis=0),
            jnp.sum(dnorm_one, axis=0),
            jnp.sum(dnorm_two * normed_two, axis=0),
            jnp.sum(dnorm_two, axis=0),
            jnp.sum(grad_wide, axis=0),
        ]
    )
    qv_sums = jnp.concatenate([placed(dq_sum, padded, slot_at * pair), placed(dv_sum, padded, slot_at * pair)])
    vectors = jnp.concatenate(
        [
            vectors.reshape(6, n_shard, tall).transpose(1, 0, 2).reshape(n_shard, 6 * tall),
            qv_sums.reshape(n_shard, 2 * rows),
            jnp.zeros((n_shard, 1024 - 6 * tall - 2 * rows), F32),
            jnp.broadcast_to(jnp.sum(dpreact, axis=0)[None], (n_shard, ff_own)),
            jnp.zeros((n_shard, 1024 - ff_own), F32),
        ],
        axis=1,
    )
    owned, ff_sums = vectors_sum(vectors.reshape(n_shard, 16, 128))
    owned = owned.reshape(1024)
    fc_bias_grad = ff_sums.reshape(4, 1024)[:, :ff_own].reshape(4 * ff_own)
    qv_grad = owned[6 * tall : 6 * tall + 2 * rows]

    def own(index):
        return owned[index * tall : index * tall + rows]

    return (
        block_output[None],
        input_grad[None],
        qkv_grad,
        qv_grad,
        out_grad_w,
        own(0),
        own(1),
        own(2),
        own(3),
        own(4),
        fc_grad,
        fc_bias_grad,
        proj_grad,
        own(5),
    )


def solution(mesh):
    n_x, n_ctx, n_y = (mesh.shape[axis] for axis in ("dp", "context", "tensor"))
    inner = Mesh(mesh.devices.reshape(n_x, n_ctx // 4, 2, 2, n_y), ("x", "h", "l", "c", "y"))
    tokens = P("x", ROW, None)
    shard = P(SHARD)
    shard_rows = P(SHARD, None)
    return jax.shard_map(
        functools.partial(on_device, (n_x, n_ctx, n_y)),
        mesh=inner,
        in_specs=(
            tokens, P("x", None), P("x", None), shard, shard, shard_rows, shard, shard_rows, shard, shard, shard,
            P(SHARD, "y"), P("y"), P("y", SHARD), shard, tokens,
        ),
        out_specs=(
            tokens, tokens, shard_rows, shard, shard_rows, shard, shard, shard, shard, shard,
            P(SHARD, "y"), P("y"), P("y", SHARD), shard,
        ),
        check_vma=False,
    )
```

```python
import functools
import math

import jax
import jax.numpy as jnp
import numpy as np
from jax import lax
from jax.experimental import pallas as pl
from jax.experimental.layout import Layout, with_layout_constraint
from jax.experimental.pallas import tpu as pltpu
from jax.sharding import Mesh
from jax.sharding import PartitionSpec as P

HEADS = 25
DOCS = 8
NORM_EPS = 1e-05
GELU_SCALE = 0.7978845608028654
GELU_CUBE = 0.044715
MASK_FLOOR = -1e30

F32 = jnp.float32
B16 = jnp.bfloat16
BLK = 256
VMEM_LIMIT = 60 * 1024 * 1024

ROW = ("h", "l", "c", "y")
CTX = ("h", "l", "c")
SHARD = ("x", "h", "l", "c")
FFG = ("l", "c", "y")


def gelu_parts(values):
    inner_arg = GELU_SCALE * (values + GELU_CUBE * values * values * values)
    tanh_value = jnp.tanh(inner_arg)
    result = 0.5 * values * (1.0 + tanh_value)
    derivative = 0.5 * (1.0 + tanh_value) + 0.5 * values * (
        1.0 - tanh_value * tanh_value
    ) * GELU_SCALE * (1.0 + 3.0 * GELU_CUBE * values * values)
    return (result, derivative)


def norm_forward(values, mask, feats):
    mean_value = jnp.sum(values, axis=-1, keepdims=True) / feats
    centered = (values - mean_value) * mask
    inv_sigma = lax.rsqrt(jnp.sum(centered * centered, axis=-1, keepdims=True) / feats + NORM_EPS)
    return (centered * inv_sigma, inv_sigma)


def norm_backward(upstream, normed, inv_sigma, norm_gain, feats):
    scaled = upstream * norm_gain
    return inv_sigma * (
        scaled
        - jnp.sum(scaled, axis=-1, keepdims=True) / feats
        - normed * (jnp.sum(scaled * normed, axis=-1, keepdims=True) / feats)
    )


def dot(left, right, left_dim, right_dim):
    return lax.dot_general(
        left, right, (((left_dim,), (right_dim,)), ((), ())), preferred_element_type=F32
    )


def sort_slots(inv_ref, src_ref, dst_ref, slot_len, start=0, width=None, factor=None):
    width = src_ref.shape[1] if width is None else width

    def body(piece, carry):
        slot = inv_ref[piece]
        rows = src_ref[pl.ds(pl.multiple_of(slot * slot_len, slot_len), slot_len), start : start + width]
        if factor is not None:
            rows = rows * jnp.asarray(factor, rows.dtype)
        dst_ref[pl.ds(pl.multiple_of(piece * slot_len, slot_len), slot_len), :] = rows
        return carry

    lax.fori_loop(0, src_ref.shape[0] // slot_len, body, 0)


def unsort_block(inv_ref, dst_ref, value, block, slot_len):
    for part in range(BLK // slot_len):
        slot = inv_ref[block * (BLK // slot_len) + part]
        dst_ref[pl.ds(pl.multiple_of(slot * slot_len, slot_len), slot_len), :] = value[
            part * slot_len : (part + 1) * slot_len
        ].astype(dst_ref.dtype)


def block_rows(block):
    return pl.ds(pl.multiple_of(block * BLK, BLK), BLK)


def mask_of(start_row, key_block, query_block, diagonal):
    key_at = key_block * BLK + lax.broadcasted_iota(jnp.int32, (BLK, BLK), 0)
    allowed = key_at >= start_row
    if diagonal:
        query_at = query_block * BLK + lax.broadcasted_iota(jnp.int32, (BLK, BLK), 1)
        allowed = jnp.logical_and(allowed, key_at <= query_at)
    return allowed


def attend_kernel(slot_len, head, inv_ref, low_ref, qkv_ref, start_ref, out_ref, lse_ref, q_s, k_s, vt_s):
    total = qkv_ref.shape[0]
    pair = 2 * head
    sort_slots(inv_ref, qkv_ref, q_s, slot_len, 0, pair, 1.0 / math.sqrt(head))
    sort_slots(inv_ref, qkv_ref, k_s, slot_len, pair, pair)

    def fill(piece, carry):
        slot = inv_ref[piece]
        rows = qkv_ref[pl.ds(pl.multiple_of(slot * slot_len, slot_len), slot_len), 2 * pair :]
        vt_s[:, pl.ds(pl.multiple_of(piece * slot_len, slot_len), slot_len)] = rows.astype(F32).T.astype(B16)
        return carry

    lax.fori_loop(0, total // slot_len, fill, 0)

    def per_query(block, carry):
        queries = q_s[block_rows(block), :]
        start_row = start_ref[block]

        def step(key_block, state, diagonal):
            allowed = mask_of(start_row, key_block, block, diagonal)
            keys = k_s[block_rows(key_block), :]
            values = vt_s[:, block_rows(key_block)]
            fresh = []
            for part in range(2):
                old_max, old_sum, old_acc = state[part]
                cols = slice(part * head, (part + 1) * head)
                scores = dot(keys[:, cols], queries[:, cols], 1, 1)
                scores = jnp.where(allowed, scores, MASK_FLOOR)
                new_max = jnp.maximum(old_max, jnp.max(scores, axis=0, keepdims=True))
                weights = jnp.where(allowed, jnp.exp(scores - new_max), 0.0)
                shrink = jnp.exp(old_max - new_max)
                new_sum = old_sum * shrink + jnp.sum(weights, axis=0, keepdims=True)
                new_acc = old_acc * shrink + dot(values[cols, :], weights.astype(B16), 1, 0)
                fresh.append((new_max, new_sum, new_acc))
            return tuple(fresh)

        first = tuple(
            (
                jnp.full((1, BLK), MASK_FLOOR, F32),
                jnp.zeros((1, BLK), F32),
                jnp.zeros((head, BLK), F32),
            )
            for part in range(2)
        )
        state = lax.fori_loop(low_ref[block], block, lambda j, s: step(j, s, False), first)
        state = step(block, state, True)
        lse_ref[block] = jnp.concatenate([s[0] + jnp.log(s[1]) for s in state], axis=0)
        result = jnp.concatenate([s[2] / s[1] for s in state], axis=0)
        unsort_block(inv_ref, out_ref, result.T, block, slot_len)
        return carry

    lax.fori_loop(0, total // BLK, per_query, 0)


def attend(inv, low, qkv, start3, slot_len, head):
    total = qkv.shape[0]
    vmem = pl.BlockSpec(memory_space=pltpu.VMEM)
    smem = pl.BlockSpec(memory_space=pltpu.SMEM)
    return pl.pallas_call(
        functools.partial(attend_kernel, slot_len, head),
        out_shape=(
            jax.ShapeDtypeStruct((total, 2 * head), B16),
            jax.ShapeDtypeStruct((total // BLK, 2, BLK), F32),
        ),
        in_specs=[smem, smem, vmem, vmem],
        out_specs=(vmem, vmem),
        scratch_shapes=[
            pltpu.VMEM((total, 2 * head), B16),
            pltpu.VMEM((total, 2 * head), B16),
            pltpu.VMEM((2 * head, total), B16),
        ],
        compiler_params=pltpu.CompilerParams(vmem_limit_bytes=VMEM_LIMIT),
        name="attend",
    )(inv, low, qkv, start3)


def attend_back_kernel(
    slot_len, head, inv_ref, low_ref, qkv_ref, out_ref, grad_ref, lse_ref, start_ref,
    dqkv_ref, q_s, k_s, v_s, kt_s, o_s, g_s, dk_s, dv_s,
):
    total = qkv_ref.shape[0]
    pair = 2 * head
    scale = 1.0 / math.sqrt(head)
    sort_slots(inv_ref, qkv_ref, q_s, slot_len, 0, pair, scale)
    sort_slots(inv_ref, qkv_ref, k_s, slot_len, pair, pair)
    sort_slots(inv_ref, qkv_ref, v_s, slot_len, 2 * pair, pair)
    sort_slots(inv_ref, out_ref, o_s, slot_len)
    sort_slots(inv_ref, grad_ref, g_s, slot_len)

    def fill(block, carry):
        kt_s[:, block_rows(block)] = k_s[block_rows(block), :].astype(F32).T.astype(B16)
        return carry

    lax.fori_loop(0, total // BLK, fill, 0)
    dk_s[...] = jnp.zeros_like(dk_s)
    dv_s[...] = jnp.zeros_like(dv_s)

    def per_query(block, carry):
        queries = q_s[block_rows(block), :]
        grads = g_s[block_rows(block), :]
        start_row = start_ref[block]
        lse = lse_ref[block]
        prod = (grads.astype(F32) * o_s[block_rows(block), :].astype(F32)).T
        delta = [jnp.sum(prod[part * head : (part + 1) * head], axis=0, keepdims=True) for part in range(2)]

        def step(key_block, state, diagonal):
            allowed = mask_of(start_row, key_block, block, diagonal)
            rows = block_rows(key_block)
            keys = k_s[rows, :]
            values = v_s[rows, :]
            flipped = kt_s[:, rows]
            fresh, dks, dvs = [], [], []
            for part in range(2):
                cols = slice(part * head, (part + 1) * head)
                scores = dot(keys[:, cols], queries[:, cols], 1, 1)
                weights = jnp.where(allowed, jnp.exp(scores - lse[part : part + 1]), 0.0)
                dprob = dot(values[:, cols], grads[:, cols], 1, 1)
                dscore = (weights * (dprob - delta[part])).astype(B16)
                dvs.append(dot(weights.astype(B16), grads[:, cols], 1, 0))
                dks.append(dot(dscore, queries[:, cols], 1, 0))
                fresh.append(state[part] + dot(flipped[cols, :], dscore, 1, 0))
            dk_s[rows, :] += jnp.concatenate(dks, axis=1)
            dv_s[rows, :] += jnp.concatenate(dvs, axis=1)
            return tuple(fresh)

        state = (jnp.zeros((head, BLK), F32), jnp.zeros((head, BLK), F32))
        state = lax.fori_loop(low_ref[block], block, lambda j, s: step(j, s, False), state)
        state = step(block, state, True)
        dq = jnp.concatenate(state, axis=0).T * scale
        for part in range(BLK // slot_len):
            slot = inv_ref[block * (BLK // slot_len) + part]
            dqkv_ref[pl.ds(pl.multiple_of(slot * slot_len, slot_len), slot_len), 0:pair] = dq[
                part * slot_len : (part + 1) * slot_len
            ]
        return carry

    lax.fori_loop(0, total // BLK, per_query, 0)

    def give(piece, carry):
        slot = inv_ref[piece]
        rows = pl.ds(pl.multiple_of(slot * slot_len, slot_len), slot_len)
        held = pl.ds(pl.multiple_of(piece * slot_len, slot_len), slot_len)
        dqkv_ref[rows, pair : 2 * pair] = dk_s[held, :]
        dqkv_ref[rows, 2 * pair :] = dv_s[held, :]
        return carry

    lax.fori_loop(0, total // slot_len, give, 0)


def attend_back(inv, low, qkv, out, grad, lse, start3, slot_len, head):
    total = qkv.shape[0]
    pair = 2 * head
    vmem = pl.BlockSpec(memory_space=pltpu.VMEM)
    smem = pl.BlockSpec(memory_space=pltpu.SMEM)
    held = pltpu.VMEM((total, pair), B16)
    return pl.pallas_call(
        functools.partial(attend_back_kernel, slot_len, head),
        out_shape=jax.ShapeDtypeStruct((total, 3 * pair), F32),
        in_specs=[smem, smem] + [vmem] * 5,
        out_specs=vmem,
        scratch_shapes=[
            held, held, held, pltpu.VMEM((pair, total), B16), held, held,
            pltpu.VMEM((total, pair), F32), pltpu.VMEM((total, pair), F32),
        ],
        compiler_params=pltpu.CompilerParams(vmem_limit_bytes=VMEM_LIMIT),
        name="attend_back",
    )(inv, low, qkv, out, grad, lse, start3)


class Place:
    def __init__(self, whole_line):
        self.x, self.h, self.l, self.c, self.y = (lax.axis_index(a) for a in ("x", "h", "l", "c", "y"))
        self.whole_line = whole_line
        self.n_z = 2 * lax.axis_size("h") if whole_line else 2
        self.z = self.h * 2 + self.l if whole_line else self.l
        self.ctx = self.z * 2 + self.c
        self.slot = self.ctx * 2 + self.y

    def at_z(self, z):
        return {"h": z // 2, "l": lax.rem(z, 2)} if self.whole_line else {"l": z}

    def at_ctx(self, k):
        return dict(self.at_z(k // 2), c=lax.rem(k, 2))

    def at_slot(self, s):
        return dict(self.at_ctx(s // 2), y=lax.rem(s, 2))

    def far_z(self):
        order = []
        for step in range(1, self.n_z // 2 + 1):
            order += [step] if 2 * step == self.n_z else [step, self.n_z - step]
        return [lax.rem(self.z + step, self.n_z) for step in order]

    def slot_of(self, z, c, y):
        return (z * 2 + c) * 2 + y


class Copies:
    def __init__(self, sems):
        self.sems = sems
        self.begun = []

    def send(self, src, dst, recv, peer, when=None):
        at = len(self.begun)
        copy = pltpu.make_async_remote_copy(
            src_ref=src,
            dst_ref=dst,
            send_sem=self.sems.at[at],
            recv_sem=recv,
            device_id=peer,
            device_id_type=pl.DeviceIdType.MESH,
        )
        if when is None:
            copy.start()
            self.begun.append(copy.wait_send)
        else:
            pl.when(when)(copy.start)
            self.begun.append(lambda: pl.when(when)(copy.wait_send))

    def local(self, src, dst, sem=None):
        copy = pltpu.make_async_copy(src, dst, self.sems.at[len(self.begun)] if sem is None else sem)
        copy.start()
        if sem is None:
            self.begun.append(copy.wait)
        return copy

    def arrived(self, dst, recv, peer):
        pltpu.make_async_remote_copy(
            src_ref=dst,
            dst_ref=dst,
            send_sem=self.sems.at[0],
            recv_sem=recv,
            device_id=peer,
            device_id_type=pl.DeviceIdType.MESH,
        ).wait_recv()

    def finish(self):
        for wait in self.begun:
            wait()


def meet(peers):
    barrier = pltpu.get_barrier_semaphore()
    for peer in peers:
        pl.semaphore_signal(barrier, inc=1, device_id=peer, device_id_type=pl.DeviceIdType.MESH)
    pl.semaphore_wait(barrier, len(peers))


def others(me, count):
    return [lax.rem(me + step, count) for step in range(1, count)]


ANY = pl.BlockSpec(memory_space=pl.ANY)
IN_VMEM = pl.BlockSpec(memory_space=pltpu.VMEM)


def dma_sems(*counts):
    return [pltpu.SemaphoreType.DMA((count,)) for count in counts]


def comm_params(collective_id):
    return pltpu.CompilerParams(
        collective_id=collective_id, has_side_effects=True, vmem_limit_bytes=VMEM_LIMIT
    )


class Line:
    def __init__(self, place, copies, block):
        self.place, self.copies, self.block = place, copies, block

    def pass_on(self, src, z, step, when):
        p = self.place
        ref, sem = self.block(z)
        peer = p.at_z(jnp.clip(p.z + step, 0, p.n_z - 1))
        self.copies.send(ref if src is None else src, ref, sem, peer, when)

    def begin(self, own):
        p = self.place
        self.pass_on(own, p.z, 1, p.z < p.n_z - 1)
        self.pass_on(own, p.z, -1, p.z > 0)

    def arrive(self, distance, then):
        p = self.place
        for side in (1, -1):
            z = p.z + side * distance
            here = jnp.logical_and(z >= 0, z < p.n_z)
            z = jnp.clip(z, 0, p.n_z - 1)
            ref, sem = self.block(z)
            peer = p.at_z(jnp.clip(p.z + side, 0, p.n_z - 1))
            pl.when(here)(lambda: self.copies.arrived(ref, sem, peer))
            beyond = p.z - side
            beyond = jnp.logical_and(beyond >= 0, beyond < p.n_z)
            self.pass_on(None, z, -side, jnp.logical_and(here, beyond))
            then(z, here)


def row_line(place, out, copies, recv):
    def block(z):
        at = place.slot_of(z, place.c, place.y)
        return out.at[at], recv.at[at]

    return Line(place, copies, block)


def gather_begin(place, own, out, copies, recv):
    peer_y, peer_c = {"y": 1 - place.y}, {"c": 1 - place.c}
    copies.local(own, out.at[place.slot])
    line = row_line(place, out, copies, recv)
    line.begin(own)
    copies.send(own, out.at[place.slot], recv.at[place.slot], peer_y)
    copies.send(own, out.at[place.slot], recv.at[place.slot], peer_c)
    return line


def gather_step(place, line, copies, distance):
    def then(z, here):
        ref, sem = line.block(z)
        copies.send(ref, ref, sem, {"y": 1 - place.y}, here)
        copies.send(ref, ref, sem, {"c": 1 - place.c}, here)

    line.arrive(distance, then)


def gather_cross(place, out, copies, recv):
    for z in [place.z] + place.far_z():
        at = place.slot_of(z, place.c, 1 - place.y)
        copies.arrived(out.at[at], recv.at[at], {"y": 1 - place.y})
        copies.send(out.at[at], out.at[at], recv.at[at], {"c": 1 - place.c})


def gather_end(place, out, copies, recv):
    for z in [place.z] + place.far_z():
        for y in (place.y, 1 - place.y):
            at = place.slot_of(z, 1 - place.c, y)
            copies.arrived(out.at[at], recv.at[at], {"c": 1 - place.c})


def gather_copies(n_z):
    return 7 * n_z


def group_gather_kernel(own, out, send, recv):
    place = Place(False)
    copies = Copies(send)
    meet([place.at_z(1 - place.z), {"y": 1 - place.y}, {"c": 1 - place.c}])
    line = gather_begin(place, own, out, copies, recv)
    gather_step(place, line, copies, 1)
    gather_cross(place, out, copies, recv)
    gather_end(place, out, copies, recv)
    copies.finish()


def group_gather(value, collective_id):
    return pl.pallas_call(
        group_gather_kernel,
        out_shape=jax.ShapeDtypeStruct((8,) + value.shape, value.dtype),
        in_specs=[ANY],
        out_specs=ANY,
        scratch_shapes=dma_sems(gather_copies(2), 8),
        compiler_params=comm_params(collective_id),
        name="group_gather",
    )(value)


def opening_kernel(
    own, blocks, ffn, out_w, out, blocks_all, ffn_all, out_w_all, send, recv, recv_w, recv_f, recv_o
):
    place, group = Place(True), Place(False)
    n_ctx = blocks.shape[0]
    copies = Copies(send)
    peer_x, peer_y = {"x": 1 - place.x}, {"y": 1 - place.y}
    far_ctx = others(place.ctx, n_ctx)
    meet([place.at_ctx(k) for k in far_ctx] + [peer_y, peer_x])
    mine = blocks_all.at[place.x, place.ctx]
    half = out_w.shape[1] // 2

    def sem_w(x, k):
        return recv_w.at[x * n_ctx + k]

    def out_block(z, x=place.x):
        at = x * place.n_z + z
        return out_w_all.at[at], recv_o.at[at]

    line = gather_begin(place, own, out, copies, recv)
    for k in far_ctx:
        copies.send(blocks.at[k], mine, sem_w(place.x, place.ctx), place.at_ctx(k))
    copies.local(blocks.at[place.ctx], mine)
    copies.send(blocks.at[place.ctx], mine, sem_w(place.x, place.ctx), peer_x)
    own_out, own_sem = out_block(place.z)
    own_half = out_w.at[:, pl.ds(pl.multiple_of(place.y * half, half), half)]
    copies.local(own_half, own_out)
    out_line = Line(place, copies, out_block)
    out_line.begin(own_half)
    copies.send(own_half, own_out, own_sem, peer_x)
    for k in others(group.ctx, 4):
        copies.send(ffn.at[:, k], ffn_all.at[:, group.ctx], recv_f.at[group.ctx], group.at_ctx(k))
    copies.local(ffn.at[:, group.ctx], ffn_all.at[:, group.ctx])

    def out_over_x(z, here):
        ref, sem = out_block(z)
        copies.send(ref, ref, sem, peer_x, here)

    for distance in range(1, place.n_z):
        gather_step(place, line, copies, distance)
        out_line.arrive(distance, out_over_x)
    for k in far_ctx:
        block = blocks_all.at[place.x, k]
        copies.arrived(block, sem_w(place.x, k), place.at_ctx(k))
        copies.send(block, block, sem_w(place.x, k), peer_x)
    gather_cross(place, out, copies, recv)
    gather_end(place, out, copies, recv)
    for k in [place.ctx] + far_ctx:
        copies.arrived(blocks_all.at[1 - place.x, k], sem_w(1 - place.x, k), peer_x)
    for k in others(group.ctx, 4):
        copies.arrived(ffn_all.at[:, k], recv_f.at[k], group.at_ctx(k))
    for z in [place.z] + place.far_z():
        ref, sem = out_block(z, 1 - place.x)
        copies.arrived(ref, sem, peer_x)
    copies.finish()


def opening(own, blocks, ffn, out_w):
    n_ctx = blocks.shape[0]
    n_z = n_ctx // 2
    sends = gather_copies(n_z) + 2 * n_ctx + 4 + 5 * n_z
    return pl.pallas_call(
        opening_kernel,
        out_shape=(
            jax.ShapeDtypeStruct((2 * n_ctx,) + own.shape, own.dtype),
            jax.ShapeDtypeStruct((2,) + blocks.shape, blocks.dtype),
            jax.ShapeDtypeStruct(ffn.shape, ffn.dtype),
            jax.ShapeDtypeStruct((n_ctx, out_w.shape[0], out_w.shape[1] // 2), out_w.dtype),
        ),
        in_specs=[ANY] * 4,
        out_specs=(ANY,) * 4,
        scratch_shapes=dma_sems(sends, 2 * n_ctx, 2 * n_ctx, 4, n_ctx),
        compiler_params=comm_params(1),
        name="opening",
    )(own, blocks, ffn, out_w)


def to_tokens_kernel(src, dst, send, recv):
    place = Place(True)
    copies = Copies(send)
    count, width = src.shape[0], src.shape[2]
    far = others(place.slot, count)
    meet([place.at_slot(s) for s in far])

    def columns(s):
        return dst.at[:, pl.ds(pl.multiple_of(s * width, width), width)]

    for s in far:
        copies.send(src.at[s], columns(place.slot), recv.at[place.slot], place.at_slot(s))
    copies.local(src.at[place.slot], columns(place.slot))
    for s in far:
        copies.arrived(columns(s), recv.at[s], place.at_slot(s))
    copies.finish()


def to_tokens(value):
    count, tokens, width = value.shape
    return pl.pallas_call(
        to_tokens_kernel,
        out_shape=jax.ShapeDtypeStruct((tokens, count * width), value.dtype),
        in_specs=[ANY],
        out_specs=ANY,
        scratch_shapes=dma_sems(count, count),
        compiler_params=comm_params(2),
        name="to_tokens",
    )(value)


def to_heads_kernel(src, dst, send, recv):
    place = Place(True)
    copies = Copies(send)
    count, width = dst.shape[0], dst.shape[2]
    far = others(place.slot, count)
    meet([place.at_slot(s) for s in far])

    def columns(s):
        return src.at[:, pl.ds(pl.multiple_of(s * width, width), width)]

    for s in far:
        copies.send(columns(s), dst.at[place.slot], recv.at[place.slot], place.at_slot(s))
    copies.local(columns(place.slot), dst.at[place.slot])
    for s in far:
        copies.arrived(dst.at[s], recv.at[s], place.at_slot(s))
    copies.finish()


def to_heads(value, count):
    tokens, width = value.shape[0], value.shape[1] // count
    return pl.pallas_call(
        to_heads_kernel,
        out_shape=jax.ShapeDtypeStruct((count, tokens, width), value.dtype),
        in_specs=[ANY],
        out_specs=ANY,
        scratch_shapes=dma_sems(count, count),
        compiler_params=comm_params(3),
        name="to_heads",
    )(value)


class Scatter:
    def __init__(self, place, part, held, from_c, from_y, from_z, out, copies, loads, rc, ry, rz):
        self.__dict__.update(locals())

    def order(self):
        return self.place.far_z() + [self.place.z]

    def begin(self):
        p = self.place
        for y in (1 - p.y, p.y):
            for z in self.order():
                at = z * 2 + y
                self.copies.send(
                    self.part.at[p.slot_of(z, 1 - p.c, y)], self.from_c.at[at], self.rc.at[at], {"c": 1 - p.c}
                )
        self.queue = [(z, y) for y in (1 - p.y, p.y) for z in self.order()]
        for at in range(min(self.held.shape[0], len(self.queue))):
            self.load(at)

    def load(self, at):
        p = self.place
        z, y = self.queue[at]
        at = at % self.held.shape[0]
        self.copies.local(self.part.at[p.slot_of(z, p.c, y)], self.held.at[at], self.loads.at[at])

    def add_c(self, step):
        z, y = self.queue[step]
        at, depth = z * 2 + y, self.held.shape[0]
        own = step % depth
        self.copies.arrived(self.from_c.at[at], self.rc.at[at], {"c": 1 - self.place.c})
        pltpu.make_async_copy(self.held.at[own], self.held.at[own], self.loads.at[own]).wait()
        self.from_c[at] = self.from_c[at] + self.held[own]
        if step + depth < len(self.queue):
            self.load(step + depth)

    def over_c_far(self):
        p = self.place
        for step, z in enumerate(self.order()):
            self.add_c(step)
            self.copies.send(self.from_c.at[z * 2 + 1 - p.y], self.from_y.at[z], self.ry.at[z], {"y": 1 - p.y})

    def over_c_near(self):
        for step in range(self.place.n_z):
            self.add_c(self.place.n_z + step)

    def over_y(self):
        p = self.place
        for z in self.order():
            self.copies.arrived(self.from_y.at[z], self.ry.at[z], {"y": 1 - p.y})
            self.from_y[z] = self.from_y[z] + self.from_c[z * 2 + p.y]
            if z is not p.z:
                self.copies.send(self.from_y.at[z], self.from_z.at[p.z], self.rz.at[p.z], p.at_z(z))

    def over_z(self):
        p = self.place
        total = self.from_y[p.z].astype(F32)
        for z in p.far_z():
            self.copies.arrived(self.from_z.at[z], self.rz.at[z], p.at_z(z))
            total = total + self.from_z[z].astype(F32)
        self.out[...] = total


def scatter_scratch(n_z, block):
    return [
        pltpu.VMEM((min(8, 2 * n_z),) + block, B16),
        pltpu.VMEM((2 * n_z,) + block, B16),
        pltpu.VMEM((n_z,) + block, B16),
        pltpu.VMEM((n_z,) + block, B16),
    ]


def scatter_sems(n_z, more=0):
    return dma_sems(4 * n_z + more, min(8, 2 * n_z), 2 * n_z, n_z, n_z)


def group_scatter_kernel(part, out, held, from_c, from_y, from_z, send, loads, rc, ry, rz):
    place = Place(False)
    copies = Copies(send)
    meet([place.at_z(1 - place.z), {"y": 1 - place.y}, {"c": 1 - place.c}])
    sums = Scatter(place, part, held, from_c, from_y, from_z, out, copies, loads, rc, ry, rz)
    sums.begin()
    sums.over_c_far()
    sums.over_c_near()
    sums.over_y()
    sums.over_z()
    copies.finish()


def group_scatter(part, collective_id):
    block = part.shape[1:]
    return pl.pallas_call(
        group_scatter_kernel,
        out_shape=jax.ShapeDtypeStruct(block, F32),
        in_specs=[ANY],
        out_specs=IN_VMEM,
        scratch_shapes=scatter_scratch(2, block) + scatter_sems(2),
        compiler_params=comm_params(collective_id),
        name="group_scatter",
    )(part)


class OutScatter:
    def __init__(self, place, part, held, from_x, from_y, from_z, out, copies, loads, rx, ry, rz, rg):
        self.__dict__.update(locals())
        self.half = out.shape[2]

    def order(self):
        return self.place.far_z() + [self.place.z]

    def columns(self, y):
        return pl.ds(pl.multiple_of(y * self.half, self.half), self.half)

    def begin(self):
        p = self.place
        for z in self.order():
            self.copies.send(self.part.at[(1 - p.x) * p.n_z + z], self.from_x.at[z], self.rx.at[z], {"x": 1 - p.x})
            self.copies.local(self.part.at[p.x * p.n_z + z], self.held.at[z], self.loads.at[z])

    def over_x(self):
        p = self.place
        for z in self.order():
            self.copies.arrived(self.from_x.at[z], self.rx.at[z], {"x": 1 - p.x})
            pltpu.make_async_copy(self.held.at[z], self.held.at[z], self.loads.at[z]).wait()
            self.from_x[z] = self.from_x[z] + self.held[z]
            self.copies.send(
                self.from_x.at[z, :, self.columns(1 - p.y)], self.from_y.at[z], self.ry.at[z], {"y": 1 - p.y}
            )

    def over_y(self):
        p = self.place
        for z in self.order():
            self.copies.arrived(self.from_y.at[z], self.ry.at[z], {"y": 1 - p.y})
            self.from_y[z] = self.from_y[z] + self.from_x[z, :, self.columns(p.y)]
            if z is not p.z:
                self.copies.send(self.from_y.at[z], self.from_z.at[p.z], self.rz.at[p.z], p.at_z(z))

    def over_z(self):
        p = self.place
        total = self.from_y[p.z].astype(F32)
        for z in p.far_z():
            self.copies.arrived(self.from_z.at[z], self.rz.at[z], p.at_z(z))
            total = total + self.from_z[z].astype(F32)
        self.out[p.y] = total.astype(B16)
        self.copies.send(self.out.at[p.y], self.out.at[p.y], self.rg.at[p.y], {"y": 1 - p.y})

    def end(self):
        p = self.place
        self.copies.arrived(self.out.at[1 - p.y], self.rg.at[1 - p.y], {"y": 1 - p.y})


def closing_kernel(
    part, grads, out_part, fc, proj, out, grads_out, out_w_out, fc_out, proj_out,
    held, from_c, from_y, from_z, own_x, from_x, o_held, o_x, o_y, o_z,
    send, loads, rc, ry, rz, load_x, rx, rk, rg, o_loads, orx, ory, orz, org, rfc, rproj,
):
    place, group = Place(True), Place(False)
    n_ctx = grads.shape[1]
    copies = Copies(send)
    far_ctx = others(place.ctx, n_ctx)
    peer_x, peer_y = {"x": 1 - place.x}, {"y": 1 - place.y}
    meet([place.at_ctx(k) for k in far_ctx] + [peer_y, peer_x])
    sums = Scatter(place, part, held, from_c, from_y, from_z, out, copies, loads, rc, ry, rz)
    outs = OutScatter(place, out_part, o_held, o_x, o_y, o_z, out_w_out, copies, o_loads, orx, ory, orz, org)
    sums.begin()
    for k in far_ctx + [place.ctx]:
        copies.send(grads.at[1 - place.x, k], from_x.at[k], rx.at[k], peer_x)
        copies.local(grads.at[place.x, k], own_x.at[k], load_x.at[k])
    outs.begin()
    for k in others(group.ctx, 4):
        copies.send(fc.at[k], fc_out.at[group.ctx], rfc.at[group.ctx], group.at_ctx(k))
        copies.send(proj.at[k], proj_out.at[group.ctx], rproj.at[group.ctx], group.at_ctx(k))
    copies.local(fc.at[group.ctx], fc_out.at[group.ctx])
    copies.local(proj.at[group.ctx], proj_out.at[group.ctx])
    sums.over_c_far()
    mine = grads_out.at[place.y, place.ctx]
    for k in far_ctx + [place.ctx]:
        copies.arrived(from_x.at[k], rx.at[k], peer_x)
        pltpu.make_async_copy(own_x.at[k], own_x.at[k], load_x.at[k]).wait()
        from_x[k] = from_x[k] + own_x[k]
        if k is not place.ctx:
            copies.send(from_x.at[k], mine, rk.at[place.ctx], place.at_ctx(k))
    copies.local(from_x.at[place.ctx], mine)
    copies.send(from_x.at[place.ctx], mine, rg.at[place.ctx], peer_y)
    sums.over_c_near()
    sums.over_y()
    outs.over_x()
    for k in far_ctx:
        block = grads_out.at[place.y, k]
        copies.arrived(block, rk.at[k], place.at_ctx(k))
        copies.send(block, block, rg.at[k], peer_y)
    outs.over_y()
    sums.over_z()
    outs.over_z()
    for k in [place.ctx] + far_ctx:
        copies.arrived(grads_out.at[1 - place.y, k], rg.at[k], peer_y)
    outs.end()
    for k in others(group.ctx, 4):
        copies.arrived(fc_out.at[k], rfc.at[k], group.at_ctx(k))
        copies.arrived(proj_out.at[k], rproj.at[k], group.at_ctx(k))
    copies.finish()


def closing(part, grads, out_part, fc, proj):
    block = part.shape[1:]
    n_ctx = grads.shape[1]
    n_z = n_ctx // 2
    piece = grads.shape[1:]
    rows, width = out_part.shape[1:]
    half = (rows, width // 2)
    return pl.pallas_call(
        closing_kernel,
        out_shape=(
            jax.ShapeDtypeStruct(block, F32),
            jax.ShapeDtypeStruct((2,) + piece, B16),
            jax.ShapeDtypeStruct((2,) + half, B16),
            jax.ShapeDtypeStruct(fc.shape, fc.dtype),
            jax.ShapeDtypeStruct(proj.shape, proj.dtype),
        ),
        in_specs=[ANY] * 5,
        out_specs=(IN_VMEM, ANY, IN_VMEM, ANY, ANY),
        scratch_shapes=scatter_scratch(n_z, block)
        + [pltpu.VMEM(piece, B16), pltpu.VMEM(piece, B16)]
        + [pltpu.VMEM((n_z, rows, width), B16), pltpu.VMEM((n_z, rows, width), B16)]
        + [pltpu.VMEM((n_z,) + half, B16), pltpu.VMEM((n_z,) + half, B16)]
        + scatter_sems(n_z, 3 * n_ctx + 4 * n_z + 8)
        + dma_sems(n_ctx, n_ctx, n_ctx, n_ctx)
        + dma_sems(n_z, n_z, n_z, n_z, 2, 4, 4),
        compiler_params=comm_params(4),
        name="closing",
    )(part, grads, out_part, fc, proj)


def vectors_kernel(src, own_out, ff_out, from_all, half, from_y, send, recv, ry):
    place = Place(True)
    count = src.shape[0]
    n_ctx = count // 2
    copies = Copies(send)
    me = place.x * n_ctx + place.ctx
    far = others(me, count)
    peer_y = {"y": 1 - place.y}

    def peer(k):
        return dict(place.at_ctx(lax.rem(k, n_ctx)), x=k // n_ctx)

    meet([peer(k) for k in far] + [peer_y])
    for k in far:
        copies.send(src.at[k], from_all.at[me], recv.at[me], peer(k))
    from_all[me] = src[me]
    for k in far:
        copies.arrived(from_all.at[k], recv.at[k], peer(k))
    total = from_all[0, 0:8, :]
    for k in range(1, count):
        total = total + from_all[k, 0:8, :]
    half[...] = total
    copies.send(half, from_y, ry.at[0], peer_y)
    for part in range(4):
        total = from_all[part, 8:16, :]
        for k in range(part + 4, count, 4):
            total = total + from_all[k, 8:16, :]
        ff_out[part] = total
    copies.arrived(from_y, ry.at[0], peer_y)
    own_out[...] = half[...] + from_y[...]
    copies.finish()


def vectors_sum(value):
    count = value.shape[0]
    flat = jax.ShapeDtypeStruct((8, 128), F32)
    return pl.pallas_call(
        vectors_kernel,
        out_shape=(flat, jax.ShapeDtypeStruct((4, 8, 128), F32)),
        in_specs=[IN_VMEM],
        out_specs=(IN_VMEM, IN_VMEM),
        scratch_shapes=[
            pltpu.VMEM(value.shape, F32),
            pltpu.VMEM((8, 128), F32),
            pltpu.VMEM((8, 128), F32),
        ]
        + dma_sems(count + 1, count, 1),
        compiler_params=comm_params(5),
        name="vectors_sum",
    )(value)


def project_kernel(feats, x_ref, gain_ref, shift_ref, mask_ref, w_ref, bias_ref, norm_ref, qkv_ref):
    x = x_ref[...].astype(F32)
    mean = jnp.sum(x, axis=1, keepdims=True) * (1.0 / feats)
    centered = (x - mean) * mask_ref[...]
    inv = lax.rsqrt(jnp.sum(centered * centered, axis=1, keepdims=True) * (1.0 / feats) + NORM_EPS)
    norm = (centered * inv * gain_ref[...] + shift_ref[...]).astype(B16)
    norm_ref[...] = norm
    qkv_ref[...] = (dot(norm, w_ref[...], 1, 0) + bias_ref[...]).astype(B16)


def project(x, gain, shift, mask, weight, bias, feats):
    total, wide = x.shape
    cols = weight.shape[1]
    step = min(256, total)

    def fixed(shape):
        return pl.BlockSpec(shape, lambda i: (0, 0))

    return pl.pallas_call(
        functools.partial(project_kernel, feats),
        grid=(total // step,),
        in_specs=[pl.BlockSpec((step, wide), lambda i: (i, 0))]
        + [fixed((1, wide))] * 3
        + [fixed((wide, cols)), fixed((1, cols))],
        out_specs=(pl.BlockSpec((step, wide), lambda i: (i, 0)), pl.BlockSpec((step, cols), lambda i: (i, 0))),
        out_shape=(jax.ShapeDtypeStruct((total, wide), B16), jax.ShapeDtypeStruct((total, cols), B16)),
        compiler_params=pltpu.CompilerParams(vmem_limit_bytes=VMEM_LIMIT),
        name="project",
    )(x, gain[None], shift[None], mask[None], weight, bias[None])


def feed_kernel(count, at_ref, *refs):
    pieces, refs = refs[:count], refs[count:]
    norm_ref, grad_ref, bias_ref, act_ref, dpre_ref, dnorm_ref, mlp_ref, sum_ref, w_fc, w_proj, sems = refs

    @pl.when(pl.program_id(0) == 0)
    def begin():
        rows = pieces[0].shape[1]
        copies = []
        for i, piece in enumerate(pieces):
            to = pl.ds(pl.multiple_of(at_ref[i], 16), rows)
            copies.append(pltpu.make_async_copy(piece.at[0], w_fc.at[to, :], sems.at[2 * i]))
            copies.append(pltpu.make_async_copy(piece.at[1], w_proj.at[to, :], sems.at[2 * i + 1]))
        for copy in copies:
            copy.start()
        for copy in copies:
            copy.wait()
        sum_ref[...] = jnp.zeros_like(sum_ref)

    preact = dot(norm_ref[...], w_fc[...], 1, 0) + bias_ref[...]
    activated, derivative = gelu_parts(preact)
    activation = activated.astype(B16)
    act_ref[...] = activation
    dpre = dot(grad_ref[...], w_proj[...], 1, 0) * derivative
    sum_ref[...] += jnp.sum(dpre, axis=0, keepdims=True)
    dpre_b = dpre.astype(B16)
    dpre_ref[...] = dpre_b
    dnorm_ref[...] = dot(dpre_b, w_fc[...], 1, 1).astype(B16)
    mlp_ref[...] = dot(activation, w_proj[...], 1, 1).astype(B16)


def feed(pieces, places, norm, grad, bias):
    total, wide = norm.shape
    ff = bias.shape[0]
    step = 256
    tokens = pl.BlockSpec((step, wide), lambda i: (i, 0))
    hidden = pl.BlockSpec((step, ff), lambda i: (i, 0))
    single = pl.BlockSpec((1, ff), lambda i: (0, 0))
    return pl.pallas_call(
        functools.partial(feed_kernel, len(pieces)),
        grid=(total // step,),
        in_specs=[pl.BlockSpec(memory_space=pltpu.SMEM)] + [ANY] * len(pieces) + [tokens, tokens, single],
        out_specs=(hidden, hidden, tokens, tokens, single),
        out_shape=(
            jax.ShapeDtypeStruct((total, ff), B16),
            jax.ShapeDtypeStruct((total, ff), B16),
            jax.ShapeDtypeStruct((total, wide), B16),
            jax.ShapeDtypeStruct((total, wide), B16),
            jax.ShapeDtypeStruct((1, ff), F32),
        ),
        scratch_shapes=[pltpu.VMEM((wide, ff), B16), pltpu.VMEM((wide, ff), B16)] + dma_sems(2 * len(pieces)),
        compiler_params=pltpu.CompilerParams(vmem_limit_bytes=VMEM_LIMIT),
        name="feed",
    )(places, *pieces, norm, grad, bias[None])


def after(value, other, unpack=False):
    value, other = lax.optimization_barrier((value, other))
    return (*value, other) if unpack else (value, other)


def shift_perm(count, step):
    return [(i, (i + step) % count) for i in range(count)]


def on_device(
    sizes, block_input, segment_ids, slot_order, first_gain, first_shift, qkv_weight, qv_bias, out_weight, out_bias,
    second_gain, second_shift, fc_weight, fc_bias, proj_weight, proj_bias, out_grad,
):
    n_x, n_ctx, n_y = sizes
    n_slot = n_ctx * n_y
    n_shard = n_x * n_ctx
    n_h = n_ctx // 4
    slot_len, feats = block_input.shape[1:]
    head = feats // HEADS
    pair = 2 * head
    rows = qkv_weight.shape[0]
    ff_own = fc_weight.shape[1] // 4
    padded = n_slot * pair
    y_at = lax.axis_index("y")
    ctx_at = lax.axis_index(CTX)
    slot_at = lax.axis_index(ROW)
    lc_at = lax.axis_index(("l", "c"))
    x_at, h_at = lax.axis_index("x"), lax.axis_index("h")

    def gather(value, axes):
        return lax.all_gather(value, axes, axis=0, tiled=True)

    tall = rows + (-rows % 16)
    wide = n_shard * tall
    row_pad = tall - rows

    def widened(value):
        lead = value.shape[:-1]
        value = value.reshape(lead + (n_shard, rows))
        return jnp.pad(value, [(0, 0)] * (len(lead) + 1) + [(0, row_pad)]).reshape(lead + (wide,))

    def narrowed(value):
        lead = value.shape[:-1]
        return value.reshape(lead + (n_shard, tall))[..., :rows].reshape(lead + (feats,))

    mask = jnp.asarray((np.arange(wide) % tall < rows).astype(np.float32))

    small = jnp.concatenate([first_gain, first_shift, out_bias, second_gain, second_shift, proj_bias, qv_bias])
    packed = jnp.pad(qkv_weight.reshape(rows, 3, feats), ((0, 0), (0, 0), (0, padded - feats)))
    packed = lax.dynamic_index_in_dim(packed.reshape(rows, 3, n_ctx, n_y, pair), y_at, 3, False)
    packed = packed.transpose(2, 0, 1, 3).reshape(n_ctx, rows, 3 * pair)
    small = jnp.pad(small, (0, row_pad * 3 * pair - small.shape[0])).reshape(1, row_pad, 3 * pair)
    packed = jnp.concatenate([packed, jnp.broadcast_to(small, (n_ctx, row_pad, 3 * pair))], axis=1)
    ffn_blocks = jnp.stack([fc_weight, proj_weight.T])
    ffn_blocks = jnp.pad(ffn_blocks, ((0, 0), (0, row_pad), (0, 0))).reshape(2, tall, 4, ff_own).transpose(0, 2, 1, 3)
    own_input = widened(block_input[0])
    grad_own = widened(out_grad[0])
    all_input, packed, ffn_blocks, w_out = opening(
        own_input, packed, ffn_blocks, widened(jnp.pad(out_weight, ((0, row_pad), (0, 0))))
    )
    ffn_blocks = ffn_blocks.reshape(2, 4 * tall, ff_own)
    along_h = [lax.ppermute(ffn_blocks, "h", shift_perm(n_h, step)) for step in range(1, n_h)]
    along_x = lax.ppermute(ffn_blocks, "x", shift_perm(n_x, 1))
    grad_late, all_input = after(grad_own, all_input)
    grad_all = gather(grad_late, FFG)
    w_out = lax.all_gather(w_out.reshape(wide // 2, wide // 2), ("c", "y"), axis=0, tiled=False)
    w_out = w_out.reshape(2, n_y, wide // 2, wide // 2)
    packed = packed.reshape(n_shard, tall, 3 * pair)
    w_qkv = packed.reshape(wide, 3 * pair)
    smalls = packed[:, rows:].reshape(n_shard, -1)[:, : 8 * rows].astype(F32)
    singles = jnp.pad(smalls[:, : 6 * rows].reshape(n_shard, 6, rows), ((0, 0), (0, 0), (0, row_pad)))
    gain_one, shift_one, bias_out, gain_two, shift_two, bias_proj = singles.transpose(1, 0, 2).reshape(6, wide)
    bias_qv = smalls[:, 6 * rows :].reshape(2, feats)
    bias_pair = lax.dynamic_slice_in_dim(
        jnp.pad(bias_qv, ((0, 0), (0, padded - feats))), slot_at * pair, pair, 1
    )
    bias_qkv = jnp.concatenate([bias_pair[0], jnp.zeros((pair,), F32), bias_pair[1]])
    b_fc = lax.dynamic_slice_in_dim(fc_bias, lc_at * ff_own, ff_own, 0).astype(F32)

    order = slot_order[0]
    pieces = jnp.arange(n_slot, dtype=jnp.int32)
    inv = jnp.sum(jnp.where(order[None, :] == pieces[:, None], pieces[None, :], 0), axis=1).astype(jnp.int32)
    segs = jnp.take(segment_ids[0].reshape(n_slot, slot_len), inv, axis=0).reshape(-1)
    docs = jnp.arange(DOCS, dtype=jnp.int32)
    counts = jnp.sum((segs[None, :] == docs[:, None]).astype(jnp.int32), axis=1)
    starts = jnp.sum(jnp.where(segs[None, :] > docs[:, None], counts[:, None], 0), axis=0).astype(jnp.int32)
    start3 = starts.reshape(-1, 1, BLK)
    low = start3[:, 0, 0] // BLK

    own_wide = own_input.astype(F32)
    norm_one, qkv = project(
        all_input.reshape(n_slot * slot_len, wide), gain_one, shift_one, mask, w_qkv, bias_qkv, feats
    )
    heads_out, lse = attend(inv, low, qkv, start3, slot_len, head)
    attention = widened(to_tokens(heads_out.reshape(n_slot, slot_len, pair))[:, :feats])
    by_core = attention.reshape(slot_len, n_shard // 2, 2, tall)
    by_core = [by_core[:, :, part].reshape(slot_len, wide // 2) for part in range(2)]
    hidden = [dot(by_core[0], w_out[0, y], 1, 0) + dot(by_core[1], w_out[1, y], 1, 0) for y in range(n_y)]
    hidden = own_wide + jnp.concatenate(hidden, axis=1) + bias_out
    normed_two, inv_two = norm_forward(hidden, mask, feats)
    norm_two = (normed_two * gain_two + shift_two).astype(B16)
    grad_wide = grad_own.astype(F32)
    along_h, norm_two = after(along_h, norm_two)
    along_both = [lax.ppermute(value, "x", shift_perm(n_x, 1)) for value in along_h]
    norm_all = group_gather(norm_two, 6).reshape(-1, wide)
    pieces, places = [ffn_blocks, along_x], [(x_at, h_at), (1 - x_at, h_at)]
    for step in range(1, n_h):
        h_from = lax.rem(h_at + n_h - step, n_h)
        pieces += [along_h[step - 1], along_both[step - 1]]
        places += [(x_at, h_from), (1 - x_at, h_from)]
    places = jnp.stack([(x * n_h + h) * (4 * tall) for x, h in places]).astype(jnp.int32)
    activation, dpreact_b, dnorm_part, mlp_part, dpreact_sum = feed(pieces, places, norm_all, grad_all, b_fc)

    def pick(value, at):
        return lax.dynamic_index_in_dim(value, at, 0, False)

    def by_owner(value):
        value = with_layout_constraint(value.astype(B16), Layout(major_to_minor=(0, 1)))
        return value.reshape(n_x, n_h, 4 * tall, ff_own)

    proj_part = by_owner(dot(grad_all, activation, 0, 0))
    proj_x = lax.ppermute(pick(proj_part, 1 - x_at), "x", shift_perm(n_x, 1))
    fc_part = by_owner(dot(norm_all, dpreact_b, 0, 0))
    fc_x = lax.ppermute(pick(fc_part, 1 - x_at), "x", shift_perm(n_x, 1))

    proj_part, fc_part, dnorm_part = after((proj_part, fc_part), dnorm_part, True)
    dnorm_two = group_scatter(dnorm_part.reshape(8, slot_len, wide), 7)

    def over_h(value):
        gives = [pick(value, lax.rem(h_at + step, n_h)) for step in range(1, n_h)]
        return [lax.ppermute(give, "h", shift_perm(n_h, step + 1)) for step, give in enumerate(gives)]

    def total(value, received):
        value = pick(value, h_at).astype(F32)
        for other in received:
            value = value + other
        return value.astype(B16).reshape(4, tall, ff_own)

    proj_x, mlp_part, dnorm_two = after((proj_x, mlp_part), dnorm_two, True)
    proj_line = pick(proj_part, x_at) + proj_x
    proj_h = over_h(proj_line)
    mlp = lax.psum_scatter(mlp_part, FFG, scatter_dimension=0, tiled=True)
    dhidden = grad_wide + norm_backward(dnorm_two, normed_two, inv_two, gain_two, feats)
    dhidden_b = dhidden.astype(B16)
    c_at = lax.axis_index("c")
    out_give = dot(jnp.where(c_at == 0, by_core[1], by_core[0]), dhidden_b, 0, 0).astype(B16)
    out_give = lax.ppermute(out_give, "c", shift_perm(2, 1))
    out_keep = dot(jnp.where(c_at == 0, by_core[0], by_core[1]), dhidden_b, 0, 0)
    grad_y = [dhidden_b[:, : wide // 2], dhidden_b[:, wide // 2 :]]
    datt = [dot(grad_y[0], w_out[c, 0], 1, 1) + dot(grad_y[1], w_out[c, 1], 1, 1) for c in range(2)]
    datt = [value.astype(B16).reshape(slot_len, -1, 1, tall) for value in datt]
    dattention = narrowed(jnp.concatenate(datt, axis=2).reshape(slot_len, wide))
    dattention = jnp.pad(dattention, ((0, 0), (0, padded - feats)))
    dattention = to_heads(dattention, n_slot).reshape(n_slot * slot_len, pair)
    out_give, fc_x, dattention = after((out_give, fc_x), dattention, True)
    out_part = (out_keep + out_give).astype(B16).reshape(n_shard // 2, tall, wide)
    fc_line = pick(fc_part, x_at) + fc_x
    fc_h = over_h(fc_line)
    dqkv = attend_back(inv, low, qkv, heads_out, dattention, lse, start3, slot_len, head)
    dqkv_b = dqkv.astype(B16)
    dnorm_one_part = dot(dqkv_b, w_qkv, 1, 1).astype(B16)
    qkv_part = dot(norm_one, dqkv_b, 0, 0).astype(B16).reshape(n_x, n_ctx, tall, 3 * pair)
    proj_h, fc_h, dnorm_one_part = after((proj_h, fc_h), dnorm_one_part, True)
    dnorm_one, qkv_all, out_all, fc_all, proj_all = closing(
        dnorm_one_part.reshape(n_slot, slot_len, wide), qkv_part, out_part, total(fc_line, fc_h), total(proj_line, proj_h)
    )
    mlp, dnorm_one = after(mlp, dnorm_one)
    block_output = narrowed(hidden + mlp.astype(F32) + bias_proj)
    proj_grad = proj_all[:, :rows].astype(F32).transpose(0, 2, 1).reshape(4 * ff_own, rows)
    fc_grad = fc_all[:, :rows].astype(F32).transpose(1, 0, 2).reshape(rows, 4 * ff_own)
    qkv_all = qkv_all[:, :, :rows].reshape(n_y, n_ctx, rows, 3, pair)
    qkv_grad = qkv_all.transpose(2, 3, 1, 0, 4).reshape(rows, 3, padded)
    qkv_grad = qkv_grad[:, :, :feats].reshape(rows, 3 * feats).astype(F32)
    out_grad_w = narrowed(out_all[:, :rows].transpose(1, 0, 2).reshape(rows, wide)).astype(F32)

    normed_one, inv_one = norm_forward(own_wide, mask, feats)
    input_grad = narrowed(dhidden + norm_backward(dnorm_one, normed_one, inv_one, gain_one, feats))

    dq_sum, dv_sum = jnp.sum(dqkv[:, :pair], axis=0), jnp.sum(dqkv[:, 2 * pair :], axis=0)

    def placed(value, width, at):
        return lax.dynamic_update_slice(jnp.zeros((width,), F32), value, (at,))[:feats]

    vectors = jnp.stack(
        [
            jnp.sum(dhidden, axis=0),
            jnp.sum(dnorm_one * normed_one, axis=0),
            jnp.sum(dnorm_one, axis=0),
            jnp.sum(dnorm_two * normed_two, axis=0),
            jnp.sum(dnorm_two, axis=0),
            jnp.sum(grad_wide, axis=0),
        ]
    )
    qv_sums = jnp.concatenate([placed(dq_sum, padded, slot_at * pair), placed(dv_sum, padded, slot_at * pair)])
    vectors = jnp.concatenate(
        [
            vectors.reshape(6, n_shard, tall).transpose(1, 0, 2).reshape(n_shard, 6 * tall),
            qv_sums.reshape(n_shard, 2 * rows),
            jnp.zeros((n_shard, 1024 - 6 * tall - 2 * rows), F32),
            jnp.broadcast_to(dpreact_sum, (n_shard, ff_own)),
            jnp.zeros((n_shard, 1024 - ff_own), F32),
        ],
        axis=1,
    )
    owned, ff_sums = vectors_sum(vectors.reshape(n_shard, 16, 128))
    owned = owned.reshape(1024)
    fc_bias_grad = ff_sums.reshape(4, 1024)[:, :ff_own].reshape(4 * ff_own)
    qv_grad = owned[6 * tall : 6 * tall + 2 * rows]

    def own(index):
        return owned[index * tall : index * tall + rows]

    return (
        block_output[None],
        input_grad[None],
        qkv_grad,
        qv_grad,
        out_grad_w,
        own(0),
        own(1),
        own(2),
        own(3),
        own(4),
        fc_grad,
        fc_bias_grad,
        proj_grad,
        own(5),
    )


def solution(mesh):
    n_x, n_ctx, n_y = (mesh.shape[axis] for axis in ("dp", "context", "tensor"))
    inner = Mesh(mesh.devices.reshape(n_x, n_ctx // 4, 2, 2, n_y), ("x", "h", "l", "c", "y"))
    tokens = P("x", ROW, None)
    shard = P(SHARD)
    shard_rows = P(SHARD, None)
    return jax.shard_map(
        functools.partial(on_device, (n_x, n_ctx, n_y)),
        mesh=inner,
        in_specs=(
            tokens, P("x", None), P("x", None), shard, shard, shard_rows, shard, shard_rows, shard, shard, shard,
            P(SHARD, "y"), P("y"), P("y", SHARD), shard, tokens,
        ),
        out_specs=(
            tokens, tokens, shard_rows, shard, shard_rows, shard, shard, shard, shard, shard,
            P(SHARD, "y"), P("y"), P("y", SHARD), shard,
        ),
        check_vma=False,
    )
```

```python
import functools
import math

import jax
import jax.numpy as jnp
import numpy as np
from jax import lax
from jax.experimental import pallas as pl
from jax.experimental.layout import Layout, with_layout_constraint
from jax.experimental.pallas import tpu as pltpu
from jax.sharding import Mesh
from jax.sharding import PartitionSpec as P

HEADS = 25
DOCS = 8
NORM_EPS = 1e-05
GELU_SCALE = 0.7978845608028654
GELU_CUBE = 0.044715
MASK_FLOOR = -1e30

F32 = jnp.float32
B16 = jnp.bfloat16
BLK = 256
VMEM_LIMIT = 60 * 1024 * 1024

ROW = ("h", "l", "c", "y")
CTX = ("h", "l", "c")
SHARD = ("x", "h", "l", "c")
FFG = ("l", "c", "y")


def gelu_parts(values):
    inner_arg = GELU_SCALE * (values + GELU_CUBE * values * values * values)
    tanh_value = jnp.tanh(inner_arg)
    result = 0.5 * values * (1.0 + tanh_value)
    derivative = 0.5 * (1.0 + tanh_value) + 0.5 * values * (
        1.0 - tanh_value * tanh_value
    ) * GELU_SCALE * (1.0 + 3.0 * GELU_CUBE * values * values)
    return (result, derivative)


def norm_forward(values, mask, feats):
    mean_value = jnp.sum(values, axis=-1, keepdims=True) / feats
    centered = (values - mean_value) * mask
    inv_sigma = lax.rsqrt(jnp.sum(centered * centered, axis=-1, keepdims=True) / feats + NORM_EPS)
    return (centered * inv_sigma, inv_sigma)


def norm_backward(upstream, normed, inv_sigma, norm_gain, feats):
    scaled = upstream * norm_gain
    return inv_sigma * (
        scaled
        - jnp.sum(scaled, axis=-1, keepdims=True) / feats
        - normed * (jnp.sum(scaled * normed, axis=-1, keepdims=True) / feats)
    )


def dot(left, right, left_dim, right_dim):
    return lax.dot_general(
        left, right, (((left_dim,), (right_dim,)), ((), ())), preferred_element_type=F32
    )


def sort_slots(inv_ref, src_ref, dst_ref, slot_len, start=0, width=None, factor=None):
    width = src_ref.shape[1] if width is None else width

    def body(piece, carry):
        slot = inv_ref[piece]
        rows = src_ref[pl.ds(pl.multiple_of(slot * slot_len, slot_len), slot_len), start : start + width]
        if factor is not None:
            rows = rows * jnp.asarray(factor, rows.dtype)
        dst_ref[pl.ds(pl.multiple_of(piece * slot_len, slot_len), slot_len), :] = rows
        return carry

    lax.fori_loop(0, src_ref.shape[0] // slot_len, body, 0)


def unsort_block(inv_ref, dst_ref, value, block, slot_len):
    for part in range(BLK // slot_len):
        slot = inv_ref[block * (BLK // slot_len) + part]
        dst_ref[pl.ds(pl.multiple_of(slot * slot_len, slot_len), slot_len), :] = value[
            part * slot_len : (part + 1) * slot_len
        ].astype(dst_ref.dtype)


def block_rows(block):
    return pl.ds(pl.multiple_of(block * BLK, BLK), BLK)


def mask_of(start_row, key_block, query_block, diagonal):
    key_at = key_block * BLK + lax.broadcasted_iota(jnp.int32, (BLK, BLK), 0)
    allowed = key_at >= start_row
    if diagonal:
        query_at = query_block * BLK + lax.broadcasted_iota(jnp.int32, (BLK, BLK), 1)
        allowed = jnp.logical_and(allowed, key_at <= query_at)
    return allowed


def attend_kernel(slot_len, head, inv_ref, low_ref, qkv_ref, start_ref, out_ref, lse_ref, q_s, k_s, vt_s):
    total = qkv_ref.shape[0]
    pair = 2 * head
    sort_slots(inv_ref, qkv_ref, q_s, slot_len, 0, pair, 1.0 / math.sqrt(head))
    sort_slots(inv_ref, qkv_ref, k_s, slot_len, pair, pair)

    def fill(piece, carry):
        slot = inv_ref[piece]
        rows = qkv_ref[pl.ds(pl.multiple_of(slot * slot_len, slot_len), slot_len), 2 * pair :]
        vt_s[:, pl.ds(pl.multiple_of(piece * slot_len, slot_len), slot_len)] = rows.astype(F32).T.astype(B16)
        return carry

    lax.fori_loop(0, total // slot_len, fill, 0)

    def per_query(block, carry):
        queries = q_s[block_rows(block), :]
        start_row = start_ref[block]

        def step(key_block, state, diagonal):
            allowed = mask_of(start_row, key_block, block, diagonal)
            keys = k_s[block_rows(key_block), :]
            values = vt_s[:, block_rows(key_block)]
            fresh = []
            for part in range(2):
                old_max, old_sum, old_acc = state[part]
                cols = slice(part * head, (part + 1) * head)
                scores = dot(keys[:, cols], queries[:, cols], 1, 1)
                scores = jnp.where(allowed, scores, MASK_FLOOR)
                new_max = jnp.maximum(old_max, jnp.max(scores, axis=0, keepdims=True))
                weights = jnp.where(allowed, jnp.exp(scores - new_max), 0.0)
                shrink = jnp.exp(old_max - new_max)
                new_sum = old_sum * shrink + jnp.sum(weights, axis=0, keepdims=True)
                new_acc = old_acc * shrink + dot(values[cols, :], weights.astype(B16), 1, 0)
                fresh.append((new_max, new_sum, new_acc))
            return tuple(fresh)

        first = tuple(
            (
                jnp.full((1, BLK), MASK_FLOOR, F32),
                jnp.zeros((1, BLK), F32),
                jnp.zeros((head, BLK), F32),
            )
            for part in range(2)
        )
        state = lax.fori_loop(low_ref[block], block, lambda j, s: step(j, s, False), first)
        state = step(block, state, True)
        lse_ref[block] = jnp.concatenate([s[0] + jnp.log(s[1]) for s in state], axis=0)
        result = jnp.concatenate([s[2] / s[1] for s in state], axis=0)
        unsort_block(inv_ref, out_ref, result.T, block, slot_len)
        return carry

    lax.fori_loop(0, total // BLK, per_query, 0)


def attend(inv, low, qkv, start3, slot_len, head):
    total = qkv.shape[0]
    vmem = pl.BlockSpec(memory_space=pltpu.VMEM)
    smem = pl.BlockSpec(memory_space=pltpu.SMEM)
    return pl.pallas_call(
        functools.partial(attend_kernel, slot_len, head),
        out_shape=(
            jax.ShapeDtypeStruct((total, 2 * head), B16),
            jax.ShapeDtypeStruct((total // BLK, 2, BLK), F32),
        ),
        in_specs=[smem, smem, vmem, vmem],
        out_specs=(vmem, vmem),
        scratch_shapes=[
            pltpu.VMEM((total, 2 * head), B16),
            pltpu.VMEM((total, 2 * head), B16),
            pltpu.VMEM((2 * head, total), B16),
        ],
        compiler_params=pltpu.CompilerParams(vmem_limit_bytes=VMEM_LIMIT),
        name="attend",
    )(inv, low, qkv, start3)


def attend_back_kernel(
    slot_len, head, inv_ref, low_ref, qkv_ref, out_ref, grad_ref, lse_ref, start_ref,
    dqkv_ref, q_s, k_s, v_s, kt_s, o_s, g_s, dk_s, dv_s,
):
    total = qkv_ref.shape[0]
    pair = 2 * head
    scale = 1.0 / math.sqrt(head)
    sort_slots(inv_ref, qkv_ref, q_s, slot_len, 0, pair, scale)
    sort_slots(inv_ref, qkv_ref, k_s, slot_len, pair, pair)
    sort_slots(inv_ref, qkv_ref, v_s, slot_len, 2 * pair, pair)
    sort_slots(inv_ref, out_ref, o_s, slot_len)
    sort_slots(inv_ref, grad_ref, g_s, slot_len)

    def fill(block, carry):
        kt_s[:, block_rows(block)] = k_s[block_rows(block), :].astype(F32).T.astype(B16)
        return carry

    lax.fori_loop(0, total // BLK, fill, 0)
    dk_s[...] = jnp.zeros_like(dk_s)
    dv_s[...] = jnp.zeros_like(dv_s)

    def per_query(block, carry):
        queries = q_s[block_rows(block), :]
        grads = g_s[block_rows(block), :]
        start_row = start_ref[block]
        lse = lse_ref[block]
        prod = (grads.astype(F32) * o_s[block_rows(block), :].astype(F32)).T
        delta = [jnp.sum(prod[part * head : (part + 1) * head], axis=0, keepdims=True) for part in range(2)]

        def step(key_block, state, diagonal):
            allowed = mask_of(start_row, key_block, block, diagonal)
            rows = block_rows(key_block)
            keys = k_s[rows, :]
            values = v_s[rows, :]
            flipped = kt_s[:, rows]
            fresh, dks, dvs = [], [], []
            for part in range(2):
                cols = slice(part * head, (part + 1) * head)
                scores = dot(keys[:, cols], queries[:, cols], 1, 1)
                weights = jnp.where(allowed, jnp.exp(scores - lse[part : part + 1]), 0.0)
                dprob = dot(values[:, cols], grads[:, cols], 1, 1)
                dscore = (weights * (dprob - delta[part])).astype(B16)
                dvs.append(dot(weights.astype(B16), grads[:, cols], 1, 0))
                dks.append(dot(dscore, queries[:, cols], 1, 0))
                fresh.append(state[part] + dot(flipped[cols, :], dscore, 1, 0))
            dk_s[rows, :] += jnp.concatenate(dks, axis=1)
            dv_s[rows, :] += jnp.concatenate(dvs, axis=1)
            return tuple(fresh)

        state = (jnp.zeros((head, BLK), F32), jnp.zeros((head, BLK), F32))
        state = lax.fori_loop(low_ref[block], block, lambda j, s: step(j, s, False), state)
        state = step(block, state, True)
        dq = jnp.concatenate(state, axis=0).T * scale
        for part in range(BLK // slot_len):
            slot = inv_ref[block * (BLK // slot_len) + part]
            dqkv_ref[pl.ds(pl.multiple_of(slot * slot_len, slot_len), slot_len), 0:pair] = dq[
                part * slot_len : (part + 1) * slot_len
            ]
        return carry

    lax.fori_loop(0, total // BLK, per_query, 0)

    def give(piece, carry):
        slot = inv_ref[piece]
        rows = pl.ds(pl.multiple_of(slot * slot_len, slot_len), slot_len)
        held = pl.ds(pl.multiple_of(piece * slot_len, slot_len), slot_len)
        dqkv_ref[rows, pair : 2 * pair] = dk_s[held, :]
        dqkv_ref[rows, 2 * pair :] = dv_s[held, :]
        return carry

    lax.fori_loop(0, total // slot_len, give, 0)


def attend_back(inv, low, qkv, out, grad, lse, start3, slot_len, head):
    total = qkv.shape[0]
    pair = 2 * head
    vmem = pl.BlockSpec(memory_space=pltpu.VMEM)
    smem = pl.BlockSpec(memory_space=pltpu.SMEM)
    held = pltpu.VMEM((total, pair), B16)
    return pl.pallas_call(
        functools.partial(attend_back_kernel, slot_len, head),
        out_shape=jax.ShapeDtypeStruct((total, 3 * pair), F32),
        in_specs=[smem, smem] + [vmem] * 5,
        out_specs=vmem,
        scratch_shapes=[
            held, held, held, pltpu.VMEM((pair, total), B16), held, held,
            pltpu.VMEM((total, pair), F32), pltpu.VMEM((total, pair), F32),
        ],
        compiler_params=pltpu.CompilerParams(vmem_limit_bytes=VMEM_LIMIT),
        name="attend_back",
    )(inv, low, qkv, out, grad, lse, start3)


class Place:
    def __init__(self, whole_line):
        self.x, self.h, self.l, self.c, self.y = (lax.axis_index(a) for a in ("x", "h", "l", "c", "y"))
        self.whole_line = whole_line
        self.n_z = 2 * lax.axis_size("h") if whole_line else 2
        self.z = self.h * 2 + self.l if whole_line else self.l
        self.ctx = self.z * 2 + self.c
        self.slot = self.ctx * 2 + self.y

    def at_z(self, z):
        return {"h": z // 2, "l": lax.rem(z, 2)} if self.whole_line else {"l": z}

    def at_ctx(self, k):
        return dict(self.at_z(k // 2), c=lax.rem(k, 2))

    def at_slot(self, s):
        return dict(self.at_ctx(s // 2), y=lax.rem(s, 2))

    def far_z(self):
        order = []
        for step in range(1, self.n_z // 2 + 1):
            order += [step] if 2 * step == self.n_z else [step, self.n_z - step]
        return [lax.rem(self.z + step, self.n_z) for step in order]

    def slot_of(self, z, c, y):
        return (z * 2 + c) * 2 + y


class Copies:
    def __init__(self, sems):
        self.sems = sems
        self.begun = []

    def send(self, src, dst, recv, peer, when=None):
        at = len(self.begun)
        copy = pltpu.make_async_remote_copy(
            src_ref=src,
            dst_ref=dst,
            send_sem=self.sems.at[at],
            recv_sem=recv,
            device_id=peer,
            device_id_type=pl.DeviceIdType.MESH,
        )
        if when is None:
            copy.start()
            self.begun.append(copy.wait_send)
        else:
            pl.when(when)(copy.start)
            self.begun.append(lambda: pl.when(when)(copy.wait_send))

    def local(self, src, dst, sem=None):
        copy = pltpu.make_async_copy(src, dst, self.sems.at[len(self.begun)] if sem is None else sem)
        copy.start()
        if sem is None:
            self.begun.append(copy.wait)
        return copy

    def arrived(self, dst, recv, peer):
        pltpu.make_async_remote_copy(
            src_ref=dst,
            dst_ref=dst,
            send_sem=self.sems.at[0],
            recv_sem=recv,
            device_id=peer,
            device_id_type=pl.DeviceIdType.MESH,
        ).wait_recv()

    def finish(self):
        for wait in self.begun:
            wait()


def meet(peers):
    barrier = pltpu.get_barrier_semaphore()
    for peer in peers:
        pl.semaphore_signal(barrier, inc=1, device_id=peer, device_id_type=pl.DeviceIdType.MESH)
    pl.semaphore_wait(barrier, len(peers))


def others(me, count):
    return [lax.rem(me + step, count) for step in range(1, count)]


ANY = pl.BlockSpec(memory_space=pl.ANY)
IN_VMEM = pl.BlockSpec(memory_space=pltpu.VMEM)


def dma_sems(*counts):
    return [pltpu.SemaphoreType.DMA((count,)) for count in counts]


def comm_params(collective_id):
    return pltpu.CompilerParams(
        collective_id=collective_id, has_side_effects=True, vmem_limit_bytes=VMEM_LIMIT
    )


class Line:
    def __init__(self, place, copies, block):
        self.place, self.copies, self.block = place, copies, block

    def pass_on(self, src, z, step, when):
        p = self.place
        ref, sem = self.block(z)
        peer = p.at_z(jnp.clip(p.z + step, 0, p.n_z - 1))
        self.copies.send(ref if src is None else src, ref, sem, peer, when)

    def begin(self, own):
        p = self.place
        self.pass_on(own, p.z, 1, p.z < p.n_z - 1)
        self.pass_on(own, p.z, -1, p.z > 0)

    def arrive(self, distance, then):
        p = self.place
        for side in (1, -1):
            z = p.z + side * distance
            here = jnp.logical_and(z >= 0, z < p.n_z)
            z = jnp.clip(z, 0, p.n_z - 1)
            ref, sem = self.block(z)
            peer = p.at_z(jnp.clip(p.z + side, 0, p.n_z - 1))
            pl.when(here)(lambda: self.copies.arrived(ref, sem, peer))
            beyond = p.z - side
            beyond = jnp.logical_and(beyond >= 0, beyond < p.n_z)
            self.pass_on(None, z, -side, jnp.logical_and(here, beyond))
            then(z, here)


def row_line(place, out, copies, recv):
    def block(z):
        at = place.slot_of(z, place.c, place.y)
        return out.at[at], recv.at[at]

    return Line(place, copies, block)


def gather_begin(place, own, out, copies, recv):
    peer_y, peer_c = {"y": 1 - place.y}, {"c": 1 - place.c}
    copies.local(own, out.at[place.slot])
    line = row_line(place, out, copies, recv)
    line.begin(own)
    copies.send(own, out.at[place.slot], recv.at[place.slot], peer_y)
    copies.send(own, out.at[place.slot], recv.at[place.slot], peer_c)
    return line


def gather_step(place, line, copies, distance):
    def then(z, here):
        ref, sem = line.block(z)
        copies.send(ref, ref, sem, {"y": 1 - place.y}, here)
        copies.send(ref, ref, sem, {"c": 1 - place.c}, here)

    line.arrive(distance, then)


def gather_cross(place, out, copies, recv):
    for z in [place.z] + place.far_z():
        at = place.slot_of(z, place.c, 1 - place.y)
        copies.arrived(out.at[at], recv.at[at], {"y": 1 - place.y})
        copies.send(out.at[at], out.at[at], recv.at[at], {"c": 1 - place.c})


def gather_end(place, out, copies, recv):
    for z in [place.z] + place.far_z():
        for y in (place.y, 1 - place.y):
            at = place.slot_of(z, 1 - place.c, y)
            copies.arrived(out.at[at], recv.at[at], {"c": 1 - place.c})


def gather_copies(n_z):
    return 7 * n_z


def group_gather_kernel(own, out, send, recv):
    place = Place(False)
    copies = Copies(send)
    meet([place.at_z(1 - place.z), {"y": 1 - place.y}, {"c": 1 - place.c}])
    line = gather_begin(place, own, out, copies, recv)
    gather_step(place, line, copies, 1)
    gather_cross(place, out, copies, recv)
    gather_end(place, out, copies, recv)
    copies.finish()


def group_gather(value, collective_id):
    return pl.pallas_call(
        group_gather_kernel,
        out_shape=jax.ShapeDtypeStruct((8,) + value.shape, value.dtype),
        in_specs=[ANY],
        out_specs=ANY,
        scratch_shapes=dma_sems(gather_copies(2), 8),
        compiler_params=comm_params(collective_id),
        name="group_gather",
    )(value)


def opening_kernel(
    own, blocks, ffn, out_w, out, blocks_all, ffn_all, out_w_all, send, recv, recv_w, recv_f, recv_o
):
    place, group = Place(True), Place(False)
    n_ctx = blocks.shape[0]
    copies = Copies(send)
    peer_x, peer_y = {"x": 1 - place.x}, {"y": 1 - place.y}
    far_ctx = others(place.ctx, n_ctx)
    meet([place.at_ctx(k) for k in far_ctx] + [peer_y, peer_x])
    mine = blocks_all.at[place.x, place.ctx]
    half = out_w.shape[1] // 2

    def sem_w(x, k):
        return recv_w.at[x * n_ctx + k]

    def out_block(z, x=place.x):
        at = x * place.n_z + z
        return out_w_all.at[at], recv_o.at[at]

    line = gather_begin(place, own, out, copies, recv)
    for k in far_ctx:
        copies.send(blocks.at[k], mine, sem_w(place.x, place.ctx), place.at_ctx(k))
    copies.local(blocks.at[place.ctx], mine)
    copies.send(blocks.at[place.ctx], mine, sem_w(place.x, place.ctx), peer_x)
    own_out, own_sem = out_block(place.z)
    own_half = out_w.at[:, pl.ds(pl.multiple_of(place.y * half, half), half)]
    copies.local(own_half, own_out)
    out_line = Line(place, copies, out_block)
    out_line.begin(own_half)
    copies.send(own_half, own_out, own_sem, peer_x)
    for k in others(group.ctx, 4):
        copies.send(ffn.at[:, k], ffn_all.at[:, group.ctx], recv_f.at[group.ctx], group.at_ctx(k))
    copies.local(ffn.at[:, group.ctx], ffn_all.at[:, group.ctx])

    def out_over_x(z, here):
        ref, sem = out_block(z)
        copies.send(ref, ref, sem, peer_x, here)

    for distance in range(1, place.n_z):
        gather_step(place, line, copies, distance)
        out_line.arrive(distance, out_over_x)
    for k in far_ctx:
        block = blocks_all.at[place.x, k]
        copies.arrived(block, sem_w(place.x, k), place.at_ctx(k))
        copies.send(block, block, sem_w(place.x, k), peer_x)
    gather_cross(place, out, copies, recv)
    gather_end(place, out, copies, recv)
    for k in [place.ctx] + far_ctx:
        copies.arrived(blocks_all.at[1 - place.x, k], sem_w(1 - place.x, k), peer_x)
    for k in others(group.ctx, 4):
        copies.arrived(ffn_all.at[:, k], recv_f.at[k], group.at_ctx(k))
    for z in [place.z] + place.far_z():
        ref, sem = out_block(z, 1 - place.x)
        copies.arrived(ref, sem, peer_x)
    copies.finish()


def opening(own, blocks, ffn, out_w):
    n_ctx = blocks.shape[0]
    n_z = n_ctx // 2
    sends = gather_copies(n_z) + 2 * n_ctx + 4 + 5 * n_z
    return pl.pallas_call(
        opening_kernel,
        out_shape=(
            jax.ShapeDtypeStruct((2 * n_ctx,) + own.shape, own.dtype),
            jax.ShapeDtypeStruct((2,) + blocks.shape, blocks.dtype),
            jax.ShapeDtypeStruct(ffn.shape, ffn.dtype),
            jax.ShapeDtypeStruct((n_ctx, out_w.shape[0], out_w.shape[1] // 2), out_w.dtype),
        ),
        in_specs=[ANY] * 4,
        out_specs=(ANY,) * 4,
        scratch_shapes=dma_sems(sends, 2 * n_ctx, 2 * n_ctx, 4, n_ctx),
        compiler_params=comm_params(1),
        name="opening",
    )(own, blocks, ffn, out_w)


def to_tokens_kernel(src, dst, send, recv):
    place = Place(True)
    copies = Copies(send)
    count, width = src.shape[0], src.shape[2]
    far = others(place.slot, count)
    meet([place.at_slot(s) for s in far])

    def columns(s):
        return dst.at[:, pl.ds(pl.multiple_of(s * width, width), width)]

    for s in far:
        copies.send(src.at[s], columns(place.slot), recv.at[place.slot], place.at_slot(s))
    copies.local(src.at[place.slot], columns(place.slot))
    for s in far:
        copies.arrived(columns(s), recv.at[s], place.at_slot(s))
    copies.finish()


def to_tokens(value):
    count, tokens, width = value.shape
    return pl.pallas_call(
        to_tokens_kernel,
        out_shape=jax.ShapeDtypeStruct((tokens, count * width), value.dtype),
        in_specs=[ANY],
        out_specs=ANY,
        scratch_shapes=dma_sems(count, count),
        compiler_params=comm_params(2),
        name="to_tokens",
    )(value)


def to_heads_kernel(src, dst, send, recv):
    place = Place(True)
    copies = Copies(send)
    count, width = dst.shape[0], dst.shape[2]
    far = others(place.slot, count)
    meet([place.at_slot(s) for s in far])

    def columns(s):
        return src.at[:, pl.ds(pl.multiple_of(s * width, width), width)]

    for s in far:
        copies.send(columns(s), dst.at[place.slot], recv.at[place.slot], place.at_slot(s))
    copies.local(columns(place.slot), dst.at[place.slot])
    for s in far:
        copies.arrived(dst.at[s], recv.at[s], place.at_slot(s))
    copies.finish()


def to_heads(value, count):
    tokens, width = value.shape[0], value.shape[1] // count
    return pl.pallas_call(
        to_heads_kernel,
        out_shape=jax.ShapeDtypeStruct((count, tokens, width), value.dtype),
        in_specs=[ANY],
        out_specs=ANY,
        scratch_shapes=dma_sems(count, count),
        compiler_params=comm_params(3),
        name="to_heads",
    )(value)


class Scatter:
    def __init__(self, place, part, held, from_c, from_y, from_z, out, copies, loads, rc, ry, rz):
        self.__dict__.update(locals())

    def order(self):
        return self.place.far_z() + [self.place.z]

    def begin(self):
        p = self.place
        for y in (1 - p.y, p.y):
            for z in self.order():
                at = z * 2 + y
                self.copies.send(
                    self.part.at[p.slot_of(z, 1 - p.c, y)], self.from_c.at[at], self.rc.at[at], {"c": 1 - p.c}
                )
        self.queue = [(z, y) for y in (1 - p.y, p.y) for z in self.order()]
        for at in range(min(self.held.shape[0], len(self.queue))):
            self.load(at)

    def load(self, at):
        p = self.place
        z, y = self.queue[at]
        at = at % self.held.shape[0]
        self.copies.local(self.part.at[p.slot_of(z, p.c, y)], self.held.at[at], self.loads.at[at])

    def add_c(self, step):
        z, y = self.queue[step]
        at, depth = z * 2 + y, self.held.shape[0]
        own = step % depth
        self.copies.arrived(self.from_c.at[at], self.rc.at[at], {"c": 1 - self.place.c})
        pltpu.make_async_copy(self.held.at[own], self.held.at[own], self.loads.at[own]).wait()
        self.from_c[at] = self.from_c[at] + self.held[own]
        if step + depth < len(self.queue):
            self.load(step + depth)

    def over_c_far(self):
        p = self.place
        for step, z in enumerate(self.order()):
            self.add_c(step)
            self.copies.send(self.from_c.at[z * 2 + 1 - p.y], self.from_y.at[z], self.ry.at[z], {"y": 1 - p.y})

    def over_c_near(self):
        for step in range(self.place.n_z):
            self.add_c(self.place.n_z + step)

    def over_y(self):
        p = self.place
        for z in self.order():
            self.copies.arrived(self.from_y.at[z], self.ry.at[z], {"y": 1 - p.y})
            self.from_y[z] = self.from_y[z] + self.from_c[z * 2 + p.y]
            if z is not p.z:
                self.copies.send(self.from_y.at[z], self.from_z.at[p.z], self.rz.at[p.z], p.at_z(z))

    def over_z(self):
        p = self.place
        total = self.from_y[p.z].astype(F32)
        for z in p.far_z():
            self.copies.arrived(self.from_z.at[z], self.rz.at[z], p.at_z(z))
            total = total + self.from_z[z].astype(F32)
        self.out[...] = total


def scatter_scratch(n_z, block):
    return [
        pltpu.VMEM((min(8, 2 * n_z),) + block, B16),
        pltpu.VMEM((2 * n_z,) + block, B16),
        pltpu.VMEM((n_z,) + block, B16),
        pltpu.VMEM((n_z,) + block, B16),
    ]


def scatter_sems(n_z, more=0):
    return dma_sems(4 * n_z + more, min(8, 2 * n_z), 2 * n_z, n_z, n_z)


def group_scatter_kernel(part, out, held, from_c, from_y, from_z, send, loads, rc, ry, rz):
    place = Place(False)
    copies = Copies(send)
    meet([place.at_z(1 - place.z), {"y": 1 - place.y}, {"c": 1 - place.c}])
    sums = Scatter(place, part, held, from_c, from_y, from_z, out, copies, loads, rc, ry, rz)
    sums.begin()
    sums.over_c_far()
    sums.over_c_near()
    sums.over_y()
    sums.over_z()
    copies.finish()


def group_scatter(part, collective_id):
    block = part.shape[1:]
    return pl.pallas_call(
        group_scatter_kernel,
        out_shape=jax.ShapeDtypeStruct(block, F32),
        in_specs=[ANY],
        out_specs=IN_VMEM,
        scratch_shapes=scatter_scratch(2, block) + scatter_sems(2),
        compiler_params=comm_params(collective_id),
        name="group_scatter",
    )(part)


class OutScatter:
    def __init__(self, place, part, held, from_x, from_y, from_z, out, copies, loads, rx, ry, rz, rg):
        self.__dict__.update(locals())
        self.half = out.shape[2]

    def order(self):
        return self.place.far_z() + [self.place.z]

    def columns(self, y):
        return pl.ds(pl.multiple_of(y * self.half, self.half), self.half)

    def begin(self):
        p = self.place
        for z in self.order():
            self.copies.send(self.part.at[(1 - p.x) * p.n_z + z], self.from_x.at[z], self.rx.at[z], {"x": 1 - p.x})
            self.copies.local(self.part.at[p.x * p.n_z + z], self.held.at[z], self.loads.at[z])

    def over_x(self):
        p = self.place
        for z in self.order():
            self.copies.arrived(self.from_x.at[z], self.rx.at[z], {"x": 1 - p.x})
            pltpu.make_async_copy(self.held.at[z], self.held.at[z], self.loads.at[z]).wait()
            self.from_x[z] = self.from_x[z] + self.held[z]
            self.copies.send(
                self.from_x.at[z, :, self.columns(1 - p.y)], self.from_y.at[z], self.ry.at[z], {"y": 1 - p.y}
            )

    def over_y(self):
        p = self.place
        for z in self.order():
            self.copies.arrived(self.from_y.at[z], self.ry.at[z], {"y": 1 - p.y})
            self.from_y[z] = self.from_y[z] + self.from_x[z, :, self.columns(p.y)]
            if z is not p.z:
                self.copies.send(self.from_y.at[z], self.from_z.at[p.z], self.rz.at[p.z], p.at_z(z))

    def over_z(self):
        p = self.place
        total = self.from_y[p.z].astype(F32)
        for z in p.far_z():
            self.copies.arrived(self.from_z.at[z], self.rz.at[z], p.at_z(z))
            total = total + self.from_z[z].astype(F32)
        self.out[p.y] = total.astype(B16)
        self.copies.send(self.out.at[p.y], self.out.at[p.y], self.rg.at[p.y], {"y": 1 - p.y})

    def end(self):
        p = self.place
        self.copies.arrived(self.out.at[1 - p.y], self.rg.at[1 - p.y], {"y": 1 - p.y})


def closing_kernel(
    part, grads, out_part, fc, proj, sums_in, gain_in, shift_in, pair_in, ff_in,
    out, grads_out, out_w_out, fc_out, proj_out, owned, pairs_out, ff_out,
    held, from_c, from_y, from_z, own_x, from_x, o_held, o_x, o_y, o_z,
    send, loads, rc, ry, rz, load_x, rx, rk, rg, o_loads, orx, ory, orz, org, rfc, rproj,
    terms, terms_all, half, pairs_half, half_y, pairs_y, rv, rvy,
):
    place, group = Place(True), Place(False)
    n_ctx = grads.shape[1]
    copies = Copies(send)
    far_ctx = others(place.ctx, n_ctx)
    peer_x, peer_y = {"x": 1 - place.x}, {"y": 1 - place.y}
    count = 2 * n_ctx
    me = place.x * n_ctx + place.ctx
    far_shards = others(me, count)

    def at_shard(k):
        return dict(place.at_ctx(lax.rem(k, n_ctx)), x=k // n_ctx)

    meet([at_shard(k) for k in far_shards] + [peer_y])
    tall = grads.shape[2]
    terms[...] = jnp.zeros_like(terms)
    for k in range(count):
        cols = slice(k * tall, (k + 1) * tall)
        terms[k, 0:4, 0:tall] = sums_in[:, cols]
        terms[k, 4:5, 0:tall] = gain_in[:, cols]
        terms[k, 5:6, 0:tall] = shift_in[:, cols]
        pair = pair_in.shape[1] // 3
        terms[k, 6:7, 0:pair] = pair_in[:, 0:pair]
        terms[k, 7:8, 0:pair] = pair_in[:, 2 * pair :]
        for row in range(-(-ff_in.shape[1] // 128)):
            width = min(128, ff_in.shape[1] - row * 128)
            terms[k, 8 + row : 9 + row, 0:width] = ff_in[:, row * 128 : row * 128 + width]
    for k in far_shards:
        copies.send(terms.at[k], terms_all.at[me], rv.at[me], at_shard(k))
    terms_all[me] = terms[me]
    sums = Scatter(place, part, held, from_c, from_y, from_z, out, copies, loads, rc, ry, rz)
    outs = OutScatter(place, out_part, o_held, o_x, o_y, o_z, out_w_out, copies, o_loads, orx, ory, orz, org)
    sums.begin()
    for k in far_ctx + [place.ctx]:
        copies.send(grads.at[1 - place.x, k], from_x.at[k], rx.at[k], peer_x)
        copies.local(grads.at[place.x, k], own_x.at[k], load_x.at[k])
    outs.begin()
    for k in others(group.ctx, 4):
        copies.send(fc.at[k], fc_out.at[group.ctx], rfc.at[group.ctx], group.at_ctx(k))
        copies.send(proj.at[k], proj_out.at[group.ctx], rproj.at[group.ctx], group.at_ctx(k))
    copies.local(fc.at[group.ctx], fc_out.at[group.ctx])
    copies.local(proj.at[group.ctx], proj_out.at[group.ctx])
    sums.over_c_far()
    mine = grads_out.at[place.y, place.ctx]
    for k in far_ctx + [place.ctx]:
        copies.arrived(from_x.at[k], rx.at[k], peer_x)
        pltpu.make_async_copy(own_x.at[k], own_x.at[k], load_x.at[k]).wait()
        from_x[k] = from_x[k] + own_x[k]
        if k is not place.ctx:
            copies.send(from_x.at[k], mine, rk.at[place.ctx], place.at_ctx(k))
    copies.local(from_x.at[place.ctx], mine)
    copies.send(from_x.at[place.ctx], mine, rg.at[place.ctx], peer_y)
    sums.over_c_near()
    sums.over_y()
    outs.over_x()
    for k in far_ctx:
        block = grads_out.at[place.y, k]
        copies.arrived(block, rk.at[k], place.at_ctx(k))
        copies.send(block, block, rg.at[k], peer_y)
    outs.over_y()
    sums.over_z()
    outs.over_z()
    for k in far_shards:
        copies.arrived(terms_all.at[k], rv.at[k], at_shard(k))
    total = terms_all[0, 0:8, :]
    for k in range(1, count):
        total = total + terms_all[k, 0:8, :]
    half[...] = total
    for k in range(n_ctx):
        pairs_half[k] = terms_all[k, 6:8, :] + terms_all[n_ctx + k, 6:8, :]
    copies.send(half, half_y, rvy.at[0], peer_y)
    copies.send(pairs_half, pairs_y, rvy.at[1], peer_y)
    for part in range(4):
        total = terms_all[part, 8:16, :]
        for k in range(part + 4, count, 4):
            total = total + terms_all[k, 8:16, :]
        ff_out[part] = total
    copies.arrived(half_y, rvy.at[0], peer_y)
    owned[...] = half[...] + half_y[...]
    copies.arrived(pairs_y, rvy.at[1], peer_y)
    pairs_out[place.y] = pairs_half[...]
    pairs_out[1 - place.y] = pairs_y[...]
    for k in [place.ctx] + far_ctx:
        copies.arrived(grads_out.at[1 - place.y, k], rg.at[k], peer_y)
    outs.end()
    for k in others(group.ctx, 4):
        copies.arrived(fc_out.at[k], rfc.at[k], group.at_ctx(k))
        copies.arrived(proj_out.at[k], rproj.at[k], group.at_ctx(k))
    copies.finish()


def closing(part, grads, out_part, fc, proj, *vectors):
    block = part.shape[1:]
    n_ctx = grads.shape[1]
    n_z = n_ctx // 2
    piece = grads.shape[1:]
    rows, width = out_part.shape[1:]
    half = (rows, width // 2)
    return pl.pallas_call(
        closing_kernel,
        out_shape=(
            jax.ShapeDtypeStruct(block, F32),
            jax.ShapeDtypeStruct((2,) + piece, B16),
            jax.ShapeDtypeStruct((2,) + half, B16),
            jax.ShapeDtypeStruct(fc.shape, fc.dtype),
            jax.ShapeDtypeStruct(proj.shape, proj.dtype),
            jax.ShapeDtypeStruct((8, 128), F32),
            jax.ShapeDtypeStruct((2, n_ctx, 2, 128), F32),
            jax.ShapeDtypeStruct((4, 8, 128), F32),
        ),
        in_specs=[ANY] * 5 + [IN_VMEM] * 5,
        out_specs=(IN_VMEM, ANY, IN_VMEM, ANY, ANY, IN_VMEM, IN_VMEM, IN_VMEM),
        scratch_shapes=scatter_scratch(n_z, block)
        + [pltpu.VMEM(piece, B16), pltpu.VMEM(piece, B16)]
        + [pltpu.VMEM((n_z, rows, width), B16), pltpu.VMEM((n_z, rows, width), B16)]
        + [pltpu.VMEM((n_z,) + half, B16), pltpu.VMEM((n_z,) + half, B16)]
        + scatter_sems(n_z, 5 * n_ctx + 4 * n_z + 10)
        + dma_sems(n_ctx, n_ctx, n_ctx, n_ctx)
        + dma_sems(n_z, n_z, n_z, n_z, 2, 4, 4)
        + [pltpu.VMEM((2 * n_ctx, 16, 128), F32), pltpu.VMEM((2 * n_ctx, 16, 128), F32)]
        + [pltpu.VMEM((8, 128), F32), pltpu.VMEM((n_ctx, 2, 128), F32)]
        + [pltpu.VMEM((8, 128), F32), pltpu.VMEM((n_ctx, 2, 128), F32)]
        + dma_sems(2 * n_ctx, 2),
        compiler_params=comm_params(4),
        name="closing",
    )(part, grads, out_part, fc, proj, *vectors)


def laid_wide(value, count, rows, tall):
    zeros = jnp.zeros((value.shape[0], tall - rows), value.dtype)
    parts = []
    for k in range(count):
        parts += [value[:, k * rows : (k + 1) * rows], zeros]
    return jnp.concatenate(parts, axis=1)


def laid_narrow(value, count, rows, tall):
    return jnp.concatenate([value[:, k * tall : k * tall + rows] for k in range(count)], axis=1)


def prepare_kernel(count, at_ref, x, grad, qkv, fc, proj, out_w, *refs):
    singles, qv, (x_out, grad_out, blocks, ffn, out_out) = refs[:6], refs[6], refs[7:]
    rows, feats = out_w.shape
    n_ctx, tall, cols = blocks.shape
    pair, ff = cols // 3, ffn.shape[3]
    x_out[...] = laid_wide(x[...].astype(F32), count, rows, tall).astype(B16)
    grad_out[...] = laid_wide(grad[...].astype(F32), count, rows, tall).astype(B16)
    below = jnp.zeros((tall - rows, feats), F32)
    out_out[...] = laid_wide(
        jnp.concatenate([out_w[...].astype(F32), below], axis=0), count, rows, tall
    ).astype(B16)
    below = jnp.zeros((tall - rows, ff), F32)
    for k in range(4):
        ffn[0, k] = jnp.concatenate([fc[:, k * ff : (k + 1) * ff].astype(F32), below], axis=0).astype(B16)
        ffn[1, k] = jnp.concatenate([proj[k * ff : (k + 1) * ff, :].astype(F32).T, below], axis=0).astype(B16)
    small = [jnp.concatenate([ref[...].astype(F32), jnp.zeros((1, cols - rows), F32)], axis=1) for ref in singles]
    small.append(jnp.concatenate([qv[...].astype(F32), jnp.zeros((1, cols - 2 * rows), F32)], axis=1))
    if tall - rows > 7:
        small.append(jnp.zeros((tall - rows - 7, cols), F32))
    small = jnp.concatenate(small, axis=0)
    first = at_ref[0] == 0
    whole = qkv[...].astype(F32)

    def columns(part, p):
        width = min(pair, feats - p * pair)
        if width <= 0:
            return jnp.zeros((rows, pair), F32)
        value = whole[:, part * feats + p * pair : part * feats + p * pair + width]
        if width < pair:
            value = jnp.concatenate([value, jnp.zeros((rows, pair - width), F32)], axis=1)
        return value

    for k in range(n_ctx):
        value = [jnp.where(first, columns(part, 2 * k), columns(part, 2 * k + 1)) for part in range(3)]
        blocks[k] = jnp.concatenate([jnp.concatenate(value, axis=1), small], axis=0).astype(B16)


def prepare(y_at, x, grad, qkv, fc, proj, out_w, singles, qv, n_ctx, tall, pair):
    rows, feats = out_w.shape
    count = feats // rows
    wide = count * tall
    tokens = x.shape[0]
    vmem = pl.BlockSpec(memory_space=pltpu.VMEM)
    return pl.pallas_call(
        functools.partial(prepare_kernel, count),
        in_specs=[pl.BlockSpec(memory_space=pltpu.SMEM)] + [vmem] * 13,
        out_shape=(
            jax.ShapeDtypeStruct((tokens, wide), B16),
            jax.ShapeDtypeStruct((tokens, wide), B16),
            jax.ShapeDtypeStruct((n_ctx, tall, 3 * pair), B16),
            jax.ShapeDtypeStruct((2, 4, tall, fc.shape[1] // 4), B16),
            jax.ShapeDtypeStruct((tall, wide), B16),
        ),
        compiler_params=pltpu.CompilerParams(vmem_limit_bytes=VMEM_LIMIT),
        name="prepare",
    )(y_at, x, grad, qkv, fc, proj, out_w, *[value[None] for value in singles], qv[None])


def project_kernel(
    rows, feats, at_ref, x_ref, packed_ref, mask_ref, w_ref, norm_ref, qkv_ref, single_ref, bias_s, held_s
):
    count, tall, cols = packed_ref.shape
    pair = cols // 3

    @pl.when(pl.program_id(0) == 0)
    def begin():
        held_s[...] = jnp.zeros_like(held_s)
        vectors = []
        for row in range(6):
            at = rows + row
            vectors.append(
                jnp.concatenate([packed_ref[k, at : at + 1, 0:tall].astype(F32) for k in range(count)], axis=1)
            )
        single_ref[...] = jnp.concatenate(vectors + [jnp.zeros((2, count * tall), F32)], axis=0)
        for part in range(2):
            blocks = range(part * count // 2, (part + 1) * count // 2)
            at = rows + 6
            held_s[part : part + 1, 0:feats] = jnp.concatenate(
                [packed_ref[k, at : at + 1, 0 : 2 * rows].astype(F32) for k in blocks], axis=1
            )
        own = pl.ds(pl.multiple_of(at_ref[0] * pair, pair), pair)
        bias_s[...] = jnp.concatenate([held_s[0:1, own], jnp.zeros((1, pair), F32), held_s[1:2, own]], axis=1)

    x = x_ref[...].astype(F32)
    mean = jnp.sum(x, axis=1, keepdims=True) * (1.0 / feats)
    centered = (x - mean) * mask_ref[...]
    inv = lax.rsqrt(jnp.sum(centered * centered, axis=1, keepdims=True) * (1.0 / feats) + NORM_EPS)
    norm = (centered * inv * single_ref[0:1, :] + single_ref[1:2, :]).astype(B16)
    norm_ref[...] = norm
    qkv_ref[...] = (dot(norm, w_ref[...], 1, 0) + bias_s[...]).astype(B16)


def project(slot_at, x, packed, mask, rows, feats, padded):
    total, wide = x.shape
    cols = packed.shape[2]
    step = min(256, total)

    def fixed(shape):
        return pl.BlockSpec(shape, lambda i: (0,) * len(shape))

    return pl.pallas_call(
        functools.partial(project_kernel, rows, feats),
        grid=(total // step,),
        in_specs=[pl.BlockSpec(memory_space=pltpu.SMEM), pl.BlockSpec((step, wide), lambda i: (i, 0))]
        + [fixed(packed.shape), fixed((1, wide)), fixed((wide, cols))],
        out_specs=(
            pl.BlockSpec((step, wide), lambda i: (i, 0)),
            pl.BlockSpec((step, cols), lambda i: (i, 0)),
            fixed((8, wide)),
        ),
        out_shape=(
            jax.ShapeDtypeStruct((total, wide), B16),
            jax.ShapeDtypeStruct((total, cols), B16),
            jax.ShapeDtypeStruct((8, wide), F32),
        ),
        scratch_shapes=[pltpu.VMEM((1, cols), F32), pltpu.VMEM((2, padded), F32)],
        compiler_params=pltpu.CompilerParams(vmem_limit_bytes=VMEM_LIMIT),
        name="project",
    )(slot_at, x, packed, mask[None], packed.reshape(wide, cols))


def project_back_kernel(feats, x_ref, grad_ref, mask_ref, w_ref, part_ref, gradb_ref, gain_ref, shift_ref, pair_ref):
    @pl.when(pl.program_id(0) == 0)
    def begin():
        gain_ref[...] = jnp.zeros_like(gain_ref)
        shift_ref[...] = jnp.zeros_like(shift_ref)
        pair_ref[...] = jnp.zeros_like(pair_ref)

    grad = grad_ref[...]
    pair_ref[...] += jnp.sum(grad, axis=0, keepdims=True)
    grad = grad.astype(B16)
    gradb_ref[...] = grad
    part = dot(grad, w_ref[...], 1, 1)
    part_ref[...] = part.astype(B16)
    x = x_ref[...].astype(F32)
    mean = jnp.sum(x, axis=1, keepdims=True) * (1.0 / feats)
    centered = (x - mean) * mask_ref[...]
    inv = lax.rsqrt(jnp.sum(centered * centered, axis=1, keepdims=True) * (1.0 / feats) + NORM_EPS)
    gain_ref[...] += jnp.sum(part * (centered * inv), axis=0, keepdims=True)
    shift_ref[...] += jnp.sum(part, axis=0, keepdims=True)


def project_back(x, grad, mask, weight, feats):
    total, wide = x.shape
    cols = weight.shape[1]
    step = min(256, total)

    def fixed(shape):
        return pl.BlockSpec(shape, lambda i: (0,) * len(shape))

    def moving(width):
        return pl.BlockSpec((step, width), lambda i: (i, 0))

    return pl.pallas_call(
        functools.partial(project_back_kernel, feats),
        grid=(total // step,),
        in_specs=[moving(wide), moving(cols), fixed((1, wide)), fixed((wide, cols))],
        out_specs=(moving(wide), moving(cols), fixed((1, wide)), fixed((1, wide)), fixed((1, cols))),
        out_shape=(
            jax.ShapeDtypeStruct((total, wide), B16),
            jax.ShapeDtypeStruct((total, cols), B16),
            jax.ShapeDtypeStruct((1, wide), F32),
            jax.ShapeDtypeStruct((1, wide), F32),
            jax.ShapeDtypeStruct((1, cols), F32),
        ),
        compiler_params=pltpu.CompilerParams(vmem_limit_bytes=VMEM_LIMIT),
        name="project_back",
    )(x, grad, mask[None], weight)


def deliver_kernel(
    rows, feats, qkv, out_w, fc, proj, mlp, hidden, dnorm, dhidden, x_ref, single, mask,
    qkv_out, out_out, fc_out, proj_out, block_out, grad_out,
):
    n_y, n_ctx, tall, cols = qkv.shape
    pair, ff, count = cols // 3, fc.shape[2], feats // rows
    parts = []
    for part in range(3):
        for p in range(-(-feats // pair)):
            width = min(pair, feats - p * pair)
            parts.append(qkv[p % n_y, p // n_y, :, part * pair : part * pair + width].astype(F32))
    qkv_out[...] = jnp.concatenate(parts, axis=1)[:rows]
    halves = jnp.concatenate([out_w[y].astype(F32) for y in range(2)], axis=1)
    out_out[...] = laid_narrow(halves, count, rows, tall)[:rows]
    fc_out[...] = jnp.concatenate([fc[k].astype(F32) for k in range(4)], axis=1)[:rows]
    for k in range(4):
        proj_out[k * ff : (k + 1) * ff, :] = proj[k].astype(F32).T[:, :rows]
    block_out[...] = laid_narrow(hidden[...] + mlp[...].astype(F32) + single[5:6, :], count, rows, tall)
    normed, inv = norm_forward(x_ref[...].astype(F32), mask[...], feats)
    grad = dhidden[...] + norm_backward(dnorm[...], normed, inv, single[0:1, :], feats)
    grad_out[...] = laid_narrow(grad, count, rows, tall)


def deliver(qkv, out_w, fc, proj, mlp, hidden, dnorm, dhidden, x, single, mask, rows, feats):
    tokens, ff = x.shape[0], fc.shape[2]
    return pl.pallas_call(
        functools.partial(deliver_kernel, rows, feats),
        out_shape=(
            jax.ShapeDtypeStruct((rows, 3 * feats), F32),
            jax.ShapeDtypeStruct((rows, feats), F32),
            jax.ShapeDtypeStruct((rows, 4 * ff), F32),
            jax.ShapeDtypeStruct((4 * ff, rows), F32),
            jax.ShapeDtypeStruct((tokens, feats), F32),
            jax.ShapeDtypeStruct((tokens, feats), F32),
        ),
        compiler_params=pltpu.CompilerParams(vmem_limit_bytes=VMEM_LIMIT),
        name="deliver",
    )(qkv, out_w, fc, proj, mlp, hidden, dnorm, dhidden, x, single, mask[None])


def feed_kernel(count, at_ref, *refs):
    pieces, refs = refs[:count], refs[count:]
    norm_ref, grad_ref, bias_ref, act_ref, dpre_ref, dnorm_ref, mlp_ref, sum_ref, w_fc, w_proj, sems = refs

    @pl.when(pl.program_id(0) == 0)
    def begin():
        rows = pieces[0].shape[1]
        copies = []
        for i, piece in enumerate(pieces):
            to = pl.ds(pl.multiple_of(at_ref[i], 16), rows)
            copies.append(pltpu.make_async_copy(piece.at[0], w_fc.at[to, :], sems.at[2 * i]))
            copies.append(pltpu.make_async_copy(piece.at[1], w_proj.at[to, :], sems.at[2 * i + 1]))
        for copy in copies:
            copy.start()
        for copy in copies:
            copy.wait()
        sum_ref[...] = jnp.zeros_like(sum_ref)

    preact = dot(norm_ref[...], w_fc[...], 1, 0) + bias_ref[...]
    activated, derivative = gelu_parts(preact)
    activation = activated.astype(B16)
    act_ref[...] = activation
    dpre = dot(grad_ref[...], w_proj[...], 1, 0) * derivative
    sum_ref[...] += jnp.sum(dpre, axis=0, keepdims=True)
    dpre_b = dpre.astype(B16)
    dpre_ref[...] = dpre_b
    dnorm_ref[...] = dot(dpre_b, w_fc[...], 1, 1).astype(B16)
    mlp_ref[...] = dot(activation, w_proj[...], 1, 1).astype(B16)


def feed(pieces, places, norm, grad, bias):
    total, wide = norm.shape
    ff = bias.shape[0]
    step = 256
    tokens = pl.BlockSpec((step, wide), lambda i: (i, 0))
    hidden = pl.BlockSpec((step, ff), lambda i: (i, 0))
    single = pl.BlockSpec((1, ff), lambda i: (0, 0))
    return pl.pallas_call(
        functools.partial(feed_kernel, len(pieces)),
        grid=(total // step,),
        in_specs=[pl.BlockSpec(memory_space=pltpu.SMEM)] + [ANY] * len(pieces) + [tokens, tokens, single],
        out_specs=(hidden, hidden, tokens, tokens, single),
        out_shape=(
            jax.ShapeDtypeStruct((total, ff), B16),
            jax.ShapeDtypeStruct((total, ff), B16),
            jax.ShapeDtypeStruct((total, wide), B16),
            jax.ShapeDtypeStruct((total, wide), B16),
            jax.ShapeDtypeStruct((1, ff), F32),
        ),
        scratch_shapes=[pltpu.VMEM((wide, ff), B16), pltpu.VMEM((wide, ff), B16)] + dma_sems(2 * len(pieces)),
        compiler_params=pltpu.CompilerParams(vmem_limit_bytes=VMEM_LIMIT),
        name="feed",
    )(places, *pieces, norm, grad, bias[None])


def after(value, other, unpack=False):
    value, other = lax.optimization_barrier((value, other))
    return (*value, other) if unpack else (value, other)


def shift_perm(count, step):
    return [(i, (i + step) % count) for i in range(count)]


def on_device(
    sizes, block_input, segment_ids, slot_order, first_gain, first_shift, qkv_weight, qv_bias, out_weight, out_bias,
    second_gain, second_shift, fc_weight, fc_bias, proj_weight, proj_bias, out_grad,
):
    n_x, n_ctx, n_y = sizes
    n_slot = n_ctx * n_y
    n_shard = n_x * n_ctx
    n_h = n_ctx // 4
    slot_len, feats = block_input.shape[1:]
    head = feats // HEADS
    pair = 2 * head
    rows = qkv_weight.shape[0]
    ff_own = fc_weight.shape[1] // 4
    padded = n_slot * pair
    y_at = lax.axis_index("y")
    ctx_at = lax.axis_index(CTX)
    slot_at = lax.axis_index(ROW)
    lc_at = lax.axis_index(("l", "c"))
    x_at, h_at = lax.axis_index("x"), lax.axis_index("h")

    def gather(value, axes):
        return lax.all_gather(value, axes, axis=0, tiled=True)

    tall = rows + (-rows % 16)
    wide = n_shard * tall
    row_pad = tall - rows

    def widened(value):
        lead = value.shape[:-1]
        value = value.reshape(lead + (n_shard, rows))
        return jnp.pad(value, [(0, 0)] * (len(lead) + 1) + [(0, row_pad)]).reshape(lead + (wide,))

    def narrowed(value):
        lead = value.shape[:-1]
        return value.reshape(lead + (n_shard, tall))[..., :rows].reshape(lead + (feats,))

    mask = jnp.asarray((np.arange(wide) % tall < rows).astype(np.float32))

    singles = (first_gain, first_shift, out_bias, second_gain, second_shift, proj_bias)
    own_input, grad_own, packed, ffn_blocks, w_out = prepare(
        y_at.astype(jnp.int32)[None], block_input[0], out_grad[0], qkv_weight, fc_weight, proj_weight, out_weight,
        singles, qv_bias, n_ctx, tall, pair,
    )
    all_input, packed, ffn_blocks, w_out = opening(
        own_input, packed, ffn_blocks, w_out
    )
    ffn_blocks = ffn_blocks.reshape(2, 4 * tall, ff_own)
    along_h = [lax.ppermute(ffn_blocks, "h", shift_perm(n_h, step)) for step in range(1, n_h)]
    along_x = lax.ppermute(ffn_blocks, "x", shift_perm(n_x, 1))
    grad_late, all_input = after(grad_own, all_input)
    grad_all = gather(grad_late, FFG)
    w_out = lax.all_gather(w_out.reshape(wide // 2, wide // 2), ("c", "y"), axis=0, tiled=False)
    w_out = w_out.reshape(2, n_y, wide // 2, wide // 2)
    packed = packed.reshape(n_shard, tall, 3 * pair)
    w_qkv = packed.reshape(wide, 3 * pair)
    b_fc = lax.dynamic_slice_in_dim(fc_bias, lc_at * ff_own, ff_own, 0).astype(F32)

    order = slot_order[0]
    pieces = jnp.arange(n_slot, dtype=jnp.int32)
    inv = jnp.sum(jnp.where(order[None, :] == pieces[:, None], pieces[None, :], 0), axis=1).astype(jnp.int32)
    segs = jnp.take(segment_ids[0].reshape(n_slot, slot_len), inv, axis=0).reshape(-1)
    docs = jnp.arange(DOCS, dtype=jnp.int32)
    counts = jnp.sum((segs[None, :] == docs[:, None]).astype(jnp.int32), axis=1)
    starts = jnp.sum(jnp.where(segs[None, :] > docs[:, None], counts[:, None], 0), axis=0).astype(jnp.int32)
    start3 = starts.reshape(-1, 1, BLK)
    low = start3[:, 0, 0] // BLK

    own_wide = own_input.astype(F32)
    all_input = all_input.reshape(n_slot * slot_len, wide)
    norm_one, qkv, singles = project(
        slot_at.astype(jnp.int32)[None], all_input, packed, mask, rows, feats, padded
    )
    bias_out, gain_two, shift_two = singles[2], singles[3], singles[4]
    heads_out, lse = attend(inv, low, qkv, start3, slot_len, head)
    attention = widened(to_tokens(heads_out.reshape(n_slot, slot_len, pair))[:, :feats])
    by_core = attention.reshape(slot_len, n_shard // 2, 2, tall)
    by_core = [by_core[:, :, part].reshape(slot_len, wide // 2) for part in range(2)]
    hidden = [dot(by_core[0], w_out[0, y], 1, 0) + dot(by_core[1], w_out[1, y], 1, 0) for y in range(n_y)]
    hidden = own_wide + jnp.concatenate(hidden, axis=1) + bias_out
    normed_two, inv_two = norm_forward(hidden, mask, feats)
    norm_two = (normed_two * gain_two + shift_two).astype(B16)
    grad_wide = grad_own.astype(F32)
    along_h, norm_two = after(along_h, norm_two)
    along_both = [lax.ppermute(value, "x", shift_perm(n_x, 1)) for value in along_h]
    norm_all = group_gather(norm_two, 6).reshape(-1, wide)
    pieces, places = [ffn_blocks, along_x], [(x_at, h_at), (1 - x_at, h_at)]
    for step in range(1, n_h):
        h_from = lax.rem(h_at + n_h - step, n_h)
        pieces += [along_h[step - 1], along_both[step - 1]]
        places += [(x_at, h_from), (1 - x_at, h_from)]
    places = jnp.stack([(x * n_h + h) * (4 * tall) for x, h in places]).astype(jnp.int32)
    activation, dpreact_b, dnorm_part, mlp_part, dpreact_sum = feed(pieces, places, norm_all, grad_all, b_fc)

    def pick(value, at):
        return lax.dynamic_index_in_dim(value, at, 0, False)

    def by_owner(value):
        value = with_layout_constraint(value.astype(B16), Layout(major_to_minor=(0, 1)))
        return value.reshape(n_x, n_h, 4 * tall, ff_own)

    proj_part = by_owner(dot(grad_all, activation, 0, 0))
    proj_x = lax.ppermute(pick(proj_part, 1 - x_at), "x", shift_perm(n_x, 1))
    fc_part = by_owner(dot(norm_all, dpreact_b, 0, 0))
    fc_x = lax.ppermute(pick(fc_part, 1 - x_at), "x", shift_perm(n_x, 1))

    proj_part, fc_part, dnorm_part = after((proj_part, fc_part), dnorm_part, True)
    dnorm_two = group_scatter(dnorm_part.reshape(8, slot_len, wide), 7)

    def over_h(value):
        gives = [pick(value, lax.rem(h_at + step, n_h)) for step in range(1, n_h)]
        return [lax.ppermute(give, "h", shift_perm(n_h, step + 1)) for step, give in enumerate(gives)]

    def total(value, received):
        value = pick(value, h_at).astype(F32)
        for other in received:
            value = value + other
        return value.astype(B16).reshape(4, tall, ff_own)

    proj_x, mlp_part, dnorm_two = after((proj_x, mlp_part), dnorm_two, True)
    proj_line = pick(proj_part, x_at) + proj_x
    proj_h = over_h(proj_line)
    mlp = lax.psum_scatter(mlp_part, FFG, scatter_dimension=0, tiled=True)
    dhidden = grad_wide + norm_backward(dnorm_two, normed_two, inv_two, gain_two, feats)
    dhidden_b = dhidden.astype(B16)
    c_at = lax.axis_index("c")
    out_give = dot(jnp.where(c_at == 0, by_core[1], by_core[0]), dhidden_b, 0, 0).astype(B16)
    out_give = lax.ppermute(out_give, "c", shift_perm(2, 1))
    out_keep = dot(jnp.where(c_at == 0, by_core[0], by_core[1]), dhidden_b, 0, 0)
    grad_y = [dhidden_b[:, : wide // 2], dhidden_b[:, wide // 2 :]]
    datt = [dot(grad_y[0], w_out[c, 0], 1, 1) + dot(grad_y[1], w_out[c, 1], 1, 1) for c in range(2)]
    datt = [value.astype(B16).reshape(slot_len, -1, 1, tall) for value in datt]
    dattention = narrowed(jnp.concatenate(datt, axis=2).reshape(slot_len, wide))
    dattention = jnp.pad(dattention, ((0, 0), (0, padded - feats)))
    dattention = to_heads(dattention, n_slot).reshape(n_slot * slot_len, pair)
    out_give, fc_x, dattention = after((out_give, fc_x), dattention, True)
    out_part = (out_keep + out_give).astype(B16).reshape(n_shard // 2, tall, wide)
    fc_line = pick(fc_part, x_at) + fc_x
    fc_h = over_h(fc_line)
    dqkv = attend_back(inv, low, qkv, heads_out, dattention, lse, start3, slot_len, head)
    dnorm_one_part, dqkv_b, gain_sum, shift_sum, pair_sum = project_back(all_input, dqkv, mask, w_qkv, feats)
    qkv_part = dot(norm_one, dqkv_b, 0, 0).astype(B16).reshape(n_x, n_ctx, tall, 3 * pair)
    proj_h, fc_h, dnorm_one_part = after((proj_h, fc_h), dnorm_one_part, True)
    token_sums = jnp.stack(
        [
            jnp.sum(dhidden, axis=0),
            jnp.sum(dnorm_two * normed_two, axis=0),
            jnp.sum(dnorm_two, axis=0),
            jnp.sum(grad_wide, axis=0),
        ]
    )
    dnorm_one, qkv_all, out_all, fc_all, proj_all, owned, pair_sums, ff_sums = closing(
        dnorm_one_part.reshape(n_slot, slot_len, wide), qkv_part, out_part, total(fc_line, fc_h), total(proj_line, proj_h),
        token_sums, gain_sum, shift_sum, pair_sum, dpreact_sum,
    )
    mlp, dnorm_one = after(mlp, dnorm_one)
    qkv_grad, out_grad_w, fc_grad, proj_grad, block_output, input_grad = deliver(
        qkv_all, out_all, fc_all, proj_all, mlp, hidden, dnorm_one, dhidden, own_input, singles, mask, rows, feats
    )
    fc_bias_grad = ff_sums.reshape(4, 1024)[:, :ff_own].reshape(4 * ff_own)
    pair_sums = pair_sums.transpose(2, 1, 0, 3).reshape(2, padded)[:, :feats].reshape(2 * feats)
    qv_grad = lax.dynamic_slice_in_dim(pair_sums, lax.axis_index(SHARD) * 2 * rows, 2 * rows, 0)

    def own(index):
        return owned[index, :rows]

    return (
        block_output[None],
        input_grad[None],
        qkv_grad,
        qv_grad,
        out_grad_w,
        own(0),
        own(4),
        own(5),
        own(1),
        own(2),
        fc_grad,
        fc_bias_grad,
        proj_grad,
        own(3),
    )


def solution(mesh):
    n_x, n_ctx, n_y = (mesh.shape[axis] for axis in ("dp", "context", "tensor"))
    inner = Mesh(mesh.devices.reshape(n_x, n_ctx // 4, 2, 2, n_y), ("x", "h", "l", "c", "y"))
    tokens = P("x", ROW, None)
    shard = P(SHARD)
    shard_rows = P(SHARD, None)
    return jax.shard_map(
        functools.partial(on_device, (n_x, n_ctx, n_y)),
        mesh=inner,
        in_specs=(
            tokens, P("x", None), P("x", None), shard, shard, shard_rows, shard, shard_rows, shard, shard, shard,
            P(SHARD, "y"), P("y"), P("y", SHARD), shard, tokens,
        ),
        out_specs=(
            tokens, tokens, shard_rows, shard, shard_rows, shard, shard, shard, shard, shard,
            P(SHARD, "y"), P("y"), P("y", SHARD), shard,
        ),
        check_vma=False,
    )
```

```python
import functools
import math

import jax
import jax.numpy as jnp
import numpy as np
from jax import lax
from jax.experimental import pallas as pl
from jax.experimental.layout import Layout, with_layout_constraint
from jax.experimental.pallas import tpu as pltpu
from jax.sharding import Mesh
from jax.sharding import PartitionSpec as P

HEADS = 25
DOCS = 8
NORM_EPS = 1e-05
GELU_SCALE = 0.7978845608028654
GELU_CUBE = 0.044715
MASK_FLOOR = -1e30

F32 = jnp.float32
B16 = jnp.bfloat16
BLK = 256
VMEM_LIMIT = 60 * 1024 * 1024

ROW = ("h", "l", "c", "y")
CTX = ("h", "l", "c")
SHARD = ("x", "h", "l", "c")
FFG = ("l", "c", "y")


def gelu_parts(values):
    inner_arg = GELU_SCALE * (values + GELU_CUBE * values * values * values)
    tanh_value = jnp.tanh(inner_arg)
    result = 0.5 * values * (1.0 + tanh_value)
    derivative = 0.5 * (1.0 + tanh_value) + 0.5 * values * (
        1.0 - tanh_value * tanh_value
    ) * GELU_SCALE * (1.0 + 3.0 * GELU_CUBE * values * values)
    return (result, derivative)


def norm_forward(values, mask, feats):
    mean_value = jnp.sum(values, axis=-1, keepdims=True) / feats
    centered = (values - mean_value) * mask
    inv_sigma = lax.rsqrt(jnp.sum(centered * centered, axis=-1, keepdims=True) / feats + NORM_EPS)
    return (centered * inv_sigma, inv_sigma)


def norm_backward(upstream, normed, inv_sigma, norm_gain, feats):
    scaled = upstream * norm_gain
    return inv_sigma * (
        scaled
        - jnp.sum(scaled, axis=-1, keepdims=True) / feats
        - normed * (jnp.sum(scaled * normed, axis=-1, keepdims=True) / feats)
    )


def dot(left, right, left_dim, right_dim):
    return lax.dot_general(
        left, right, (((left_dim,), (right_dim,)), ((), ())), preferred_element_type=F32
    )


def sort_slots(inv_ref, src_ref, dst_ref, slot_len, start=0, width=None, factor=None):
    width = src_ref.shape[1] if width is None else width

    def body(piece, carry):
        slot = inv_ref[piece]
        rows = src_ref[pl.ds(pl.multiple_of(slot * slot_len, slot_len), slot_len), start : start + width]
        if factor is not None:
            rows = rows * jnp.asarray(factor, rows.dtype)
        dst_ref[pl.ds(pl.multiple_of(piece * slot_len, slot_len), slot_len), :] = rows
        return carry

    lax.fori_loop(0, src_ref.shape[0] // slot_len, body, 0)


def unsort_block(inv_ref, dst_ref, value, block, slot_len):
    for part in range(BLK // slot_len):
        slot = inv_ref[block * (BLK // slot_len) + part]
        dst_ref[pl.ds(pl.multiple_of(slot * slot_len, slot_len), slot_len), :] = value[
            part * slot_len : (part + 1) * slot_len
        ].astype(dst_ref.dtype)


def block_rows(block):
    return pl.ds(pl.multiple_of(block * BLK, BLK), BLK)


def mask_of(start_row, key_block, query_block, diagonal):
    key_at = key_block * BLK + lax.broadcasted_iota(jnp.int32, (BLK, BLK), 0)
    allowed = key_at >= start_row
    if diagonal:
        query_at = query_block * BLK + lax.broadcasted_iota(jnp.int32, (BLK, BLK), 1)
        allowed = jnp.logical_and(allowed, key_at <= query_at)
    return allowed


def attend_kernel(slot_len, head, inv_ref, low_ref, qkv_ref, start_ref, out_ref, lse_ref, q_s, k_s, vt_s):
    total = qkv_ref.shape[0]
    pair = 2 * head
    sort_slots(inv_ref, qkv_ref, q_s, slot_len, 0, pair, 1.0 / math.sqrt(head))
    sort_slots(inv_ref, qkv_ref, k_s, slot_len, pair, pair)

    def fill(piece, carry):
        slot = inv_ref[piece]
        rows = qkv_ref[pl.ds(pl.multiple_of(slot * slot_len, slot_len), slot_len), 2 * pair :]
        vt_s[:, pl.ds(pl.multiple_of(piece * slot_len, slot_len), slot_len)] = rows.astype(F32).T.astype(B16)
        return carry

    lax.fori_loop(0, total // slot_len, fill, 0)

    def per_query(block, carry):
        queries = q_s[block_rows(block), :]
        start_row = start_ref[block]

        def step(key_block, state, diagonal):
            allowed = mask_of(start_row, key_block, block, diagonal)
            keys = k_s[block_rows(key_block), :]
            values = vt_s[:, block_rows(key_block)]
            fresh = []
            for part in range(2):
                old_max, old_sum, old_acc = state[part]
                cols = slice(part * head, (part + 1) * head)
                scores = dot(keys[:, cols], queries[:, cols], 1, 1)
                scores = jnp.where(allowed, scores, MASK_FLOOR)
                new_max = jnp.maximum(old_max, jnp.max(scores, axis=0, keepdims=True))
                weights = jnp.where(allowed, jnp.exp(scores - new_max), 0.0)
                shrink = jnp.exp(old_max - new_max)
                new_sum = old_sum * shrink + jnp.sum(weights, axis=0, keepdims=True)
                new_acc = old_acc * shrink + dot(values[cols, :], weights.astype(B16), 1, 0)
                fresh.append((new_max, new_sum, new_acc))
            return tuple(fresh)

        first = tuple(
            (
                jnp.full((1, BLK), MASK_FLOOR, F32),
                jnp.zeros((1, BLK), F32),
                jnp.zeros((head, BLK), F32),
            )
            for part in range(2)
        )
        state = lax.fori_loop(low_ref[block], block, lambda j, s: step(j, s, False), first)
        state = step(block, state, True)
        lse_ref[block] = jnp.concatenate([s[0] + jnp.log(s[1]) for s in state], axis=0)
        result = jnp.concatenate([s[2] / s[1] for s in state], axis=0)
        unsort_block(inv_ref, out_ref, result.T, block, slot_len)
        return carry

    lax.fori_loop(0, total // BLK, per_query, 0)


def attend(inv, low, qkv, start3, slot_len, head):
    total = qkv.shape[0]
    vmem = pl.BlockSpec(memory_space=pltpu.VMEM)
    smem = pl.BlockSpec(memory_space=pltpu.SMEM)
    return pl.pallas_call(
        functools.partial(attend_kernel, slot_len, head),
        out_shape=(
            jax.ShapeDtypeStruct((total, 2 * head), B16),
            jax.ShapeDtypeStruct((total // BLK, 2, BLK), F32),
        ),
        in_specs=[smem, smem, vmem, vmem],
        out_specs=(vmem, vmem),
        scratch_shapes=[
            pltpu.VMEM((total, 2 * head), B16),
            pltpu.VMEM((total, 2 * head), B16),
            pltpu.VMEM((2 * head, total), B16),
        ],
        compiler_params=pltpu.CompilerParams(vmem_limit_bytes=VMEM_LIMIT),
        name="attend",
    )(inv, low, qkv, start3)


def attend_back_kernel(
    slot_len, head, inv_ref, low_ref, qkv_ref, out_ref, grad_ref, lse_ref, start_ref,
    dqkv_ref, q_s, k_s, v_s, kt_s, o_s, g_s, dk_s, dv_s,
):
    total = qkv_ref.shape[0]
    pair = 2 * head
    scale = 1.0 / math.sqrt(head)
    sort_slots(inv_ref, qkv_ref, q_s, slot_len, 0, pair, scale)
    sort_slots(inv_ref, qkv_ref, k_s, slot_len, pair, pair)
    sort_slots(inv_ref, qkv_ref, v_s, slot_len, 2 * pair, pair)
    sort_slots(inv_ref, out_ref, o_s, slot_len)
    sort_slots(inv_ref, grad_ref, g_s, slot_len)

    def fill(block, carry):
        kt_s[:, block_rows(block)] = k_s[block_rows(block), :].astype(F32).T.astype(B16)
        return carry

    lax.fori_loop(0, total // BLK, fill, 0)
    dk_s[...] = jnp.zeros_like(dk_s)
    dv_s[...] = jnp.zeros_like(dv_s)

    def per_query(block, carry):
        queries = q_s[block_rows(block), :]
        grads = g_s[block_rows(block), :]
        start_row = start_ref[block]
        lse = lse_ref[block]
        prod = (grads.astype(F32) * o_s[block_rows(block), :].astype(F32)).T
        delta = [jnp.sum(prod[part * head : (part + 1) * head], axis=0, keepdims=True) for part in range(2)]

        def step(key_block, state, diagonal):
            allowed = mask_of(start_row, key_block, block, diagonal)
            rows = block_rows(key_block)
            keys = k_s[rows, :]
            values = v_s[rows, :]
            flipped = kt_s[:, rows]
            fresh, dks, dvs = [], [], []
            for part in range(2):
                cols = slice(part * head, (part + 1) * head)
                scores = dot(keys[:, cols], queries[:, cols], 1, 1)
                weights = jnp.where(allowed, jnp.exp(scores - lse[part : part + 1]), 0.0)
                dprob = dot(values[:, cols], grads[:, cols], 1, 1)
                dscore = (weights * (dprob - delta[part])).astype(B16)
                dvs.append(dot(weights.astype(B16), grads[:, cols], 1, 0))
                dks.append(dot(dscore, queries[:, cols], 1, 0))
                fresh.append(state[part] + dot(flipped[cols, :], dscore, 1, 0))
            dk_s[rows, :] += jnp.concatenate(dks, axis=1)
            dv_s[rows, :] += jnp.concatenate(dvs, axis=1)
            return tuple(fresh)

        state = (jnp.zeros((head, BLK), F32), jnp.zeros((head, BLK), F32))
        state = lax.fori_loop(low_ref[block], block, lambda j, s: step(j, s, False), state)
        state = step(block, state, True)
        dq = jnp.concatenate(state, axis=0).T * scale
        for part in range(BLK // slot_len):
            slot = inv_ref[block * (BLK // slot_len) + part]
            dqkv_ref[pl.ds(pl.multiple_of(slot * slot_len, slot_len), slot_len), 0:pair] = dq[
                part * slot_len : (part + 1) * slot_len
            ]
        return carry

    lax.fori_loop(0, total // BLK, per_query, 0)

    def give(piece, carry):
        slot = inv_ref[piece]
        rows = pl.ds(pl.multiple_of(slot * slot_len, slot_len), slot_len)
        held = pl.ds(pl.multiple_of(piece * slot_len, slot_len), slot_len)
        dqkv_ref[rows, pair : 2 * pair] = dk_s[held, :]
        dqkv_ref[rows, 2 * pair :] = dv_s[held, :]
        return carry

    lax.fori_loop(0, total // slot_len, give, 0)


def attend_back(inv, low, qkv, out, grad, lse, start3, slot_len, head):
    total = qkv.shape[0]
    pair = 2 * head
    vmem = pl.BlockSpec(memory_space=pltpu.VMEM)
    smem = pl.BlockSpec(memory_space=pltpu.SMEM)
    held = pltpu.VMEM((total, pair), B16)
    return pl.pallas_call(
        functools.partial(attend_back_kernel, slot_len, head),
        out_shape=jax.ShapeDtypeStruct((total, 3 * pair), F32),
        in_specs=[smem, smem] + [vmem] * 5,
        out_specs=vmem,
        scratch_shapes=[
            held, held, held, pltpu.VMEM((pair, total), B16), held, held,
            pltpu.VMEM((total, pair), F32), pltpu.VMEM((total, pair), F32),
        ],
        compiler_params=pltpu.CompilerParams(vmem_limit_bytes=VMEM_LIMIT),
        name="attend_back",
    )(inv, low, qkv, out, grad, lse, start3)


class Place:
    def __init__(self, whole_line):
        self.x, self.h, self.l, self.c, self.y = (lax.axis_index(a) for a in ("x", "h", "l", "c", "y"))
        self.whole_line = whole_line
        self.n_z = 2 * lax.axis_size("h") if whole_line else 2
        self.z = self.h * 2 + self.l if whole_line else self.l
        self.ctx = self.z * 2 + self.c
        self.slot = self.ctx * 2 + self.y

    def at_z(self, z):
        return {"h": z // 2, "l": lax.rem(z, 2)} if self.whole_line else {"l": z}

    def at_ctx(self, k):
        return dict(self.at_z(k // 2), c=lax.rem(k, 2))

    def at_slot(self, s):
        return dict(self.at_ctx(s // 2), y=lax.rem(s, 2))

    def far_z(self):
        order = []
        for step in range(1, self.n_z // 2 + 1):
            order += [step] if 2 * step == self.n_z else [step, self.n_z - step]
        return [lax.rem(self.z + step, self.n_z) for step in order]

    def slot_of(self, z, c, y):
        return (z * 2 + c) * 2 + y


class Copies:
    def __init__(self, sems):
        self.sems = sems
        self.begun = []

    def send(self, src, dst, recv, peer, when=None):
        at = len(self.begun)
        copy = pltpu.make_async_remote_copy(
            src_ref=src,
            dst_ref=dst,
            send_sem=self.sems.at[at],
            recv_sem=recv,
            device_id=peer,
            device_id_type=pl.DeviceIdType.MESH,
        )
        if when is None:
            copy.start()
            self.begun.append(copy.wait_send)
        else:
            pl.when(when)(copy.start)
            self.begun.append(lambda: pl.when(when)(copy.wait_send))

    def local(self, src, dst, sem=None):
        copy = pltpu.make_async_copy(src, dst, self.sems.at[len(self.begun)] if sem is None else sem)
        copy.start()
        if sem is None:
            self.begun.append(copy.wait)
        return copy

    def arrived(self, dst, recv, peer):
        pltpu.make_async_remote_copy(
            src_ref=dst,
            dst_ref=dst,
            send_sem=self.sems.at[0],
            recv_sem=recv,
            device_id=peer,
            device_id_type=pl.DeviceIdType.MESH,
        ).wait_recv()

    def finish(self):
        for wait in self.begun:
            wait()


def meet(peers):
    barrier = pltpu.get_barrier_semaphore()
    for peer in peers:
        pl.semaphore_signal(barrier, inc=1, device_id=peer, device_id_type=pl.DeviceIdType.MESH)
    pl.semaphore_wait(barrier, len(peers))


def others(me, count):
    return [lax.rem(me + step, count) for step in range(1, count)]


ANY = pl.BlockSpec(memory_space=pl.ANY)
IN_VMEM = pl.BlockSpec(memory_space=pltpu.VMEM)


def dma_sems(*counts):
    return [pltpu.SemaphoreType.DMA((count,)) for count in counts]


def comm_params(collective_id):
    return pltpu.CompilerParams(
        collective_id=collective_id, has_side_effects=True, vmem_limit_bytes=VMEM_LIMIT
    )


class Line:
    def __init__(self, place, copies, block):
        self.place, self.copies, self.block = place, copies, block

    def pass_on(self, src, z, step, when):
        p = self.place
        ref, sem = self.block(z)
        peer = p.at_z(jnp.clip(p.z + step, 0, p.n_z - 1))
        self.copies.send(ref if src is None else src, ref, sem, peer, when)

    def begin(self, own):
        p = self.place
        self.pass_on(own, p.z, 1, p.z < p.n_z - 1)
        self.pass_on(own, p.z, -1, p.z > 0)

    def arrive(self, distance, then):
        p = self.place
        for side in (1, -1):
            z = p.z + side * distance
            here = jnp.logical_and(z >= 0, z < p.n_z)
            z = jnp.clip(z, 0, p.n_z - 1)
            ref, sem = self.block(z)
            peer = p.at_z(jnp.clip(p.z + side, 0, p.n_z - 1))
            pl.when(here)(lambda: self.copies.arrived(ref, sem, peer))
            beyond = p.z - side
            beyond = jnp.logical_and(beyond >= 0, beyond < p.n_z)
            self.pass_on(None, z, -side, jnp.logical_and(here, beyond))
            then(z, here)


def row_line(place, out, copies, recv):
    def block(z):
        at = place.slot_of(z, place.c, place.y)
        return out.at[at], recv.at[at]

    return Line(place, copies, block)


def gather_begin(place, own, out, copies, recv):
    peer_y, peer_c = {"y": 1 - place.y}, {"c": 1 - place.c}
    copies.local(own, out.at[place.slot])
    line = row_line(place, out, copies, recv)
    line.begin(own)
    copies.send(own, out.at[place.slot], recv.at[place.slot], peer_y)
    copies.send(own, out.at[place.slot], recv.at[place.slot], peer_c)
    return line


def gather_step(place, line, copies, distance):
    def then(z, here):
        ref, sem = line.block(z)
        copies.send(ref, ref, sem, {"y": 1 - place.y}, here)
        copies.send(ref, ref, sem, {"c": 1 - place.c}, here)

    line.arrive(distance, then)


def gather_cross(place, out, copies, recv):
    for z in [place.z] + place.far_z():
        at = place.slot_of(z, place.c, 1 - place.y)
        copies.arrived(out.at[at], recv.at[at], {"y": 1 - place.y})
        copies.send(out.at[at], out.at[at], recv.at[at], {"c": 1 - place.c})


def gather_end(place, out, copies, recv):
    for z in [place.z] + place.far_z():
        for y in (place.y, 1 - place.y):
            at = place.slot_of(z, 1 - place.c, y)
            copies.arrived(out.at[at], recv.at[at], {"c": 1 - place.c})


def gather_copies(n_z):
    return 7 * n_z


def group_gather_kernel(own, out, send, recv):
    place = Place(False)
    copies = Copies(send)
    peer_z, peer_y, peer_c = place.at_z(1 - place.z), {"y": 1 - place.y}, {"c": 1 - place.c}
    meet([peer_z, peer_y, peer_c])
    rows = own.shape[0] // 2

    def part(at, half):
        return out.at[at, pl.ds(half * rows, rows)], recv.at[2 * at + half]

    def give(at, half, peer, src=None):
        ref, sem = part(at, half)
        copies.send(ref if src is None else src, ref, sem, peer)

    def got(at, half, peer):
        ref, sem = part(at, half)
        copies.arrived(ref, sem, peer)

    for half in range(2):
        src = own.at[pl.ds(half * rows, rows)]
        other = own.at[pl.ds((1 - half) * rows, rows)]
        give(place.slot, half, peer_y, src)
        give(place.slot, 1 - half, peer_z, other)
    copies.local(own, out.at[place.slot])
    for half in range(2):
        give(place.slot, half, peer_c, own.at[pl.ds(half * rows, rows)])
    near_y = place.slot_of(place.z, place.c, 1 - place.y)
    near_z = place.slot_of(1 - place.z, place.c, place.y)
    across = place.slot_of(1 - place.z, place.c, 1 - place.y)
    got(near_y, 0, peer_y)
    give(near_y, 0, peer_z)
    got(near_z, 1, peer_z)
    give(near_z, 1, peer_y)
    give(near_y, 0, peer_c)
    give(near_z, 1, peer_c)
    got(near_y, 1, peer_y)
    give(near_y, 1, peer_c)
    got(near_z, 0, peer_z)
    give(near_z, 0, peer_c)
    got(across, 0, peer_z)
    give(across, 0, peer_c)
    got(across, 1, peer_y)
    give(across, 1, peer_c)
    for z in range(2):
        for y in range(2):
            for half in range(2):
                got(place.slot_of(z, 1 - place.c, y), half, peer_c)
    copies.finish()


def group_gather(value, collective_id):
    return pl.pallas_call(
        group_gather_kernel,
        out_shape=jax.ShapeDtypeStruct((8,) + value.shape, value.dtype),
        in_specs=[ANY],
        out_specs=ANY,
        scratch_shapes=dma_sems(16, 16),
        compiler_params=comm_params(collective_id),
        name="group_gather",
    )(value)


def opening_kernel(
    own, blocks, ffn, out_w, out, blocks_all, ffn_all, out_w_all, send, recv, recv_w, recv_f, recv_o
):
    place, group = Place(True), Place(False)
    n_ctx = blocks.shape[0]
    copies = Copies(send)
    peer_x, peer_y = {"x": 1 - place.x}, {"y": 1 - place.y}
    far_ctx = others(place.ctx, n_ctx)
    meet([place.at_ctx(k) for k in far_ctx] + [peer_y, peer_x])
    mine = blocks_all.at[place.x, place.ctx]
    half = out_w.shape[1] // 2

    def sem_w(x, k):
        return recv_w.at[x * n_ctx + k]

    def out_block(z, x=place.x):
        at = x * place.n_z + z
        return out_w_all.at[at], recv_o.at[at]

    line = gather_begin(place, own, out, copies, recv)
    for k in far_ctx:
        copies.send(blocks.at[k], mine, sem_w(place.x, place.ctx), place.at_ctx(k))
    copies.local(blocks.at[place.ctx], mine)
    copies.send(blocks.at[place.ctx], mine, sem_w(place.x, place.ctx), peer_x)
    own_out, own_sem = out_block(place.z)
    own_half = out_w.at[:, pl.ds(pl.multiple_of(place.y * half, half), half)]
    copies.local(own_half, own_out)
    out_line = Line(place, copies, out_block)

    def out_over_x(z, here):
        ref, sem = out_block(z)
        copies.send(ref, ref, sem, peer_x, here)

    for distance in range(1, place.n_z):
        gather_step(place, line, copies, distance)
        if distance == 1:
            out_line.begin(own_half)
            copies.send(own_half, own_out, own_sem, peer_x)
            copies.local(ffn.at[:, group.ctx], ffn_all.at[:, group.ctx])
        if distance == 2:
            for k in others(group.ctx, 4):
                copies.send(ffn.at[:, k], ffn_all.at[:, group.ctx], recv_f.at[group.ctx], group.at_ctx(k))
        if distance > 1:
            out_line.arrive(distance - 1, out_over_x)
    out_line.arrive(place.n_z - 1, out_over_x)
    for k in far_ctx:
        block = blocks_all.at[place.x, k]
        copies.arrived(block, sem_w(place.x, k), place.at_ctx(k))
        copies.send(block, block, sem_w(place.x, k), peer_x)
    gather_cross(place, out, copies, recv)
    gather_end(place, out, copies, recv)
    for k in [place.ctx] + far_ctx:
        copies.arrived(blocks_all.at[1 - place.x, k], sem_w(1 - place.x, k), peer_x)
    for k in others(group.ctx, 4):
        copies.arrived(ffn_all.at[:, k], recv_f.at[k], group.at_ctx(k))
    for z in [place.z] + place.far_z():
        ref, sem = out_block(z, 1 - place.x)
        copies.arrived(ref, sem, peer_x)
    copies.finish()


def opening(own, blocks, ffn, out_w):
    n_ctx = blocks.shape[0]
    n_z = n_ctx // 2
    sends = gather_copies(n_z) + 2 * n_ctx + 4 + 5 * n_z
    return pl.pallas_call(
        opening_kernel,
        out_shape=(
            jax.ShapeDtypeStruct((2 * n_ctx,) + own.shape, own.dtype),
            jax.ShapeDtypeStruct((2,) + blocks.shape, blocks.dtype),
            jax.ShapeDtypeStruct(ffn.shape, ffn.dtype),
            jax.ShapeDtypeStruct((n_ctx, out_w.shape[0], out_w.shape[1] // 2), out_w.dtype),
        ),
        in_specs=[ANY] * 4,
        out_specs=(ANY,) * 4,
        scratch_shapes=dma_sems(sends, 2 * n_ctx, 2 * n_ctx, 4, n_ctx),
        compiler_params=comm_params(1),
        name="opening",
    )(own, blocks, ffn, out_w)


def to_tokens_kernel(src, dst, send, recv):
    place = Place(True)
    copies = Copies(send)
    count, width = src.shape[0], src.shape[2]
    far = others(place.slot, count)
    meet([place.at_slot(s) for s in far])

    def columns(s):
        return dst.at[:, pl.ds(pl.multiple_of(s * width, width), width)]

    for s in far:
        copies.send(src.at[s], columns(place.slot), recv.at[place.slot], place.at_slot(s))
    copies.local(src.at[place.slot], columns(place.slot))
    for s in far:
        copies.arrived(columns(s), recv.at[s], place.at_slot(s))
    copies.finish()


def to_tokens(value):
    count, tokens, width = value.shape
    return pl.pallas_call(
        to_tokens_kernel,
        out_shape=jax.ShapeDtypeStruct((tokens, count * width), value.dtype),
        in_specs=[ANY],
        out_specs=ANY,
        scratch_shapes=dma_sems(count, count),
        compiler_params=comm_params(2),
        name="to_tokens",
    )(value)


def to_heads_kernel(src, dst, send, recv):
    place = Place(True)
    copies = Copies(send)
    count, width = dst.shape[0], dst.shape[2]
    far = others(place.slot, count)
    meet([place.at_slot(s) for s in far])

    def columns(s):
        return src.at[:, pl.ds(pl.multiple_of(s * width, width), width)]

    for s in far:
        copies.send(columns(s), dst.at[place.slot], recv.at[place.slot], place.at_slot(s))
    copies.local(columns(place.slot), dst.at[place.slot])
    for s in far:
        copies.arrived(dst.at[s], recv.at[s], place.at_slot(s))
    copies.finish()


def to_heads(value, count):
    tokens, width = value.shape[0], value.shape[1] // count
    return pl.pallas_call(
        to_heads_kernel,
        out_shape=jax.ShapeDtypeStruct((count, tokens, width), value.dtype),
        in_specs=[ANY],
        out_specs=ANY,
        scratch_shapes=dma_sems(count, count),
        compiler_params=comm_params(3),
        name="to_heads",
    )(value)


class Scatter:
    def __init__(self, place, part, held, from_c, from_y, from_z, out, copies, loads, rc, ry, rz):
        self.__dict__.update(locals())

    def order(self):
        return self.place.far_z() + [self.place.z]

    def begin(self):
        p = self.place
        for y in (1 - p.y, p.y):
            for z in self.order():
                at = z * 2 + y
                self.copies.send(
                    self.part.at[p.slot_of(z, 1 - p.c, y)], self.from_c.at[at], self.rc.at[at], {"c": 1 - p.c}
                )
        self.queue = [(z, y) for y in (1 - p.y, p.y) for z in self.order()]
        for at in range(min(self.held.shape[0], len(self.queue))):
            self.load(at)

    def load(self, at):
        p = self.place
        z, y = self.queue[at]
        at = at % self.held.shape[0]
        self.copies.local(self.part.at[p.slot_of(z, p.c, y)], self.held.at[at], self.loads.at[at])

    def add_c(self, step):
        z, y = self.queue[step]
        at, depth = z * 2 + y, self.held.shape[0]
        own = step % depth
        self.copies.arrived(self.from_c.at[at], self.rc.at[at], {"c": 1 - self.place.c})
        pltpu.make_async_copy(self.held.at[own], self.held.at[own], self.loads.at[own]).wait()
        self.from_c[at] = self.from_c[at] + self.held[own]
        if step + depth < len(self.queue):
            self.load(step + depth)

    def over_c_far(self):
        p = self.place
        for step, z in enumerate(self.order()):
            self.add_c(step)
            self.copies.send(self.from_c.at[z * 2 + 1 - p.y], self.from_y.at[z], self.ry.at[z], {"y": 1 - p.y})

    def over_c_near(self):
        for step in range(self.place.n_z):
            self.add_c(self.place.n_z + step)

    def over_y(self):
        p = self.place
        for z in self.order():
            self.copies.arrived(self.from_y.at[z], self.ry.at[z], {"y": 1 - p.y})
            self.from_y[z] = self.from_y[z] + self.from_c[z * 2 + p.y]
            if z is not p.z:
                self.copies.send(self.from_y.at[z], self.from_z.at[p.z], self.rz.at[p.z], p.at_z(z))

    def over_z(self):
        p = self.place
        total = self.from_y[p.z].astype(F32)
        for z in p.far_z():
            self.copies.arrived(self.from_z.at[z], self.rz.at[z], p.at_z(z))
            total = total + self.from_z[z].astype(F32)
        self.out[...] = total


def scatter_scratch(n_z, block):
    return [
        pltpu.VMEM((min(8, 2 * n_z),) + block, B16),
        pltpu.VMEM((2 * n_z,) + block, B16),
        pltpu.VMEM((n_z,) + block, B16),
        pltpu.VMEM((n_z,) + block, B16),
    ]


def scatter_sems(n_z, more=0):
    return dma_sems(4 * n_z + more, min(8, 2 * n_z), 2 * n_z, n_z, n_z)


def group_scatter_kernel(part, out, held, from_c, over_y, over_z, last, send, loads, rc, ry, rz, rl):
    place = Place(False)
    copies = Copies(send)
    peer_z, peer_y, peer_c = place.at_z(1 - place.z), {"y": 1 - place.y}, {"c": 1 - place.c}
    meet([peer_z, peer_y, peer_c])
    rows = part.shape[1] // 2
    first, second = slice(0, rows), slice(rows, 2 * rows)
    own_y, far_y, own_z, far_z = place.y, 1 - place.y, place.z, 1 - place.z
    order = [(far_z, far_y), (far_z, own_y), (own_z, far_y), (own_z, own_y)]
    for z, y in order:
        at = z * 2 + y
        copies.send(part.at[place.slot_of(z, 1 - place.c, y)], from_c.at[at], rc.at[at], peer_c)
        copies.local(part.at[place.slot_of(z, place.c, y)], held.at[at], loads.at[at])

    def over_c(z, y):
        at = z * 2 + y
        copies.arrived(from_c.at[at], rc.at[at], peer_c)
        pltpu.make_async_copy(held.at[at], held.at[at], loads.at[at]).wait()
        from_c[at] = from_c[at] + held[at]
        return from_c.at[at]

    across = over_c(far_z, far_y)
    copies.send(across.at[first], over_y, ry.at[0], peer_y)
    copies.send(across.at[second], over_z, rz.at[0], peer_z)
    beside_z = over_c(far_z, own_y)
    copies.send(beside_z.at[second], last.at[0], rl.at[0], peer_z)
    beside_y = over_c(own_z, far_y)
    copies.send(beside_y.at[first], last.at[1], rl.at[1], peer_y)
    copies.arrived(over_y, ry.at[0], peer_y)
    over_y[...] = over_y[...] + beside_z[first, :]
    copies.send(over_y, last.at[2], rl.at[2], peer_z)
    copies.arrived(over_z, rz.at[0], peer_z)
    over_z[...] = over_z[...] + beside_y[second, :]
    copies.send(over_z, last.at[3], rl.at[3], peer_y)
    mine = over_c(own_z, own_y)
    copies.arrived(last.at[1], rl.at[1], peer_y)
    copies.arrived(last.at[0], rl.at[0], peer_z)
    copies.arrived(last.at[2], rl.at[2], peer_z)
    out[first, :] = mine[first, :].astype(F32) + last[1].astype(F32) + last[2].astype(F32)
    copies.arrived(last.at[3], rl.at[3], peer_y)
    out[second, :] = mine[second, :].astype(F32) + last[0].astype(F32) + last[3].astype(F32)
    copies.finish()


def group_scatter(part, collective_id):
    block = part.shape[1:]
    half = (block[0] // 2, block[1])
    return pl.pallas_call(
        group_scatter_kernel,
        out_shape=jax.ShapeDtypeStruct(block, F32),
        in_specs=[ANY],
        out_specs=IN_VMEM,
        scratch_shapes=[
            pltpu.VMEM((4,) + block, B16),
            pltpu.VMEM((4,) + block, B16),
            pltpu.VMEM(half, B16),
            pltpu.VMEM(half, B16),
            pltpu.VMEM((4,) + half, B16),
        ]
        + dma_sems(10, 4, 4, 1, 1, 4),
        compiler_params=comm_params(collective_id),
        name="group_scatter",
    )(part)


class OutScatter:
    def __init__(self, place, part, held, from_x, from_y, from_z, out, copies, loads, rx, ry, rz, rg):
        self.__dict__.update(locals())
        self.half = out.shape[2]

    def order(self):
        return self.place.far_z() + [self.place.z]

    def columns(self, y):
        return pl.ds(pl.multiple_of(y * self.half, self.half), self.half)

    def begin(self):
        p = self.place
        for z in self.order():
            self.copies.send(self.part.at[(1 - p.x) * p.n_z + z], self.from_x.at[z], self.rx.at[z], {"x": 1 - p.x})
            self.copies.local(self.part.at[p.x * p.n_z + z], self.held.at[z], self.loads.at[z])

    def over_x(self):
        p = self.place
        for z in self.order():
            self.copies.arrived(self.from_x.at[z], self.rx.at[z], {"x": 1 - p.x})
            pltpu.make_async_copy(self.held.at[z], self.held.at[z], self.loads.at[z]).wait()
            self.from_x[z] = self.from_x[z] + self.held[z]
            self.copies.send(
                self.from_x.at[z, :, self.columns(1 - p.y)], self.from_y.at[z], self.ry.at[z], {"y": 1 - p.y}
            )

    def over_y(self):
        p = self.place
        for z in self.order():
            self.copies.arrived(self.from_y.at[z], self.ry.at[z], {"y": 1 - p.y})
            self.from_y[z] = self.from_y[z] + self.from_x[z, :, self.columns(p.y)]
            if z is not p.z:
                self.copies.send(self.from_y.at[z], self.from_z.at[p.z], self.rz.at[p.z], p.at_z(z))

    def over_z(self):
        p = self.place
        total = self.from_y[p.z].astype(F32)
        for z in p.far_z():
            self.copies.arrived(self.from_z.at[z], self.rz.at[z], p.at_z(z))
            total = total + self.from_z[z].astype(F32)
        self.out[p.y] = total.astype(B16)
        self.copies.send(self.out.at[p.y], self.out.at[p.y], self.rg.at[p.y], {"y": 1 - p.y})

    def end(self):
        p = self.place
        self.copies.arrived(self.out.at[1 - p.y], self.rg.at[1 - p.y], {"y": 1 - p.y})


def closing_kernel(
    part, grads, out_part, fc, proj, sums_in, gain_in, shift_in, pair_in, ff_in,
    out, grads_out, out_w_out, fc_out, proj_out, owned, pairs_out, ff_out,
    held, from_c, from_y, from_z, own_x, from_x, o_held, o_x, o_y, o_z,
    send, loads, rc, ry, rz, load_x, rx, rk, rg, o_loads, orx, ory, orz, org, rfc, rproj,
    terms, terms_all, half, pairs_half, half_y, pairs_y, rv, rvy,
):
    place, group = Place(True), Place(False)
    n_ctx = grads.shape[1]
    copies = Copies(send)
    far_ctx = others(place.ctx, n_ctx)
    peer_x, peer_y = {"x": 1 - place.x}, {"y": 1 - place.y}
    count = 2 * n_ctx
    me = place.x * n_ctx + place.ctx
    far_shards = others(me, count)

    def at_shard(k):
        return dict(place.at_ctx(lax.rem(k, n_ctx)), x=k // n_ctx)

    meet([at_shard(k) for k in far_shards] + [peer_y])
    tall = grads.shape[2]
    terms[...] = jnp.zeros_like(terms)
    for k in range(count):
        cols = slice(k * tall, (k + 1) * tall)
        terms[k, 0:4, 0:tall] = sums_in[:, cols]
        terms[k, 4:5, 0:tall] = gain_in[:, cols]
        terms[k, 5:6, 0:tall] = shift_in[:, cols]
        pair = pair_in.shape[1] // 3
        terms[k, 6:7, 0:pair] = pair_in[:, 0:pair]
        terms[k, 7:8, 0:pair] = pair_in[:, 2 * pair :]
        for row in range(-(-ff_in.shape[1] // 128)):
            width = min(128, ff_in.shape[1] - row * 128)
            terms[k, 8 + row : 9 + row, 0:width] = ff_in[:, row * 128 : row * 128 + width]
    for k in far_shards:
        copies.send(terms.at[k], terms_all.at[me], rv.at[me], at_shard(k))
    terms_all[me] = terms[me]
    sums = Scatter(place, part, held, from_c, from_y, from_z, out, copies, loads, rc, ry, rz)
    outs = OutScatter(place, out_part, o_held, o_x, o_y, o_z, out_w_out, copies, o_loads, orx, ory, orz, org)
    sums.begin()
    for k in far_ctx + [place.ctx]:
        copies.send(grads.at[1 - place.x, k], from_x.at[k], rx.at[k], peer_x)
        copies.local(grads.at[place.x, k], own_x.at[k], load_x.at[k])
    outs.begin()
    for k in others(group.ctx, 4):
        copies.send(fc.at[k], fc_out.at[group.ctx], rfc.at[group.ctx], group.at_ctx(k))
        copies.send(proj.at[k], proj_out.at[group.ctx], rproj.at[group.ctx], group.at_ctx(k))
    copies.local(fc.at[group.ctx], fc_out.at[group.ctx])
    copies.local(proj.at[group.ctx], proj_out.at[group.ctx])
    sums.over_c_far()
    mine = grads_out.at[place.y, place.ctx]
    for k in far_ctx + [place.ctx]:
        copies.arrived(from_x.at[k], rx.at[k], peer_x)
        pltpu.make_async_copy(own_x.at[k], own_x.at[k], load_x.at[k]).wait()
        from_x[k] = from_x[k] + own_x[k]
        if k is not place.ctx:
            copies.send(from_x.at[k], mine, rk.at[place.ctx], place.at_ctx(k))
    copies.local(from_x.at[place.ctx], mine)
    copies.send(from_x.at[place.ctx], mine, rg.at[place.ctx], peer_y)
    sums.over_c_near()
    sums.over_y()
    outs.over_x()
    for k in far_ctx:
        block = grads_out.at[place.y, k]
        copies.arrived(block, rk.at[k], place.at_ctx(k))
        copies.send(block, block, rg.at[k], peer_y)
    outs.over_y()
    sums.over_z()
    outs.over_z()
    for k in far_shards:
        copies.arrived(terms_all.at[k], rv.at[k], at_shard(k))
    total = terms_all[0, 0:8, :]
    for k in range(1, count):
        total = total + terms_all[k, 0:8, :]
    half[...] = total
    for k in range(n_ctx):
        pairs_half[k] = terms_all[k, 6:8, :] + terms_all[n_ctx + k, 6:8, :]
    copies.send(half, half_y, rvy.at[0], peer_y)
    copies.send(pairs_half, pairs_y, rvy.at[1], peer_y)
    for part in range(4):
        total = terms_all[part, 8:16, :]
        for k in range(part + 4, count, 4):
            total = total + terms_all[k, 8:16, :]
        ff_out[part] = total
    copies.arrived(half_y, rvy.at[0], peer_y)
    owned[...] = half[...] + half_y[...]
    copies.arrived(pairs_y, rvy.at[1], peer_y)
    pairs_out[place.y] = pairs_half[...]
    pairs_out[1 - place.y] = pairs_y[...]
    for k in [place.ctx] + far_ctx:
        copies.arrived(grads_out.at[1 - place.y, k], rg.at[k], peer_y)
    outs.end()
    for k in others(group.ctx, 4):
        copies.arrived(fc_out.at[k], rfc.at[k], group.at_ctx(k))
        copies.arrived(proj_out.at[k], rproj.at[k], group.at_ctx(k))
    copies.finish()


def closing(part, grads, out_part, fc, proj, *vectors):
    block = part.shape[1:]
    n_ctx = grads.shape[1]
    n_z = n_ctx // 2
    piece = grads.shape[1:]
    rows, width = out_part.shape[1:]
    half = (rows, width // 2)
    return pl.pallas_call(
        closing_kernel,
        out_shape=(
            jax.ShapeDtypeStruct(block, F32),
            jax.ShapeDtypeStruct((2,) + piece, B16),
            jax.ShapeDtypeStruct((2,) + half, B16),
            jax.ShapeDtypeStruct(fc.shape, fc.dtype),
            jax.ShapeDtypeStruct(proj.shape, proj.dtype),
            jax.ShapeDtypeStruct((8, 128), F32),
            jax.ShapeDtypeStruct((2, n_ctx, 2, 128), F32),
            jax.ShapeDtypeStruct((4, 8, 128), F32),
        ),
        in_specs=[ANY] * 5 + [IN_VMEM] * 5,
        out_specs=(IN_VMEM, ANY, IN_VMEM, ANY, ANY, IN_VMEM, IN_VMEM, IN_VMEM),
        scratch_shapes=scatter_scratch(n_z, block)
        + [pltpu.VMEM(piece, B16), pltpu.VMEM(piece, B16)]
        + [pltpu.VMEM((n_z, rows, width), B16), pltpu.VMEM((n_z, rows, width), B16)]
        + [pltpu.VMEM((n_z,) + half, B16), pltpu.VMEM((n_z,) + half, B16)]
        + scatter_sems(n_z, 5 * n_ctx + 4 * n_z + 10)
        + dma_sems(n_ctx, n_ctx, n_ctx, n_ctx)
        + dma_sems(n_z, n_z, n_z, n_z, 2, 4, 4)
        + [pltpu.VMEM((2 * n_ctx, 16, 128), F32), pltpu.VMEM((2 * n_ctx, 16, 128), F32)]
        + [pltpu.VMEM((8, 128), F32), pltpu.VMEM((n_ctx, 2, 128), F32)]
        + [pltpu.VMEM((8, 128), F32), pltpu.VMEM((n_ctx, 2, 128), F32)]
        + dma_sems(2 * n_ctx, 2),
        compiler_params=comm_params(4),
        name="closing",
    )(part, grads, out_part, fc, proj, *vectors)


def laid_wide(value, count, rows, tall):
    zeros = jnp.zeros((value.shape[0], tall - rows), value.dtype)
    parts = []
    for k in range(count):
        parts += [value[:, k * rows : (k + 1) * rows], zeros]
    return jnp.concatenate(parts, axis=1)


def laid_tall(value, count, rows, tall):
    zeros = jnp.zeros((tall - rows, value.shape[1]), value.dtype)
    parts = []
    for k in range(count):
        parts += [value[k * rows : (k + 1) * rows], zeros]
    return jnp.concatenate(parts, axis=0)


def laid_short(value, count, rows, tall):
    return jnp.concatenate([value[k * tall : k * tall + rows] for k in range(count)], axis=0)


def laid_narrow(value, count, rows, tall):
    return jnp.concatenate([value[:, k * tall : k * tall + rows] for k in range(count)], axis=1)


def prepare_kernel(count, at_ref, x, grad, qkv, fc, proj, out_w, *refs):
    singles, qv, (x_out, grad_out, blocks, ffn, out_out) = refs[:6], refs[6], refs[7:]
    rows, feats = out_w.shape
    n_ctx, tall, cols = blocks.shape
    pair, ff = cols // 3, ffn.shape[3]
    x_out[...] = laid_tall(x[...].astype(F32), count, rows, tall).T.astype(B16)
    grad_out[...] = laid_tall(grad[...].astype(F32), count, rows, tall).T.astype(B16)
    below = jnp.zeros((tall - rows, feats), F32)
    out_out[...] = laid_wide(
        jnp.concatenate([out_w[...].astype(F32), below], axis=0), count, rows, tall
    ).astype(B16)
    below = jnp.zeros((tall - rows, ff), F32)
    for k in range(4):
        ffn[0, k] = jnp.concatenate([fc[:, k * ff : (k + 1) * ff].astype(F32), below], axis=0).astype(B16)
        ffn[1, k] = jnp.concatenate([proj[:, k * ff : (k + 1) * ff].astype(F32), below], axis=0).astype(B16)
    small = [jnp.concatenate([ref[...].astype(F32), jnp.zeros((1, cols - rows), F32)], axis=1) for ref in singles]
    small.append(jnp.concatenate([qv[...].astype(F32), jnp.zeros((1, cols - 2 * rows), F32)], axis=1))
    if tall - rows > 7:
        small.append(jnp.zeros((tall - rows - 7, cols), F32))
    small = jnp.concatenate(small, axis=0)
    first = at_ref[0] == 0
    whole = qkv[...].astype(F32)

    def columns(part, p):
        width = min(pair, feats - p * pair)
        if width <= 0:
            return jnp.zeros((rows, pair), F32)
        value = whole[:, part * feats + p * pair : part * feats + p * pair + width]
        if width < pair:
            value = jnp.concatenate([value, jnp.zeros((rows, pair - width), F32)], axis=1)
        return value

    for k in range(n_ctx):
        value = [jnp.where(first, columns(part, 2 * k), columns(part, 2 * k + 1)) for part in range(3)]
        blocks[k] = jnp.concatenate([jnp.concatenate(value, axis=1), small], axis=0).astype(B16)


def prepare(y_at, x, grad, qkv, fc, proj, out_w, singles, qv, n_ctx, tall, pair):
    rows, feats = out_w.shape
    count = feats // rows
    wide = count * tall
    tokens = x.shape[1]
    vmem = pl.BlockSpec(memory_space=pltpu.VMEM)
    return pl.pallas_call(
        functools.partial(prepare_kernel, count),
        in_specs=[pl.BlockSpec(memory_space=pltpu.SMEM)] + [vmem] * 13,
        out_shape=(
            jax.ShapeDtypeStruct((tokens, wide), B16),
            jax.ShapeDtypeStruct((tokens, wide), B16),
            jax.ShapeDtypeStruct((n_ctx, tall, 3 * pair), B16),
            jax.ShapeDtypeStruct((2, 4, tall, fc.shape[1] // 4), B16),
            jax.ShapeDtypeStruct((tall, wide), B16),
        ),
        compiler_params=pltpu.CompilerParams(vmem_limit_bytes=VMEM_LIMIT),
        name="prepare",
    )(y_at, x, grad, qkv, fc, proj, out_w, *[value[None] for value in singles], qv[None])


def project_kernel(
    rows, feats, at_ref, x_ref, packed_ref, mask_ref, w_ref, norm_ref, qkv_ref, single_ref, bias_s, held_s
):
    count, tall, cols = packed_ref.shape
    pair = cols // 3

    @pl.when(pl.program_id(0) == 0)
    def begin():
        held_s[...] = jnp.zeros_like(held_s)
        vectors = []
        for row in range(6):
            at = rows + row
            vectors.append(
                jnp.concatenate([packed_ref[k, at : at + 1, 0:tall].astype(F32) for k in range(count)], axis=1)
            )
        single_ref[...] = jnp.concatenate(vectors + [jnp.zeros((2, count * tall), F32)], axis=0)
        for part in range(2):
            blocks = range(part * count // 2, (part + 1) * count // 2)
            at = rows + 6
            held_s[part : part + 1, 0:feats] = jnp.concatenate(
                [packed_ref[k, at : at + 1, 0 : 2 * rows].astype(F32) for k in blocks], axis=1
            )
        own = pl.ds(pl.multiple_of(at_ref[0] * pair, pair), pair)
        bias_s[...] = jnp.concatenate([held_s[0:1, own], jnp.zeros((1, pair), F32), held_s[1:2, own]], axis=1)

    x = x_ref[...].astype(F32)
    mean = jnp.sum(x, axis=1, keepdims=True) * (1.0 / feats)
    centered = (x - mean) * mask_ref[...]
    inv = lax.rsqrt(jnp.sum(centered * centered, axis=1, keepdims=True) * (1.0 / feats) + NORM_EPS)
    norm = (centered * inv * single_ref[0:1, :] + single_ref[1:2, :]).astype(B16)
    norm_ref[...] = norm
    qkv_ref[...] = (dot(norm, w_ref[...], 1, 0) + bias_s[...]).astype(B16)


def project(slot_at, x, packed, mask, rows, feats, padded):
    total, wide = x.shape
    cols = packed.shape[2]
    step = min(256, total)

    def fixed(shape):
        return pl.BlockSpec(shape, lambda i: (0,) * len(shape))

    return pl.pallas_call(
        functools.partial(project_kernel, rows, feats),
        grid=(total // step,),
        in_specs=[pl.BlockSpec(memory_space=pltpu.SMEM), pl.BlockSpec((step, wide), lambda i: (i, 0))]
        + [fixed(packed.shape), fixed((1, wide)), fixed((wide, cols))],
        out_specs=(
            pl.BlockSpec((step, wide), lambda i: (i, 0)),
            pl.BlockSpec((step, cols), lambda i: (i, 0)),
            fixed((8, wide)),
        ),
        out_shape=(
            jax.ShapeDtypeStruct((total, wide), B16),
            jax.ShapeDtypeStruct((total, cols), B16),
            jax.ShapeDtypeStruct((8, wide), F32),
        ),
        scratch_shapes=[pltpu.VMEM((1, cols), F32), pltpu.VMEM((2, padded), F32)],
        compiler_params=pltpu.CompilerParams(vmem_limit_bytes=VMEM_LIMIT),
        name="project",
    )(slot_at, x, packed, mask[None], packed.reshape(wide, cols))


def project_back_kernel(feats, x_ref, grad_ref, mask_ref, w_ref, part_ref, gradb_ref, gain_ref, shift_ref, pair_ref):
    @pl.when(pl.program_id(0) == 0)
    def begin():
        gain_ref[...] = jnp.zeros_like(gain_ref)
        shift_ref[...] = jnp.zeros_like(shift_ref)
        pair_ref[...] = jnp.zeros_like(pair_ref)

    grad = grad_ref[...]
    pair_ref[...] += jnp.sum(grad, axis=0, keepdims=True)
    grad = grad.astype(B16)
    gradb_ref[...] = grad
    part = dot(grad, w_ref[...], 1, 1)
    part_ref[...] = part.astype(B16)
    x = x_ref[...].astype(F32)
    mean = jnp.sum(x, axis=1, keepdims=True) * (1.0 / feats)
    centered = (x - mean) * mask_ref[...]
    inv = lax.rsqrt(jnp.sum(centered * centered, axis=1, keepdims=True) * (1.0 / feats) + NORM_EPS)
    gain_ref[...] += jnp.sum(part * (centered * inv), axis=0, keepdims=True)
    shift_ref[...] += jnp.sum(part, axis=0, keepdims=True)


def project_back(x, grad, mask, weight, feats):
    total, wide = x.shape
    cols = weight.shape[1]
    step = min(256, total)

    def fixed(shape):
        return pl.BlockSpec(shape, lambda i: (0,) * len(shape))

    def moving(width):
        return pl.BlockSpec((step, width), lambda i: (i, 0))

    return pl.pallas_call(
        functools.partial(project_back_kernel, feats),
        grid=(total // step,),
        in_specs=[moving(wide), moving(cols), fixed((1, wide)), fixed((wide, cols))],
        out_specs=(moving(wide), moving(cols), fixed((1, wide)), fixed((1, wide)), fixed((1, cols))),
        out_shape=(
            jax.ShapeDtypeStruct((total, wide), B16),
            jax.ShapeDtypeStruct((total, cols), B16),
            jax.ShapeDtypeStruct((1, wide), F32),
            jax.ShapeDtypeStruct((1, wide), F32),
            jax.ShapeDtypeStruct((1, cols), F32),
        ),
        compiler_params=pltpu.CompilerParams(vmem_limit_bytes=VMEM_LIMIT),
        name="project_back",
    )(x, grad, mask[None], weight)


def deliver_kernel(
    rows, feats, qkv, out_w, fc, proj, mlp, hidden, dnorm, dhidden, x_ref, single, mask,
    qkv_out, out_out, fc_out, proj_out, block_out, grad_out,
):
    n_y, n_ctx, tall, cols = qkv.shape
    pair, ff, count = cols // 3, fc.shape[2], feats // rows
    parts = []
    for part in range(3):
        for p in range(-(-feats // pair)):
            width = min(pair, feats - p * pair)
            parts.append(qkv[p % n_y, p // n_y, :, part * pair : part * pair + width].astype(F32))
    qkv_out[...] = jnp.concatenate(parts, axis=1)[:rows]
    halves = jnp.concatenate([out_w[y].astype(F32) for y in range(2)], axis=1)
    out_out[...] = laid_narrow(halves, count, rows, tall)[:rows]
    fc_out[...] = jnp.concatenate([fc[k].astype(F32) for k in range(4)], axis=1)[:rows]
    for k in range(4):
        proj_out[:, k * ff : (k + 1) * ff] = proj[k].astype(F32)[:rows]
    block = hidden[...] + mlp[...].astype(F32) + single[5:6, :]
    block_out[...] = laid_short(block.T, count, rows, tall)
    normed, inv = norm_forward(x_ref[...].astype(F32), mask[...], feats)
    grad = dhidden[...] + norm_backward(dnorm[...], normed, inv, single[0:1, :], feats)
    grad_out[...] = laid_short(grad.T, count, rows, tall)


def deliver(qkv, out_w, fc, proj, mlp, hidden, dnorm, dhidden, x, single, mask, rows, feats):
    tokens, ff = x.shape[0], fc.shape[2]
    return pl.pallas_call(
        functools.partial(deliver_kernel, rows, feats),
        out_shape=(
            jax.ShapeDtypeStruct((rows, 3 * feats), F32),
            jax.ShapeDtypeStruct((rows, feats), F32),
            jax.ShapeDtypeStruct((rows, 4 * ff), F32),
            jax.ShapeDtypeStruct((rows, 4 * ff), F32),
            jax.ShapeDtypeStruct((feats, tokens), F32),
            jax.ShapeDtypeStruct((feats, tokens), F32),
        ),
        compiler_params=pltpu.CompilerParams(vmem_limit_bytes=VMEM_LIMIT),
        name="deliver",
    )(qkv, out_w, fc, proj, mlp, hidden, dnorm, dhidden, x, single, mask[None])


def feed_kernel(pairs, singles, at_ref, *refs):
    count = pairs + 2 * singles
    pieces, refs = refs[:count], refs[count:]
    norm_ref, grad_ref, bias_ref, act_ref, dpre_ref, dnorm_ref, mlp_ref, sum_ref, w_fc, w_proj, sems = refs

    @pl.when(pl.program_id(0) == 0)
    def begin():
        rows = pieces[0].shape[1]
        parts = [(piece.at[0], piece.at[1]) for piece in pieces[:pairs]]
        parts += list(zip(pieces[pairs : pairs + singles], pieces[pairs + singles :]))
        copies = []
        for i, (fc, proj) in enumerate(parts):
            to = pl.ds(pl.multiple_of(at_ref[i], 16), rows)
            copies.append(pltpu.make_async_copy(fc, w_fc.at[to, :], sems.at[2 * i]))
            copies.append(pltpu.make_async_copy(proj, w_proj.at[to, :], sems.at[2 * i + 1]))
        for copy in copies:
            copy.start()
        for copy in copies:
            copy.wait()
        sum_ref[...] = jnp.zeros_like(sum_ref)

    preact = dot(norm_ref[...], w_fc[...], 1, 0) + bias_ref[...]
    activated, derivative = gelu_parts(preact)
    activation = activated.astype(B16)
    act_ref[...] = activation
    dpre = dot(grad_ref[...], w_proj[...], 1, 0) * derivative
    sum_ref[...] += jnp.sum(dpre, axis=0, keepdims=True)
    dpre_b = dpre.astype(B16)
    dpre_ref[...] = dpre_b
    dnorm_ref[...] = dot(dpre_b, w_fc[...], 1, 1).astype(B16)
    mlp_ref[...] = dot(activation, w_proj[...], 1, 1).astype(B16)


def feed(pairs, fcs, projs, places, norm, grad, bias):
    pieces = pairs + fcs + projs
    total, wide = norm.shape
    ff = bias.shape[0]
    step = 256
    tokens = pl.BlockSpec((step, wide), lambda i: (i, 0))
    hidden = pl.BlockSpec((step, ff), lambda i: (i, 0))
    single = pl.BlockSpec((1, ff), lambda i: (0, 0))
    return pl.pallas_call(
        functools.partial(feed_kernel, len(pairs), len(fcs)),
        grid=(total // step,),
        in_specs=[pl.BlockSpec(memory_space=pltpu.SMEM)] + [ANY] * len(pieces) + [tokens, tokens, single],
        out_specs=(hidden, hidden, tokens, tokens, single),
        out_shape=(
            jax.ShapeDtypeStruct((total, ff), B16),
            jax.ShapeDtypeStruct((total, ff), B16),
            jax.ShapeDtypeStruct((total, wide), B16),
            jax.ShapeDtypeStruct((total, wide), B16),
            jax.ShapeDtypeStruct((1, ff), F32),
        ),
        scratch_shapes=[pltpu.VMEM((wide, ff), B16), pltpu.VMEM((wide, ff), B16)] + dma_sems(2 * len(pieces)),
        compiler_params=pltpu.CompilerParams(vmem_limit_bytes=VMEM_LIMIT),
        name="feed",
    )(places, *pieces, norm, grad, bias[None])


def after(value, other, unpack=False):
    value, other = lax.optimization_barrier((value, other))
    return (*value, other) if unpack else (value, other)


def shift_perm(count, step):
    return [(i, (i + step) % count) for i in range(count)]


def on_device(
    sizes, block_input, segment_ids, slot_order, first_gain, first_shift, qkv_weight, qv_bias, out_weight, out_bias,
    second_gain, second_shift, fc_weight, fc_bias, proj_weight, proj_bias, out_grad,
):
    n_x, n_ctx, n_y = sizes
    n_slot = n_ctx * n_y
    n_shard = n_x * n_ctx
    n_h = n_ctx // 4
    slot_len, feats = block_input.shape[1:]
    head = feats // HEADS
    pair = 2 * head
    rows = qkv_weight.shape[0]
    ff_own = fc_weight.shape[1] // 4
    padded = n_slot * pair
    y_at = lax.axis_index("y")
    ctx_at = lax.axis_index(CTX)
    slot_at = lax.axis_index(ROW)
    lc_at = lax.axis_index(("l", "c"))
    x_at, h_at = lax.axis_index("x"), lax.axis_index("h")

    def gather(value, axes):
        return lax.all_gather(value, axes, axis=0, tiled=True)

    tall = rows + (-rows % 16)
    wide = n_shard * tall
    row_pad = tall - rows

    def widened(value):
        lead = value.shape[:-1]
        value = value.reshape(lead + (n_shard, rows))
        return jnp.pad(value, [(0, 0)] * (len(lead) + 1) + [(0, row_pad)]).reshape(lead + (wide,))

    def narrowed(value):
        lead = value.shape[:-1]
        return value.reshape(lead + (n_shard, tall))[..., :rows].reshape(lead + (feats,))

    mask = jnp.asarray((np.arange(wide) % tall < rows).astype(np.float32))

    singles = (first_gain, first_shift, out_bias, second_gain, second_shift, proj_bias)
    own_input, grad_own, packed, ffn_blocks, w_out = prepare(
        y_at.astype(jnp.int32)[None], block_input[0].T, out_grad[0].T, qkv_weight, fc_weight, proj_weight.T, out_weight,
        singles, qv_bias, n_ctx, tall, pair,
    )
    all_input, packed, ffn_blocks, w_out = opening(
        own_input, packed, ffn_blocks, w_out
    )
    ffn_blocks = ffn_blocks.reshape(2, 4 * tall, ff_own)
    fc_h = [lax.ppermute(ffn_blocks[0], "h", shift_perm(n_h, step)) for step in range(1, n_h)]
    along_x = lax.ppermute(ffn_blocks, "x", shift_perm(n_x, 1))
    grad_late, all_input = after(grad_own, all_input)
    grad_all = gather(grad_late, FFG)
    w_out = lax.all_gather(w_out.reshape(wide // 2, wide // 2), ("c", "y"), axis=0, tiled=False)
    w_out = w_out.reshape(2, n_y, wide // 2, wide // 2)
    packed = packed.reshape(n_shard, tall, 3 * pair)
    w_qkv = packed.reshape(wide, 3 * pair)
    b_fc = lax.dynamic_slice_in_dim(fc_bias, lc_at * ff_own, ff_own, 0).astype(F32)

    order = slot_order[0]
    pieces = jnp.arange(n_slot, dtype=jnp.int32)
    inv = jnp.sum(jnp.where(order[None, :] == pieces[:, None], pieces[None, :], 0), axis=1).astype(jnp.int32)
    segs = jnp.take(segment_ids[0].reshape(n_slot, slot_len), inv, axis=0).reshape(-1)
    docs = jnp.arange(DOCS, dtype=jnp.int32)
    counts = jnp.sum((segs[None, :] == docs[:, None]).astype(jnp.int32), axis=1)
    starts = jnp.sum(jnp.where(segs[None, :] > docs[:, None], counts[:, None], 0), axis=0).astype(jnp.int32)
    start3 = starts.reshape(-1, 1, BLK)
    low = start3[:, 0, 0] // BLK

    own_wide = own_input.astype(F32)
    all_input = all_input.reshape(n_slot * slot_len, wide)
    norm_one, qkv, singles = project(
        slot_at.astype(jnp.int32)[None], all_input, packed, mask, rows, feats, padded
    )
    bias_out, gain_two, shift_two = singles[2], singles[3], singles[4]
    heads_out, lse = attend(inv, low, qkv, start3, slot_len, head)
    fc_h, proj_late, heads_out = after((fc_h, ffn_blocks[1]), heads_out, True)
    fc_xh = [lax.ppermute(value, "x", shift_perm(n_x, 1)) for value in fc_h]
    proj_h = [lax.ppermute(proj_late, "h", shift_perm(n_h, step)) for step in range(1, n_h)]
    attention = widened(to_tokens(heads_out.reshape(n_slot, slot_len, pair))[:, :feats])
    by_core = attention.reshape(slot_len, n_shard // 2, 2, tall)
    by_core = [by_core[:, :, part].reshape(slot_len, wide // 2) for part in range(2)]
    hidden = [dot(by_core[0], w_out[0, y], 1, 0) + dot(by_core[1], w_out[1, y], 1, 0) for y in range(n_y)]
    hidden = own_wide + jnp.concatenate(hidden, axis=1) + bias_out
    normed_two, inv_two = norm_forward(hidden, mask, feats)
    norm_two = (normed_two * gain_two + shift_two).astype(B16)
    grad_wide = grad_own.astype(F32)
    proj_h, norm_two = after(proj_h, norm_two)
    proj_xh = [lax.ppermute(value, "x", shift_perm(n_x, 1)) for value in proj_h]
    norm_all = group_gather(norm_two, 6).reshape(-1, wide)
    places = [(x_at, h_at), (1 - x_at, h_at)]
    for step in range(1, n_h):
        h_from = lax.rem(h_at + n_h - step, n_h)
        places += [(x_at, h_from), (1 - x_at, h_from)]

    def mixed(one, two):
        return [value for both in zip(one, two) for value in both]

    places = jnp.stack([(x * n_h + h) * (4 * tall) for x, h in places]).astype(jnp.int32)
    activation, dpreact_b, dnorm_part, mlp_part, dpreact_sum = feed(
        [ffn_blocks, along_x], mixed(fc_h, fc_xh), mixed(proj_h, proj_xh), places, norm_all, grad_all, b_fc
    )

    def pick(value, at):
        return lax.dynamic_index_in_dim(value, at, 0, False)

    def by_owner(value):
        value = with_layout_constraint(value.astype(B16), Layout(major_to_minor=(0, 1)))
        return value.reshape(n_x, n_h, 4 * tall, ff_own)

    proj_part = by_owner(dot(grad_all, activation, 0, 0))
    proj_x = lax.ppermute(pick(proj_part, 1 - x_at), "x", shift_perm(n_x, 1))
    fc_part = by_owner(dot(norm_all, dpreact_b, 0, 0))
    fc_x = lax.ppermute(pick(fc_part, 1 - x_at), "x", shift_perm(n_x, 1))

    proj_part, fc_part, dnorm_part = after((proj_part, fc_part), dnorm_part, True)
    dnorm_two = group_scatter(dnorm_part.reshape(8, slot_len, wide), 7)

    def over_h(value):
        gives = [pick(value, lax.rem(h_at + step, n_h)) for step in range(1, n_h)]
        return [lax.ppermute(give, "h", shift_perm(n_h, step + 1)) for step, give in enumerate(gives)]

    def total(value, received):
        value = pick(value, h_at).astype(F32)
        for other in received:
            value = value + other
        return value.astype(B16).reshape(4, tall, ff_own)

    proj_x, mlp_part, dnorm_two = after((proj_x, mlp_part), dnorm_two, True)
    proj_line = pick(proj_part, x_at) + proj_x
    proj_h = over_h(proj_line)
    mlp = lax.psum_scatter(mlp_part, FFG, scatter_dimension=0, tiled=True)
    dhidden = grad_wide + norm_backward(dnorm_two, normed_two, inv_two, gain_two, feats)
    dhidden_b = dhidden.astype(B16)
    c_at = lax.axis_index("c")
    out_give = dot(jnp.where(c_at == 0, by_core[1], by_core[0]), dhidden_b, 0, 0).astype(B16)
    out_give = lax.ppermute(out_give, "c", shift_perm(2, 1))
    out_keep = dot(jnp.where(c_at == 0, by_core[0], by_core[1]), dhidden_b, 0, 0).astype(B16)
    grad_y = [dhidden_b[:, : wide // 2], dhidden_b[:, wide // 2 :]]
    datt = [dot(grad_y[0], w_out[c, 0], 1, 1) + dot(grad_y[1], w_out[c, 1], 1, 1) for c in range(2)]
    datt = [value.astype(B16).reshape(slot_len, -1, 1, tall) for value in datt]
    dattention = narrowed(jnp.concatenate(datt, axis=2).reshape(slot_len, wide))
    dattention = jnp.pad(dattention, ((0, 0), (0, padded - feats)))
    dattention = to_heads(dattention, n_slot).reshape(n_slot * slot_len, pair)
    out_give, fc_x, dattention = after((out_give, fc_x), dattention, True)
    out_part = (out_keep + out_give).reshape(n_shard // 2, tall, wide)
    fc_line = pick(fc_part, x_at) + fc_x
    fc_h = over_h(fc_line)
    dqkv = attend_back(inv, low, qkv, heads_out, dattention, lse, start3, slot_len, head)
    dnorm_one_part, dqkv_b, gain_sum, shift_sum, pair_sum = project_back(all_input, dqkv, mask, w_qkv, feats)
    qkv_part = dot(norm_one, dqkv_b, 0, 0).astype(B16).reshape(n_x, n_ctx, tall, 3 * pair)
    proj_h, fc_h, dnorm_one_part = after((proj_h, fc_h), dnorm_one_part, True)
    token_sums = jnp.stack(
        [
            jnp.sum(dhidden, axis=0),
            jnp.sum(dnorm_two * normed_two, axis=0),
            jnp.sum(dnorm_two, axis=0),
            jnp.sum(grad_wide, axis=0),
        ]
    )
    dnorm_one, qkv_all, out_all, fc_all, proj_all, owned, pair_sums, ff_sums = closing(
        dnorm_one_part.reshape(n_slot, slot_len, wide), qkv_part, out_part, total(fc_line, fc_h), total(proj_line, proj_h),
        token_sums, gain_sum, shift_sum, pair_sum, dpreact_sum,
    )
    mlp, dnorm_one = after(mlp, dnorm_one)
    qkv_grad, out_grad_w, fc_grad, proj_grad, block_output, input_grad = deliver(
        qkv_all, out_all, fc_all, proj_all, mlp, hidden, dnorm_one, dhidden, own_input, singles, mask, rows, feats
    )
    fc_bias_grad = ff_sums.reshape(4, 1024)[:, :ff_own].reshape(4 * ff_own)
    pair_sums = pair_sums.transpose(2, 1, 0, 3).reshape(2, padded)[:, :feats].reshape(2 * feats)
    qv_grad = lax.dynamic_slice_in_dim(pair_sums, lax.axis_index(SHARD) * 2 * rows, 2 * rows, 0)

    def own(index):
        return owned[index, :rows]

    return (
        block_output.T[None],
        input_grad.T[None],
        qkv_grad,
        qv_grad,
        out_grad_w,
        own(0),
        own(4),
        own(5),
        own(1),
        own(2),
        fc_grad,
        fc_bias_grad,
        proj_grad.T,
        own(3),
    )


def solution(mesh):
    n_x, n_ctx, n_y = (mesh.shape[axis] for axis in ("dp", "context", "tensor"))
    inner = Mesh(mesh.devices.reshape(n_x, n_ctx // 4, 2, 2, n_y), ("x", "h", "l", "c", "y"))
    tokens = P("x", ROW, None)
    shard = P(SHARD)
    shard_rows = P(SHARD, None)
    return jax.shard_map(
        functools.partial(on_device, (n_x, n_ctx, n_y)),
        mesh=inner,
        in_specs=(
            tokens, P("x", None), P("x", None), shard, shard, shard_rows, shard, shard_rows, shard, shard, shard,
            P(SHARD, "y"), P("y"), P("y", SHARD), shard, tokens,
        ),
        out_specs=(
            tokens, tokens, shard_rows, shard, shard_rows, shard, shard, shard, shard, shard,
            P(SHARD, "y"), P("y"), P("y", SHARD), shard,
        ),
        check_vma=False,
    )
```

```python
import functools
import math

import jax
import jax.numpy as jnp
import numpy as np
from jax import lax
from jax.experimental import pallas as pl
from jax.experimental.layout import Layout, with_layout_constraint
from jax.experimental.pallas import tpu as pltpu
from jax.sharding import Mesh
from jax.sharding import PartitionSpec as P

HEADS = 25
DOCS = 8
NORM_EPS = 1e-05
GELU_SCALE = 0.7978845608028654
GELU_CUBE = 0.044715
MASK_FLOOR = -1e30

F32 = jnp.float32
B16 = jnp.bfloat16
BLK = 256
VMEM_LIMIT = 60 * 1024 * 1024

ROW = ("h", "l", "c", "y")
CTX = ("h", "l", "c")
SHARD = ("x", "h", "l", "c")
FFG = ("l", "c", "y")


def gelu_parts(values):
    inner_arg = GELU_SCALE * (values + GELU_CUBE * values * values * values)
    tanh_value = jnp.tanh(inner_arg)
    result = 0.5 * values * (1.0 + tanh_value)
    derivative = 0.5 * (1.0 + tanh_value) + 0.5 * values * (
        1.0 - tanh_value * tanh_value
    ) * GELU_SCALE * (1.0 + 3.0 * GELU_CUBE * values * values)
    return (result, derivative)


def norm_forward(values, mask, feats):
    mean_value = jnp.sum(values, axis=-1, keepdims=True) / feats
    centered = (values - mean_value) * mask
    inv_sigma = lax.rsqrt(jnp.sum(centered * centered, axis=-1, keepdims=True) / feats + NORM_EPS)
    return (centered * inv_sigma, inv_sigma)


def norm_backward(upstream, normed, inv_sigma, norm_gain, feats):
    scaled = upstream * norm_gain
    return inv_sigma * (
        scaled
        - jnp.sum(scaled, axis=-1, keepdims=True) / feats
        - normed * (jnp.sum(scaled * normed, axis=-1, keepdims=True) / feats)
    )


def dot(left, right, left_dim, right_dim):
    return lax.dot_general(
        left, right, (((left_dim,), (right_dim,)), ((), ())), preferred_element_type=F32
    )


def sort_slots(inv_ref, src_ref, dst_ref, slot_len, start=0, width=None, factor=None):
    width = src_ref.shape[1] if width is None else width

    def body(piece, carry):
        slot = inv_ref[piece]
        rows = src_ref[pl.ds(pl.multiple_of(slot * slot_len, slot_len), slot_len), start : start + width]
        if factor is not None:
            rows = rows * jnp.asarray(factor, rows.dtype)
        dst_ref[pl.ds(pl.multiple_of(piece * slot_len, slot_len), slot_len), :] = rows
        return carry

    lax.fori_loop(0, src_ref.shape[0] // slot_len, body, 0)


def unsort_block(inv_ref, dst_ref, value, block, slot_len):
    for part in range(BLK // slot_len):
        slot = inv_ref[block * (BLK // slot_len) + part]
        dst_ref[pl.ds(pl.multiple_of(slot * slot_len, slot_len), slot_len), :] = value[
            part * slot_len : (part + 1) * slot_len
        ].astype(dst_ref.dtype)


def block_rows(block):
    return pl.ds(pl.multiple_of(block * BLK, BLK), BLK)


def mask_of(start_row, first, query_block, diagonal):
    key_at = first * BLK + lax.broadcasted_iota(jnp.int32, (2 * BLK, BLK), 0)
    allowed = key_at >= start_row
    if diagonal:
        query_at = query_block * BLK + lax.broadcasted_iota(jnp.int32, (2 * BLK, BLK), 1)
        allowed = jnp.logical_and(allowed, key_at <= query_at)
    return allowed


def two_rows(first):
    return block_rows(jnp.maximum(first, 0)), block_rows(first + 1)


def over_pairs(low, block, step, state):
    earlier = (block - low) // 2
    state = lax.fori_loop(0, earlier, lambda t, s: step(block - 1 - 2 * (earlier - t), s, False), state)
    return step(block - 1, state, True)


def attend_kernel(slot_len, head, inv_ref, low_ref, qkv_ref, start_ref, out_ref, lse_ref, q_s, k_s, vt_s):
    total = qkv_ref.shape[0]
    pair = 2 * head
    sort_slots(inv_ref, qkv_ref, q_s, slot_len, 0, pair, 1.0 / math.sqrt(head))
    sort_slots(inv_ref, qkv_ref, k_s, slot_len, pair, pair)

    def fill(piece, carry):
        slot = inv_ref[piece]
        rows = qkv_ref[pl.ds(pl.multiple_of(slot * slot_len, slot_len), slot_len), 2 * pair :]
        vt_s[:, pl.ds(pl.multiple_of(piece * slot_len, slot_len), slot_len)] = rows.astype(F32).T.astype(B16)
        return carry

    lax.fori_loop(0, total // slot_len, fill, 0)

    def per_query(block, carry):
        queries = q_s[block_rows(block), :]
        start_row = start_ref[block]

        def step(first, state, diagonal):
            allowed = mask_of(start_row, first, block, diagonal)
            rows = two_rows(first)
            keys = jnp.concatenate([k_s[r, :] for r in rows], axis=0)
            values = jnp.concatenate([vt_s[:, r] for r in rows], axis=1)
            fresh = []
            for part in range(2):
                old_max, old_sum, old_acc = state[part]
                cols = slice(part * head, (part + 1) * head)
                scores = dot(keys[:, cols], queries[:, cols], 1, 1)
                scores = jnp.where(allowed, scores, MASK_FLOOR)
                new_max = jnp.maximum(old_max, jnp.max(scores, axis=0, keepdims=True))
                weights = jnp.where(allowed, jnp.exp(scores - new_max), 0.0)
                shrink = jnp.exp(old_max - new_max)
                new_sum = old_sum * shrink + jnp.sum(weights, axis=0, keepdims=True)
                new_acc = old_acc * shrink + dot(values[cols, :], weights.astype(B16), 1, 0)
                fresh.append((new_max, new_sum, new_acc))
            return tuple(fresh)

        first = tuple(
            (
                jnp.full((1, BLK), MASK_FLOOR, F32),
                jnp.zeros((1, BLK), F32),
                jnp.zeros((head, BLK), F32),
            )
            for part in range(2)
        )
        state = over_pairs(low_ref[block], block, step, first)
        lse_ref[block] = jnp.concatenate([s[0] + jnp.log(s[1]) for s in state], axis=0)
        result = jnp.concatenate([s[2] / s[1] for s in state], axis=0)
        unsort_block(inv_ref, out_ref, result.T, block, slot_len)
        return carry

    lax.fori_loop(0, total // BLK, per_query, 0)


def attend(inv, low, qkv, start3, slot_len, head):
    total = qkv.shape[0]
    vmem = pl.BlockSpec(memory_space=pltpu.VMEM)
    smem = pl.BlockSpec(memory_space=pltpu.SMEM)
    return pl.pallas_call(
        functools.partial(attend_kernel, slot_len, head),
        out_shape=(
            jax.ShapeDtypeStruct((total, 2 * head), B16),
            jax.ShapeDtypeStruct((total // BLK, 2, BLK), F32),
        ),
        in_specs=[smem, smem, vmem, vmem],
        out_specs=(vmem, vmem),
        scratch_shapes=[
            pltpu.VMEM((total, 2 * head), B16),
            pltpu.VMEM((total, 2 * head), B16),
            pltpu.VMEM((2 * head, total), B16),
        ],
        compiler_params=pltpu.CompilerParams(vmem_limit_bytes=VMEM_LIMIT),
        name="attend",
    )(inv, low, qkv, start3)


def attend_back_kernel(
    slot_len, head, inv_ref, low_ref, qkv_ref, out_ref, grad_ref, lse_ref, start_ref,
    dqkv_ref, q_s, k_s, v_s, kt_s, o_s, g_s, dk_s, dv_s,
):
    total = qkv_ref.shape[0]
    pair = 2 * head
    scale = 1.0 / math.sqrt(head)
    sort_slots(inv_ref, qkv_ref, q_s, slot_len, 0, pair, scale)
    sort_slots(inv_ref, qkv_ref, k_s, slot_len, pair, pair)
    sort_slots(inv_ref, qkv_ref, v_s, slot_len, 2 * pair, pair)
    sort_slots(inv_ref, out_ref, o_s, slot_len)
    sort_slots(inv_ref, grad_ref, g_s, slot_len)

    def fill(block, carry):
        kt_s[:, block_rows(block)] = k_s[block_rows(block), :].astype(F32).T.astype(B16)
        return carry

    lax.fori_loop(0, total // BLK, fill, 0)
    dk_s[...] = jnp.zeros_like(dk_s)
    dv_s[...] = jnp.zeros_like(dv_s)

    def per_query(block, carry):
        queries = q_s[block_rows(block), :]
        grads = g_s[block_rows(block), :]
        start_row = start_ref[block]
        lse = lse_ref[block]
        prod = (grads.astype(F32) * o_s[block_rows(block), :].astype(F32)).T
        delta = [jnp.sum(prod[part * head : (part + 1) * head], axis=0, keepdims=True) for part in range(2)]

        def step(first, state, diagonal):
            allowed = mask_of(start_row, first, block, diagonal)
            rows = two_rows(first)
            keys = jnp.concatenate([k_s[r, :] for r in rows], axis=0)
            values = jnp.concatenate([v_s[r, :] for r in rows], axis=0)
            flipped = jnp.concatenate([kt_s[:, r] for r in rows], axis=1)
            fresh, dks, dvs = [], [], []
            for part in range(2):
                cols = slice(part * head, (part + 1) * head)
                scores = dot(keys[:, cols], queries[:, cols], 1, 1)
                weights = jnp.where(allowed, jnp.exp(scores - lse[part : part + 1]), 0.0)
                dprob = dot(values[:, cols], grads[:, cols], 1, 1)
                dscore = (weights * (dprob - delta[part])).astype(B16)
                dvs.append(dot(weights.astype(B16), grads[:, cols], 1, 0))
                dks.append(dot(dscore, queries[:, cols], 1, 0))
                fresh.append(state[part] + dot(flipped[cols, :], dscore, 1, 0))
            dk, dv = jnp.concatenate(dks, axis=1), jnp.concatenate(dvs, axis=1)
            for i, r in enumerate(rows):
                dk_s[r, :] += dk[i * BLK : (i + 1) * BLK]
                dv_s[r, :] += dv[i * BLK : (i + 1) * BLK]
            return tuple(fresh)

        state = (jnp.zeros((head, BLK), F32), jnp.zeros((head, BLK), F32))
        state = over_pairs(low_ref[block], block, step, state)
        dq = jnp.concatenate(state, axis=0).T * scale
        for part in range(BLK // slot_len):
            slot = inv_ref[block * (BLK // slot_len) + part]
            dqkv_ref[pl.ds(pl.multiple_of(slot * slot_len, slot_len), slot_len), 0:pair] = dq[
                part * slot_len : (part + 1) * slot_len
            ]
        return carry

    lax.fori_loop(0, total // BLK, per_query, 0)

    def give(piece, carry):
        slot = inv_ref[piece]
        rows = pl.ds(pl.multiple_of(slot * slot_len, slot_len), slot_len)
        held = pl.ds(pl.multiple_of(piece * slot_len, slot_len), slot_len)
        dqkv_ref[rows, pair : 2 * pair] = dk_s[held, :]
        dqkv_ref[rows, 2 * pair :] = dv_s[held, :]
        return carry

    lax.fori_loop(0, total // slot_len, give, 0)


def attend_back(inv, low, qkv, out, grad, lse, start3, slot_len, head):
    total = qkv.shape[0]
    pair = 2 * head
    vmem = pl.BlockSpec(memory_space=pltpu.VMEM)
    smem = pl.BlockSpec(memory_space=pltpu.SMEM)
    held = pltpu.VMEM((total, pair), B16)
    return pl.pallas_call(
        functools.partial(attend_back_kernel, slot_len, head),
        out_shape=jax.ShapeDtypeStruct((total, 3 * pair), F32),
        in_specs=[smem, smem] + [vmem] * 5,
        out_specs=vmem,
        scratch_shapes=[
            held, held, held, pltpu.VMEM((pair, total), B16), held, held,
            pltpu.VMEM((total, pair), F32), pltpu.VMEM((total, pair), F32),
        ],
        compiler_params=pltpu.CompilerParams(vmem_limit_bytes=VMEM_LIMIT),
        name="attend_back",
    )(inv, low, qkv, out, grad, lse, start3)


class Place:
    def __init__(self, whole_line):
        self.x, self.h, self.l, self.c, self.y = (lax.axis_index(a) for a in ("x", "h", "l", "c", "y"))
        self.whole_line = whole_line
        self.n_z = 2 * lax.axis_size("h") if whole_line else 2
        self.z = self.h * 2 + self.l if whole_line else self.l
        self.ctx = self.z * 2 + self.c
        self.slot = self.ctx * 2 + self.y

    def at_z(self, z):
        return {"h": z // 2, "l": lax.rem(z, 2)} if self.whole_line else {"l": z}

    def at_ctx(self, k):
        return dict(self.at_z(k // 2), c=lax.rem(k, 2))

    def at_slot(self, s):
        return dict(self.at_ctx(s // 2), y=lax.rem(s, 2))

    def far_z(self):
        order = []
        for step in range(1, self.n_z // 2 + 1):
            order += [step] if 2 * step == self.n_z else [step, self.n_z - step]
        return [lax.rem(self.z + step, self.n_z) for step in order]

    def slot_of(self, z, c, y):
        return (z * 2 + c) * 2 + y


class Copies:
    def __init__(self, sems):
        self.sems = sems
        self.begun = []

    def send(self, src, dst, recv, peer, when=None):
        at = len(self.begun)
        copy = pltpu.make_async_remote_copy(
            src_ref=src,
            dst_ref=dst,
            send_sem=self.sems.at[at],
            recv_sem=recv,
            device_id=peer,
            device_id_type=pl.DeviceIdType.MESH,
        )
        if when is None:
            copy.start()
            self.begun.append(copy.wait_send)
        else:
            pl.when(when)(copy.start)
            self.begun.append(lambda: pl.when(when)(copy.wait_send))

    def local(self, src, dst, sem=None):
        copy = pltpu.make_async_copy(src, dst, self.sems.at[len(self.begun)] if sem is None else sem)
        copy.start()
        if sem is None:
            self.begun.append(copy.wait)
        return copy

    def arrived(self, dst, recv, peer):
        pltpu.make_async_remote_copy(
            src_ref=dst,
            dst_ref=dst,
            send_sem=self.sems.at[0],
            recv_sem=recv,
            device_id=peer,
            device_id_type=pl.DeviceIdType.MESH,
        ).wait_recv()

    def finish(self):
        for wait in self.begun:
            wait()


def meet(peers):
    barrier = pltpu.get_barrier_semaphore()
    for peer in peers:
        pl.semaphore_signal(barrier, inc=1, device_id=peer, device_id_type=pl.DeviceIdType.MESH)
    pl.semaphore_wait(barrier, len(peers))


def others(me, count):
    return [lax.rem(me + step, count) for step in range(1, count)]


ANY = pl.BlockSpec(memory_space=pl.ANY)
IN_VMEM = pl.BlockSpec(memory_space=pltpu.VMEM)


def dma_sems(*counts):
    return [pltpu.SemaphoreType.DMA((count,)) for count in counts]


def comm_params(collective_id):
    return pltpu.CompilerParams(
        collective_id=collective_id, has_side_effects=True, vmem_limit_bytes=VMEM_LIMIT
    )


class Line:
    def __init__(self, place, copies, block):
        self.place, self.copies, self.block = place, copies, block

    def pass_on(self, src, z, step, when):
        p = self.place
        ref, sem = self.block(z)
        peer = p.at_z(jnp.clip(p.z + step, 0, p.n_z - 1))
        self.copies.send(ref if src is None else src, ref, sem, peer, when)

    def begin(self, own):
        p = self.place
        self.pass_on(own, p.z, 1, p.z < p.n_z - 1)
        self.pass_on(own, p.z, -1, p.z > 0)

    def arrive(self, distance, then):
        p = self.place
        for side in (1, -1):
            z = p.z + side * distance
            here = jnp.logical_and(z >= 0, z < p.n_z)
            z = jnp.clip(z, 0, p.n_z - 1)
            ref, sem = self.block(z)
            peer = p.at_z(jnp.clip(p.z + side, 0, p.n_z - 1))
            pl.when(here)(lambda: self.copies.arrived(ref, sem, peer))
            beyond = p.z - side
            beyond = jnp.logical_and(beyond >= 0, beyond < p.n_z)
            self.pass_on(None, z, -side, jnp.logical_and(here, beyond))
            then(z, here)


def row_line(place, out, copies, recv):
    def block(z):
        at = place.slot_of(z, place.c, place.y)
        return out.at[at], recv.at[at]

    return Line(place, copies, block)


def gather_begin(place, own, out, copies, recv):
    peer_y, peer_c = {"y": 1 - place.y}, {"c": 1 - place.c}
    copies.local(own, out.at[place.slot])
    line = row_line(place, out, copies, recv)
    line.begin(own)
    copies.send(own, out.at[place.slot], recv.at[place.slot], peer_y)
    copies.send(own, out.at[place.slot], recv.at[place.slot], peer_c)
    return line


def gather_step(place, line, copies, distance):
    def then(z, here):
        ref, sem = line.block(z)
        copies.send(ref, ref, sem, {"y": 1 - place.y}, here)
        copies.send(ref, ref, sem, {"c": 1 - place.c}, here)

    line.arrive(distance, then)


def gather_cross(place, out, copies, recv):
    for z in [place.z] + place.far_z():
        at = place.slot_of(z, place.c, 1 - place.y)
        copies.arrived(out.at[at], recv.at[at], {"y": 1 - place.y})
        copies.send(out.at[at], out.at[at], recv.at[at], {"c": 1 - place.c})


def gather_end(place, out, copies, recv):
    for z in [place.z] + place.far_z():
        for y in (place.y, 1 - place.y):
            at = place.slot_of(z, 1 - place.c, y)
            copies.arrived(out.at[at], recv.at[at], {"c": 1 - place.c})


def gather_copies(n_z):
    return 7 * n_z


def group_gather_kernel(own, out, send, recv):
    place = Place(False)
    copies = Copies(send)
    peer_z, peer_y, peer_c = place.at_z(1 - place.z), {"y": 1 - place.y}, {"c": 1 - place.c}
    meet([peer_z, peer_y, peer_c])
    rows = own.shape[0] // 2

    def part(at, half):
        return out.at[at, pl.ds(half * rows, rows)], recv.at[2 * at + half]

    def give(at, half, peer, src=None):
        ref, sem = part(at, half)
        copies.send(ref if src is None else src, ref, sem, peer)

    def got(at, half, peer):
        ref, sem = part(at, half)
        copies.arrived(ref, sem, peer)

    for half in range(2):
        src = own.at[pl.ds(half * rows, rows)]
        other = own.at[pl.ds((1 - half) * rows, rows)]
        give(place.slot, half, peer_y, src)
        give(place.slot, 1 - half, peer_z, other)
    copies.local(own, out.at[place.slot])
    for half in range(2):
        give(place.slot, half, peer_c, own.at[pl.ds(half * rows, rows)])
    near_y = place.slot_of(place.z, place.c, 1 - place.y)
    near_z = place.slot_of(1 - place.z, place.c, place.y)
    across = place.slot_of(1 - place.z, place.c, 1 - place.y)
    got(near_y, 0, peer_y)
    give(near_y, 0, peer_z)
    got(near_z, 1, peer_z)
    give(near_z, 1, peer_y)
    give(near_y, 0, peer_c)
    give(near_z, 1, peer_c)
    got(near_y, 1, peer_y)
    give(near_y, 1, peer_c)
    got(near_z, 0, peer_z)
    give(near_z, 0, peer_c)
    got(across, 0, peer_z)
    give(across, 0, peer_c)
    got(across, 1, peer_y)
    give(across, 1, peer_c)
    for z in range(2):
        for y in range(2):
            for half in range(2):
                got(place.slot_of(z, 1 - place.c, y), half, peer_c)
    copies.finish()


def group_gather(value, collective_id):
    return pl.pallas_call(
        group_gather_kernel,
        out_shape=jax.ShapeDtypeStruct((8,) + value.shape, value.dtype),
        in_specs=[ANY],
        out_specs=ANY,
        scratch_shapes=dma_sems(16, 16),
        compiler_params=comm_params(collective_id),
        name="group_gather",
    )(value)


def opening_kernel(
    own, blocks, ffn, out_w, out, blocks_all, ffn_all, out_w_all, send, recv, recv_w, recv_f, recv_o
):
    place, group = Place(True), Place(False)
    n_ctx = blocks.shape[0]
    copies = Copies(send)
    peer_x, peer_y = {"x": 1 - place.x}, {"y": 1 - place.y}
    far_ctx = others(place.ctx, n_ctx)
    meet([place.at_ctx(k) for k in far_ctx] + [peer_y, peer_x])
    mine = blocks_all.at[place.x, place.ctx]
    half = out_w.shape[1] // 2

    def sem_w(x, k):
        return recv_w.at[x * n_ctx + k]

    def out_block(z, x=place.x):
        at = x * place.n_z + z
        return out_w_all.at[at], recv_o.at[at]

    line = gather_begin(place, own, out, copies, recv)
    for k in far_ctx:
        copies.send(blocks.at[k], mine, sem_w(place.x, place.ctx), place.at_ctx(k))
    copies.local(blocks.at[place.ctx], mine)
    copies.send(blocks.at[place.ctx], mine, sem_w(place.x, place.ctx), peer_x)
    own_out, own_sem = out_block(place.z)
    own_half = out_w.at[:, pl.ds(pl.multiple_of(place.y * half, half), half)]
    copies.local(own_half, own_out)
    out_line = Line(place, copies, out_block)

    def out_over_x(z, here):
        ref, sem = out_block(z)
        copies.send(ref, ref, sem, peer_x, here)

    for distance in range(1, place.n_z):
        gather_step(place, line, copies, distance)
        if distance == 1:
            out_line.begin(own_half)
            copies.send(own_half, own_out, own_sem, peer_x)
            copies.local(ffn.at[:, group.ctx], ffn_all.at[:, group.ctx])
        if distance == 2:
            for k in others(group.ctx, 4):
                copies.send(ffn.at[:, k], ffn_all.at[:, group.ctx], recv_f.at[group.ctx], group.at_ctx(k))
        if distance > 1:
            out_line.arrive(distance - 1, out_over_x)
    out_line.arrive(place.n_z - 1, out_over_x)
    for k in far_ctx:
        block = blocks_all.at[place.x, k]
        copies.arrived(block, sem_w(place.x, k), place.at_ctx(k))
        copies.send(block, block, sem_w(place.x, k), peer_x)
    gather_cross(place, out, copies, recv)
    gather_end(place, out, copies, recv)
    for k in [place.ctx] + far_ctx:
        copies.arrived(blocks_all.at[1 - place.x, k], sem_w(1 - place.x, k), peer_x)
    for k in others(group.ctx, 4):
        copies.arrived(ffn_all.at[:, k], recv_f.at[k], group.at_ctx(k))
    for z in [place.z] + place.far_z():
        ref, sem = out_block(z, 1 - place.x)
        copies.arrived(ref, sem, peer_x)
    copies.finish()


def opening(own, blocks, ffn, out_w):
    n_ctx = blocks.shape[0]
    n_z = n_ctx // 2
    sends = gather_copies(n_z) + 2 * n_ctx + 4 + 5 * n_z
    return pl.pallas_call(
        opening_kernel,
        out_shape=(
            jax.ShapeDtypeStruct((2 * n_ctx,) + own.shape, own.dtype),
            jax.ShapeDtypeStruct((2,) + blocks.shape, blocks.dtype),
            jax.ShapeDtypeStruct(ffn.shape, ffn.dtype),
            jax.ShapeDtypeStruct((n_ctx, out_w.shape[0], out_w.shape[1] // 2), out_w.dtype),
        ),
        in_specs=[ANY] * 4,
        out_specs=(ANY,) * 4,
        scratch_shapes=dma_sems(sends, 2 * n_ctx, 2 * n_ctx, 4, n_ctx),
        compiler_params=comm_params(1),
        name="opening",
    )(own, blocks, ffn, out_w)


def to_tokens_kernel(src, dst, send, recv):
    place = Place(True)
    copies = Copies(send)
    count, width = src.shape[0], src.shape[2]
    far = others(place.slot, count)
    meet([place.at_slot(s) for s in far])

    def columns(s):
        return dst.at[:, pl.ds(pl.multiple_of(s * width, width), width)]

    for s in far:
        copies.send(src.at[s], columns(place.slot), recv.at[place.slot], place.at_slot(s))
    copies.local(src.at[place.slot], columns(place.slot))
    for s in far:
        copies.arrived(columns(s), recv.at[s], place.at_slot(s))
    copies.finish()


def to_tokens(value):
    count, tokens, width = value.shape
    return pl.pallas_call(
        to_tokens_kernel,
        out_shape=jax.ShapeDtypeStruct((tokens, count * width), value.dtype),
        in_specs=[ANY],
        out_specs=ANY,
        scratch_shapes=dma_sems(count, count),
        compiler_params=comm_params(2),
        name="to_tokens",
    )(value)


def to_heads_kernel(src, dst, send, recv):
    place = Place(True)
    copies = Copies(send)
    count, width = dst.shape[0], dst.shape[2]
    far = others(place.slot, count)
    meet([place.at_slot(s) for s in far])

    def columns(s):
        return src.at[:, pl.ds(pl.multiple_of(s * width, width), width)]

    for s in far:
        copies.send(columns(s), dst.at[place.slot], recv.at[place.slot], place.at_slot(s))
    copies.local(columns(place.slot), dst.at[place.slot])
    for s in far:
        copies.arrived(dst.at[s], recv.at[s], place.at_slot(s))
    copies.finish()


def to_heads(value, count):
    tokens, width = value.shape[0], value.shape[1] // count
    return pl.pallas_call(
        to_heads_kernel,
        out_shape=jax.ShapeDtypeStruct((count, tokens, width), value.dtype),
        in_specs=[ANY],
        out_specs=ANY,
        scratch_shapes=dma_sems(count, count),
        compiler_params=comm_params(3),
        name="to_heads",
    )(value)


class Scatter:
    def __init__(self, place, part, held, from_c, from_y, from_z, out, copies, loads, rc, ry, rz):
        self.__dict__.update(locals())

    def order(self):
        return self.place.far_z() + [self.place.z]

    def begin(self):
        p = self.place
        for y in (1 - p.y, p.y):
            for z in self.order():
                at = z * 2 + y
                self.copies.send(
                    self.part.at[p.slot_of(z, 1 - p.c, y)], self.from_c.at[at], self.rc.at[at], {"c": 1 - p.c}
                )
        self.queue = [(z, y) for y in (1 - p.y, p.y) for z in self.order()]
        for at in range(min(self.held.shape[0], len(self.queue))):
            self.load(at)

    def load(self, at):
        p = self.place
        z, y = self.queue[at]
        at = at % self.held.shape[0]
        self.copies.local(self.part.at[p.slot_of(z, p.c, y)], self.held.at[at], self.loads.at[at])

    def add_c(self, step):
        z, y = self.queue[step]
        at, depth = z * 2 + y, self.held.shape[0]
        own = step % depth
        self.copies.arrived(self.from_c.at[at], self.rc.at[at], {"c": 1 - self.place.c})
        pltpu.make_async_copy(self.held.at[own], self.held.at[own], self.loads.at[own]).wait()
        self.from_c[at] = self.from_c[at] + self.held[own]
        if step + depth < len(self.queue):
            self.load(step + depth)

    def over_c_far(self):
        p = self.place
        for step, z in enumerate(self.order()):
            self.add_c(step)
            self.copies.send(self.from_c.at[z * 2 + 1 - p.y], self.from_y.at[z], self.ry.at[z], {"y": 1 - p.y})

    def over_c_near(self):
        for step in range(self.place.n_z):
            self.add_c(self.place.n_z + step)

    def over_y(self):
        p = self.place
        for z in self.order():
            self.copies.arrived(self.from_y.at[z], self.ry.at[z], {"y": 1 - p.y})
            self.from_y[z] = self.from_y[z] + self.from_c[z * 2 + p.y]
            if z is not p.z:
                self.copies.send(self.from_y.at[z], self.from_z.at[p.z], self.rz.at[p.z], p.at_z(z))

    def over_z(self):
        p = self.place
        total = self.from_y[p.z].astype(F32)
        for z in p.far_z():
            self.copies.arrived(self.from_z.at[z], self.rz.at[z], p.at_z(z))
            total = total + self.from_z[z].astype(F32)
        self.out[...] = total


def scatter_scratch(n_z, block):
    return [
        pltpu.VMEM((min(8, 2 * n_z),) + block, B16),
        pltpu.VMEM((2 * n_z,) + block, B16),
        pltpu.VMEM((n_z,) + block, B16),
        pltpu.VMEM((n_z,) + block, B16),
    ]


def scatter_sems(n_z, more=0):
    return dma_sems(4 * n_z + more, min(8, 2 * n_z), 2 * n_z, n_z, n_z)


def group_scatter_kernel(part, out, held, from_c, over_y, over_z, last, send, loads, rc, ry, rz, rl):
    place = Place(False)
    copies = Copies(send)
    peer_z, peer_y, peer_c = place.at_z(1 - place.z), {"y": 1 - place.y}, {"c": 1 - place.c}
    meet([peer_z, peer_y, peer_c])
    rows = part.shape[1] // 2
    first, second = slice(0, rows), slice(rows, 2 * rows)
    own_y, far_y, own_z, far_z = place.y, 1 - place.y, place.z, 1 - place.z
    order = [(far_z, far_y), (far_z, own_y), (own_z, far_y), (own_z, own_y)]
    for z, y in order:
        at = z * 2 + y
        copies.send(part.at[place.slot_of(z, 1 - place.c, y)], from_c.at[at], rc.at[at], peer_c)
        copies.local(part.at[place.slot_of(z, place.c, y)], held.at[at], loads.at[at])

    def over_c(z, y):
        at = z * 2 + y
        copies.arrived(from_c.at[at], rc.at[at], peer_c)
        pltpu.make_async_copy(held.at[at], held.at[at], loads.at[at]).wait()
        from_c[at] = from_c[at] + held[at]
        return from_c.at[at]

    across = over_c(far_z, far_y)
    copies.send(across.at[first], over_y, ry.at[0], peer_y)
    copies.send(across.at[second], over_z, rz.at[0], peer_z)
    beside_z = over_c(far_z, own_y)
    copies.send(beside_z.at[second], last.at[0], rl.at[0], peer_z)
    beside_y = over_c(own_z, far_y)
    copies.send(beside_y.at[first], last.at[1], rl.at[1], peer_y)
    copies.arrived(over_y, ry.at[0], peer_y)
    over_y[...] = over_y[...] + beside_z[first, :]
    copies.send(over_y, last.at[2], rl.at[2], peer_z)
    copies.arrived(over_z, rz.at[0], peer_z)
    over_z[...] = over_z[...] + beside_y[second, :]
    copies.send(over_z, last.at[3], rl.at[3], peer_y)
    mine = over_c(own_z, own_y)
    copies.arrived(last.at[1], rl.at[1], peer_y)
    copies.arrived(last.at[0], rl.at[0], peer_z)
    copies.arrived(last.at[2], rl.at[2], peer_z)
    out[first, :] = mine[first, :].astype(F32) + last[1].astype(F32) + last[2].astype(F32)
    copies.arrived(last.at[3], rl.at[3], peer_y)
    out[second, :] = mine[second, :].astype(F32) + last[0].astype(F32) + last[3].astype(F32)
    copies.finish()


def group_scatter(part, collective_id):
    block = part.shape[1:]
    half = (block[0] // 2, block[1])
    return pl.pallas_call(
        group_scatter_kernel,
        out_shape=jax.ShapeDtypeStruct(block, F32),
        in_specs=[ANY],
        out_specs=IN_VMEM,
        scratch_shapes=[
            pltpu.VMEM((4,) + block, B16),
            pltpu.VMEM((4,) + block, B16),
            pltpu.VMEM(half, B16),
            pltpu.VMEM(half, B16),
            pltpu.VMEM((4,) + half, B16),
        ]
        + dma_sems(10, 4, 4, 1, 1, 4),
        compiler_params=comm_params(collective_id),
        name="group_scatter",
    )(part)


class OutScatter:
    def __init__(self, place, part, held, from_x, from_y, from_z, out, copies, loads, rx, ry, rz, rg):
        self.__dict__.update(locals())
        self.half = out.shape[2]

    def order(self):
        return self.place.far_z() + [self.place.z]

    def columns(self, y):
        return pl.ds(pl.multiple_of(y * self.half, self.half), self.half)

    def begin(self):
        p = self.place
        for z in self.order():
            self.copies.send(self.part.at[(1 - p.x) * p.n_z + z], self.from_x.at[z], self.rx.at[z], {"x": 1 - p.x})
            self.copies.local(self.part.at[p.x * p.n_z + z], self.held.at[z], self.loads.at[z])

    def over_x(self):
        p = self.place
        for z in self.order():
            self.copies.arrived(self.from_x.at[z], self.rx.at[z], {"x": 1 - p.x})
            pltpu.make_async_copy(self.held.at[z], self.held.at[z], self.loads.at[z]).wait()
            self.from_x[z] = self.from_x[z] + self.held[z]
            self.copies.send(
                self.from_x.at[z, :, self.columns(1 - p.y)], self.from_y.at[z], self.ry.at[z], {"y": 1 - p.y}
            )

    def over_y(self):
        p = self.place
        for z in self.order():
            self.copies.arrived(self.from_y.at[z], self.ry.at[z], {"y": 1 - p.y})
            self.from_y[z] = self.from_y[z] + self.from_x[z, :, self.columns(p.y)]
            if z is not p.z:
                self.copies.send(self.from_y.at[z], self.from_z.at[p.z], self.rz.at[p.z], p.at_z(z))

    def over_z(self):
        p = self.place
        total = self.from_y[p.z].astype(F32)
        for z in p.far_z():
            self.copies.arrived(self.from_z.at[z], self.rz.at[z], p.at_z(z))
            total = total + self.from_z[z].astype(F32)
        self.out[p.y] = total.astype(B16)
        self.copies.send(self.out.at[p.y], self.out.at[p.y], self.rg.at[p.y], {"y": 1 - p.y})

    def end(self):
        p = self.place
        self.copies.arrived(self.out.at[1 - p.y], self.rg.at[1 - p.y], {"y": 1 - p.y})


def closing_kernel(
    part, grads, out_part, fc, proj, sums_in, gain_in, shift_in, pair_in, ff_in,
    out, grads_out, out_w_out, fc_out, proj_out, owned, pairs_out, ff_out,
    held, from_c, from_y, from_z, own_x, from_x, o_held, o_x, o_y, o_z,
    send, loads, rc, ry, rz, load_x, rx, rk, rg, o_loads, orx, ory, orz, org, rfc, rproj,
    terms, terms_all, half, pairs_half, half_y, pairs_y, rv, rvy,
):
    place, group = Place(True), Place(False)
    n_ctx = grads.shape[1]
    copies = Copies(send)
    far_ctx = others(place.ctx, n_ctx)
    peer_x, peer_y = {"x": 1 - place.x}, {"y": 1 - place.y}
    count = 2 * n_ctx
    me = place.x * n_ctx + place.ctx
    far_shards = others(me, count)

    def at_shard(k):
        return dict(place.at_ctx(lax.rem(k, n_ctx)), x=k // n_ctx)

    meet([at_shard(k) for k in far_shards] + [peer_y])
    tall = grads.shape[2]
    terms[...] = jnp.zeros_like(terms)
    for k in range(count):
        cols = slice(k * tall, (k + 1) * tall)
        terms[k, 0:4, 0:tall] = sums_in[:, cols]
        terms[k, 4:5, 0:tall] = gain_in[:, cols]
        terms[k, 5:6, 0:tall] = shift_in[:, cols]
        pair = pair_in.shape[1] // 3
        terms[k, 6:7, 0:pair] = pair_in[:, 0:pair]
        terms[k, 7:8, 0:pair] = pair_in[:, 2 * pair :]
        for row in range(-(-ff_in.shape[1] // 128)):
            width = min(128, ff_in.shape[1] - row * 128)
            terms[k, 8 + row : 9 + row, 0:width] = ff_in[:, row * 128 : row * 128 + width]
    for k in far_shards:
        copies.send(terms.at[k], terms_all.at[me], rv.at[me], at_shard(k))
    terms_all[me] = terms[me]
    sums = Scatter(place, part, held, from_c, from_y, from_z, out, copies, loads, rc, ry, rz)
    outs = OutScatter(place, out_part, o_held, o_x, o_y, o_z, out_w_out, copies, o_loads, orx, ory, orz, org)
    sums.begin()
    for k in far_ctx + [place.ctx]:
        copies.send(grads.at[1 - place.x, k], from_x.at[k], rx.at[k], peer_x)
        copies.local(grads.at[place.x, k], own_x.at[k], load_x.at[k])
    outs.begin()
    for k in others(group.ctx, 4):
        copies.send(fc.at[k], fc_out.at[group.ctx], rfc.at[group.ctx], group.at_ctx(k))
        copies.send(proj.at[k], proj_out.at[group.ctx], rproj.at[group.ctx], group.at_ctx(k))
    copies.local(fc.at[group.ctx], fc_out.at[group.ctx])
    copies.local(proj.at[group.ctx], proj_out.at[group.ctx])
    sums.over_c_far()
    mine = grads_out.at[place.y, place.ctx]
    for k in far_ctx + [place.ctx]:
        copies.arrived(from_x.at[k], rx.at[k], peer_x)
        pltpu.make_async_copy(own_x.at[k], own_x.at[k], load_x.at[k]).wait()
        from_x[k] = from_x[k] + own_x[k]
        if k is not place.ctx:
            copies.send(from_x.at[k], mine, rk.at[place.ctx], place.at_ctx(k))
    copies.local(from_x.at[place.ctx], mine)
    copies.send(from_x.at[place.ctx], mine, rg.at[place.ctx], peer_y)
    sums.over_c_near()
    sums.over_y()
    outs.over_x()
    for k in far_ctx:
        block = grads_out.at[place.y, k]
        copies.arrived(block, rk.at[k], place.at_ctx(k))
        copies.send(block, block, rg.at[k], peer_y)
    outs.over_y()
    sums.over_z()
    outs.over_z()
    for k in far_shards:
        copies.arrived(terms_all.at[k], rv.at[k], at_shard(k))
    total = terms_all[0, 0:8, :]
    for k in range(1, count):
        total = total + terms_all[k, 0:8, :]
    half[...] = total
    for k in range(n_ctx):
        pairs_half[k] = terms_all[k, 6:8, :] + terms_all[n_ctx + k, 6:8, :]
    copies.send(half, half_y, rvy.at[0], peer_y)
    copies.send(pairs_half, pairs_y, rvy.at[1], peer_y)
    for part in range(4):
        total = terms_all[part, 8:16, :]
        for k in range(part + 4, count, 4):
            total = total + terms_all[k, 8:16, :]
        ff_out[part] = total
    copies.arrived(half_y, rvy.at[0], peer_y)
    owned[...] = half[...] + half_y[...]
    copies.arrived(pairs_y, rvy.at[1], peer_y)
    pairs_out[place.y] = pairs_half[...]
    pairs_out[1 - place.y] = pairs_y[...]
    for k in [place.ctx] + far_ctx:
        copies.arrived(grads_out.at[1 - place.y, k], rg.at[k], peer_y)
    outs.end()
    for k in others(group.ctx, 4):
        copies.arrived(fc_out.at[k], rfc.at[k], group.at_ctx(k))
        copies.arrived(proj_out.at[k], rproj.at[k], group.at_ctx(k))
    copies.finish()


def closing(part, grads, out_part, fc, proj, *vectors):
    block = part.shape[1:]
    n_ctx = grads.shape[1]
    n_z = n_ctx // 2
    piece = grads.shape[1:]
    rows, width = out_part.shape[1:]
    half = (rows, width // 2)
    return pl.pallas_call(
        closing_kernel,
        out_shape=(
            jax.ShapeDtypeStruct(block, F32),
            jax.ShapeDtypeStruct((2,) + piece, B16),
            jax.ShapeDtypeStruct((2,) + half, B16),
            jax.ShapeDtypeStruct(fc.shape, fc.dtype),
            jax.ShapeDtypeStruct(proj.shape, proj.dtype),
            jax.ShapeDtypeStruct((8, 128), F32),
            jax.ShapeDtypeStruct((2, n_ctx, 2, 128), F32),
            jax.ShapeDtypeStruct((4, 8, 128), F32),
        ),
        in_specs=[ANY] * 5 + [IN_VMEM] * 5,
        out_specs=(IN_VMEM, ANY, IN_VMEM, ANY, ANY, IN_VMEM, IN_VMEM, IN_VMEM),
        scratch_shapes=scatter_scratch(n_z, block)
        + [pltpu.VMEM(piece, B16), pltpu.VMEM(piece, B16)]
        + [pltpu.VMEM((n_z, rows, width), B16), pltpu.VMEM((n_z, rows, width), B16)]
        + [pltpu.VMEM((n_z,) + half, B16), pltpu.VMEM((n_z,) + half, B16)]
        + scatter_sems(n_z, 5 * n_ctx + 4 * n_z + 10)
        + dma_sems(n_ctx, n_ctx, n_ctx, n_ctx)
        + dma_sems(n_z, n_z, n_z, n_z, 2, 4, 4)
        + [pltpu.VMEM((2 * n_ctx, 16, 128), F32), pltpu.VMEM((2 * n_ctx, 16, 128), F32)]
        + [pltpu.VMEM((8, 128), F32), pltpu.VMEM((n_ctx, 2, 128), F32)]
        + [pltpu.VMEM((8, 128), F32), pltpu.VMEM((n_ctx, 2, 128), F32)]
        + dma_sems(2 * n_ctx, 2),
        compiler_params=comm_params(4),
        name="closing",
    )(part, grads, out_part, fc, proj, *vectors)


def laid_wide(value, count, rows, tall):
    zeros = jnp.zeros((value.shape[0], tall - rows), value.dtype)
    parts = []
    for k in range(count):
        parts += [value[:, k * rows : (k + 1) * rows], zeros]
    return jnp.concatenate(parts, axis=1)


def laid_tall(value, count, rows, tall):
    zeros = jnp.zeros((tall - rows, value.shape[1]), value.dtype)
    parts = []
    for k in range(count):
        parts += [value[k * rows : (k + 1) * rows], zeros]
    return jnp.concatenate(parts, axis=0)


def laid_short(value, count, rows, tall):
    return jnp.concatenate([value[k * tall : k * tall + rows] for k in range(count)], axis=0)


def laid_narrow(value, count, rows, tall):
    return jnp.concatenate([value[:, k * tall : k * tall + rows] for k in range(count)], axis=1)


def prepare_kernel(count, at_ref, x, grad, qkv, fc, proj, out_w, *refs):
    singles, qv, (x_out, grad_out, blocks, ffn, out_out) = refs[:6], refs[6], refs[7:]
    rows, feats = out_w.shape
    n_ctx, tall, cols = blocks.shape
    pair, ff = cols // 3, ffn.shape[3]
    x_out[...] = laid_tall(x[...].astype(F32), count, rows, tall).T.astype(B16)
    grad_out[...] = laid_tall(grad[...].astype(F32), count, rows, tall).T.astype(B16)
    below = jnp.zeros((tall - rows, feats), F32)
    out_out[...] = laid_wide(
        jnp.concatenate([out_w[...].astype(F32), below], axis=0), count, rows, tall
    ).astype(B16)
    below = jnp.zeros((tall - rows, ff), F32)
    for k in range(4):
        ffn[0, k] = jnp.concatenate([fc[:, k * ff : (k + 1) * ff].astype(F32), below], axis=0).astype(B16)
        ffn[1, k] = jnp.concatenate([proj[:, k * ff : (k + 1) * ff].astype(F32), below], axis=0).astype(B16)
    small = [jnp.concatenate([ref[...].astype(F32), jnp.zeros((1, cols - rows), F32)], axis=1) for ref in singles]
    small.append(jnp.concatenate([qv[...].astype(F32), jnp.zeros((1, cols - 2 * rows), F32)], axis=1))
    if tall - rows > 7:
        small.append(jnp.zeros((tall - rows - 7, cols), F32))
    small = jnp.concatenate(small, axis=0)
    first = at_ref[0] == 0
    whole = qkv[...].astype(F32)

    def columns(part, p):
        width = min(pair, feats - p * pair)
        if width <= 0:
            return jnp.zeros((rows, pair), F32)
        value = whole[:, part * feats + p * pair : part * feats + p * pair + width]
        if width < pair:
            value = jnp.concatenate([value, jnp.zeros((rows, pair - width), F32)], axis=1)
        return value

    for k in range(n_ctx):
        value = [jnp.where(first, columns(part, 2 * k), columns(part, 2 * k + 1)) for part in range(3)]
        blocks[k] = jnp.concatenate([jnp.concatenate(value, axis=1), small], axis=0).astype(B16)


def prepare(y_at, x, grad, qkv, fc, proj, out_w, singles, qv, n_ctx, tall, pair):
    rows, feats = out_w.shape
    count = feats // rows
    wide = count * tall
    tokens = x.shape[1]
    vmem = pl.BlockSpec(memory_space=pltpu.VMEM)
    return pl.pallas_call(
        functools.partial(prepare_kernel, count),
        in_specs=[pl.BlockSpec(memory_space=pltpu.SMEM)] + [vmem] * 13,
        out_shape=(
            jax.ShapeDtypeStruct((tokens, wide), B16),
            jax.ShapeDtypeStruct((tokens, wide), B16),
            jax.ShapeDtypeStruct((n_ctx, tall, 3 * pair), B16),
            jax.ShapeDtypeStruct((2, 4, tall, fc.shape[1] // 4), B16),
            jax.ShapeDtypeStruct((tall, wide), B16),
        ),
        compiler_params=pltpu.CompilerParams(vmem_limit_bytes=VMEM_LIMIT),
        name="prepare",
    )(y_at, x, grad, qkv, fc, proj, out_w, *[value[None] for value in singles], qv[None])


def project_kernel(
    rows, feats, at_ref, x_ref, packed_ref, mask_ref, w_ref, norm_ref, qkv_ref, single_ref, bias_s, held_s
):
    count, tall, cols = packed_ref.shape
    pair = cols // 3

    @pl.when(pl.program_id(0) == 0)
    def begin():
        held_s[...] = jnp.zeros_like(held_s)
        vectors = []
        for row in range(6):
            at = rows + row
            vectors.append(
                jnp.concatenate([packed_ref[k, at : at + 1, 0:tall].astype(F32) for k in range(count)], axis=1)
            )
        single_ref[...] = jnp.concatenate(vectors + [jnp.zeros((2, count * tall), F32)], axis=0)
        for part in range(2):
            blocks = range(part * count // 2, (part + 1) * count // 2)
            at = rows + 6
            held_s[part : part + 1, 0:feats] = jnp.concatenate(
                [packed_ref[k, at : at + 1, 0 : 2 * rows].astype(F32) for k in blocks], axis=1
            )
        own = pl.ds(pl.multiple_of(at_ref[0] * pair, pair), pair)
        bias_s[...] = jnp.concatenate([held_s[0:1, own], jnp.zeros((1, pair), F32), held_s[1:2, own]], axis=1)

    x = x_ref[...].astype(F32)
    mean = jnp.sum(x, axis=1, keepdims=True) * (1.0 / feats)
    centered = (x - mean) * mask_ref[...]
    inv = lax.rsqrt(jnp.sum(centered * centered, axis=1, keepdims=True) * (1.0 / feats) + NORM_EPS)
    norm = (centered * inv * single_ref[0:1, :] + single_ref[1:2, :]).astype(B16)
    norm_ref[...] = norm
    qkv_ref[...] = (dot(norm, w_ref[...], 1, 0) + bias_s[...]).astype(B16)


def project(slot_at, x, packed, mask, rows, feats, padded):
    total, wide = x.shape
    cols = packed.shape[2]
    step = min(256, total)

    def fixed(shape):
        return pl.BlockSpec(shape, lambda i: (0,) * len(shape))

    return pl.pallas_call(
        functools.partial(project_kernel, rows, feats),
        grid=(total // step,),
        in_specs=[pl.BlockSpec(memory_space=pltpu.SMEM), pl.BlockSpec((step, wide), lambda i: (i, 0))]
        + [fixed(packed.shape), fixed((1, wide)), fixed((wide, cols))],
        out_specs=(
            pl.BlockSpec((step, wide), lambda i: (i, 0)),
            pl.BlockSpec((step, cols), lambda i: (i, 0)),
            fixed((8, wide)),
        ),
        out_shape=(
            jax.ShapeDtypeStruct((total, wide), B16),
            jax.ShapeDtypeStruct((total, cols), B16),
            jax.ShapeDtypeStruct((8, wide), F32),
        ),
        scratch_shapes=[pltpu.VMEM((1, cols), F32), pltpu.VMEM((2, padded), F32)],
        compiler_params=pltpu.CompilerParams(vmem_limit_bytes=VMEM_LIMIT),
        name="project",
    )(slot_at, x, packed, mask[None], packed.reshape(wide, cols))


def project_back_kernel(feats, x_ref, grad_ref, mask_ref, w_ref, part_ref, gradb_ref, gain_ref, shift_ref, pair_ref):
    @pl.when(pl.program_id(0) == 0)
    def begin():
        gain_ref[...] = jnp.zeros_like(gain_ref)
        shift_ref[...] = jnp.zeros_like(shift_ref)
        pair_ref[...] = jnp.zeros_like(pair_ref)

    grad = grad_ref[...]
    pair_ref[...] += jnp.sum(grad, axis=0, keepdims=True)
    grad = grad.astype(B16)
    gradb_ref[...] = grad
    part = dot(grad, w_ref[...], 1, 1)
    part_ref[...] = part.astype(B16)
    x = x_ref[...].astype(F32)
    mean = jnp.sum(x, axis=1, keepdims=True) * (1.0 / feats)
    centered = (x - mean) * mask_ref[...]
    inv = lax.rsqrt(jnp.sum(centered * centered, axis=1, keepdims=True) * (1.0 / feats) + NORM_EPS)
    gain_ref[...] += jnp.sum(part * (centered * inv), axis=0, keepdims=True)
    shift_ref[...] += jnp.sum(part, axis=0, keepdims=True)


def project_back(x, grad, mask, weight, feats):
    total, wide = x.shape
    cols = weight.shape[1]
    step = min(256, total)

    def fixed(shape):
        return pl.BlockSpec(shape, lambda i: (0,) * len(shape))

    def moving(width):
        return pl.BlockSpec((step, width), lambda i: (i, 0))

    return pl.pallas_call(
        functools.partial(project_back_kernel, feats),
        grid=(total // step,),
        in_specs=[moving(wide), moving(cols), fixed((1, wide)), fixed((wide, cols))],
        out_specs=(moving(wide), moving(cols), fixed((1, wide)), fixed((1, wide)), fixed((1, cols))),
        out_shape=(
            jax.ShapeDtypeStruct((total, wide), B16),
            jax.ShapeDtypeStruct((total, cols), B16),
            jax.ShapeDtypeStruct((1, wide), F32),
            jax.ShapeDtypeStruct((1, wide), F32),
            jax.ShapeDtypeStruct((1, cols), F32),
        ),
        compiler_params=pltpu.CompilerParams(vmem_limit_bytes=VMEM_LIMIT),
        name="project_back",
    )(x, grad, mask[None], weight)


def deliver_kernel(
    rows, feats, qkv, out_w, fc, proj, mlp, hidden, dnorm, dhidden, x_ref, single, mask,
    qkv_out, out_out, fc_out, proj_out, block_out, grad_out,
):
    n_y, n_ctx, tall, cols = qkv.shape
    pair, ff, count = cols // 3, fc.shape[2], feats // rows
    parts = []
    for part in range(3):
        for p in range(-(-feats // pair)):
            width = min(pair, feats - p * pair)
            parts.append(qkv[p % n_y, p // n_y, :, part * pair : part * pair + width].astype(F32))
    qkv_out[...] = jnp.concatenate(parts, axis=1)[:rows]
    halves = jnp.concatenate([out_w[y].astype(F32) for y in range(2)], axis=1)
    out_out[...] = laid_narrow(halves, count, rows, tall)[:rows]
    fc_out[...] = jnp.concatenate([fc[k].astype(F32) for k in range(4)], axis=1)[:rows]
    for k in range(4):
        proj_out[:, k * ff : (k + 1) * ff] = proj[k].astype(F32)[:rows]
    block = hidden[...] + mlp[...].astype(F32) + single[5:6, :]
    block_out[...] = laid_short(block.T, count, rows, tall)
    normed, inv = norm_forward(x_ref[...].astype(F32), mask[...], feats)
    grad = dhidden[...] + norm_backward(dnorm[...], normed, inv, single[0:1, :], feats)
    grad_out[...] = laid_short(grad.T, count, rows, tall)


def deliver(qkv, out_w, fc, proj, mlp, hidden, dnorm, dhidden, x, single, mask, rows, feats):
    tokens, ff = x.shape[0], fc.shape[2]
    return pl.pallas_call(
        functools.partial(deliver_kernel, rows, feats),
        out_shape=(
            jax.ShapeDtypeStruct((rows, 3 * feats), F32),
            jax.ShapeDtypeStruct((rows, feats), F32),
            jax.ShapeDtypeStruct((rows, 4 * ff), F32),
            jax.ShapeDtypeStruct((rows, 4 * ff), F32),
            jax.ShapeDtypeStruct((feats, tokens), F32),
            jax.ShapeDtypeStruct((feats, tokens), F32),
        ),
        compiler_params=pltpu.CompilerParams(vmem_limit_bytes=VMEM_LIMIT),
        name="deliver",
    )(qkv, out_w, fc, proj, mlp, hidden, dnorm, dhidden, x, single, mask[None])


def hidden_kernel(rows, feats, att, w_out, x_ref, single, mask, by_core, hidden_out, norm_out):
    half = w_out.shape[2]
    count = feats // rows
    tall = 2 * half // count
    value = att[...].astype(F32)
    zeros = jnp.zeros((value.shape[0], tall - rows), F32)
    parts = []
    for core in range(2):
        blocks = []
        for k in range(core, count, 2):
            blocks += [value[:, k * rows : (k + 1) * rows], zeros]
        parts.append(jnp.concatenate(blocks, axis=1).astype(B16))
        by_core[core] = parts[core]
    hidden = [dot(parts[0], w_out[0, y], 1, 0) + dot(parts[1], w_out[1, y], 1, 0) for y in range(2)]
    hidden = x_ref[...].astype(F32) + jnp.concatenate(hidden, axis=1) + single[2:3, :]
    hidden_out[...] = hidden
    normed, unused = norm_forward(hidden, mask[...], feats)
    norm_out[...] = (normed * single[3:4, :] + single[4:5, :]).astype(B16)


def hidden_forward(att, w_out, x, single, mask, rows, feats):
    tokens, wide = x.shape
    return pl.pallas_call(
        functools.partial(hidden_kernel, rows, feats),
        out_shape=(
            jax.ShapeDtypeStruct((2, tokens, wide // 2), B16),
            jax.ShapeDtypeStruct((tokens, wide), F32),
            jax.ShapeDtypeStruct((tokens, wide), B16),
        ),
        compiler_params=pltpu.CompilerParams(vmem_limit_bytes=VMEM_LIMIT),
        name="hidden_forward",
    )(att, w_out, x, single, mask[None])


def hidden_back_kernel(
    rows, feats, dnorm_ref, hidden, grad_ref, w_out, single, mask, dhidden_out, dhidden_b, sums, datt_out
):
    half = w_out.shape[2]
    count = feats // rows
    tall = 2 * half // count
    dnorm = dnorm_ref[...]
    grad = grad_ref[...].astype(F32)
    normed, inv = norm_forward(hidden[...], mask[...], feats)
    dhidden = grad + norm_backward(dnorm, normed, inv, single[3:4, :], feats)
    dhidden_out[...] = dhidden
    rounded = dhidden.astype(B16)
    dhidden_b[...] = rounded
    sums[0:1, :] = jnp.sum(dhidden, axis=0, keepdims=True)
    sums[1:2, :] = jnp.sum(dnorm * normed, axis=0, keepdims=True)
    sums[2:3, :] = jnp.sum(dnorm, axis=0, keepdims=True)
    sums[3:4, :] = jnp.sum(grad, axis=0, keepdims=True)
    grads = [rounded[:, :half], rounded[:, half:]]
    datt = [dot(grads[0], w_out[c, 0], 1, 1) + dot(grads[1], w_out[c, 1], 1, 1) for c in range(2)]
    parts = [datt[k % 2][:, k // 2 * tall : k // 2 * tall + rows] for k in range(count)]
    if datt_out.shape[1] > feats:
        parts.append(jnp.zeros((dnorm.shape[0], datt_out.shape[1] - feats), F32))
    datt_out[...] = jnp.concatenate(parts, axis=1).astype(B16)


def hidden_back(dnorm, hidden, grad, w_out, single, mask, rows, feats, padded):
    tokens, wide = hidden.shape
    return pl.pallas_call(
        functools.partial(hidden_back_kernel, rows, feats),
        out_shape=(
            jax.ShapeDtypeStruct((tokens, wide), F32),
            jax.ShapeDtypeStruct((tokens, wide), B16),
            jax.ShapeDtypeStruct((4, wide), F32),
            jax.ShapeDtypeStruct((tokens, padded), B16),
        ),
        compiler_params=pltpu.CompilerParams(vmem_limit_bytes=VMEM_LIMIT),
        name="hidden_back",
    )(dnorm, hidden, grad, w_out, single, mask[None])


def load_pieces(at_ref, pieces, whole, sems, first=0):
    rows = whole.shape[0] // len(pieces)
    copies = []
    for i, piece in enumerate(pieces):
        to = whole.at[pl.ds(pl.multiple_of(at_ref[i], 16), rows), :]
        copies.append(pltpu.make_async_copy(piece, to, sems.at[first + i]))
    for copy in copies:
        copy.start()
    return copies


def as_pieces(pairs, refs, which):
    return [ref.at[which] for ref in refs[:pairs]] + list(refs[pairs:])


def feed_up_kernel(pairs, count, at_ref, *refs):
    pieces, (norm_ref, bias_ref, act_ref, slope_ref, w_fc, sems) = refs[:count], refs[count:]

    @pl.when(pl.program_id(0) == 0)
    def begin():
        for copy in load_pieces(at_ref, as_pieces(pairs, pieces, 0), w_fc, sems):
            copy.wait()

    activated, slope = gelu_parts(dot(norm_ref[...], w_fc[...], 1, 0) + bias_ref[...])
    act_ref[...] = activated.astype(B16)
    slope_ref[...] = slope


FEED_STEP = 256


def feed_up(pairs, fcs, places, norm, bias):
    pieces = pairs + fcs
    total, wide = norm.shape
    ff = bias.shape[0]
    hidden = pl.BlockSpec((FEED_STEP, ff), lambda i: (i, 0))
    return pl.pallas_call(
        functools.partial(feed_up_kernel, len(pairs), len(pieces)),
        grid=(total // FEED_STEP,),
        in_specs=[pl.BlockSpec(memory_space=pltpu.SMEM)]
        + [ANY] * len(pieces)
        + [pl.BlockSpec((FEED_STEP, wide), lambda i: (i, 0)), pl.BlockSpec((1, ff), lambda i: (0, 0))],
        out_specs=(hidden, hidden),
        out_shape=(jax.ShapeDtypeStruct((total, ff), B16), jax.ShapeDtypeStruct((total, ff), F32)),
        scratch_shapes=[pltpu.VMEM((wide, ff), B16)] + dma_sems(len(pieces)),
        compiler_params=pltpu.CompilerParams(vmem_limit_bytes=VMEM_LIMIT),
        name="feed_up",
    )(places, *pieces, norm, bias[None])


def feed_down_kernel(pairs, singles, at_ref, *refs):
    count = pairs + 2 * singles
    pieces, refs = refs[:count], refs[count:]
    grad_ref, act_ref, slope_ref, dpre_ref, dnorm_ref, mlp_ref, sum_ref, w_fc, w_proj, sems = refs

    @pl.when(pl.program_id(0) == 0)
    def begin():
        fcs = as_pieces(pairs, pieces[: pairs + singles], 0)
        projs = as_pieces(pairs, pieces[:pairs] + pieces[pairs + singles :], 1)
        copies = load_pieces(at_ref, projs, w_proj, sems)
        copies += load_pieces(at_ref, fcs, w_fc, sems, pairs + singles)
        for copy in copies:
            copy.wait()
        sum_ref[...] = jnp.zeros_like(sum_ref)

    dpre = dot(grad_ref[...], w_proj[...], 1, 0) * slope_ref[...]
    sum_ref[...] += jnp.sum(dpre, axis=0, keepdims=True)
    dpre_b = dpre.astype(B16)
    dpre_ref[...] = dpre_b
    dnorm_ref[...] = dot(dpre_b, w_fc[...], 1, 1).astype(B16)
    mlp_ref[...] = dot(act_ref[...], w_proj[...], 1, 1).astype(B16)


def feed_down(pairs, fcs, projs, places, grad, act, slope):
    pieces = pairs + fcs + projs
    total, wide = grad.shape
    ff = act.shape[1]
    tokens = pl.BlockSpec((FEED_STEP, wide), lambda i: (i, 0))
    hidden = pl.BlockSpec((FEED_STEP, ff), lambda i: (i, 0))
    single = pl.BlockSpec((1, ff), lambda i: (0, 0))
    return pl.pallas_call(
        functools.partial(feed_down_kernel, len(pairs), len(fcs)),
        grid=(total // FEED_STEP,),
        in_specs=[pl.BlockSpec(memory_space=pltpu.SMEM)] + [ANY] * len(pieces) + [tokens, hidden, hidden],
        out_specs=(hidden, tokens, tokens, single),
        out_shape=(
            jax.ShapeDtypeStruct((total, ff), B16),
            jax.ShapeDtypeStruct((total, wide), B16),
            jax.ShapeDtypeStruct((total, wide), B16),
            jax.ShapeDtypeStruct((1, ff), F32),
        ),
        scratch_shapes=[pltpu.VMEM((wide, ff), B16), pltpu.VMEM((wide, ff), B16)]
        + dma_sems(2 * (len(pairs) + len(fcs))),
        compiler_params=pltpu.CompilerParams(vmem_limit_bytes=VMEM_LIMIT),
        name="feed_down",
    )(places, *pieces, grad, act, slope)


def after(value, other, unpack=False):
    value, other = lax.optimization_barrier((value, other))
    return (*value, other) if unpack else (value, other)


def shift_perm(count, step):
    return [(i, (i + step) % count) for i in range(count)]


def on_device(
    sizes, block_input, segment_ids, slot_order, first_gain, first_shift, qkv_weight, qv_bias, out_weight, out_bias,
    second_gain, second_shift, fc_weight, fc_bias, proj_weight, proj_bias, out_grad,
):
    n_x, n_ctx, n_y = sizes
    n_slot = n_ctx * n_y
    n_shard = n_x * n_ctx
    n_h = n_ctx // 4
    slot_len, feats = block_input.shape[1:]
    head = feats // HEADS
    pair = 2 * head
    rows = qkv_weight.shape[0]
    ff_own = fc_weight.shape[1] // 4
    padded = n_slot * pair
    y_at = lax.axis_index("y")
    ctx_at = lax.axis_index(CTX)
    slot_at = lax.axis_index(ROW)
    lc_at = lax.axis_index(("l", "c"))
    x_at, h_at = lax.axis_index("x"), lax.axis_index("h")

    def gather(value, axes):
        return lax.all_gather(value, axes, axis=0, tiled=True)

    tall = rows + (-rows % 16)
    wide = n_shard * tall
    row_pad = tall - rows

    mask = jnp.asarray((np.arange(wide) % tall < rows).astype(np.float32))

    singles = (first_gain, first_shift, out_bias, second_gain, second_shift, proj_bias)
    own_input, grad_own, packed, ffn_blocks, w_out = prepare(
        y_at.astype(jnp.int32)[None], block_input[0].T, out_grad[0].T, qkv_weight, fc_weight, proj_weight.T, out_weight,
        singles, qv_bias, n_ctx, tall, pair,
    )
    all_input, packed, ffn_blocks, w_out = opening(
        own_input, packed, ffn_blocks, w_out
    )
    ffn_blocks = ffn_blocks.reshape(2, 4 * tall, ff_own)
    fc_h = [lax.ppermute(ffn_blocks[0], "h", shift_perm(n_h, step)) for step in range(1, n_h)]
    along_x = lax.ppermute(ffn_blocks, "x", shift_perm(n_x, 1))
    grad_late, all_input = after(grad_own, all_input)
    grad_all = gather(grad_late, FFG)
    w_out = lax.all_gather(w_out.reshape(wide // 2, wide // 2), ("c", "y"), axis=0, tiled=False)
    w_out = w_out.reshape(2, n_y, wide // 2, wide // 2)
    packed = packed.reshape(n_shard, tall, 3 * pair)
    w_qkv = packed.reshape(wide, 3 * pair)
    b_fc = lax.dynamic_slice_in_dim(fc_bias, lc_at * ff_own, ff_own, 0).astype(F32)

    order = slot_order[0]
    pieces = jnp.arange(n_slot, dtype=jnp.int32)
    inv = jnp.sum(jnp.where(order[None, :] == pieces[:, None], pieces[None, :], 0), axis=1).astype(jnp.int32)
    segs = jnp.take(segment_ids[0].reshape(n_slot, slot_len), inv, axis=0).reshape(-1)
    docs = jnp.arange(DOCS, dtype=jnp.int32)
    counts = jnp.sum((segs[None, :] == docs[:, None]).astype(jnp.int32), axis=1)
    starts = jnp.sum(jnp.where(segs[None, :] > docs[:, None], counts[:, None], 0), axis=0).astype(jnp.int32)
    start3 = starts.reshape(-1, 1, BLK)
    low = start3[:, 0, 0] // BLK

    all_input = all_input.reshape(n_slot * slot_len, wide)
    norm_one, qkv, singles = project(
        slot_at.astype(jnp.int32)[None], all_input, packed, mask, rows, feats, padded
    )
    heads_out, lse = attend(inv, low, qkv, start3, slot_len, head)
    fc_h, proj_late, heads_out = after((fc_h, ffn_blocks[1]), heads_out, True)
    fc_xh = [lax.ppermute(value, "x", shift_perm(n_x, 1)) for value in fc_h]
    proj_h = [lax.ppermute(proj_late, "h", shift_perm(n_h, step)) for step in range(1, n_h)]
    by_core, hidden, norm_two = hidden_forward(
        to_tokens(heads_out.reshape(n_slot, slot_len, pair)), w_out, own_input, singles, mask, rows, feats
    )
    proj_h, norm_two = after(proj_h, norm_two)
    proj_xh = [lax.ppermute(value, "x", shift_perm(n_x, 1)) for value in proj_h]
    norm_all = group_gather(norm_two, 6).reshape(-1, wide)
    places = [(x_at, h_at), (1 - x_at, h_at)]
    for step in range(1, n_h):
        h_from = lax.rem(h_at + n_h - step, n_h)
        places += [(x_at, h_from), (1 - x_at, h_from)]

    def mixed(one, two):
        return [value for both in zip(one, two) for value in both]

    places = jnp.stack([(x * n_h + h) * (4 * tall) for x, h in places]).astype(jnp.int32)
    pairs, fcs, projs = [ffn_blocks, along_x], mixed(fc_h, fc_xh), mixed(proj_h, proj_xh)
    activation, slope = feed_up(pairs, fcs, places, norm_all, b_fc)

    def pick(value, at):
        return lax.dynamic_index_in_dim(value, at, 0, False)

    def by_owner(value):
        value = with_layout_constraint(value.astype(B16), Layout(major_to_minor=(0, 1)))
        return value.reshape(n_x, n_h, 4 * tall, ff_own)

    proj_part = by_owner(dot(grad_all, activation, 0, 0))
    proj_give = pick(proj_part, 1 - x_at)
    proj_give, activation = after(proj_give, activation)
    proj_x = lax.ppermute(proj_give, "x", shift_perm(n_x, 1))
    dpreact_b, dnorm_part, mlp_part, dpreact_sum = feed_down(pairs, fcs, projs, places, grad_all, activation, slope)

    fc_part = by_owner(dot(norm_all, dpreact_b, 0, 0))
    fc_x = lax.ppermute(pick(fc_part, 1 - x_at), "x", shift_perm(n_x, 1))
    fc_part, dnorm_part = after(fc_part, dnorm_part)
    dnorm_two = group_scatter(dnorm_part.reshape(8, slot_len, wide), 7)

    def over_h(value):
        gives = [pick(value, lax.rem(h_at + step, n_h)) for step in range(1, n_h)]
        return [lax.ppermute(give, "h", shift_perm(n_h, step + 1)) for step, give in enumerate(gives)]

    def total(value, received):
        value = pick(value, h_at).astype(F32)
        for other in received:
            value = value + other
        return value.astype(B16).reshape(4, tall, ff_own)

    proj_x, mlp_part, dnorm_two = after((proj_x, mlp_part), dnorm_two, True)
    proj_line = pick(proj_part, x_at) + proj_x
    proj_h = over_h(proj_line)
    mlp = lax.psum_scatter(mlp_part, FFG, scatter_dimension=0, tiled=True)
    dhidden, dhidden_b, token_sums, dattention = hidden_back(
        dnorm_two, hidden, grad_own, w_out, singles, mask, rows, feats, padded
    )
    c_at = lax.axis_index("c")
    out_give = dot(jnp.where(c_at == 0, by_core[1], by_core[0]), dhidden_b, 0, 0).astype(B16)
    out_give = lax.ppermute(out_give, "c", shift_perm(2, 1))
    out_keep = dot(jnp.where(c_at == 0, by_core[0], by_core[1]), dhidden_b, 0, 0).astype(B16)
    dattention = to_heads(dattention, n_slot).reshape(n_slot * slot_len, pair)
    out_give, fc_x, dattention = after((out_give, fc_x), dattention, True)
    out_part = (out_keep + out_give).reshape(n_shard // 2, tall, wide)
    fc_line = pick(fc_part, x_at) + fc_x
    fc_h = over_h(fc_line)
    dqkv = attend_back(inv, low, qkv, heads_out, dattention, lse, start3, slot_len, head)
    dnorm_one_part, dqkv_b, gain_sum, shift_sum, pair_sum = project_back(all_input, dqkv, mask, w_qkv, feats)
    qkv_part = dot(norm_one, dqkv_b, 0, 0).astype(B16).reshape(n_x, n_ctx, tall, 3 * pair)
    proj_h, fc_h, dnorm_one_part = after((proj_h, fc_h), dnorm_one_part, True)
    dnorm_one, qkv_all, out_all, fc_all, proj_all, owned, pair_sums, ff_sums = closing(
        dnorm_one_part.reshape(n_slot, slot_len, wide), qkv_part, out_part, total(fc_line, fc_h), total(proj_line, proj_h),
        token_sums, gain_sum, shift_sum, pair_sum, dpreact_sum,
    )
    mlp, dnorm_one = after(mlp, dnorm_one)
    qkv_grad, out_grad_w, fc_grad, proj_grad, block_output, input_grad = deliver(
        qkv_all, out_all, fc_all, proj_all, mlp, hidden, dnorm_one, dhidden, own_input, singles, mask, rows, feats
    )
    fc_bias_grad = ff_sums.reshape(4, 1024)[:, :ff_own].reshape(4 * ff_own)
    pair_sums = pair_sums.transpose(2, 1, 0, 3).reshape(2, padded)[:, :feats].reshape(2 * feats)
    qv_grad = lax.dynamic_slice_in_dim(pair_sums, lax.axis_index(SHARD) * 2 * rows, 2 * rows, 0)

    def own(index):
        return owned[index, :rows]

    return (
        block_output.T[None],
        input_grad.T[None],
        qkv_grad,
        qv_grad,
        out_grad_w,
        own(0),
        own(4),
        own(5),
        own(1),
        own(2),
        fc_grad,
        fc_bias_grad,
        proj_grad.T,
        own(3),
    )


def solution(mesh):
    n_x, n_ctx, n_y = (mesh.shape[axis] for axis in ("dp", "context", "tensor"))
    inner = Mesh(mesh.devices.reshape(n_x, n_ctx // 4, 2, 2, n_y), ("x", "h", "l", "c", "y"))
    tokens = P("x", ROW, None)
    shard = P(SHARD)
    shard_rows = P(SHARD, None)
    return jax.shard_map(
        functools.partial(on_device, (n_x, n_ctx, n_y)),
        mesh=inner,
        in_specs=(
            tokens, P("x", None), P("x", None), shard, shard, shard_rows, shard, shard_rows, shard, shard, shard,
            P(SHARD, "y"), P("y"), P("y", SHARD), shard, tokens,
        ),
        out_specs=(
            tokens, tokens, shard_rows, shard, shard_rows, shard, shard, shard, shard, shard,
            P(SHARD, "y"), P("y"), P("y", SHARD), shard,
        ),
        check_vma=False,
    )
```

```python
import functools
import math

import jax
import jax.numpy as jnp
import numpy as np
from jax import lax
from jax.experimental import pallas as pl
from jax.experimental.layout import Layout, with_layout_constraint
from jax.experimental.pallas import tpu as pltpu
from jax.sharding import Mesh
from jax.sharding import PartitionSpec as P

HEADS = 25
DOCS = 8
NORM_EPS = 1e-05
GELU_SCALE = 0.7978845608028654
GELU_CUBE = 0.044715
MASK_FLOOR = -1e30

F32 = jnp.float32
B16 = jnp.bfloat16
BLK = 256
VMEM_LIMIT = 60 * 1024 * 1024

ROW = ("h", "l", "c", "y")
CTX = ("h", "l", "c")
SHARD = ("x", "h", "l", "c")
FFG = ("l", "c", "y")


def gelu_parts(values):
    inner_arg = GELU_SCALE * (values + GELU_CUBE * values * values * values)
    tanh_value = jnp.tanh(inner_arg)
    result = 0.5 * values * (1.0 + tanh_value)
    derivative = 0.5 * (1.0 + tanh_value) + 0.5 * values * (
        1.0 - tanh_value * tanh_value
    ) * GELU_SCALE * (1.0 + 3.0 * GELU_CUBE * values * values)
    return (result, derivative)


def norm_forward(values, mask, feats):
    mean_value = jnp.sum(values, axis=-1, keepdims=True) / feats
    centered = (values - mean_value) * mask
    inv_sigma = lax.rsqrt(jnp.sum(centered * centered, axis=-1, keepdims=True) / feats + NORM_EPS)
    return (centered * inv_sigma, inv_sigma)


def norm_backward(upstream, normed, inv_sigma, norm_gain, feats):
    scaled = upstream * norm_gain
    return inv_sigma * (
        scaled
        - jnp.sum(scaled, axis=-1, keepdims=True) / feats
        - normed * (jnp.sum(scaled * normed, axis=-1, keepdims=True) / feats)
    )


def dot(left, right, left_dim, right_dim):
    return lax.dot_general(
        left, right, (((left_dim,), (right_dim,)), ((), ())), preferred_element_type=F32
    )


def sort_slots(inv_ref, src_ref, dst_ref, slot_len, start=0, width=None, factor=None):
    width = src_ref.shape[1] if width is None else width

    def body(piece, carry):
        slot = inv_ref[piece]
        rows = src_ref[pl.ds(pl.multiple_of(slot * slot_len, slot_len), slot_len), start : start + width]
        if factor is not None:
            rows = rows * jnp.asarray(factor, rows.dtype)
        dst_ref[pl.ds(pl.multiple_of(piece * slot_len, slot_len), slot_len), :] = rows
        return carry

    lax.fori_loop(0, src_ref.shape[0] // slot_len, body, 0)


def unsort_block(inv_ref, dst_ref, value, block, slot_len):
    for part in range(BLK // slot_len):
        slot = inv_ref[block * (BLK // slot_len) + part]
        dst_ref[pl.ds(pl.multiple_of(slot * slot_len, slot_len), slot_len), :] = value[
            part * slot_len : (part + 1) * slot_len
        ].astype(dst_ref.dtype)


def block_rows(block):
    return pl.ds(pl.multiple_of(block * BLK, BLK), BLK)


def mask_of(start_row, first, query_block, diagonal):
    key_at = first * BLK + lax.broadcasted_iota(jnp.int32, (2 * BLK, BLK), 0)
    allowed = key_at >= start_row
    if diagonal:
        query_at = query_block * BLK + lax.broadcasted_iota(jnp.int32, (2 * BLK, BLK), 1)
        allowed = jnp.logical_and(allowed, key_at <= query_at)
    return allowed


def two_rows(first):
    return block_rows(jnp.maximum(first, 0)), block_rows(first + 1)


def over_pairs(low, block, step, state):
    earlier = (block - low) // 2
    state = lax.fori_loop(0, earlier, lambda t, s: step(block - 1 - 2 * (earlier - t), s, False), state)
    return step(block - 1, state, True)


def attend_kernel(slot_len, head, inv_ref, low_ref, qkv_ref, start_ref, out_ref, lse_ref, q_s, k_s, vt_s):
    total = qkv_ref.shape[0]
    pair = 2 * head
    sort_slots(inv_ref, qkv_ref, q_s, slot_len, 0, pair, 1.0 / math.sqrt(head))
    sort_slots(inv_ref, qkv_ref, k_s, slot_len, pair, pair)

    def fill(piece, carry):
        slot = inv_ref[piece]
        rows = qkv_ref[pl.ds(pl.multiple_of(slot * slot_len, slot_len), slot_len), 2 * pair :]
        vt_s[:, pl.ds(pl.multiple_of(piece * slot_len, slot_len), slot_len)] = rows.astype(F32).T.astype(B16)
        return carry

    lax.fori_loop(0, total // slot_len, fill, 0)

    def per_query(block, carry):
        queries = q_s[block_rows(block), :]
        start_row = start_ref[block]

        def step(first, state, diagonal):
            allowed = mask_of(start_row, first, block, diagonal)
            rows = two_rows(first)
            keys = jnp.concatenate([k_s[r, :] for r in rows], axis=0)
            values = jnp.concatenate([vt_s[:, r] for r in rows], axis=1)
            fresh = []
            for part in range(2):
                old_max, old_sum, old_acc = state[part]
                cols = slice(part * head, (part + 1) * head)
                scores = dot(keys[:, cols], queries[:, cols], 1, 1)
                scores = jnp.where(allowed, scores, MASK_FLOOR)
                new_max = jnp.maximum(old_max, jnp.max(scores, axis=0, keepdims=True))
                weights = jnp.where(allowed, jnp.exp(scores - new_max), 0.0)
                shrink = jnp.exp(old_max - new_max)
                new_sum = old_sum * shrink + jnp.sum(weights, axis=0, keepdims=True)
                new_acc = old_acc * shrink + dot(values[cols, :], weights.astype(B16), 1, 0)
                fresh.append((new_max, new_sum, new_acc))
            return tuple(fresh)

        first = tuple(
            (
                jnp.full((1, BLK), MASK_FLOOR, F32),
                jnp.zeros((1, BLK), F32),
                jnp.zeros((head, BLK), F32),
            )
            for part in range(2)
        )
        state = over_pairs(low_ref[block], block, step, first)
        lse_ref[block] = jnp.concatenate([s[0] + jnp.log(s[1]) for s in state], axis=0)
        result = jnp.concatenate([s[2] / s[1] for s in state], axis=0)
        unsort_block(inv_ref, out_ref, result.T, block, slot_len)
        return carry

    lax.fori_loop(0, total // BLK, per_query, 0)


def attend(inv, low, qkv, start3, slot_len, head):
    total = qkv.shape[0]
    vmem = pl.BlockSpec(memory_space=pltpu.VMEM)
    smem = pl.BlockSpec(memory_space=pltpu.SMEM)
    return pl.pallas_call(
        functools.partial(attend_kernel, slot_len, head),
        out_shape=(
            jax.ShapeDtypeStruct((total, 2 * head), B16),
            jax.ShapeDtypeStruct((total // BLK, 2, BLK), F32),
        ),
        in_specs=[smem, smem, vmem, vmem],
        out_specs=(vmem, vmem),
        scratch_shapes=[
            pltpu.VMEM((total, 2 * head), B16),
            pltpu.VMEM((total, 2 * head), B16),
            pltpu.VMEM((2 * head, total), B16),
        ],
        compiler_params=pltpu.CompilerParams(vmem_limit_bytes=VMEM_LIMIT),
        name="attend",
    )(inv, low, qkv, start3)


def attend_back_kernel(
    slot_len, head, inv_ref, low_ref, qkv_ref, out_ref, grad_ref, lse_ref, start_ref,
    dqkv_ref, q_s, k_s, v_s, kt_s, o_s, g_s, dk_s, dv_s,
):
    total = qkv_ref.shape[0]
    pair = 2 * head
    scale = 1.0 / math.sqrt(head)
    sort_slots(inv_ref, qkv_ref, q_s, slot_len, 0, pair, scale)
    sort_slots(inv_ref, qkv_ref, k_s, slot_len, pair, pair)
    sort_slots(inv_ref, qkv_ref, v_s, slot_len, 2 * pair, pair)
    sort_slots(inv_ref, out_ref, o_s, slot_len)
    sort_slots(inv_ref, grad_ref, g_s, slot_len)

    def fill(block, carry):
        kt_s[:, block_rows(block)] = k_s[block_rows(block), :].astype(F32).T.astype(B16)
        return carry

    lax.fori_loop(0, total // BLK, fill, 0)
    dk_s[...] = jnp.zeros_like(dk_s)
    dv_s[...] = jnp.zeros_like(dv_s)

    def per_query(block, carry):
        queries = q_s[block_rows(block), :]
        grads = g_s[block_rows(block), :]
        start_row = start_ref[block]
        lse = lse_ref[block]
        prod = (grads.astype(F32) * o_s[block_rows(block), :].astype(F32)).T
        delta = [jnp.sum(prod[part * head : (part + 1) * head], axis=0, keepdims=True) for part in range(2)]

        def step(first, state, diagonal):
            allowed = mask_of(start_row, first, block, diagonal)
            rows = two_rows(first)
            keys = jnp.concatenate([k_s[r, :] for r in rows], axis=0)
            values = jnp.concatenate([v_s[r, :] for r in rows], axis=0)
            flipped = jnp.concatenate([kt_s[:, r] for r in rows], axis=1)
            fresh, dks, dvs = [], [], []
            for part in range(2):
                cols = slice(part * head, (part + 1) * head)
                scores = dot(keys[:, cols], queries[:, cols], 1, 1)
                weights = jnp.where(allowed, jnp.exp(scores - lse[part : part + 1]), 0.0)
                dprob = dot(values[:, cols], grads[:, cols], 1, 1)
                dscore = (weights * (dprob - delta[part])).astype(B16)
                dvs.append(dot(weights.astype(B16), grads[:, cols], 1, 0))
                dks.append(dot(dscore, queries[:, cols], 1, 0))
                fresh.append(state[part] + dot(flipped[cols, :], dscore, 1, 0))
            dk, dv = jnp.concatenate(dks, axis=1), jnp.concatenate(dvs, axis=1)
            for i, r in enumerate(rows):
                dk_s[r, :] += dk[i * BLK : (i + 1) * BLK]
                dv_s[r, :] += dv[i * BLK : (i + 1) * BLK]
            return tuple(fresh)

        state = (jnp.zeros((head, BLK), F32), jnp.zeros((head, BLK), F32))
        state = over_pairs(low_ref[block], block, step, state)
        dq = jnp.concatenate(state, axis=0).T * scale
        for part in range(BLK // slot_len):
            slot = inv_ref[block * (BLK // slot_len) + part]
            dqkv_ref[pl.ds(pl.multiple_of(slot * slot_len, slot_len), slot_len), 0:pair] = dq[
                part * slot_len : (part + 1) * slot_len
            ]
        return carry

    lax.fori_loop(0, total // BLK, per_query, 0)

    def give(piece, carry):
        slot = inv_ref[piece]
        rows = pl.ds(pl.multiple_of(slot * slot_len, slot_len), slot_len)
        held = pl.ds(pl.multiple_of(piece * slot_len, slot_len), slot_len)
        dqkv_ref[rows, pair : 2 * pair] = dk_s[held, :]
        dqkv_ref[rows, 2 * pair :] = dv_s[held, :]
        return carry

    lax.fori_loop(0, total // slot_len, give, 0)


def attend_back(inv, low, qkv, out, grad, lse, start3, slot_len, head):
    total = qkv.shape[0]
    pair = 2 * head
    vmem = pl.BlockSpec(memory_space=pltpu.VMEM)
    smem = pl.BlockSpec(memory_space=pltpu.SMEM)
    held = pltpu.VMEM((total, pair), B16)
    return pl.pallas_call(
        functools.partial(attend_back_kernel, slot_len, head),
        out_shape=jax.ShapeDtypeStruct((total, 3 * pair), F32),
        in_specs=[smem, smem] + [vmem] * 5,
        out_specs=vmem,
        scratch_shapes=[
            held, held, held, pltpu.VMEM((pair, total), B16), held, held,
            pltpu.VMEM((total, pair), F32), pltpu.VMEM((total, pair), F32),
        ],
        compiler_params=pltpu.CompilerParams(vmem_limit_bytes=VMEM_LIMIT),
        name="attend_back",
    )(inv, low, qkv, out, grad, lse, start3)


class Place:
    def __init__(self, whole_line):
        self.x, self.h, self.l, self.c, self.y = (lax.axis_index(a) for a in ("x", "h", "l", "c", "y"))
        self.whole_line = whole_line
        self.n_z = 2 * lax.axis_size("h") if whole_line else 2
        self.z = self.h * 2 + self.l if whole_line else self.l
        self.ctx = self.z * 2 + self.c
        self.slot = self.ctx * 2 + self.y

    def at_z(self, z):
        return {"h": z // 2, "l": lax.rem(z, 2)} if self.whole_line else {"l": z}

    def at_ctx(self, k):
        return dict(self.at_z(k // 2), c=lax.rem(k, 2))

    def at_slot(self, s):
        return dict(self.at_ctx(s // 2), y=lax.rem(s, 2))

    def far_z(self):
        order = []
        for step in range(1, self.n_z // 2 + 1):
            order += [step] if 2 * step == self.n_z else [step, self.n_z - step]
        return [lax.rem(self.z + step, self.n_z) for step in order]

    def slot_of(self, z, c, y):
        return (z * 2 + c) * 2 + y


class Copies:
    def __init__(self, sems):
        self.sems = sems
        self.begun = []

    def send(self, src, dst, recv, peer, when=None):
        at = len(self.begun)
        copy = pltpu.make_async_remote_copy(
            src_ref=src,
            dst_ref=dst,
            send_sem=self.sems.at[at],
            recv_sem=recv,
            device_id=peer,
            device_id_type=pl.DeviceIdType.MESH,
        )
        if when is None:
            copy.start()
            self.begun.append(copy.wait_send)
        else:
            pl.when(when)(copy.start)
            self.begun.append(lambda: pl.when(when)(copy.wait_send))

    def local(self, src, dst, sem=None):
        copy = pltpu.make_async_copy(src, dst, self.sems.at[len(self.begun)] if sem is None else sem)
        copy.start()
        if sem is None:
            self.begun.append(copy.wait)
        return copy

    def arrived(self, dst, recv, peer):
        pltpu.make_async_remote_copy(
            src_ref=dst,
            dst_ref=dst,
            send_sem=self.sems.at[0],
            recv_sem=recv,
            device_id=peer,
            device_id_type=pl.DeviceIdType.MESH,
        ).wait_recv()

    def finish(self):
        for wait in self.begun:
            wait()


def meet(peers):
    barrier = pltpu.get_barrier_semaphore()
    for peer in peers:
        pl.semaphore_signal(barrier, inc=1, device_id=peer, device_id_type=pl.DeviceIdType.MESH)
    pl.semaphore_wait(barrier, len(peers))


def others(me, count):
    return [lax.rem(me + step, count) for step in range(1, count)]


ANY = pl.BlockSpec(memory_space=pl.ANY)
IN_VMEM = pl.BlockSpec(memory_space=pltpu.VMEM)


def dma_sems(*counts):
    return [pltpu.SemaphoreType.DMA((count,)) for count in counts]


def comm_params(collective_id):
    return pltpu.CompilerParams(
        collective_id=collective_id, has_side_effects=True, vmem_limit_bytes=VMEM_LIMIT
    )


class Line:
    def __init__(self, place, copies, block):
        self.place, self.copies, self.block = place, copies, block

    def pass_on(self, src, z, step, when):
        p = self.place
        ref, sem = self.block(z)
        peer = p.at_z(jnp.clip(p.z + step, 0, p.n_z - 1))
        self.copies.send(ref if src is None else src, ref, sem, peer, when)

    def begin(self, own):
        p = self.place
        self.pass_on(own, p.z, 1, p.z < p.n_z - 1)
        self.pass_on(own, p.z, -1, p.z > 0)

    def arrive(self, distance, then):
        p = self.place
        for side in (1, -1):
            z = p.z + side * distance
            here = jnp.logical_and(z >= 0, z < p.n_z)
            z = jnp.clip(z, 0, p.n_z - 1)
            ref, sem = self.block(z)
            peer = p.at_z(jnp.clip(p.z + side, 0, p.n_z - 1))
            pl.when(here)(lambda: self.copies.arrived(ref, sem, peer))
            beyond = p.z - side
            beyond = jnp.logical_and(beyond >= 0, beyond < p.n_z)
            self.pass_on(None, z, -side, jnp.logical_and(here, beyond))
            then(z, here)


def row_line(place, out, copies, recv):
    def block(z):
        at = place.slot_of(z, place.c, place.y)
        return out.at[at], recv.at[at]

    return Line(place, copies, block)


def gather_begin(place, own, out, copies, recv):
    peer_y, peer_c = {"y": 1 - place.y}, {"c": 1 - place.c}
    copies.local(own, out.at[place.slot])
    line = row_line(place, out, copies, recv)
    line.begin(own)
    copies.send(own, out.at[place.slot], recv.at[place.slot], peer_y)
    copies.send(own, out.at[place.slot], recv.at[place.slot], peer_c)
    return line


def gather_step(place, line, copies, distance):
    def then(z, here):
        ref, sem = line.block(z)
        copies.send(ref, ref, sem, {"y": 1 - place.y}, here)
        copies.send(ref, ref, sem, {"c": 1 - place.c}, here)

    line.arrive(distance, then)


def gather_cross(place, out, copies, recv):
    for z in [place.z] + place.far_z():
        at = place.slot_of(z, place.c, 1 - place.y)
        copies.arrived(out.at[at], recv.at[at], {"y": 1 - place.y})
        copies.send(out.at[at], out.at[at], recv.at[at], {"c": 1 - place.c})


def gather_end(place, out, copies, recv):
    for z in [place.z] + place.far_z():
        for y in (place.y, 1 - place.y):
            at = place.slot_of(z, 1 - place.c, y)
            copies.arrived(out.at[at], recv.at[at], {"c": 1 - place.c})


def gather_copies(n_z):
    return 7 * n_z


def group_gather_kernel(own, out, send, recv):
    place = Place(False)
    copies = Copies(send)
    peer_z, peer_y, peer_c = place.at_z(1 - place.z), {"y": 1 - place.y}, {"c": 1 - place.c}
    meet([peer_z, peer_y, peer_c])
    rows = own.shape[0] // 2

    def part(at, half):
        return out.at[at, pl.ds(half * rows, rows)], recv.at[2 * at + half]

    def give(at, half, peer, src=None):
        ref, sem = part(at, half)
        copies.send(ref if src is None else src, ref, sem, peer)

    def got(at, half, peer):
        ref, sem = part(at, half)
        copies.arrived(ref, sem, peer)

    for half in range(2):
        src = own.at[pl.ds(half * rows, rows)]
        other = own.at[pl.ds((1 - half) * rows, rows)]
        give(place.slot, half, peer_y, src)
        give(place.slot, 1 - half, peer_z, other)
    copies.local(own, out.at[place.slot])
    for half in range(2):
        give(place.slot, half, peer_c, own.at[pl.ds(half * rows, rows)])
    near_y = place.slot_of(place.z, place.c, 1 - place.y)
    near_z = place.slot_of(1 - place.z, place.c, place.y)
    across = place.slot_of(1 - place.z, place.c, 1 - place.y)
    got(near_y, 0, peer_y)
    give(near_y, 0, peer_z)
    got(near_z, 1, peer_z)
    give(near_z, 1, peer_y)
    give(near_y, 0, peer_c)
    give(near_z, 1, peer_c)
    got(near_y, 1, peer_y)
    give(near_y, 1, peer_c)
    got(near_z, 0, peer_z)
    give(near_z, 0, peer_c)
    got(across, 0, peer_z)
    give(across, 0, peer_c)
    got(across, 1, peer_y)
    give(across, 1, peer_c)
    for z in range(2):
        for y in range(2):
            for half in range(2):
                got(place.slot_of(z, 1 - place.c, y), half, peer_c)
    copies.finish()


def group_gather(value, collective_id):
    return pl.pallas_call(
        group_gather_kernel,
        out_shape=jax.ShapeDtypeStruct((8,) + value.shape, value.dtype),
        in_specs=[ANY],
        out_specs=ANY,
        scratch_shapes=dma_sems(16, 16),
        compiler_params=comm_params(collective_id),
        name="group_gather",
    )(value)


def opening_kernel(
    own, blocks, ffn, out_w, out, blocks_all, ffn_all, out_w_all, send, recv, recv_w, recv_f, recv_o
):
    place, group = Place(True), Place(False)
    n_ctx = blocks.shape[0]
    copies = Copies(send)
    peer_x, peer_y = {"x": 1 - place.x}, {"y": 1 - place.y}
    far_ctx = others(place.ctx, n_ctx)
    meet([place.at_ctx(k) for k in far_ctx] + [peer_y, peer_x])
    mine = blocks_all.at[place.x, place.ctx]
    half = out_w.shape[1] // 2

    def sem_w(x, k):
        return recv_w.at[x * n_ctx + k]

    def out_block(z, x=place.x):
        at = x * place.n_z + z
        return out_w_all.at[at], recv_o.at[at]

    line = gather_begin(place, own, out, copies, recv)
    for k in far_ctx:
        copies.send(blocks.at[k], mine, sem_w(place.x, place.ctx), place.at_ctx(k))
    copies.local(blocks.at[place.ctx], mine)
    copies.send(blocks.at[place.ctx], mine, sem_w(place.x, place.ctx), peer_x)
    own_out, own_sem = out_block(place.z)
    own_half = out_w.at[:, pl.ds(pl.multiple_of(place.y * half, half), half)]
    copies.local(own_half, own_out)
    out_line = Line(place, copies, out_block)

    def out_over_x(z, here):
        ref, sem = out_block(z)
        copies.send(ref, ref, sem, peer_x, here)

    for distance in range(1, place.n_z):
        gather_step(place, line, copies, distance)
        if distance == 1:
            out_line.begin(own_half)
            copies.send(own_half, own_out, own_sem, peer_x)
            copies.local(ffn.at[:, group.ctx], ffn_all.at[:, group.ctx])
        if distance == 2:
            for k in others(group.ctx, 4):
                copies.send(ffn.at[:, k], ffn_all.at[:, group.ctx], recv_f.at[group.ctx], group.at_ctx(k))
        if distance > 1:
            out_line.arrive(distance - 1, out_over_x)
    out_line.arrive(place.n_z - 1, out_over_x)
    for k in far_ctx:
        block = blocks_all.at[place.x, k]
        copies.arrived(block, sem_w(place.x, k), place.at_ctx(k))
        copies.send(block, block, sem_w(place.x, k), peer_x)
    gather_cross(place, out, copies, recv)
    gather_end(place, out, copies, recv)
    for k in [place.ctx] + far_ctx:
        copies.arrived(blocks_all.at[1 - place.x, k], sem_w(1 - place.x, k), peer_x)
    for k in others(group.ctx, 4):
        copies.arrived(ffn_all.at[:, k], recv_f.at[k], group.at_ctx(k))
    for z in [place.z] + place.far_z():
        ref, sem = out_block(z, 1 - place.x)
        copies.arrived(ref, sem, peer_x)
    copies.finish()


def opening(own, blocks, ffn, out_w):
    n_ctx = blocks.shape[0]
    n_z = n_ctx // 2
    sends = gather_copies(n_z) + 2 * n_ctx + 4 + 5 * n_z
    return pl.pallas_call(
        opening_kernel,
        out_shape=(
            jax.ShapeDtypeStruct((2 * n_ctx,) + own.shape, own.dtype),
            jax.ShapeDtypeStruct((2,) + blocks.shape, blocks.dtype),
            jax.ShapeDtypeStruct(ffn.shape, ffn.dtype),
            jax.ShapeDtypeStruct((n_ctx, out_w.shape[0], out_w.shape[1] // 2), out_w.dtype),
        ),
        in_specs=[ANY] * 4,
        out_specs=(ANY,) * 4,
        scratch_shapes=dma_sems(sends, 2 * n_ctx, 2 * n_ctx, 4, n_ctx),
        compiler_params=comm_params(1),
        name="opening",
    )(own, blocks, ffn, out_w)


def to_tokens_kernel(src, dst, send, recv):
    place = Place(True)
    copies = Copies(send)
    count, width = src.shape[0], src.shape[2]
    far = others(place.slot, count)
    meet([place.at_slot(s) for s in far])

    def columns(s):
        return dst.at[:, pl.ds(pl.multiple_of(s * width, width), width)]

    for s in far:
        copies.send(src.at[s], columns(place.slot), recv.at[place.slot], place.at_slot(s))
    copies.local(src.at[place.slot], columns(place.slot))
    for s in far:
        copies.arrived(columns(s), recv.at[s], place.at_slot(s))
    copies.finish()


def to_tokens(value):
    count, tokens, width = value.shape
    return pl.pallas_call(
        to_tokens_kernel,
        out_shape=jax.ShapeDtypeStruct((tokens, count * width), value.dtype),
        in_specs=[ANY],
        out_specs=ANY,
        scratch_shapes=dma_sems(count, count),
        compiler_params=comm_params(2),
        name="to_tokens",
    )(value)


def to_heads_kernel(src, dst, send, recv):
    place = Place(True)
    copies = Copies(send)
    count, width = dst.shape[0], dst.shape[2]
    far = others(place.slot, count)
    meet([place.at_slot(s) for s in far])

    def columns(s):
        return src.at[:, pl.ds(pl.multiple_of(s * width, width), width)]

    for s in far:
        copies.send(columns(s), dst.at[place.slot], recv.at[place.slot], place.at_slot(s))
    copies.local(columns(place.slot), dst.at[place.slot])
    for s in far:
        copies.arrived(dst.at[s], recv.at[s], place.at_slot(s))
    copies.finish()


def to_heads(value, count):
    tokens, width = value.shape[0], value.shape[1] // count
    return pl.pallas_call(
        to_heads_kernel,
        out_shape=jax.ShapeDtypeStruct((count, tokens, width), value.dtype),
        in_specs=[ANY],
        out_specs=ANY,
        scratch_shapes=dma_sems(count, count),
        compiler_params=comm_params(3),
        name="to_heads",
    )(value)


class Scatter:
    def __init__(self, place, part, held, from_c, from_y, from_z, out, copies, loads, rc, ry, rz):
        self.__dict__.update(locals())

    def order(self):
        return self.place.far_z() + [self.place.z]

    def begin(self):
        p = self.place
        for y in (1 - p.y, p.y):
            for z in self.order():
                at = z * 2 + y
                self.copies.send(
                    self.part.at[p.slot_of(z, 1 - p.c, y)], self.from_c.at[at], self.rc.at[at], {"c": 1 - p.c}
                )
        self.queue = [(z, y) for y in (1 - p.y, p.y) for z in self.order()]
        for at in range(min(self.held.shape[0], len(self.queue))):
            self.load(at)

    def load(self, at):
        p = self.place
        z, y = self.queue[at]
        at = at % self.held.shape[0]
        self.copies.local(self.part.at[p.slot_of(z, p.c, y)], self.held.at[at], self.loads.at[at])

    def add_c(self, step):
        z, y = self.queue[step]
        at, depth = z * 2 + y, self.held.shape[0]
        own = step % depth
        self.copies.arrived(self.from_c.at[at], self.rc.at[at], {"c": 1 - self.place.c})
        pltpu.make_async_copy(self.held.at[own], self.held.at[own], self.loads.at[own]).wait()
        self.from_c[at] = self.from_c[at] + self.held[own]
        if step + depth < len(self.queue):
            self.load(step + depth)

    def over_c_far(self):
        p = self.place
        for step, z in enumerate(self.order()):
            self.add_c(step)
            self.copies.send(self.from_c.at[z * 2 + 1 - p.y], self.from_y.at[z], self.ry.at[z], {"y": 1 - p.y})

    def over_c_near(self):
        for step in range(self.place.n_z):
            self.add_c(self.place.n_z + step)

    def over_y(self):
        p = self.place
        for z in self.order():
            self.copies.arrived(self.from_y.at[z], self.ry.at[z], {"y": 1 - p.y})
            self.from_y[z] = self.from_y[z] + self.from_c[z * 2 + p.y]
            if z is not p.z:
                self.copies.send(self.from_y.at[z], self.from_z.at[p.z], self.rz.at[p.z], p.at_z(z))

    def over_z(self):
        p = self.place
        total = self.from_y[p.z].astype(F32)
        for z in p.far_z():
            self.copies.arrived(self.from_z.at[z], self.rz.at[z], p.at_z(z))
            total = total + self.from_z[z].astype(F32)
        self.out[...] = total


def scatter_scratch(n_z, block):
    return [
        pltpu.VMEM((min(8, 2 * n_z),) + block, B16),
        pltpu.VMEM((2 * n_z,) + block, B16),
        pltpu.VMEM((n_z,) + block, B16),
        pltpu.VMEM((n_z,) + block, B16),
    ]


def scatter_sems(n_z, more=0):
    return dma_sems(4 * n_z + more, min(8, 2 * n_z), 2 * n_z, n_z, n_z)


def group_scatter_kernel(part, out, held, from_c, over_y, over_z, last, send, loads, rc, ry, rz, rl):
    place = Place(False)
    copies = Copies(send)
    peer_z, peer_y, peer_c = place.at_z(1 - place.z), {"y": 1 - place.y}, {"c": 1 - place.c}
    meet([peer_z, peer_y, peer_c])
    rows = part.shape[1] // 2
    first, second = slice(0, rows), slice(rows, 2 * rows)
    own_y, far_y, own_z, far_z = place.y, 1 - place.y, place.z, 1 - place.z
    order = [(far_z, far_y), (far_z, own_y), (own_z, far_y), (own_z, own_y)]
    for z, y in order:
        at = z * 2 + y
        copies.send(part.at[place.slot_of(z, 1 - place.c, y)], from_c.at[at], rc.at[at], peer_c)
        copies.local(part.at[place.slot_of(z, place.c, y)], held.at[at], loads.at[at])

    def over_c(z, y):
        at = z * 2 + y
        copies.arrived(from_c.at[at], rc.at[at], peer_c)
        pltpu.make_async_copy(held.at[at], held.at[at], loads.at[at]).wait()
        from_c[at] = from_c[at] + held[at]
        return from_c.at[at]

    across = over_c(far_z, far_y)
    copies.send(across.at[first], over_y, ry.at[0], peer_y)
    copies.send(across.at[second], over_z, rz.at[0], peer_z)
    beside_z = over_c(far_z, own_y)
    copies.send(beside_z.at[second], last.at[0], rl.at[0], peer_z)
    beside_y = over_c(own_z, far_y)
    copies.send(beside_y.at[first], last.at[1], rl.at[1], peer_y)
    copies.arrived(over_y, ry.at[0], peer_y)
    over_y[...] = over_y[...] + beside_z[first, :]
    copies.send(over_y, last.at[2], rl.at[2], peer_z)
    copies.arrived(over_z, rz.at[0], peer_z)
    over_z[...] = over_z[...] + beside_y[second, :]
    copies.send(over_z, last.at[3], rl.at[3], peer_y)
    mine = over_c(own_z, own_y)
    copies.arrived(last.at[1], rl.at[1], peer_y)
    copies.arrived(last.at[0], rl.at[0], peer_z)
    copies.arrived(last.at[2], rl.at[2], peer_z)
    out[first, :] = mine[first, :].astype(F32) + last[1].astype(F32) + last[2].astype(F32)
    copies.arrived(last.at[3], rl.at[3], peer_y)
    out[second, :] = mine[second, :].astype(F32) + last[0].astype(F32) + last[3].astype(F32)
    copies.finish()


def group_scatter(part, collective_id):
    block = part.shape[1:]
    half = (block[0] // 2, block[1])
    return pl.pallas_call(
        group_scatter_kernel,
        out_shape=jax.ShapeDtypeStruct(block, F32),
        in_specs=[ANY],
        out_specs=IN_VMEM,
        scratch_shapes=[
            pltpu.VMEM((4,) + block, B16),
            pltpu.VMEM((4,) + block, B16),
            pltpu.VMEM(half, B16),
            pltpu.VMEM(half, B16),
            pltpu.VMEM((4,) + half, B16),
        ]
        + dma_sems(10, 4, 4, 1, 1, 4),
        compiler_params=comm_params(collective_id),
        name="group_scatter",
    )(part)


class OutScatter:
    def __init__(self, place, part, held, from_x, from_y, from_z, out, copies, loads, rx, ry, rz, rg):
        self.__dict__.update(locals())
        self.half = out.shape[2]

    def order(self):
        return self.place.far_z() + [self.place.z]

    def columns(self, y):
        return pl.ds(pl.multiple_of(y * self.half, self.half), self.half)

    def begin(self):
        p = self.place
        for z in self.order():
            self.copies.send(self.part.at[(1 - p.x) * p.n_z + z], self.from_x.at[z], self.rx.at[z], {"x": 1 - p.x})
            self.copies.local(self.part.at[p.x * p.n_z + z], self.held.at[z], self.loads.at[z])

    def over_x(self):
        p = self.place
        for z in self.order():
            self.copies.arrived(self.from_x.at[z], self.rx.at[z], {"x": 1 - p.x})
            pltpu.make_async_copy(self.held.at[z], self.held.at[z], self.loads.at[z]).wait()
            self.from_x[z] = self.from_x[z] + self.held[z]
            self.copies.send(
                self.from_x.at[z, :, self.columns(1 - p.y)], self.from_y.at[z], self.ry.at[z], {"y": 1 - p.y}
            )

    def over_y(self):
        p = self.place
        for z in self.order():
            self.copies.arrived(self.from_y.at[z], self.ry.at[z], {"y": 1 - p.y})
            self.from_y[z] = self.from_y[z] + self.from_x[z, :, self.columns(p.y)]
            if z is not p.z:
                self.copies.send(self.from_y.at[z], self.from_z.at[p.z], self.rz.at[p.z], p.at_z(z))

    def over_z(self):
        p = self.place
        total = self.from_y[p.z].astype(F32)
        for z in p.far_z():
            self.copies.arrived(self.from_z.at[z], self.rz.at[z], p.at_z(z))
            total = total + self.from_z[z].astype(F32)
        self.out[p.y] = total.astype(B16)
        self.copies.send(self.out.at[p.y], self.out.at[p.y], self.rg.at[p.y], {"y": 1 - p.y})

    def end(self):
        p = self.place
        self.copies.arrived(self.out.at[1 - p.y], self.rg.at[1 - p.y], {"y": 1 - p.y})


def closing_kernel(
    part, grads, out_part, fc, proj, sums_in, gain_in, shift_in, pair_in, ff_in,
    out, grads_out, out_w_out, fc_out, proj_out, owned, pairs_out, ff_out,
    held, from_c, from_y, from_z, own_x, from_x, o_held, o_x, o_y, o_z,
    send, loads, rc, ry, rz, load_x, rx, rk, rg, o_loads, orx, ory, orz, org, rfc, rproj,
    terms, terms_all, half, pairs_half, half_y, pairs_y, rv, rvy,
):
    place, group = Place(True), Place(False)
    n_ctx = grads.shape[1]
    copies = Copies(send)
    far_ctx = others(place.ctx, n_ctx)
    peer_x, peer_y = {"x": 1 - place.x}, {"y": 1 - place.y}
    count = 2 * n_ctx
    me = place.x * n_ctx + place.ctx
    far_shards = others(me, count)

    def at_shard(k):
        return dict(place.at_ctx(lax.rem(k, n_ctx)), x=k // n_ctx)

    meet([at_shard(k) for k in far_shards] + [peer_y])
    tall = grads.shape[2]
    terms[...] = jnp.zeros_like(terms)
    for k in range(count):
        cols = slice(k * tall, (k + 1) * tall)
        terms[k, 0:4, 0:tall] = sums_in[:, cols]
        terms[k, 4:5, 0:tall] = gain_in[:, cols]
        terms[k, 5:6, 0:tall] = shift_in[:, cols]
        pair = pair_in.shape[1] // 3
        terms[k, 6:7, 0:pair] = pair_in[:, 0:pair]
        terms[k, 7:8, 0:pair] = pair_in[:, 2 * pair :]
        for row in range(-(-ff_in.shape[1] // 128)):
            width = min(128, ff_in.shape[1] - row * 128)
            terms[k, 8 + row : 9 + row, 0:width] = ff_in[:, row * 128 : row * 128 + width]
    for k in far_shards:
        copies.send(terms.at[k], terms_all.at[me], rv.at[me], at_shard(k))
    terms_all[me] = terms[me]
    sums = Scatter(place, part, held, from_c, from_y, from_z, out, copies, loads, rc, ry, rz)
    outs = OutScatter(place, out_part, o_held, o_x, o_y, o_z, out_w_out, copies, o_loads, orx, ory, orz, org)
    sums.begin()
    for k in far_ctx + [place.ctx]:
        copies.send(grads.at[1 - place.x, k], from_x.at[k], rx.at[k], peer_x)
        copies.local(grads.at[place.x, k], own_x.at[k], load_x.at[k])
    outs.begin()
    for k in others(group.ctx, 4):
        copies.send(fc.at[k], fc_out.at[group.ctx], rfc.at[group.ctx], group.at_ctx(k))
        copies.send(proj.at[k], proj_out.at[group.ctx], rproj.at[group.ctx], group.at_ctx(k))
    copies.local(fc.at[group.ctx], fc_out.at[group.ctx])
    copies.local(proj.at[group.ctx], proj_out.at[group.ctx])
    sums.over_c_far()
    mine = grads_out.at[place.y, place.ctx]
    for k in far_ctx + [place.ctx]:
        copies.arrived(from_x.at[k], rx.at[k], peer_x)
        pltpu.make_async_copy(own_x.at[k], own_x.at[k], load_x.at[k]).wait()
        from_x[k] = from_x[k] + own_x[k]
        if k is not place.ctx:
            copies.send(from_x.at[k], mine, rk.at[place.ctx], place.at_ctx(k))
    copies.local(from_x.at[place.ctx], mine)
    copies.send(from_x.at[place.ctx], mine, rg.at[place.ctx], peer_y)
    sums.over_c_near()
    sums.over_y()
    outs.over_x()
    for k in far_ctx:
        block = grads_out.at[place.y, k]
        copies.arrived(block, rk.at[k], place.at_ctx(k))
        copies.send(block, block, rg.at[k], peer_y)
    outs.over_y()
    sums.over_z()
    outs.over_z()
    for k in far_shards:
        copies.arrived(terms_all.at[k], rv.at[k], at_shard(k))
    total = terms_all[0, 0:8, :]
    for k in range(1, count):
        total = total + terms_all[k, 0:8, :]
    half[...] = total
    for k in range(n_ctx):
        pairs_half[k] = terms_all[k, 6:8, :] + terms_all[n_ctx + k, 6:8, :]
    copies.send(half, half_y, rvy.at[0], peer_y)
    copies.send(pairs_half, pairs_y, rvy.at[1], peer_y)
    for part in range(4):
        total = terms_all[part, 8:16, :]
        for k in range(part + 4, count, 4):
            total = total + terms_all[k, 8:16, :]
        ff_out[part] = total
    copies.arrived(half_y, rvy.at[0], peer_y)
    owned[...] = half[...] + half_y[...]
    copies.arrived(pairs_y, rvy.at[1], peer_y)
    pairs_out[place.y] = pairs_half[...]
    pairs_out[1 - place.y] = pairs_y[...]
    for k in [place.ctx] + far_ctx:
        copies.arrived(grads_out.at[1 - place.y, k], rg.at[k], peer_y)
    outs.end()
    for k in others(group.ctx, 4):
        copies.arrived(fc_out.at[k], rfc.at[k], group.at_ctx(k))
        copies.arrived(proj_out.at[k], rproj.at[k], group.at_ctx(k))
    copies.finish()


def closing(part, grads, out_part, fc, proj, *vectors):
    block = part.shape[1:]
    n_ctx = grads.shape[1]
    n_z = n_ctx // 2
    piece = grads.shape[1:]
    rows, width = out_part.shape[1:]
    half = (rows, width // 2)
    return pl.pallas_call(
        closing_kernel,
        out_shape=(
            jax.ShapeDtypeStruct(block, F32),
            jax.ShapeDtypeStruct((2,) + piece, B16),
            jax.ShapeDtypeStruct((2,) + half, B16),
            jax.ShapeDtypeStruct(fc.shape, fc.dtype),
            jax.ShapeDtypeStruct(proj.shape, proj.dtype),
            jax.ShapeDtypeStruct((8, 128), F32),
            jax.ShapeDtypeStruct((2, n_ctx, 2, 128), F32),
            jax.ShapeDtypeStruct((4, 8, 128), F32),
        ),
        in_specs=[ANY] * 5 + [IN_VMEM] * 5,
        out_specs=(IN_VMEM, ANY, IN_VMEM, ANY, ANY, IN_VMEM, IN_VMEM, IN_VMEM),
        scratch_shapes=scatter_scratch(n_z, block)
        + [pltpu.VMEM(piece, B16), pltpu.VMEM(piece, B16)]
        + [pltpu.VMEM((n_z, rows, width), B16), pltpu.VMEM((n_z, rows, width), B16)]
        + [pltpu.VMEM((n_z,) + half, B16), pltpu.VMEM((n_z,) + half, B16)]
        + scatter_sems(n_z, 5 * n_ctx + 4 * n_z + 10)
        + dma_sems(n_ctx, n_ctx, n_ctx, n_ctx)
        + dma_sems(n_z, n_z, n_z, n_z, 2, 4, 4)
        + [pltpu.VMEM((2 * n_ctx, 16, 128), F32), pltpu.VMEM((2 * n_ctx, 16, 128), F32)]
        + [pltpu.VMEM((8, 128), F32), pltpu.VMEM((n_ctx, 2, 128), F32)]
        + [pltpu.VMEM((8, 128), F32), pltpu.VMEM((n_ctx, 2, 128), F32)]
        + dma_sems(2 * n_ctx, 2),
        compiler_params=comm_params(4),
        name="closing",
    )(part, grads, out_part, fc, proj, *vectors)


def laid_wide(value, count, rows, tall):
    zeros = jnp.zeros((value.shape[0], tall - rows), value.dtype)
    parts = []
    for k in range(count):
        parts += [value[:, k * rows : (k + 1) * rows], zeros]
    return jnp.concatenate(parts, axis=1)


def laid_tall(value, count, rows, tall):
    zeros = jnp.zeros((tall - rows, value.shape[1]), value.dtype)
    parts = []
    for k in range(count):
        parts += [value[k * rows : (k + 1) * rows], zeros]
    return jnp.concatenate(parts, axis=0)


def laid_short(value, count, rows, tall):
    return jnp.concatenate([value[k * tall : k * tall + rows] for k in range(count)], axis=0)


def laid_narrow(value, count, rows, tall):
    return jnp.concatenate([value[:, k * tall : k * tall + rows] for k in range(count)], axis=1)


def prepare_kernel(count, at_ref, x, grad, qkv, fc, proj, out_w, *refs):
    singles, qv, (x_out, grad_out, blocks, ffn, out_out) = refs[:6], refs[6], refs[7:]
    rows, feats = out_w.shape
    n_ctx, tall, cols = blocks.shape
    pair, ff = cols // 3, ffn.shape[3]
    x_out[...] = laid_tall(x[...].astype(F32), count, rows, tall).T.astype(B16)
    grad_out[...] = laid_tall(grad[...].astype(F32), count, rows, tall).T.astype(B16)
    below = jnp.zeros((tall - rows, feats), F32)
    out_out[...] = laid_wide(
        jnp.concatenate([out_w[...].astype(F32), below], axis=0), count, rows, tall
    ).astype(B16)
    below = jnp.zeros((tall - rows, ff), F32)
    for k in range(4):
        ffn[0, k] = jnp.concatenate([fc[:, k * ff : (k + 1) * ff].astype(F32), below], axis=0).astype(B16)
        ffn[1, k] = jnp.concatenate([proj[:, k * ff : (k + 1) * ff].astype(F32), below], axis=0).astype(B16)
    small = [jnp.concatenate([ref[...].astype(F32), jnp.zeros((1, cols - rows), F32)], axis=1) for ref in singles]
    small.append(jnp.concatenate([qv[...].astype(F32), jnp.zeros((1, cols - 2 * rows), F32)], axis=1))
    if tall - rows > 7:
        small.append(jnp.zeros((tall - rows - 7, cols), F32))
    small = jnp.concatenate(small, axis=0)
    first = at_ref[0] == 0
    whole = qkv[...].astype(F32)

    def columns(part, p):
        width = min(pair, feats - p * pair)
        if width <= 0:
            return jnp.zeros((rows, pair), F32)
        value = whole[:, part * feats + p * pair : part * feats + p * pair + width]
        if width < pair:
            value = jnp.concatenate([value, jnp.zeros((rows, pair - width), F32)], axis=1)
        return value

    for k in range(n_ctx):
        value = [jnp.where(first, columns(part, 2 * k), columns(part, 2 * k + 1)) for part in range(3)]
        blocks[k] = jnp.concatenate([jnp.concatenate(value, axis=1), small], axis=0).astype(B16)


def prepare(y_at, x, grad, qkv, fc, proj, out_w, singles, qv, n_ctx, tall, pair):
    rows, feats = out_w.shape
    count = feats // rows
    wide = count * tall
    tokens = x.shape[1]
    vmem = pl.BlockSpec(memory_space=pltpu.VMEM)
    return pl.pallas_call(
        functools.partial(prepare_kernel, count),
        in_specs=[pl.BlockSpec(memory_space=pltpu.SMEM)] + [vmem] * 13,
        out_shape=(
            jax.ShapeDtypeStruct((tokens, wide), B16),
            jax.ShapeDtypeStruct((tokens, wide), B16),
            jax.ShapeDtypeStruct((n_ctx, tall, 3 * pair), B16),
            jax.ShapeDtypeStruct((2, 4, tall, fc.shape[1] // 4), B16),
            jax.ShapeDtypeStruct((tall, wide), B16),
        ),
        compiler_params=pltpu.CompilerParams(vmem_limit_bytes=VMEM_LIMIT),
        name="prepare",
    )(y_at, x, grad, qkv, fc, proj, out_w, *[value[None] for value in singles], qv[None])


def project_kernel(
    rows, feats, at_ref, x_ref, packed_ref, mask_ref, w_ref, norm_ref, qkv_ref, single_ref, bias_s, held_s
):
    count, tall, cols = packed_ref.shape
    pair = cols // 3

    @pl.when(pl.program_id(0) == 0)
    def begin():
        held_s[...] = jnp.zeros_like(held_s)
        vectors = []
        for row in range(6):
            at = rows + row
            vectors.append(
                jnp.concatenate([packed_ref[k, at : at + 1, 0:tall].astype(F32) for k in range(count)], axis=1)
            )
        single_ref[...] = jnp.concatenate(vectors + [jnp.zeros((2, count * tall), F32)], axis=0)
        for part in range(2):
            blocks = range(part * count // 2, (part + 1) * count // 2)
            at = rows + 6
            held_s[part : part + 1, 0:feats] = jnp.concatenate(
                [packed_ref[k, at : at + 1, 0 : 2 * rows].astype(F32) for k in blocks], axis=1
            )
        own = pl.ds(pl.multiple_of(at_ref[0] * pair, pair), pair)
        bias_s[...] = jnp.concatenate([held_s[0:1, own], jnp.zeros((1, pair), F32), held_s[1:2, own]], axis=1)

    x = x_ref[...].astype(F32)
    mean = jnp.sum(x, axis=1, keepdims=True) * (1.0 / feats)
    centered = (x - mean) * mask_ref[...]
    inv = lax.rsqrt(jnp.sum(centered * centered, axis=1, keepdims=True) * (1.0 / feats) + NORM_EPS)
    norm = (centered * inv * single_ref[0:1, :] + single_ref[1:2, :]).astype(B16)
    norm_ref[...] = norm
    qkv_ref[...] = (dot(norm, w_ref[...], 1, 0) + bias_s[...]).astype(B16)


def project(slot_at, x, packed, mask, rows, feats, padded):
    total, wide = x.shape
    cols = packed.shape[2]
    step = min(256, total)

    def fixed(shape):
        return pl.BlockSpec(shape, lambda i: (0,) * len(shape))

    return pl.pallas_call(
        functools.partial(project_kernel, rows, feats),
        grid=(total // step,),
        in_specs=[pl.BlockSpec(memory_space=pltpu.SMEM), pl.BlockSpec((step, wide), lambda i: (i, 0))]
        + [fixed(packed.shape), fixed((1, wide)), fixed((wide, cols))],
        out_specs=(
            pl.BlockSpec((step, wide), lambda i: (i, 0)),
            pl.BlockSpec((step, cols), lambda i: (i, 0)),
            fixed((8, wide)),
        ),
        out_shape=(
            jax.ShapeDtypeStruct((total, wide), B16),
            jax.ShapeDtypeStruct((total, cols), B16),
            jax.ShapeDtypeStruct((8, wide), F32),
        ),
        scratch_shapes=[pltpu.VMEM((1, cols), F32), pltpu.VMEM((2, padded), F32)],
        compiler_params=pltpu.CompilerParams(vmem_limit_bytes=VMEM_LIMIT),
        name="project",
    )(slot_at, x, packed, mask[None], packed.reshape(wide, cols))


def project_back_kernel(feats, x_ref, grad_ref, mask_ref, w_ref, part_ref, gradb_ref, gain_ref, shift_ref, pair_ref):
    @pl.when(pl.program_id(0) == 0)
    def begin():
        gain_ref[...] = jnp.zeros_like(gain_ref)
        shift_ref[...] = jnp.zeros_like(shift_ref)
        pair_ref[...] = jnp.zeros_like(pair_ref)

    grad = grad_ref[...]
    pair_ref[...] += jnp.sum(grad, axis=0, keepdims=True)
    grad = grad.astype(B16)
    gradb_ref[...] = grad
    part = dot(grad, w_ref[...], 1, 1)
    part_ref[...] = part.astype(B16)
    x = x_ref[...].astype(F32)
    mean = jnp.sum(x, axis=1, keepdims=True) * (1.0 / feats)
    centered = (x - mean) * mask_ref[...]
    inv = lax.rsqrt(jnp.sum(centered * centered, axis=1, keepdims=True) * (1.0 / feats) + NORM_EPS)
    gain_ref[...] += jnp.sum(part * (centered * inv), axis=0, keepdims=True)
    shift_ref[...] += jnp.sum(part, axis=0, keepdims=True)


def project_back(x, grad, mask, weight, feats):
    total, wide = x.shape
    cols = weight.shape[1]
    step = min(256, total)

    def fixed(shape):
        return pl.BlockSpec(shape, lambda i: (0,) * len(shape))

    def moving(width):
        return pl.BlockSpec((step, width), lambda i: (i, 0))

    return pl.pallas_call(
        functools.partial(project_back_kernel, feats),
        grid=(total // step,),
        in_specs=[moving(wide), moving(cols), fixed((1, wide)), fixed((wide, cols))],
        out_specs=(moving(wide), moving(cols), fixed((1, wide)), fixed((1, wide)), fixed((1, cols))),
        out_shape=(
            jax.ShapeDtypeStruct((total, wide), B16),
            jax.ShapeDtypeStruct((total, cols), B16),
            jax.ShapeDtypeStruct((1, wide), F32),
            jax.ShapeDtypeStruct((1, wide), F32),
            jax.ShapeDtypeStruct((1, cols), F32),
        ),
        compiler_params=pltpu.CompilerParams(vmem_limit_bytes=VMEM_LIMIT),
        name="project_back",
    )(x, grad, mask[None], weight)


def deliver_kernel(
    rows, feats, qkv, out_w, fc, proj, mlp, hidden, dnorm, dhidden, x_ref, single, mask,
    qkv_out, out_out, fc_out, proj_out, block_out, grad_out,
):
    n_y, n_ctx, tall, cols = qkv.shape
    pair, ff, count = cols // 3, fc.shape[2], feats // rows
    parts = []
    for part in range(3):
        for p in range(-(-feats // pair)):
            width = min(pair, feats - p * pair)
            parts.append(qkv[p % n_y, p // n_y, :, part * pair : part * pair + width].astype(F32))
    qkv_out[...] = jnp.concatenate(parts, axis=1)[:rows]
    halves = jnp.concatenate([out_w[y].astype(F32) for y in range(2)], axis=1)
    out_out[...] = laid_narrow(halves, count, rows, tall)[:rows]
    fc_out[...] = jnp.concatenate([fc[k].astype(F32) for k in range(4)], axis=1)[:rows]
    for k in range(4):
        proj_out[:, k * ff : (k + 1) * ff] = proj[k].astype(F32)[:rows]
    block = hidden[...] + mlp[...].astype(F32) + single[5:6, :]
    block_out[...] = laid_short(block.T, count, rows, tall)
    normed, inv = norm_forward(x_ref[...].astype(F32), mask[...], feats)
    grad = dhidden[...] + norm_backward(dnorm[...], normed, inv, single[0:1, :], feats)
    grad_out[...] = laid_short(grad.T, count, rows, tall)


def deliver(qkv, out_w, fc, proj, mlp, hidden, dnorm, dhidden, x, single, mask, rows, feats):
    tokens, ff = x.shape[0], fc.shape[2]
    return pl.pallas_call(
        functools.partial(deliver_kernel, rows, feats),
        out_shape=(
            jax.ShapeDtypeStruct((rows, 3 * feats), F32),
            jax.ShapeDtypeStruct((rows, feats), F32),
            jax.ShapeDtypeStruct((rows, 4 * ff), F32),
            jax.ShapeDtypeStruct((rows, 4 * ff), F32),
            jax.ShapeDtypeStruct((feats, tokens), F32),
            jax.ShapeDtypeStruct((feats, tokens), F32),
        ),
        compiler_params=pltpu.CompilerParams(vmem_limit_bytes=VMEM_LIMIT),
        name="deliver",
    )(qkv, out_w, fc, proj, mlp, hidden, dnorm, dhidden, x, single, mask[None])


def hidden_kernel(rows, feats, att, w_out, x_ref, single, mask, by_core, hidden_out, norm_out):
    half = w_out.shape[2]
    count = feats // rows
    tall = 2 * half // count
    value = att[...].astype(F32)
    zeros = jnp.zeros((value.shape[0], tall - rows), F32)
    parts = []
    for core in range(2):
        blocks = []
        for k in range(core, count, 2):
            blocks += [value[:, k * rows : (k + 1) * rows], zeros]
        parts.append(jnp.concatenate(blocks, axis=1).astype(B16))
        by_core[core] = parts[core]
    hidden = [dot(parts[0], w_out[0, y], 1, 0) + dot(parts[1], w_out[1, y], 1, 0) for y in range(2)]
    hidden = x_ref[...].astype(F32) + jnp.concatenate(hidden, axis=1) + single[2:3, :]
    hidden_out[...] = hidden
    normed, unused = norm_forward(hidden, mask[...], feats)
    norm_out[...] = (normed * single[3:4, :] + single[4:5, :]).astype(B16)


def hidden_forward(att, w_out, x, single, mask, rows, feats):
    tokens, wide = x.shape
    return pl.pallas_call(
        functools.partial(hidden_kernel, rows, feats),
        out_shape=(
            jax.ShapeDtypeStruct((2, tokens, wide // 2), B16),
            jax.ShapeDtypeStruct((tokens, wide), F32),
            jax.ShapeDtypeStruct((tokens, wide), B16),
        ),
        compiler_params=pltpu.CompilerParams(vmem_limit_bytes=VMEM_LIMIT),
        name="hidden_forward",
    )(att, w_out, x, single, mask[None])


def hidden_back_kernel(
    rows, feats, dnorm_ref, hidden, grad_ref, w_out, single, mask, dhidden_out, dhidden_b, sums, datt_out
):
    half = w_out.shape[2]
    count = feats // rows
    tall = 2 * half // count
    dnorm = dnorm_ref[...]
    grad = grad_ref[...].astype(F32)
    normed, inv = norm_forward(hidden[...], mask[...], feats)
    dhidden = grad + norm_backward(dnorm, normed, inv, single[3:4, :], feats)
    dhidden_out[...] = dhidden
    rounded = dhidden.astype(B16)
    dhidden_b[...] = rounded
    sums[0:1, :] = jnp.sum(dhidden, axis=0, keepdims=True)
    sums[1:2, :] = jnp.sum(dnorm * normed, axis=0, keepdims=True)
    sums[2:3, :] = jnp.sum(dnorm, axis=0, keepdims=True)
    sums[3:4, :] = jnp.sum(grad, axis=0, keepdims=True)
    grads = [rounded[:, :half], rounded[:, half:]]
    datt = [dot(grads[0], w_out[c, 0], 1, 1) + dot(grads[1], w_out[c, 1], 1, 1) for c in range(2)]
    parts = [datt[k % 2][:, k // 2 * tall : k // 2 * tall + rows] for k in range(count)]
    if datt_out.shape[1] > feats:
        parts.append(jnp.zeros((dnorm.shape[0], datt_out.shape[1] - feats), F32))
    datt_out[...] = jnp.concatenate(parts, axis=1).astype(B16)


def hidden_back(dnorm, hidden, grad, w_out, single, mask, rows, feats, padded):
    tokens, wide = hidden.shape
    return pl.pallas_call(
        functools.partial(hidden_back_kernel, rows, feats),
        out_shape=(
            jax.ShapeDtypeStruct((tokens, wide), F32),
            jax.ShapeDtypeStruct((tokens, wide), B16),
            jax.ShapeDtypeStruct((4, wide), F32),
            jax.ShapeDtypeStruct((tokens, padded), B16),
        ),
        compiler_params=pltpu.CompilerParams(vmem_limit_bytes=VMEM_LIMIT),
        name="hidden_back",
    )(dnorm, hidden, grad, w_out, single, mask[None])


def load_pieces(at_ref, pieces, whole, sems, first=0):
    rows = whole.shape[0] // len(pieces)
    copies = []
    for i, piece in enumerate(pieces):
        to = whole.at[pl.ds(pl.multiple_of(at_ref[i], 16), rows), :]
        copies.append(pltpu.make_async_copy(piece, to, sems.at[first + i]))
    for copy in copies:
        copy.start()
    return copies


def as_pieces(pairs, refs, which):
    return [ref.at[which] for ref in refs[:pairs]] + list(refs[pairs:])


def feed_up_kernel(pairs, count, at_ref, *refs):
    pieces, (norm_ref, bias_ref, act_ref, slope_ref, w_fc, sems) = refs[:count], refs[count:]

    @pl.when(pl.program_id(0) == 0)
    def begin():
        for copy in load_pieces(at_ref, as_pieces(pairs, pieces, 0), w_fc, sems):
            copy.wait()

    activated, slope = gelu_parts(dot(norm_ref[...], w_fc[...], 1, 0) + bias_ref[...])
    act_ref[...] = activated.astype(B16)
    slope_ref[...] = slope


FEED_STEP = 256


def feed_up(pairs, fcs, places, norm, bias):
    pieces = pairs + fcs
    total, wide = norm.shape
    ff = bias.shape[0]
    hidden = pl.BlockSpec((FEED_STEP, ff), lambda i: (i, 0))
    return pl.pallas_call(
        functools.partial(feed_up_kernel, len(pairs), len(pieces)),
        grid=(total // FEED_STEP,),
        in_specs=[pl.BlockSpec(memory_space=pltpu.SMEM)]
        + [ANY] * len(pieces)
        + [pl.BlockSpec((FEED_STEP, wide), lambda i: (i, 0)), pl.BlockSpec((1, ff), lambda i: (0, 0))],
        out_specs=(hidden, hidden),
        out_shape=(jax.ShapeDtypeStruct((total, ff), B16), jax.ShapeDtypeStruct((total, ff), F32)),
        scratch_shapes=[pltpu.VMEM((wide, ff), B16)] + dma_sems(len(pieces)),
        compiler_params=pltpu.CompilerParams(vmem_limit_bytes=VMEM_LIMIT),
        name="feed_up",
    )(places, *pieces, norm, bias[None])


def feed_down_kernel(pairs, singles, at_ref, *refs):
    count = pairs + 2 * singles
    pieces, refs = refs[:count], refs[count:]
    grad_ref, act_ref, slope_ref, dpre_ref, dnorm_ref, mlp_ref, sum_ref, w_fc, w_proj, sems = refs

    @pl.when(pl.program_id(0) == 0)
    def begin():
        fcs = as_pieces(pairs, pieces[: pairs + singles], 0)
        projs = as_pieces(pairs, pieces[:pairs] + pieces[pairs + singles :], 1)
        copies = load_pieces(at_ref, projs, w_proj, sems)
        copies += load_pieces(at_ref, fcs, w_fc, sems, pairs + singles)
        for copy in copies:
            copy.wait()
        sum_ref[...] = jnp.zeros_like(sum_ref)

    dpre = dot(grad_ref[...], w_proj[...], 1, 0) * slope_ref[...]
    sum_ref[...] += jnp.sum(dpre, axis=0, keepdims=True)
    dpre_b = dpre.astype(B16)
    dpre_ref[...] = dpre_b
    dnorm_ref[...] = dot(dpre_b, w_fc[...], 1, 1).astype(B16)
    mlp_ref[...] = dot(act_ref[...], w_proj[...], 1, 1).astype(B16)


def feed_down(pairs, fcs, projs, places, grad, act, slope):
    pieces = pairs + fcs + projs
    total, wide = grad.shape
    ff = act.shape[1]
    tokens = pl.BlockSpec((FEED_STEP, wide), lambda i: (i, 0))
    hidden = pl.BlockSpec((FEED_STEP, ff), lambda i: (i, 0))
    single = pl.BlockSpec((1, ff), lambda i: (0, 0))
    return pl.pallas_call(
        functools.partial(feed_down_kernel, len(pairs), len(fcs)),
        grid=(total // FEED_STEP,),
        in_specs=[pl.BlockSpec(memory_space=pltpu.SMEM)] + [ANY] * len(pieces) + [tokens, hidden, hidden],
        out_specs=(hidden, tokens, tokens, single),
        out_shape=(
            jax.ShapeDtypeStruct((total, ff), B16),
            jax.ShapeDtypeStruct((total, wide), B16),
            jax.ShapeDtypeStruct((total, wide), B16),
            jax.ShapeDtypeStruct((1, ff), F32),
        ),
        scratch_shapes=[pltpu.VMEM((wide, ff), B16), pltpu.VMEM((wide, ff), B16)]
        + dma_sems(2 * (len(pairs) + len(fcs))),
        compiler_params=pltpu.CompilerParams(vmem_limit_bytes=VMEM_LIMIT),
        name="feed_down",
    )(places, *pieces, grad, act, slope)


def after(value, other, unpack=False):
    value, other = lax.optimization_barrier((value, other))
    return (*value, other) if unpack else (value, other)


def shift_perm(count, step):
    return [(i, (i + step) % count) for i in range(count)]


def on_device(
    sizes, block_input, segment_ids, slot_order, first_gain, first_shift, qkv_weight, qv_bias, out_weight, out_bias,
    second_gain, second_shift, fc_weight, fc_bias, proj_weight, proj_bias, out_grad,
):
    n_x, n_ctx, n_y = sizes
    n_slot = n_ctx * n_y
    n_shard = n_x * n_ctx
    n_h = n_ctx // 4
    slot_len, feats = block_input.shape[1:]
    head = feats // HEADS
    pair = 2 * head
    rows = qkv_weight.shape[0]
    ff_own = fc_weight.shape[1] // 4
    padded = n_slot * pair
    y_at = lax.axis_index("y")
    ctx_at = lax.axis_index(CTX)
    slot_at = lax.axis_index(ROW)
    lc_at = lax.axis_index(("l", "c"))
    x_at, h_at = lax.axis_index("x"), lax.axis_index("h")

    def gather(value, axes):
        return lax.all_gather(value, axes, axis=0, tiled=True)

    tall = rows + (-rows % 16)
    wide = n_shard * tall
    row_pad = tall - rows

    mask = jnp.asarray((np.arange(wide) % tall < rows).astype(np.float32))

    singles = (first_gain, first_shift, out_bias, second_gain, second_shift, proj_bias)
    own_input, grad_own, packed, ffn_blocks, w_out = prepare(
        y_at.astype(jnp.int32)[None], block_input[0].T, out_grad[0].T, qkv_weight, fc_weight, proj_weight.T, out_weight,
        singles, qv_bias, n_ctx, tall, pair,
    )
    all_input, packed, ffn_blocks, w_out = opening(
        own_input, packed, ffn_blocks, w_out
    )
    ffn_blocks = ffn_blocks.reshape(2, 4 * tall, ff_own)
    fc_h = [lax.ppermute(ffn_blocks[0], "h", shift_perm(n_h, step)) for step in range(1, n_h)]
    along_x = lax.ppermute(ffn_blocks, "x", shift_perm(n_x, 1))
    grad_late, all_input = after(grad_own, all_input)
    grad_all = gather(grad_late, FFG)
    w_out = lax.all_gather(w_out.reshape(wide // 2, wide // 2), ("c", "y"), axis=0, tiled=False)
    w_out = w_out.reshape(2, n_y, wide // 2, wide // 2)
    packed = packed.reshape(n_shard, tall, 3 * pair)
    w_qkv = packed.reshape(wide, 3 * pair)
    b_fc = lax.dynamic_slice_in_dim(fc_bias, lc_at * ff_own, ff_own, 0).astype(F32)

    order = slot_order[0]
    pieces = jnp.arange(n_slot, dtype=jnp.int32)
    inv = jnp.sum(jnp.where(order[None, :] == pieces[:, None], pieces[None, :], 0), axis=1).astype(jnp.int32)
    segs = jnp.take(segment_ids[0].reshape(n_slot, slot_len), inv, axis=0).reshape(-1)
    docs = jnp.arange(DOCS, dtype=jnp.int32)
    counts = jnp.sum((segs[None, :] == docs[:, None]).astype(jnp.int32), axis=1)
    starts = jnp.sum(jnp.where(segs[None, :] > docs[:, None], counts[:, None], 0), axis=0).astype(jnp.int32)
    start3 = starts.reshape(-1, 1, BLK)
    low = start3[:, 0, 0] // BLK

    all_input = all_input.reshape(n_slot * slot_len, wide)
    norm_one, qkv, singles = project(
        slot_at.astype(jnp.int32)[None], all_input, packed, mask, rows, feats, padded
    )
    heads_out, lse = attend(inv, low, qkv, start3, slot_len, head)
    fc_h, along_x, heads_out = after((fc_h, along_x), heads_out, True)
    fc_xh = [lax.ppermute(value, "x", shift_perm(n_x, 1)) for value in fc_h]
    tokens_out = to_tokens(heads_out.reshape(n_slot, slot_len, pair))
    proj_late, tokens_out = after(ffn_blocks[1], tokens_out)
    proj_h = [lax.ppermute(proj_late, "h", shift_perm(n_h, step)) for step in range(1, n_h)]
    by_core, hidden, norm_two = hidden_forward(
        tokens_out, w_out, own_input, singles, mask, rows, feats
    )
    norm_all = group_gather(norm_two, 6).reshape(-1, wide)
    proj_h, norm_all = after(proj_h, norm_all)
    proj_xh = [lax.ppermute(value, "x", shift_perm(n_x, 1)) for value in proj_h]
    places = [(x_at, h_at), (1 - x_at, h_at)]
    for step in range(1, n_h):
        h_from = lax.rem(h_at + n_h - step, n_h)
        places += [(x_at, h_from), (1 - x_at, h_from)]

    def mixed(one, two):
        return [value for both in zip(one, two) for value in both]

    places = jnp.stack([(x * n_h + h) * (4 * tall) for x, h in places]).astype(jnp.int32)
    pairs, fcs, projs = [ffn_blocks, along_x], mixed(fc_h, fc_xh), mixed(proj_h, proj_xh)
    activation, slope = feed_up(pairs, fcs, places, norm_all, b_fc)

    def pick(value, at):
        return lax.dynamic_index_in_dim(value, at, 0, False)

    def by_owner(value):
        value = with_layout_constraint(value.astype(B16), Layout(major_to_minor=(0, 1)))
        return value.reshape(n_x, n_h, 4 * tall, ff_own)

    proj_part = by_owner(dot(grad_all, activation, 0, 0))
    proj_give = pick(proj_part, 1 - x_at)
    proj_give, activation = after(proj_give, activation)
    proj_x = lax.ppermute(proj_give, "x", shift_perm(n_x, 1))
    dpreact_b, dnorm_part, mlp_part, dpreact_sum = feed_down(pairs, fcs, projs, places, grad_all, activation, slope)

    fc_part = by_owner(dot(norm_all, dpreact_b, 0, 0))
    fc_x = lax.ppermute(pick(fc_part, 1 - x_at), "x", shift_perm(n_x, 1))
    fc_part, dnorm_part = after(fc_part, dnorm_part)
    dnorm_two = group_scatter(dnorm_part.reshape(8, slot_len, wide), 7)

    def over_h(value):
        gives = [pick(value, lax.rem(h_at + step, n_h)) for step in range(1, n_h)]
        return [lax.ppermute(give, "h", shift_perm(n_h, step + 1)) for step, give in enumerate(gives)]

    def total(value, received):
        value = pick(value, h_at).astype(F32)
        for other in received:
            value = value + other
        return value.astype(B16).reshape(4, tall, ff_own)

    proj_x, mlp_part, dnorm_two = after((proj_x, mlp_part), dnorm_two, True)
    proj_line = pick(proj_part, x_at) + proj_x
    proj_h = over_h(proj_line)
    mlp = lax.psum_scatter(mlp_part, FFG, scatter_dimension=0, tiled=True)
    dhidden, dhidden_b, token_sums, dattention = hidden_back(
        dnorm_two, hidden, grad_own, w_out, singles, mask, rows, feats, padded
    )
    c_at = lax.axis_index("c")
    out_give = dot(jnp.where(c_at == 0, by_core[1], by_core[0]), dhidden_b, 0, 0).astype(B16)
    out_give = lax.ppermute(out_give, "c", shift_perm(2, 1))
    out_keep = dot(jnp.where(c_at == 0, by_core[0], by_core[1]), dhidden_b, 0, 0).astype(B16)
    dattention = to_heads(dattention, n_slot).reshape(n_slot * slot_len, pair)
    out_give, fc_x, dattention = after((out_give, fc_x), dattention, True)
    out_part = (out_keep + out_give).reshape(n_shard // 2, tall, wide)
    fc_line = pick(fc_part, x_at) + fc_x
    fc_h = over_h(fc_line)
    dqkv = attend_back(inv, low, qkv, heads_out, dattention, lse, start3, slot_len, head)
    dnorm_one_part, dqkv_b, gain_sum, shift_sum, pair_sum = project_back(all_input, dqkv, mask, w_qkv, feats)
    qkv_part = dot(norm_one, dqkv_b, 0, 0).astype(B16).reshape(n_x, n_ctx, tall, 3 * pair)
    proj_h, fc_h, dnorm_one_part = after((proj_h, fc_h), dnorm_one_part, True)
    dnorm_one, qkv_all, out_all, fc_all, proj_all, owned, pair_sums, ff_sums = closing(
        dnorm_one_part.reshape(n_slot, slot_len, wide), qkv_part, out_part, total(fc_line, fc_h), total(proj_line, proj_h),
        token_sums, gain_sum, shift_sum, pair_sum, dpreact_sum,
    )
    mlp, dnorm_one = after(mlp, dnorm_one)
    qkv_grad, out_grad_w, fc_grad, proj_grad, block_output, input_grad = deliver(
        qkv_all, out_all, fc_all, proj_all, mlp, hidden, dnorm_one, dhidden, own_input, singles, mask, rows, feats
    )
    fc_bias_grad = ff_sums.reshape(4, 1024)[:, :ff_own].reshape(4 * ff_own)
    pair_sums = pair_sums.transpose(2, 1, 0, 3).reshape(2, padded)[:, :feats].reshape(2 * feats)
    qv_grad = lax.dynamic_slice_in_dim(pair_sums, lax.axis_index(SHARD) * 2 * rows, 2 * rows, 0)

    def own(index):
        return owned[index, :rows]

    return (
        block_output.T[None],
        input_grad.T[None],
        qkv_grad,
        qv_grad,
        out_grad_w,
        own(0),
        own(4),
        own(5),
        own(1),
        own(2),
        fc_grad,
        fc_bias_grad,
        proj_grad.T,
        own(3),
    )


def solution(mesh):
    n_x, n_ctx, n_y = (mesh.shape[axis] for axis in ("dp", "context", "tensor"))
    inner = Mesh(mesh.devices.reshape(n_x, n_ctx // 4, 2, 2, n_y), ("x", "h", "l", "c", "y"))
    tokens = P("x", ROW, None)
    shard = P(SHARD)
    shard_rows = P(SHARD, None)
    return jax.shard_map(
        functools.partial(on_device, (n_x, n_ctx, n_y)),
        mesh=inner,
        in_specs=(
            tokens, P("x", None), P("x", None), shard, shard, shard_rows, shard, shard_rows, shard, shard, shard,
            P(SHARD, "y"), P("y"), P("y", SHARD), shard, tokens,
        ),
        out_specs=(
            tokens, tokens, shard_rows, shard, shard_rows, shard, shard, shard, shard, shard,
            P(SHARD, "y"), P("y"), P("y", SHARD), shard,
        ),
        check_vma=False,
    )
```

```python
import functools
import math

import jax
import jax.numpy as jnp
import numpy as np
from jax import lax
from jax.experimental import pallas as pl
from jax.experimental.layout import Layout, with_layout_constraint
from jax.experimental.pallas import tpu as pltpu
from jax.sharding import Mesh
from jax.sharding import PartitionSpec as P

HEADS = 25
DOCS = 8
NORM_EPS = 1e-05
GELU_SCALE = 0.7978845608028654
GELU_CUBE = 0.044715
MASK_FLOOR = -1e30

F32 = jnp.float32
B16 = jnp.bfloat16
BLK = 256
VMEM_LIMIT = 60 * 1024 * 1024

ROW = ("h", "l", "c", "y")
CTX = ("h", "l", "c")
SHARD = ("x", "h", "l", "c")
FFG = ("l", "c", "y")


def gelu_parts(values):
    inner_arg = GELU_SCALE * (values + GELU_CUBE * values * values * values)
    tanh_value = jnp.tanh(inner_arg)
    result = 0.5 * values * (1.0 + tanh_value)
    derivative = 0.5 * (1.0 + tanh_value) + 0.5 * values * (
        1.0 - tanh_value * tanh_value
    ) * GELU_SCALE * (1.0 + 3.0 * GELU_CUBE * values * values)
    return (result, derivative)


def norm_forward(values, mask, feats):
    mean_value = jnp.sum(values, axis=-1, keepdims=True) / feats
    centered = (values - mean_value) * mask
    inv_sigma = lax.rsqrt(jnp.sum(centered * centered, axis=-1, keepdims=True) / feats + NORM_EPS)
    return (centered * inv_sigma, inv_sigma)


def norm_backward(upstream, normed, inv_sigma, norm_gain, feats):
    scaled = upstream * norm_gain
    return inv_sigma * (
        scaled
        - jnp.sum(scaled, axis=-1, keepdims=True) / feats
        - normed * (jnp.sum(scaled * normed, axis=-1, keepdims=True) / feats)
    )


def dot(left, right, left_dim, right_dim):
    return lax.dot_general(
        left, right, (((left_dim,), (right_dim,)), ((), ())), preferred_element_type=F32
    )


def sort_slots(inv_ref, src_ref, dst_ref, slot_len, start=0, width=None, factor=None):
    width = src_ref.shape[1] if width is None else width

    def body(piece, carry):
        slot = inv_ref[piece]
        rows = src_ref[pl.ds(pl.multiple_of(slot * slot_len, slot_len), slot_len), start : start + width]
        if factor is not None:
            rows = rows * jnp.asarray(factor, rows.dtype)
        dst_ref[pl.ds(pl.multiple_of(piece * slot_len, slot_len), slot_len), :] = rows
        return carry

    lax.fori_loop(0, src_ref.shape[0] // slot_len, body, 0)


def unsort_block(inv_ref, dst_ref, value, block, slot_len):
    for part in range(BLK // slot_len):
        slot = inv_ref[block * (BLK // slot_len) + part]
        dst_ref[pl.ds(pl.multiple_of(slot * slot_len, slot_len), slot_len), :] = value[
            part * slot_len : (part + 1) * slot_len
        ].astype(dst_ref.dtype)


def block_rows(block):
    return pl.ds(pl.multiple_of(block * BLK, BLK), BLK)


def mask_of(start_row, first, query_block, diagonal):
    key_at = first * BLK + lax.broadcasted_iota(jnp.int32, (2 * BLK, BLK), 0)
    allowed = key_at >= start_row
    if diagonal:
        query_at = query_block * BLK + lax.broadcasted_iota(jnp.int32, (2 * BLK, BLK), 1)
        allowed = jnp.logical_and(allowed, key_at <= query_at)
    return allowed


def two_rows(first):
    return block_rows(jnp.maximum(first, 0)), block_rows(first + 1)


def over_pairs(low, block, step, state):
    earlier = (block - low) // 2
    state = lax.fori_loop(0, earlier, lambda t, s: step(block - 1 - 2 * (earlier - t), s, False), state)
    return step(block - 1, state, True)


def attend_kernel(slot_len, head, inv_ref, low_ref, qkv_ref, start_ref, out_ref, lse_ref, q_s, k_s, vt_s):
    total = qkv_ref.shape[0]
    pair = 2 * head
    sort_slots(inv_ref, qkv_ref, q_s, slot_len, 0, pair, 1.0 / math.sqrt(head))
    sort_slots(inv_ref, qkv_ref, k_s, slot_len, pair, pair)

    def fill(piece, carry):
        slot = inv_ref[piece]
        rows = qkv_ref[pl.ds(pl.multiple_of(slot * slot_len, slot_len), slot_len), 2 * pair :]
        vt_s[:, pl.ds(pl.multiple_of(piece * slot_len, slot_len), slot_len)] = rows.astype(F32).T.astype(B16)
        return carry

    lax.fori_loop(0, total // slot_len, fill, 0)

    def per_query(block, carry):
        queries = q_s[block_rows(block), :]
        start_row = start_ref[block]

        def step(first, state, diagonal):
            allowed = mask_of(start_row, first, block, diagonal)
            rows = two_rows(first)
            keys = jnp.concatenate([k_s[r, :] for r in rows], axis=0)
            values = jnp.concatenate([vt_s[:, r] for r in rows], axis=1)
            fresh = []
            for part in range(2):
                old_max, old_sum, old_acc = state[part]
                cols = slice(part * head, (part + 1) * head)
                scores = dot(keys[:, cols], queries[:, cols], 1, 1)
                scores = jnp.where(allowed, scores, MASK_FLOOR)
                new_max = jnp.maximum(old_max, jnp.max(scores, axis=0, keepdims=True))
                weights = jnp.where(allowed, jnp.exp(scores - new_max), 0.0)
                shrink = jnp.exp(old_max - new_max)
                new_sum = old_sum * shrink + jnp.sum(weights, axis=0, keepdims=True)
                new_acc = old_acc * shrink + dot(values[cols, :], weights.astype(B16), 1, 0)
                fresh.append((new_max, new_sum, new_acc))
            return tuple(fresh)

        first = tuple(
            (
                jnp.full((1, BLK), MASK_FLOOR, F32),
                jnp.zeros((1, BLK), F32),
                jnp.zeros((head, BLK), F32),
            )
            for part in range(2)
        )
        state = over_pairs(low_ref[block], block, step, first)
        lse_ref[block] = jnp.concatenate([s[0] + jnp.log(s[1]) for s in state], axis=0)
        result = jnp.concatenate([s[2] / s[1] for s in state], axis=0)
        unsort_block(inv_ref, out_ref, result.T, block, slot_len)
        return carry

    lax.fori_loop(0, total // BLK, per_query, 0)


def attend(inv, low, qkv, start3, slot_len, head):
    total = qkv.shape[0]
    vmem = pl.BlockSpec(memory_space=pltpu.VMEM)
    smem = pl.BlockSpec(memory_space=pltpu.SMEM)
    return pl.pallas_call(
        functools.partial(attend_kernel, slot_len, head),
        out_shape=(
            jax.ShapeDtypeStruct((total, 2 * head), B16),
            jax.ShapeDtypeStruct((total // BLK, 2, BLK), F32),
        ),
        in_specs=[smem, smem, vmem, vmem],
        out_specs=(vmem, vmem),
        scratch_shapes=[
            pltpu.VMEM((total, 2 * head), B16),
            pltpu.VMEM((total, 2 * head), B16),
            pltpu.VMEM((2 * head, total), B16),
        ],
        compiler_params=pltpu.CompilerParams(vmem_limit_bytes=VMEM_LIMIT),
        name="attend",
    )(inv, low, qkv, start3)


def attend_back_kernel(
    slot_len, head, inv_ref, low_ref, qkv_ref, out_ref, grad_ref, lse_ref, start_ref,
    dqkv_ref, q_s, k_s, v_s, kt_s, o_s, g_s, dk_s, dv_s,
):
    total = qkv_ref.shape[0]
    pair = 2 * head
    scale = 1.0 / math.sqrt(head)
    sort_slots(inv_ref, qkv_ref, q_s, slot_len, 0, pair, scale)
    sort_slots(inv_ref, qkv_ref, k_s, slot_len, pair, pair)
    sort_slots(inv_ref, qkv_ref, v_s, slot_len, 2 * pair, pair)
    sort_slots(inv_ref, out_ref, o_s, slot_len)
    sort_slots(inv_ref, grad_ref, g_s, slot_len)

    def fill(block, carry):
        kt_s[:, block_rows(block)] = k_s[block_rows(block), :].astype(F32).T.astype(B16)
        return carry

    lax.fori_loop(0, total // BLK, fill, 0)
    dk_s[...] = jnp.zeros_like(dk_s)
    dv_s[...] = jnp.zeros_like(dv_s)

    def per_query(block, carry):
        queries = q_s[block_rows(block), :]
        grads = g_s[block_rows(block), :]
        start_row = start_ref[block]
        lse = lse_ref[block]
        prod = (grads.astype(F32) * o_s[block_rows(block), :].astype(F32)).T
        delta = [jnp.sum(prod[part * head : (part + 1) * head], axis=0, keepdims=True) for part in range(2)]

        def step(first, state, diagonal):
            allowed = mask_of(start_row, first, block, diagonal)
            rows = two_rows(first)
            keys = jnp.concatenate([k_s[r, :] for r in rows], axis=0)
            values = jnp.concatenate([v_s[r, :] for r in rows], axis=0)
            flipped = jnp.concatenate([kt_s[:, r] for r in rows], axis=1)
            fresh, dks, dvs = [], [], []
            for part in range(2):
                cols = slice(part * head, (part + 1) * head)
                scores = dot(keys[:, cols], queries[:, cols], 1, 1)
                weights = jnp.where(allowed, jnp.exp(scores - lse[part : part + 1]), 0.0)
                dprob = dot(values[:, cols], grads[:, cols], 1, 1)
                dscore = (weights * (dprob - delta[part])).astype(B16)
                dvs.append(dot(weights.astype(B16), grads[:, cols], 1, 0))
                dks.append(dot(dscore, queries[:, cols], 1, 0))
                fresh.append(state[part] + dot(flipped[cols, :], dscore, 1, 0))
            dk, dv = jnp.concatenate(dks, axis=1), jnp.concatenate(dvs, axis=1)
            for i, r in enumerate(rows):
                dk_s[r, :] += dk[i * BLK : (i + 1) * BLK]
                dv_s[r, :] += dv[i * BLK : (i + 1) * BLK]
            return tuple(fresh)

        state = (jnp.zeros((head, BLK), F32), jnp.zeros((head, BLK), F32))
        state = over_pairs(low_ref[block], block, step, state)
        dq = jnp.concatenate(state, axis=0).T * scale
        for part in range(BLK // slot_len):
            slot = inv_ref[block * (BLK // slot_len) + part]
            dqkv_ref[pl.ds(pl.multiple_of(slot * slot_len, slot_len), slot_len), 0:pair] = dq[
                part * slot_len : (part + 1) * slot_len
            ]
        return carry

    lax.fori_loop(0, total // BLK, per_query, 0)

    def give(piece, carry):
        slot = inv_ref[piece]
        rows = pl.ds(pl.multiple_of(slot * slot_len, slot_len), slot_len)
        held = pl.ds(pl.multiple_of(piece * slot_len, slot_len), slot_len)
        dqkv_ref[rows, pair : 2 * pair] = dk_s[held, :]
        dqkv_ref[rows, 2 * pair :] = dv_s[held, :]
        return carry

    lax.fori_loop(0, total // slot_len, give, 0)


def attend_back(inv, low, qkv, out, grad, lse, start3, slot_len, head):
    total = qkv.shape[0]
    pair = 2 * head
    vmem = pl.BlockSpec(memory_space=pltpu.VMEM)
    smem = pl.BlockSpec(memory_space=pltpu.SMEM)
    held = pltpu.VMEM((total, pair), B16)
    return pl.pallas_call(
        functools.partial(attend_back_kernel, slot_len, head),
        out_shape=jax.ShapeDtypeStruct((total, 3 * pair), F32),
        in_specs=[smem, smem] + [vmem] * 5,
        out_specs=vmem,
        scratch_shapes=[
            held, held, held, pltpu.VMEM((pair, total), B16), held, held,
            pltpu.VMEM((total, pair), F32), pltpu.VMEM((total, pair), F32),
        ],
        compiler_params=pltpu.CompilerParams(vmem_limit_bytes=VMEM_LIMIT),
        name="attend_back",
    )(inv, low, qkv, out, grad, lse, start3)


class Place:
    def __init__(self, whole_line):
        self.x, self.h, self.l, self.c, self.y = (lax.axis_index(a) for a in ("x", "h", "l", "c", "y"))
        self.whole_line = whole_line
        self.n_z = 2 * lax.axis_size("h") if whole_line else 2
        self.z = self.h * 2 + self.l if whole_line else self.l
        self.ctx = self.z * 2 + self.c
        self.slot = self.ctx * 2 + self.y

    def at_z(self, z):
        return {"h": z // 2, "l": lax.rem(z, 2)} if self.whole_line else {"l": z}

    def at_ctx(self, k):
        return dict(self.at_z(k // 2), c=lax.rem(k, 2))

    def at_slot(self, s):
        return dict(self.at_ctx(s // 2), y=lax.rem(s, 2))

    def far_z(self):
        order = []
        for step in range(1, self.n_z // 2 + 1):
            order += [step] if 2 * step == self.n_z else [step, self.n_z - step]
        return [lax.rem(self.z + step, self.n_z) for step in order]

    def slot_of(self, z, c, y):
        return (z * 2 + c) * 2 + y


class Copies:
    def __init__(self, sems):
        self.sems = sems
        self.begun = []

    def send(self, src, dst, recv, peer, when=None):
        at = len(self.begun)
        copy = pltpu.make_async_remote_copy(
            src_ref=src,
            dst_ref=dst,
            send_sem=self.sems.at[at],
            recv_sem=recv,
            device_id=peer,
            device_id_type=pl.DeviceIdType.MESH,
        )
        if when is None:
            copy.start()
            self.begun.append(copy.wait_send)
        else:
            pl.when(when)(copy.start)
            self.begun.append(lambda: pl.when(when)(copy.wait_send))

    def local(self, src, dst, sem=None):
        copy = pltpu.make_async_copy(src, dst, self.sems.at[len(self.begun)] if sem is None else sem)
        copy.start()
        if sem is None:
            self.begun.append(copy.wait)
        return copy

    def arrived(self, dst, recv, peer):
        pltpu.make_async_remote_copy(
            src_ref=dst,
            dst_ref=dst,
            send_sem=self.sems.at[0],
            recv_sem=recv,
            device_id=peer,
            device_id_type=pl.DeviceIdType.MESH,
        ).wait_recv()

    def finish(self):
        for wait in self.begun:
            wait()


def meet(peers):
    barrier = pltpu.get_barrier_semaphore()
    for peer in peers:
        pl.semaphore_signal(barrier, inc=1, device_id=peer, device_id_type=pl.DeviceIdType.MESH)
    pl.semaphore_wait(barrier, len(peers))


def others(me, count):
    return [lax.rem(me + step, count) for step in range(1, count)]


ANY = pl.BlockSpec(memory_space=pl.ANY)
IN_VMEM = pl.BlockSpec(memory_space=pltpu.VMEM)


def dma_sems(*counts):
    return [pltpu.SemaphoreType.DMA((count,)) for count in counts]


def comm_params(collective_id):
    return pltpu.CompilerParams(
        collective_id=collective_id, has_side_effects=True, vmem_limit_bytes=VMEM_LIMIT
    )


class Line:
    def __init__(self, place, copies, block):
        self.place, self.copies, self.block = place, copies, block

    def pass_on(self, src, z, step, when):
        p = self.place
        ref, sem = self.block(z)
        peer = p.at_z(jnp.clip(p.z + step, 0, p.n_z - 1))
        self.copies.send(ref if src is None else src, ref, sem, peer, when)

    def begin(self, own):
        p = self.place
        self.pass_on(own, p.z, 1, p.z < p.n_z - 1)
        self.pass_on(own, p.z, -1, p.z > 0)

    def arrive(self, distance, then):
        p = self.place
        for side in (1, -1):
            z = p.z + side * distance
            here = jnp.logical_and(z >= 0, z < p.n_z)
            z = jnp.clip(z, 0, p.n_z - 1)
            ref, sem = self.block(z)
            peer = p.at_z(jnp.clip(p.z + side, 0, p.n_z - 1))
            pl.when(here)(lambda: self.copies.arrived(ref, sem, peer))
            beyond = p.z - side
            beyond = jnp.logical_and(beyond >= 0, beyond < p.n_z)
            self.pass_on(None, z, -side, jnp.logical_and(here, beyond))
            then(z, here)


def row_line(place, out, copies, recv):
    def block(z):
        at = place.slot_of(z, place.c, place.y)
        return out.at[at], recv.at[at]

    return Line(place, copies, block)


def gather_begin(place, own, out, copies, recv):
    peer_y, peer_c = {"y": 1 - place.y}, {"c": 1 - place.c}
    copies.local(own, out.at[place.slot])
    line = row_line(place, out, copies, recv)
    line.begin(own)
    copies.send(own, out.at[place.slot], recv.at[place.slot], peer_y)
    copies.send(own, out.at[place.slot], recv.at[place.slot], peer_c)
    return line


def gather_step(place, line, copies, distance):
    def then(z, here):
        ref, sem = line.block(z)
        copies.send(ref, ref, sem, {"y": 1 - place.y}, here)
        copies.send(ref, ref, sem, {"c": 1 - place.c}, here)

    line.arrive(distance, then)


def gather_cross(place, out, copies, recv):
    for z in [place.z] + place.far_z():
        at = place.slot_of(z, place.c, 1 - place.y)
        copies.arrived(out.at[at], recv.at[at], {"y": 1 - place.y})
        copies.send(out.at[at], out.at[at], recv.at[at], {"c": 1 - place.c})


def gather_end(place, out, copies, recv):
    for z in [place.z] + place.far_z():
        for y in (place.y, 1 - place.y):
            at = place.slot_of(z, 1 - place.c, y)
            copies.arrived(out.at[at], recv.at[at], {"c": 1 - place.c})


def gather_copies(n_z):
    return 7 * n_z


def group_gather_kernel(own, out, send, recv):
    place = Place(False)
    copies = Copies(send)
    peer_z, peer_y, peer_c = place.at_z(1 - place.z), {"y": 1 - place.y}, {"c": 1 - place.c}
    meet([peer_z, peer_y, peer_c])
    rows = own.shape[0] // 2

    def part(at, half):
        return out.at[at, pl.ds(half * rows, rows)], recv.at[2 * at + half]

    def give(at, half, peer, src=None):
        ref, sem = part(at, half)
        copies.send(ref if src is None else src, ref, sem, peer)

    def got(at, half, peer):
        ref, sem = part(at, half)
        copies.arrived(ref, sem, peer)

    for half in range(2):
        src = own.at[pl.ds(half * rows, rows)]
        other = own.at[pl.ds((1 - half) * rows, rows)]
        give(place.slot, half, peer_y, src)
        give(place.slot, 1 - half, peer_z, other)
    copies.local(own, out.at[place.slot])
    for half in range(2):
        give(place.slot, half, peer_c, own.at[pl.ds(half * rows, rows)])
    near_y = place.slot_of(place.z, place.c, 1 - place.y)
    near_z = place.slot_of(1 - place.z, place.c, place.y)
    across = place.slot_of(1 - place.z, place.c, 1 - place.y)
    got(near_y, 0, peer_y)
    give(near_y, 0, peer_z)
    got(near_z, 1, peer_z)
    give(near_z, 1, peer_y)
    give(near_y, 0, peer_c)
    give(near_z, 1, peer_c)
    got(near_y, 1, peer_y)
    give(near_y, 1, peer_c)
    got(near_z, 0, peer_z)
    give(near_z, 0, peer_c)
    got(across, 0, peer_z)
    give(across, 0, peer_c)
    got(across, 1, peer_y)
    give(across, 1, peer_c)
    for z in range(2):
        for y in range(2):
            for half in range(2):
                got(place.slot_of(z, 1 - place.c, y), half, peer_c)
    copies.finish()


def group_gather(value, collective_id):
    return pl.pallas_call(
        group_gather_kernel,
        out_shape=jax.ShapeDtypeStruct((8,) + value.shape, value.dtype),
        in_specs=[ANY],
        out_specs=ANY,
        scratch_shapes=dma_sems(16, 16),
        compiler_params=comm_params(collective_id),
        name="group_gather",
    )(value)


def opening_kernel(
    own, blocks, ffn, out_w, out, blocks_all, ffn_all, out_w_all, send, recv, recv_w, recv_f, recv_o
):
    place, group = Place(True), Place(False)
    n_ctx = blocks.shape[0]
    copies = Copies(send)
    peer_x, peer_y = {"x": 1 - place.x}, {"y": 1 - place.y}
    far_ctx = others(place.ctx, n_ctx)
    meet([place.at_ctx(k) for k in far_ctx] + [peer_y, peer_x])
    mine = blocks_all.at[place.x, place.ctx]
    half = out_w.shape[1] // 2

    def sem_w(x, k):
        return recv_w.at[x * n_ctx + k]

    def out_block(z, x=place.x):
        at = x * place.n_z + z
        return out_w_all.at[at], recv_o.at[at]

    line = gather_begin(place, own, out, copies, recv)
    for k in far_ctx:
        copies.send(blocks.at[k], mine, sem_w(place.x, place.ctx), place.at_ctx(k))
    copies.local(blocks.at[place.ctx], mine)
    copies.send(blocks.at[place.ctx], mine, sem_w(place.x, place.ctx), peer_x)
    own_out, own_sem = out_block(place.z)
    own_half = out_w.at[:, pl.ds(pl.multiple_of(place.y * half, half), half)]
    copies.local(own_half, own_out)
    out_line = Line(place, copies, out_block)

    def out_over_x(z, here):
        ref, sem = out_block(z)
        copies.send(ref, ref, sem, peer_x, here)

    for distance in range(1, place.n_z):
        gather_step(place, line, copies, distance)
        if distance == 1:
            out_line.begin(own_half)
            copies.send(own_half, own_out, own_sem, peer_x)
            copies.local(ffn.at[:, group.ctx], ffn_all.at[:, group.ctx])
        if distance == 2:
            for k in others(group.ctx, 4):
                copies.send(ffn.at[:, k], ffn_all.at[:, group.ctx], recv_f.at[group.ctx], group.at_ctx(k))
        if distance > 1:
            out_line.arrive(distance - 1, out_over_x)
    out_line.arrive(place.n_z - 1, out_over_x)
    for k in far_ctx:
        block = blocks_all.at[place.x, k]
        copies.arrived(block, sem_w(place.x, k), place.at_ctx(k))
        copies.send(block, block, sem_w(place.x, k), peer_x)
    gather_cross(place, out, copies, recv)
    gather_end(place, out, copies, recv)
    for k in [place.ctx] + far_ctx:
        copies.arrived(blocks_all.at[1 - place.x, k], sem_w(1 - place.x, k), peer_x)
    for k in others(group.ctx, 4):
        copies.arrived(ffn_all.at[:, k], recv_f.at[k], group.at_ctx(k))
    for z in [place.z] + place.far_z():
        ref, sem = out_block(z, 1 - place.x)
        copies.arrived(ref, sem, peer_x)
    copies.finish()


def opening(own, blocks, ffn, out_w):
    n_ctx = blocks.shape[0]
    n_z = n_ctx // 2
    sends = gather_copies(n_z) + 2 * n_ctx + 4 + 5 * n_z
    return pl.pallas_call(
        opening_kernel,
        out_shape=(
            jax.ShapeDtypeStruct((2 * n_ctx,) + own.shape, own.dtype),
            jax.ShapeDtypeStruct((2,) + blocks.shape, blocks.dtype),
            jax.ShapeDtypeStruct(ffn.shape, ffn.dtype),
            jax.ShapeDtypeStruct((n_ctx, out_w.shape[0], out_w.shape[1] // 2), out_w.dtype),
        ),
        in_specs=[ANY] * 4,
        out_specs=(ANY,) * 4,
        scratch_shapes=dma_sems(sends, 2 * n_ctx, 2 * n_ctx, 4, n_ctx),
        compiler_params=comm_params(1),
        name="opening",
    )(own, blocks, ffn, out_w)


def to_tokens_kernel(src, dst, send, recv):
    place = Place(True)
    copies = Copies(send)
    count, width = src.shape[0], src.shape[2]
    far = others(place.slot, count)
    meet([place.at_slot(s) for s in far])

    def columns(s):
        return dst.at[:, pl.ds(pl.multiple_of(s * width, width), width)]

    for s in far:
        copies.send(src.at[s], columns(place.slot), recv.at[place.slot], place.at_slot(s))
    copies.local(src.at[place.slot], columns(place.slot))
    for s in far:
        copies.arrived(columns(s), recv.at[s], place.at_slot(s))
    copies.finish()


def to_tokens(value):
    count, tokens, width = value.shape
    return pl.pallas_call(
        to_tokens_kernel,
        out_shape=jax.ShapeDtypeStruct((tokens, count * width), value.dtype),
        in_specs=[ANY],
        out_specs=ANY,
        scratch_shapes=dma_sems(count, count),
        compiler_params=comm_params(2),
        name="to_tokens",
    )(value)


def to_heads_kernel(src, dst, send, recv):
    place = Place(True)
    copies = Copies(send)
    count, width = dst.shape[0], dst.shape[2]
    far = others(place.slot, count)
    meet([place.at_slot(s) for s in far])

    def columns(s):
        return src.at[:, pl.ds(pl.multiple_of(s * width, width), width)]

    for s in far:
        copies.send(columns(s), dst.at[place.slot], recv.at[place.slot], place.at_slot(s))
    copies.local(columns(place.slot), dst.at[place.slot])
    for s in far:
        copies.arrived(dst.at[s], recv.at[s], place.at_slot(s))
    copies.finish()


def to_heads(value, count):
    tokens, width = value.shape[0], value.shape[1] // count
    return pl.pallas_call(
        to_heads_kernel,
        out_shape=jax.ShapeDtypeStruct((count, tokens, width), value.dtype),
        in_specs=[ANY],
        out_specs=ANY,
        scratch_shapes=dma_sems(count, count),
        compiler_params=comm_params(3),
        name="to_heads",
    )(value)


class Scatter:
    def __init__(self, place, part, held, from_c, from_y, from_z, out, copies, loads, rc, ry, rz):
        self.__dict__.update(locals())

    def order(self):
        return self.place.far_z() + [self.place.z]

    def begin(self):
        p = self.place
        for y in (1 - p.y, p.y):
            for z in self.order():
                at = z * 2 + y
                self.copies.send(
                    self.part.at[p.slot_of(z, 1 - p.c, y)], self.from_c.at[at], self.rc.at[at], {"c": 1 - p.c}
                )
        self.queue = [(z, y) for y in (1 - p.y, p.y) for z in self.order()]
        for at in range(min(self.held.shape[0], len(self.queue))):
            self.load(at)

    def load(self, at):
        p = self.place
        z, y = self.queue[at]
        at = at % self.held.shape[0]
        self.copies.local(self.part.at[p.slot_of(z, p.c, y)], self.held.at[at], self.loads.at[at])

    def add_c(self, step):
        z, y = self.queue[step]
        at, depth = z * 2 + y, self.held.shape[0]
        own = step % depth
        self.copies.arrived(self.from_c.at[at], self.rc.at[at], {"c": 1 - self.place.c})
        pltpu.make_async_copy(self.held.at[own], self.held.at[own], self.loads.at[own]).wait()
        self.from_c[at] = self.from_c[at] + self.held[own]
        if step + depth < len(self.queue):
            self.load(step + depth)

    def over_c_far(self):
        p = self.place
        for step, z in enumerate(self.order()):
            self.add_c(step)
            self.copies.send(self.from_c.at[z * 2 + 1 - p.y], self.from_y.at[z], self.ry.at[z], {"y": 1 - p.y})

    def over_c_near(self):
        for step in range(self.place.n_z):
            self.add_c(self.place.n_z + step)

    def over_y(self):
        p = self.place
        for z in self.order():
            self.copies.arrived(self.from_y.at[z], self.ry.at[z], {"y": 1 - p.y})
            self.from_y[z] = self.from_y[z] + self.from_c[z * 2 + p.y]
            if z is not p.z:
                self.copies.send(self.from_y.at[z], self.from_z.at[p.z], self.rz.at[p.z], p.at_z(z))

    def over_z(self):
        p = self.place
        total = self.from_y[p.z].astype(F32)
        for z in p.far_z():
            self.copies.arrived(self.from_z.at[z], self.rz.at[z], p.at_z(z))
            total = total + self.from_z[z].astype(F32)
        self.out[...] = total


def scatter_scratch(n_z, block):
    return [
        pltpu.VMEM((min(8, 2 * n_z),) + block, B16),
        pltpu.VMEM((2 * n_z,) + block, B16),
        pltpu.VMEM((n_z,) + block, B16),
        pltpu.VMEM((n_z,) + block, B16),
    ]


def scatter_sems(n_z, more=0):
    return dma_sems(4 * n_z + more, min(8, 2 * n_z), 2 * n_z, n_z, n_z)


def group_scatter_kernel(part, out, held, from_c, over_y, over_z, last, send, loads, rc, ry, rz, rl):
    place = Place(False)
    copies = Copies(send)
    peer_z, peer_y, peer_c = place.at_z(1 - place.z), {"y": 1 - place.y}, {"c": 1 - place.c}
    meet([peer_z, peer_y, peer_c])
    rows = part.shape[1] // 2
    first, second = slice(0, rows), slice(rows, 2 * rows)
    own_y, far_y, own_z, far_z = place.y, 1 - place.y, place.z, 1 - place.z
    order = [(far_z, far_y), (far_z, own_y), (own_z, far_y), (own_z, own_y)]
    for z, y in order:
        at = z * 2 + y
        copies.send(part.at[place.slot_of(z, 1 - place.c, y)], from_c.at[at], rc.at[at], peer_c)
        copies.local(part.at[place.slot_of(z, place.c, y)], held.at[at], loads.at[at])

    def over_c(z, y):
        at = z * 2 + y
        copies.arrived(from_c.at[at], rc.at[at], peer_c)
        pltpu.make_async_copy(held.at[at], held.at[at], loads.at[at]).wait()
        from_c[at] = from_c[at] + held[at]
        return from_c.at[at]

    across = over_c(far_z, far_y)
    copies.send(across.at[first], over_y, ry.at[0], peer_y)
    copies.send(across.at[second], over_z, rz.at[0], peer_z)
    beside_z = over_c(far_z, own_y)
    copies.send(beside_z.at[second], last.at[0], rl.at[0], peer_z)
    beside_y = over_c(own_z, far_y)
    copies.send(beside_y.at[first], last.at[1], rl.at[1], peer_y)
    copies.arrived(over_y, ry.at[0], peer_y)
    over_y[...] = over_y[...] + beside_z[first, :]
    copies.send(over_y, last.at[2], rl.at[2], peer_z)
    copies.arrived(over_z, rz.at[0], peer_z)
    over_z[...] = over_z[...] + beside_y[second, :]
    copies.send(over_z, last.at[3], rl.at[3], peer_y)
    mine = over_c(own_z, own_y)
    copies.arrived(last.at[1], rl.at[1], peer_y)
    copies.arrived(last.at[0], rl.at[0], peer_z)
    copies.arrived(last.at[2], rl.at[2], peer_z)
    out[first, :] = mine[first, :].astype(F32) + last[1].astype(F32) + last[2].astype(F32)
    copies.arrived(last.at[3], rl.at[3], peer_y)
    out[second, :] = mine[second, :].astype(F32) + last[0].astype(F32) + last[3].astype(F32)
    copies.finish()


def group_scatter(part, collective_id):
    block = part.shape[1:]
    half = (block[0] // 2, block[1])
    return pl.pallas_call(
        group_scatter_kernel,
        out_shape=jax.ShapeDtypeStruct(block, F32),
        in_specs=[ANY],
        out_specs=IN_VMEM,
        scratch_shapes=[
            pltpu.VMEM((4,) + block, B16),
            pltpu.VMEM((4,) + block, B16),
            pltpu.VMEM(half, B16),
            pltpu.VMEM(half, B16),
            pltpu.VMEM((4,) + half, B16),
        ]
        + dma_sems(10, 4, 4, 1, 1, 4),
        compiler_params=comm_params(collective_id),
        name="group_scatter",
    )(part)


class OutScatter:
    def __init__(self, place, part, held, from_x, from_y, from_z, out, copies, loads, rx, ry, rz, rg):
        self.__dict__.update(locals())
        self.half = out.shape[2]

    def order(self):
        return self.place.far_z() + [self.place.z]

    def columns(self, y):
        return pl.ds(pl.multiple_of(y * self.half, self.half), self.half)

    def begin(self):
        p = self.place
        for z in self.order():
            self.copies.send(self.part.at[(1 - p.x) * p.n_z + z], self.from_x.at[z], self.rx.at[z], {"x": 1 - p.x})
            self.copies.local(self.part.at[p.x * p.n_z + z], self.held.at[z], self.loads.at[z])

    def over_x(self):
        p = self.place
        for z in self.order():
            self.copies.arrived(self.from_x.at[z], self.rx.at[z], {"x": 1 - p.x})
            pltpu.make_async_copy(self.held.at[z], self.held.at[z], self.loads.at[z]).wait()
            self.from_x[z] = self.from_x[z] + self.held[z]
            self.copies.send(
                self.from_x.at[z, :, self.columns(1 - p.y)], self.from_y.at[z], self.ry.at[z], {"y": 1 - p.y}
            )

    def over_y(self):
        p = self.place
        for z in self.order():
            self.copies.arrived(self.from_y.at[z], self.ry.at[z], {"y": 1 - p.y})
            self.from_y[z] = self.from_y[z] + self.from_x[z, :, self.columns(p.y)]
            if z is not p.z:
                self.copies.send(self.from_y.at[z], self.from_z.at[p.z], self.rz.at[p.z], p.at_z(z))

    def over_z(self):
        p = self.place
        total = self.from_y[p.z].astype(F32)
        for z in p.far_z():
            self.copies.arrived(self.from_z.at[z], self.rz.at[z], p.at_z(z))
            total = total + self.from_z[z].astype(F32)
        self.out[p.y] = total.astype(B16)
        self.copies.send(self.out.at[p.y], self.out.at[p.y], self.rg.at[p.y], {"y": 1 - p.y})

    def end(self):
        p = self.place
        self.copies.arrived(self.out.at[1 - p.y], self.rg.at[1 - p.y], {"y": 1 - p.y})


def closing_kernel(
    part, grads, out_part, fc, proj, sums_in, gain_in, shift_in, pair_in, ff_in,
    out, grads_out, out_w_out, fc_out, proj_out, owned, pairs_out, ff_out,
    held, from_c, from_y, from_z, own_x, from_x, o_held, o_x, o_y, o_z,
    send, loads, rc, ry, rz, load_x, rx, rk, rg, o_loads, orx, ory, orz, org, rfc, rproj,
    terms, terms_all, half, pairs_half, half_y, pairs_y, rv, rvy,
):
    place, group = Place(True), Place(False)
    n_ctx = grads.shape[1]
    copies = Copies(send)
    far_ctx = others(place.ctx, n_ctx)
    peer_x, peer_y = {"x": 1 - place.x}, {"y": 1 - place.y}
    count = 2 * n_ctx
    me = place.x * n_ctx + place.ctx
    far_shards = others(me, count)

    def at_shard(k):
        return dict(place.at_ctx(lax.rem(k, n_ctx)), x=k // n_ctx)

    meet([at_shard(k) for k in far_shards] + [peer_y])
    tall = grads.shape[2]
    terms[...] = jnp.zeros_like(terms)
    for k in range(count):
        cols = slice(k * tall, (k + 1) * tall)
        terms[k, 0:4, 0:tall] = sums_in[:, cols]
        terms[k, 4:5, 0:tall] = gain_in[:, cols]
        terms[k, 5:6, 0:tall] = shift_in[:, cols]
        pair = pair_in.shape[1] // 3
        terms[k, 6:7, 0:pair] = pair_in[:, 0:pair]
        terms[k, 7:8, 0:pair] = pair_in[:, 2 * pair :]
        for row in range(-(-ff_in.shape[1] // 128)):
            width = min(128, ff_in.shape[1] - row * 128)
            terms[k, 8 + row : 9 + row, 0:width] = ff_in[:, row * 128 : row * 128 + width]
    for k in far_shards:
        copies.send(terms.at[k], terms_all.at[me], rv.at[me], at_shard(k))
    terms_all[me] = terms[me]
    sums = Scatter(place, part, held, from_c, from_y, from_z, out, copies, loads, rc, ry, rz)
    outs = OutScatter(place, out_part, o_held, o_x, o_y, o_z, out_w_out, copies, o_loads, orx, ory, orz, org)
    sums.begin()
    for k in far_ctx + [place.ctx]:
        copies.send(grads.at[1 - place.x, k], from_x.at[k], rx.at[k], peer_x)
        copies.local(grads.at[place.x, k], own_x.at[k], load_x.at[k])
    outs.begin()
    for k in others(group.ctx, 4):
        copies.send(fc.at[k], fc_out.at[group.ctx], rfc.at[group.ctx], group.at_ctx(k))
        copies.send(proj.at[k], proj_out.at[group.ctx], rproj.at[group.ctx], group.at_ctx(k))
    copies.local(fc.at[group.ctx], fc_out.at[group.ctx])
    copies.local(proj.at[group.ctx], proj_out.at[group.ctx])
    sums.over_c_far()
    mine = grads_out.at[place.y, place.ctx]
    for k in far_ctx + [place.ctx]:
        copies.arrived(from_x.at[k], rx.at[k], peer_x)
        pltpu.make_async_copy(own_x.at[k], own_x.at[k], load_x.at[k]).wait()
        from_x[k] = from_x[k] + own_x[k]
        if k is not place.ctx:
            copies.send(from_x.at[k], mine, rk.at[place.ctx], place.at_ctx(k))
    copies.local(from_x.at[place.ctx], mine)
    copies.send(from_x.at[place.ctx], mine, rg.at[place.ctx], peer_y)
    sums.over_c_near()
    sums.over_y()
    outs.over_x()
    for k in far_ctx:
        block = grads_out.at[place.y, k]
        copies.arrived(block, rk.at[k], place.at_ctx(k))
        copies.send(block, block, rg.at[k], peer_y)
    outs.over_y()
    sums.over_z()
    outs.over_z()
    for k in far_shards:
        copies.arrived(terms_all.at[k], rv.at[k], at_shard(k))
    total = terms_all[0, 0:8, :]
    for k in range(1, count):
        total = total + terms_all[k, 0:8, :]
    half[...] = total
    for k in range(n_ctx):
        pairs_half[k] = terms_all[k, 6:8, :] + terms_all[n_ctx + k, 6:8, :]
    copies.send(half, half_y, rvy.at[0], peer_y)
    copies.send(pairs_half, pairs_y, rvy.at[1], peer_y)
    for part in range(4):
        total = terms_all[part, 8:16, :]
        for k in range(part + 4, count, 4):
            total = total + terms_all[k, 8:16, :]
        ff_out[part] = total
    copies.arrived(half_y, rvy.at[0], peer_y)
    owned[...] = half[...] + half_y[...]
    copies.arrived(pairs_y, rvy.at[1], peer_y)
    pairs_out[place.y] = pairs_half[...]
    pairs_out[1 - place.y] = pairs_y[...]
    for k in [place.ctx] + far_ctx:
        copies.arrived(grads_out.at[1 - place.y, k], rg.at[k], peer_y)
    outs.end()
    for k in others(group.ctx, 4):
        copies.arrived(fc_out.at[k], rfc.at[k], group.at_ctx(k))
        copies.arrived(proj_out.at[k], rproj.at[k], group.at_ctx(k))
    copies.finish()


def closing(part, grads, out_part, fc, proj, *vectors):
    block = part.shape[1:]
    n_ctx = grads.shape[1]
    n_z = n_ctx // 2
    piece = grads.shape[1:]
    rows, width = out_part.shape[1:]
    half = (rows, width // 2)
    return pl.pallas_call(
        closing_kernel,
        out_shape=(
            jax.ShapeDtypeStruct(block, F32),
            jax.ShapeDtypeStruct((2,) + piece, B16),
            jax.ShapeDtypeStruct((2,) + half, B16),
            jax.ShapeDtypeStruct(fc.shape, fc.dtype),
            jax.ShapeDtypeStruct(proj.shape, proj.dtype),
            jax.ShapeDtypeStruct((8, 128), F32),
            jax.ShapeDtypeStruct((2, n_ctx, 2, 128), F32),
            jax.ShapeDtypeStruct((4, 8, 128), F32),
        ),
        in_specs=[ANY] * 5 + [IN_VMEM] * 5,
        out_specs=(IN_VMEM, ANY, IN_VMEM, ANY, ANY, IN_VMEM, IN_VMEM, IN_VMEM),
        scratch_shapes=scatter_scratch(n_z, block)
        + [pltpu.VMEM(piece, B16), pltpu.VMEM(piece, B16)]
        + [pltpu.VMEM((n_z, rows, width), B16), pltpu.VMEM((n_z, rows, width), B16)]
        + [pltpu.VMEM((n_z,) + half, B16), pltpu.VMEM((n_z,) + half, B16)]
        + scatter_sems(n_z, 5 * n_ctx + 4 * n_z + 10)
        + dma_sems(n_ctx, n_ctx, n_ctx, n_ctx)
        + dma_sems(n_z, n_z, n_z, n_z, 2, 4, 4)
        + [pltpu.VMEM((2 * n_ctx, 16, 128), F32), pltpu.VMEM((2 * n_ctx, 16, 128), F32)]
        + [pltpu.VMEM((8, 128), F32), pltpu.VMEM((n_ctx, 2, 128), F32)]
        + [pltpu.VMEM((8, 128), F32), pltpu.VMEM((n_ctx, 2, 128), F32)]
        + dma_sems(2 * n_ctx, 2),
        compiler_params=comm_params(4),
        name="closing",
    )(part, grads, out_part, fc, proj, *vectors)


def laid_wide(value, count, rows, tall):
    zeros = jnp.zeros((value.shape[0], tall - rows), value.dtype)
    parts = []
    for k in range(count):
        parts += [value[:, k * rows : (k + 1) * rows], zeros]
    return jnp.concatenate(parts, axis=1)


def laid_tall(value, count, rows, tall):
    zeros = jnp.zeros((tall - rows, value.shape[1]), value.dtype)
    parts = []
    for k in range(count):
        parts += [value[k * rows : (k + 1) * rows], zeros]
    return jnp.concatenate(parts, axis=0)


def laid_short(value, count, rows, tall):
    return jnp.concatenate([value[k * tall : k * tall + rows] for k in range(count)], axis=0)


def laid_narrow(value, count, rows, tall):
    return jnp.concatenate([value[:, k * tall : k * tall + rows] for k in range(count)], axis=1)


def prepare_kernel(count, at_ref, x, grad, qkv, fc, proj, out_w, *refs):
    singles, qv, (x_out, grad_out, blocks, ffn, out_out) = refs[:6], refs[6], refs[7:]
    rows, feats = out_w.shape
    n_ctx, tall, cols = blocks.shape
    pair, ff = cols // 3, ffn.shape[3]
    x_out[...] = laid_tall(x[...].astype(F32), count, rows, tall).T.astype(B16)
    grad_out[...] = laid_tall(grad[...].astype(F32), count, rows, tall).T.astype(B16)
    below = jnp.zeros((tall - rows, feats), F32)
    out_out[...] = laid_wide(
        jnp.concatenate([out_w[...].astype(F32), below], axis=0), count, rows, tall
    ).astype(B16)
    below = jnp.zeros((tall - rows, ff), F32)
    for k in range(4):
        ffn[0, k] = jnp.concatenate([fc[:, k * ff : (k + 1) * ff].astype(F32), below], axis=0).astype(B16)
        ffn[1, k] = jnp.concatenate([proj[:, k * ff : (k + 1) * ff].astype(F32), below], axis=0).astype(B16)
    small = [jnp.concatenate([ref[...].astype(F32), jnp.zeros((1, cols - rows), F32)], axis=1) for ref in singles]
    small.append(jnp.concatenate([qv[...].astype(F32), jnp.zeros((1, cols - 2 * rows), F32)], axis=1))
    if tall - rows > 7:
        small.append(jnp.zeros((tall - rows - 7, cols), F32))
    small = jnp.concatenate(small, axis=0)
    first = at_ref[0] == 0
    whole = qkv[...].astype(F32)

    def columns(part, p):
        width = min(pair, feats - p * pair)
        if width <= 0:
            return jnp.zeros((rows, pair), F32)
        value = whole[:, part * feats + p * pair : part * feats + p * pair + width]
        if width < pair:
            value = jnp.concatenate([value, jnp.zeros((rows, pair - width), F32)], axis=1)
        return value

    for k in range(n_ctx):
        value = [jnp.where(first, columns(part, 2 * k), columns(part, 2 * k + 1)) for part in range(3)]
        blocks[k] = jnp.concatenate([jnp.concatenate(value, axis=1), small], axis=0).astype(B16)


def prepare(y_at, x, grad, qkv, fc, proj, out_w, singles, qv, n_ctx, tall, pair):
    rows, feats = out_w.shape
    count = feats // rows
    wide = count * tall
    tokens = x.shape[1]
    vmem = pl.BlockSpec(memory_space=pltpu.VMEM)
    return pl.pallas_call(
        functools.partial(prepare_kernel, count),
        in_specs=[pl.BlockSpec(memory_space=pltpu.SMEM)] + [vmem] * 13,
        out_shape=(
            jax.ShapeDtypeStruct((tokens, wide), B16),
            jax.ShapeDtypeStruct((tokens, wide), B16),
            jax.ShapeDtypeStruct((n_ctx, tall, 3 * pair), B16),
            jax.ShapeDtypeStruct((2, 4, tall, fc.shape[1] // 4), B16),
            jax.ShapeDtypeStruct((tall, wide), B16),
        ),
        compiler_params=pltpu.CompilerParams(vmem_limit_bytes=VMEM_LIMIT),
        name="prepare",
    )(y_at, x, grad, qkv, fc, proj, out_w, *[value[None] for value in singles], qv[None])


def project_kernel(
    rows, feats, at_ref, x_ref, packed_ref, mask_ref, w_ref, norm_ref, qkv_ref, single_ref, bias_s, held_s
):
    count, tall, cols = packed_ref.shape
    pair = cols // 3

    @pl.when(pl.program_id(0) == 0)
    def begin():
        held_s[...] = jnp.zeros_like(held_s)
        vectors = []
        for row in range(6):
            at = rows + row
            vectors.append(
                jnp.concatenate([packed_ref[k, at : at + 1, 0:tall].astype(F32) for k in range(count)], axis=1)
            )
        single_ref[...] = jnp.concatenate(vectors + [jnp.zeros((2, count * tall), F32)], axis=0)
        for part in range(2):
            blocks = range(part * count // 2, (part + 1) * count // 2)
            at = rows + 6
            held_s[part : part + 1, 0:feats] = jnp.concatenate(
                [packed_ref[k, at : at + 1, 0 : 2 * rows].astype(F32) for k in blocks], axis=1
            )
        own = pl.ds(pl.multiple_of(at_ref[0] * pair, pair), pair)
        bias_s[...] = jnp.concatenate([held_s[0:1, own], jnp.zeros((1, pair), F32), held_s[1:2, own]], axis=1)

    x = x_ref[...].astype(F32)
    mean = jnp.sum(x, axis=1, keepdims=True) * (1.0 / feats)
    centered = (x - mean) * mask_ref[...]
    inv = lax.rsqrt(jnp.sum(centered * centered, axis=1, keepdims=True) * (1.0 / feats) + NORM_EPS)
    norm = (centered * inv * single_ref[0:1, :] + single_ref[1:2, :]).astype(B16)
    norm_ref[...] = norm
    qkv_ref[...] = (dot(norm, w_ref[...], 1, 0) + bias_s[...]).astype(B16)


def project(slot_at, x, packed, mask, rows, feats, padded):
    total, wide = x.shape
    cols = packed.shape[2]
    step = min(512, total)

    def fixed(shape):
        return pl.BlockSpec(shape, lambda i: (0,) * len(shape))

    return pl.pallas_call(
        functools.partial(project_kernel, rows, feats),
        grid=(total // step,),
        in_specs=[pl.BlockSpec(memory_space=pltpu.SMEM), pl.BlockSpec((step, wide), lambda i: (i, 0))]
        + [fixed(packed.shape), fixed((1, wide)), fixed((wide, cols))],
        out_specs=(
            pl.BlockSpec((step, wide), lambda i: (i, 0)),
            pl.BlockSpec((step, cols), lambda i: (i, 0)),
            fixed((8, wide)),
        ),
        out_shape=(
            jax.ShapeDtypeStruct((total, wide), B16),
            jax.ShapeDtypeStruct((total, cols), B16),
            jax.ShapeDtypeStruct((8, wide), F32),
        ),
        scratch_shapes=[pltpu.VMEM((1, cols), F32), pltpu.VMEM((2, padded), F32)],
        compiler_params=pltpu.CompilerParams(vmem_limit_bytes=VMEM_LIMIT),
        name="project",
    )(slot_at, x, packed, mask[None], packed.reshape(wide, cols))


def project_back_kernel(feats, x_ref, grad_ref, mask_ref, w_ref, part_ref, gradb_ref, gain_ref, shift_ref, pair_ref):
    @pl.when(pl.program_id(0) == 0)
    def begin():
        gain_ref[...] = jnp.zeros_like(gain_ref)
        shift_ref[...] = jnp.zeros_like(shift_ref)
        pair_ref[...] = jnp.zeros_like(pair_ref)

    grad = grad_ref[...]
    pair_ref[...] += jnp.sum(grad, axis=0, keepdims=True)
    grad = grad.astype(B16)
    gradb_ref[...] = grad
    part = dot(grad, w_ref[...], 1, 1)
    part_ref[...] = part.astype(B16)
    x = x_ref[...].astype(F32)
    mean = jnp.sum(x, axis=1, keepdims=True) * (1.0 / feats)
    centered = (x - mean) * mask_ref[...]
    inv = lax.rsqrt(jnp.sum(centered * centered, axis=1, keepdims=True) * (1.0 / feats) + NORM_EPS)
    gain_ref[...] += jnp.sum(part * (centered * inv), axis=0, keepdims=True)
    shift_ref[...] += jnp.sum(part, axis=0, keepdims=True)


def project_back(x, grad, mask, weight, feats):
    total, wide = x.shape
    cols = weight.shape[1]
    step = min(512, total)

    def fixed(shape):
        return pl.BlockSpec(shape, lambda i: (0,) * len(shape))

    def moving(width):
        return pl.BlockSpec((step, width), lambda i: (i, 0))

    return pl.pallas_call(
        functools.partial(project_back_kernel, feats),
        grid=(total // step,),
        in_specs=[moving(wide), moving(cols), fixed((1, wide)), fixed((wide, cols))],
        out_specs=(moving(wide), moving(cols), fixed((1, wide)), fixed((1, wide)), fixed((1, cols))),
        out_shape=(
            jax.ShapeDtypeStruct((total, wide), B16),
            jax.ShapeDtypeStruct((total, cols), B16),
            jax.ShapeDtypeStruct((1, wide), F32),
            jax.ShapeDtypeStruct((1, wide), F32),
            jax.ShapeDtypeStruct((1, cols), F32),
        ),
        compiler_params=pltpu.CompilerParams(vmem_limit_bytes=VMEM_LIMIT),
        name="project_back",
    )(x, grad, mask[None], weight)


def deliver_kernel(
    rows, feats, qkv, out_w, fc, proj, mlp, hidden, dnorm, dhidden, x_ref, single, mask,
    qkv_out, out_out, fc_out, proj_out, block_out, grad_out,
):
    n_y, n_ctx, tall, cols = qkv.shape
    pair, ff, count = cols // 3, fc.shape[2], feats // rows
    parts = []
    for part in range(3):
        for p in range(-(-feats // pair)):
            width = min(pair, feats - p * pair)
            parts.append(qkv[p % n_y, p // n_y, :, part * pair : part * pair + width].astype(F32))
    qkv_out[...] = jnp.concatenate(parts, axis=1)[:rows]
    halves = jnp.concatenate([out_w[y].astype(F32) for y in range(2)], axis=1)
    out_out[...] = laid_narrow(halves, count, rows, tall)[:rows]
    fc_out[...] = jnp.concatenate([fc[k].astype(F32) for k in range(4)], axis=1)[:rows]
    for k in range(4):
        proj_out[:, k * ff : (k + 1) * ff] = proj[k].astype(F32)[:rows]
    block = hidden[...] + mlp[...].astype(F32) + single[5:6, :]
    block_out[...] = laid_short(block.T, count, rows, tall)
    normed, inv = norm_forward(x_ref[...].astype(F32), mask[...], feats)
    grad = dhidden[...] + norm_backward(dnorm[...], normed, inv, single[0:1, :], feats)
    grad_out[...] = laid_short(grad.T, count, rows, tall)


def deliver(qkv, out_w, fc, proj, mlp, hidden, dnorm, dhidden, x, single, mask, rows, feats):
    tokens, ff = x.shape[0], fc.shape[2]
    return pl.pallas_call(
        functools.partial(deliver_kernel, rows, feats),
        out_shape=(
            jax.ShapeDtypeStruct((rows, 3 * feats), F32),
            jax.ShapeDtypeStruct((rows, feats), F32),
            jax.ShapeDtypeStruct((rows, 4 * ff), F32),
            jax.ShapeDtypeStruct((rows, 4 * ff), F32),
            jax.ShapeDtypeStruct((feats, tokens), F32),
            jax.ShapeDtypeStruct((feats, tokens), F32),
        ),
        compiler_params=pltpu.CompilerParams(vmem_limit_bytes=VMEM_LIMIT),
        name="deliver",
    )(qkv, out_w, fc, proj, mlp, hidden, dnorm, dhidden, x, single, mask[None])


def hidden_kernel(rows, feats, att, w_out, x_ref, single, mask, by_core, hidden_out, norm_out):
    half = w_out.shape[2]
    count = feats // rows
    tall = 2 * half // count
    value = att[...].astype(F32)
    zeros = jnp.zeros((value.shape[0], tall - rows), F32)
    parts = []
    for core in range(2):
        blocks = []
        for k in range(core, count, 2):
            blocks += [value[:, k * rows : (k + 1) * rows], zeros]
        parts.append(jnp.concatenate(blocks, axis=1).astype(B16))
        by_core[core] = parts[core]
    hidden = [dot(parts[0], w_out[0, y], 1, 0) + dot(parts[1], w_out[1, y], 1, 0) for y in range(2)]
    hidden = x_ref[...].astype(F32) + jnp.concatenate(hidden, axis=1) + single[2:3, :]
    hidden_out[...] = hidden
    normed, unused = norm_forward(hidden, mask[...], feats)
    norm_out[...] = (normed * single[3:4, :] + single[4:5, :]).astype(B16)


def hidden_forward(att, w_out, x, single, mask, rows, feats):
    tokens, wide = x.shape
    return pl.pallas_call(
        functools.partial(hidden_kernel, rows, feats),
        out_shape=(
            jax.ShapeDtypeStruct((2, tokens, wide // 2), B16),
            jax.ShapeDtypeStruct((tokens, wide), F32),
            jax.ShapeDtypeStruct((tokens, wide), B16),
        ),
        compiler_params=pltpu.CompilerParams(vmem_limit_bytes=VMEM_LIMIT),
        name="hidden_forward",
    )(att, w_out, x, single, mask[None])


def hidden_back_kernel(
    rows, feats, dnorm_ref, hidden, grad_ref, w_out, single, mask, dhidden_out, dhidden_b, sums, datt_out
):
    half = w_out.shape[2]
    count = feats // rows
    tall = 2 * half // count
    dnorm = dnorm_ref[...]
    grad = grad_ref[...].astype(F32)
    normed, inv = norm_forward(hidden[...], mask[...], feats)
    dhidden = grad + norm_backward(dnorm, normed, inv, single[3:4, :], feats)
    dhidden_out[...] = dhidden
    rounded = dhidden.astype(B16)
    dhidden_b[...] = rounded
    sums[0:1, :] = jnp.sum(dhidden, axis=0, keepdims=True)
    sums[1:2, :] = jnp.sum(dnorm * normed, axis=0, keepdims=True)
    sums[2:3, :] = jnp.sum(dnorm, axis=0, keepdims=True)
    sums[3:4, :] = jnp.sum(grad, axis=0, keepdims=True)
    grads = [rounded[:, :half], rounded[:, half:]]
    datt = [dot(grads[0], w_out[c, 0], 1, 1) + dot(grads[1], w_out[c, 1], 1, 1) for c in range(2)]
    parts = [datt[k % 2][:, k // 2 * tall : k // 2 * tall + rows] for k in range(count)]
    if datt_out.shape[1] > feats:
        parts.append(jnp.zeros((dnorm.shape[0], datt_out.shape[1] - feats), F32))
    datt_out[...] = jnp.concatenate(parts, axis=1).astype(B16)


def hidden_back(dnorm, hidden, grad, w_out, single, mask, rows, feats, padded):
    tokens, wide = hidden.shape
    return pl.pallas_call(
        functools.partial(hidden_back_kernel, rows, feats),
        out_shape=(
            jax.ShapeDtypeStruct((tokens, wide), F32),
            jax.ShapeDtypeStruct((tokens, wide), B16),
            jax.ShapeDtypeStruct((4, wide), F32),
            jax.ShapeDtypeStruct((tokens, padded), B16),
        ),
        compiler_params=pltpu.CompilerParams(vmem_limit_bytes=VMEM_LIMIT),
        name="hidden_back",
    )(dnorm, hidden, grad, w_out, single, mask[None])


def load_pieces(at_ref, pieces, whole, sems, first=0):
    rows = whole.shape[0] // len(pieces)
    copies = []
    for i, piece in enumerate(pieces):
        to = whole.at[pl.ds(pl.multiple_of(at_ref[i], 16), rows), :]
        copies.append(pltpu.make_async_copy(piece, to, sems.at[first + i]))
    for copy in copies:
        copy.start()
    return copies


def as_pieces(pairs, refs, which):
    return [ref.at[which] for ref in refs[:pairs]] + list(refs[pairs:])


def feed_up_kernel(pairs, count, at_ref, *refs):
    pieces, (norm_ref, bias_ref, act_ref, slope_ref, w_fc, sems) = refs[:count], refs[count:]

    @pl.when(pl.program_id(0) == 0)
    def begin():
        for copy in load_pieces(at_ref, as_pieces(pairs, pieces, 0), w_fc, sems):
            copy.wait()

    activated, slope = gelu_parts(dot(norm_ref[...], w_fc[...], 1, 0) + bias_ref[...])
    act_ref[...] = activated.astype(B16)
    slope_ref[...] = slope


FEED_STEP = 256


def feed_up(pairs, fcs, places, norm, bias):
    pieces = pairs + fcs
    total, wide = norm.shape
    ff = bias.shape[0]
    hidden = pl.BlockSpec((FEED_STEP, ff), lambda i: (i, 0))
    return pl.pallas_call(
        functools.partial(feed_up_kernel, len(pairs), len(pieces)),
        grid=(total // FEED_STEP,),
        in_specs=[pl.BlockSpec(memory_space=pltpu.SMEM)]
        + [ANY] * len(pieces)
        + [pl.BlockSpec((FEED_STEP, wide), lambda i: (i, 0)), pl.BlockSpec((1, ff), lambda i: (0, 0))],
        out_specs=(hidden, hidden),
        out_shape=(jax.ShapeDtypeStruct((total, ff), B16), jax.ShapeDtypeStruct((total, ff), F32)),
        scratch_shapes=[pltpu.VMEM((wide, ff), B16)] + dma_sems(len(pieces)),
        compiler_params=pltpu.CompilerParams(vmem_limit_bytes=VMEM_LIMIT),
        name="feed_up",
    )(places, *pieces, norm, bias[None])


def feed_down_kernel(pairs, singles, at_ref, *refs):
    count = pairs + 2 * singles
    pieces, refs = refs[:count], refs[count:]
    grad_ref, act_ref, slope_ref, dpre_ref, dnorm_ref, mlp_ref, sum_ref, w_fc, w_proj, sems = refs

    @pl.when(pl.program_id(0) == 0)
    def begin():
        fcs = as_pieces(pairs, pieces[: pairs + singles], 0)
        projs = as_pieces(pairs, pieces[:pairs] + pieces[pairs + singles :], 1)
        copies = load_pieces(at_ref, projs, w_proj, sems)
        copies += load_pieces(at_ref, fcs, w_fc, sems, pairs + singles)
        for copy in copies:
            copy.wait()
        sum_ref[...] = jnp.zeros_like(sum_ref)

    dpre = dot(grad_ref[...], w_proj[...], 1, 0) * slope_ref[...]
    sum_ref[...] += jnp.sum(dpre, axis=0, keepdims=True)
    dpre_b = dpre.astype(B16)
    dpre_ref[...] = dpre_b
    dnorm_ref[...] = dot(dpre_b, w_fc[...], 1, 1).astype(B16)
    mlp_ref[...] = dot(act_ref[...], w_proj[...], 1, 1).astype(B16)


def feed_down(pairs, fcs, projs, places, grad, act, slope):
    pieces = pairs + fcs + projs
    total, wide = grad.shape
    ff = act.shape[1]
    tokens = pl.BlockSpec((FEED_STEP, wide), lambda i: (i, 0))
    hidden = pl.BlockSpec((FEED_STEP, ff), lambda i: (i, 0))
    single = pl.BlockSpec((1, ff), lambda i: (0, 0))
    return pl.pallas_call(
        functools.partial(feed_down_kernel, len(pairs), len(fcs)),
        grid=(total // FEED_STEP,),
        in_specs=[pl.BlockSpec(memory_space=pltpu.SMEM)] + [ANY] * len(pieces) + [tokens, hidden, hidden],
        out_specs=(hidden, tokens, tokens, single),
        out_shape=(
            jax.ShapeDtypeStruct((total, ff), B16),
            jax.ShapeDtypeStruct((total, wide), B16),
            jax.ShapeDtypeStruct((total, wide), B16),
            jax.ShapeDtypeStruct((1, ff), F32),
        ),
        scratch_shapes=[pltpu.VMEM((wide, ff), B16), pltpu.VMEM((wide, ff), B16)]
        + dma_sems(2 * (len(pairs) + len(fcs))),
        compiler_params=pltpu.CompilerParams(vmem_limit_bytes=VMEM_LIMIT),
        name="feed_down",
    )(places, *pieces, grad, act, slope)


def after(value, other, unpack=False):
    value, other = lax.optimization_barrier((value, other))
    return (*value, other) if unpack else (value, other)


def shift_perm(count, step):
    return [(i, (i + step) % count) for i in range(count)]


def on_device(
    sizes, block_input, segment_ids, slot_order, first_gain, first_shift, qkv_weight, qv_bias, out_weight, out_bias,
    second_gain, second_shift, fc_weight, fc_bias, proj_weight, proj_bias, out_grad,
):
    n_x, n_ctx, n_y = sizes
    n_slot = n_ctx * n_y
    n_shard = n_x * n_ctx
    n_h = n_ctx // 4
    slot_len, feats = block_input.shape[1:]
    head = feats // HEADS
    pair = 2 * head
    rows = qkv_weight.shape[0]
    ff_own = fc_weight.shape[1] // 4
    padded = n_slot * pair
    y_at = lax.axis_index("y")
    ctx_at = lax.axis_index(CTX)
    slot_at = lax.axis_index(ROW)
    lc_at = lax.axis_index(("l", "c"))
    x_at, h_at = lax.axis_index("x"), lax.axis_index("h")

    def gather(value, axes):
        return lax.all_gather(value, axes, axis=0, tiled=True)

    tall = rows + (-rows % 16)
    wide = n_shard * tall
    row_pad = tall - rows

    mask = jnp.asarray((np.arange(wide) % tall < rows).astype(np.float32))

    singles = (first_gain, first_shift, out_bias, second_gain, second_shift, proj_bias)
    own_input, grad_own, packed, ffn_blocks, w_out = prepare(
        y_at.astype(jnp.int32)[None], block_input[0].T, out_grad[0].T, qkv_weight, fc_weight, proj_weight.T, out_weight,
        singles, qv_bias, n_ctx, tall, pair,
    )
    all_input, packed, ffn_blocks, w_out = opening(
        own_input, packed, ffn_blocks, w_out
    )
    ffn_blocks = ffn_blocks.reshape(2, 4 * tall, ff_own)
    fc_h = [lax.ppermute(ffn_blocks[0], "h", shift_perm(n_h, step)) for step in range(1, n_h)]
    along_x = lax.ppermute(ffn_blocks, "x", shift_perm(n_x, 1))
    grad_late, all_input = after(grad_own, all_input)
    grad_all = gather(grad_late, FFG)
    w_out = lax.all_gather(w_out.reshape(wide // 2, wide // 2), ("c", "y"), axis=0, tiled=False)
    w_out = w_out.reshape(2, n_y, wide // 2, wide // 2)
    packed = packed.reshape(n_shard, tall, 3 * pair)
    w_qkv = packed.reshape(wide, 3 * pair)
    b_fc = lax.dynamic_slice_in_dim(fc_bias, lc_at * ff_own, ff_own, 0).astype(F32)

    order = slot_order[0]
    pieces = jnp.arange(n_slot, dtype=jnp.int32)
    inv = jnp.sum(jnp.where(order[None, :] == pieces[:, None], pieces[None, :], 0), axis=1).astype(jnp.int32)
    segs = jnp.take(segment_ids[0].reshape(n_slot, slot_len), inv, axis=0).reshape(-1)
    docs = jnp.arange(DOCS, dtype=jnp.int32)
    counts = jnp.sum((segs[None, :] == docs[:, None]).astype(jnp.int32), axis=1)
    starts = jnp.sum(jnp.where(segs[None, :] > docs[:, None], counts[:, None], 0), axis=0).astype(jnp.int32)
    start3 = starts.reshape(-1, 1, BLK)
    low = start3[:, 0, 0] // BLK

    all_input = all_input.reshape(n_slot * slot_len, wide)
    norm_one, qkv, singles = project(
        slot_at.astype(jnp.int32)[None], all_input, packed, mask, rows, feats, padded
    )
    heads_out, lse = attend(inv, low, qkv, start3, slot_len, head)
    fc_h, along_x, heads_out = after((fc_h, along_x), heads_out, True)
    fc_xh = [lax.ppermute(value, "x", shift_perm(n_x, 1)) for value in fc_h]
    tokens_out = to_tokens(heads_out.reshape(n_slot, slot_len, pair))
    proj_late, tokens_out = after(ffn_blocks[1], tokens_out)
    proj_h = [lax.ppermute(proj_late, "h", shift_perm(n_h, step)) for step in range(1, n_h)]
    by_core, hidden, norm_two = hidden_forward(
        tokens_out, w_out, own_input, singles, mask, rows, feats
    )
    norm_all = group_gather(norm_two, 6).reshape(-1, wide)
    proj_h, norm_all = after(proj_h, norm_all)
    proj_xh = [lax.ppermute(value, "x", shift_perm(n_x, 1)) for value in proj_h]
    places = [(x_at, h_at), (1 - x_at, h_at)]
    for step in range(1, n_h):
        h_from = lax.rem(h_at + n_h - step, n_h)
        places += [(x_at, h_from), (1 - x_at, h_from)]

    def mixed(one, two):
        return [value for both in zip(one, two) for value in both]

    places = jnp.stack([(x * n_h + h) * (4 * tall) for x, h in places]).astype(jnp.int32)
    pairs, fcs, projs = [ffn_blocks, along_x], mixed(fc_h, fc_xh), mixed(proj_h, proj_xh)
    activation, slope = feed_up(pairs, fcs, places, norm_all, b_fc)

    def pick(value, at):
        return lax.dynamic_index_in_dim(value, at, 0, False)

    def by_owner(value):
        value = with_layout_constraint(value.astype(B16), Layout(major_to_minor=(0, 1)))
        return value.reshape(n_x, n_h, 4 * tall, ff_own)

    proj_part = by_owner(dot(grad_all, activation, 0, 0))
    proj_give = pick(proj_part, 1 - x_at)
    proj_give, activation = after(proj_give, activation)
    proj_x = lax.ppermute(proj_give, "x", shift_perm(n_x, 1))
    dpreact_b, dnorm_part, mlp_part, dpreact_sum = feed_down(pairs, fcs, projs, places, grad_all, activation, slope)

    fc_part = by_owner(dot(norm_all, dpreact_b, 0, 0))
    fc_x = lax.ppermute(pick(fc_part, 1 - x_at), "x", shift_perm(n_x, 1))
    fc_part, dnorm_part = after(fc_part, dnorm_part)
    dnorm_two = group_scatter(dnorm_part.reshape(8, slot_len, wide), 7)

    def over_h(value):
        gives = [pick(value, lax.rem(h_at + step, n_h)) for step in range(1, n_h)]
        return [lax.ppermute(give, "h", shift_perm(n_h, step + 1)) for step, give in enumerate(gives)]

    def total(value, received):
        value = pick(value, h_at).astype(F32)
        for other in received:
            value = value + other
        return value.astype(B16).reshape(4, tall, ff_own)

    proj_x, mlp_part, dnorm_two = after((proj_x, mlp_part), dnorm_two, True)
    proj_line = pick(proj_part, x_at) + proj_x
    proj_h = over_h(proj_line)
    mlp = lax.psum_scatter(mlp_part, FFG, scatter_dimension=0, tiled=True)
    dhidden, dhidden_b, token_sums, dattention = hidden_back(
        dnorm_two, hidden, grad_own, w_out, singles, mask, rows, feats, padded
    )
    c_at = lax.axis_index("c")
    out_give = dot(jnp.where(c_at == 0, by_core[1], by_core[0]), dhidden_b, 0, 0).astype(B16)
    out_give = lax.ppermute(out_give, "c", shift_perm(2, 1))
    out_keep = dot(jnp.where(c_at == 0, by_core[0], by_core[1]), dhidden_b, 0, 0).astype(B16)
    dattention = to_heads(dattention, n_slot).reshape(n_slot * slot_len, pair)
    out_give, fc_x, dattention = after((out_give, fc_x), dattention, True)
    out_part = (out_keep + out_give).reshape(n_shard // 2, tall, wide)
    fc_line = pick(fc_part, x_at) + fc_x
    fc_h = over_h(fc_line)
    dqkv = attend_back(inv, low, qkv, heads_out, dattention, lse, start3, slot_len, head)
    dnorm_one_part, dqkv_b, gain_sum, shift_sum, pair_sum = project_back(all_input, dqkv, mask, w_qkv, feats)
    qkv_part = dot(norm_one, dqkv_b, 0, 0).astype(B16).reshape(n_x, n_ctx, tall, 3 * pair)
    proj_h, fc_h, dnorm_one_part = after((proj_h, fc_h), dnorm_one_part, True)
    dnorm_one, qkv_all, out_all, fc_all, proj_all, owned, pair_sums, ff_sums = closing(
        dnorm_one_part.reshape(n_slot, slot_len, wide), qkv_part, out_part, total(fc_line, fc_h), total(proj_line, proj_h),
        token_sums, gain_sum, shift_sum, pair_sum, dpreact_sum,
    )
    mlp, dnorm_one = after(mlp, dnorm_one)
    qkv_grad, out_grad_w, fc_grad, proj_grad, block_output, input_grad = deliver(
        qkv_all, out_all, fc_all, proj_all, mlp, hidden, dnorm_one, dhidden, own_input, singles, mask, rows, feats
    )
    fc_bias_grad = ff_sums.reshape(4, 1024)[:, :ff_own].reshape(4 * ff_own)
    pair_sums = pair_sums.transpose(2, 1, 0, 3).reshape(2, padded)[:, :feats].reshape(2 * feats)
    qv_grad = lax.dynamic_slice_in_dim(pair_sums, lax.axis_index(SHARD) * 2 * rows, 2 * rows, 0)

    def own(index):
        return owned[index, :rows]

    return (
        block_output.T[None],
        input_grad.T[None],
        qkv_grad,
        qv_grad,
        out_grad_w,
        own(0),
        own(4),
        own(5),
        own(1),
        own(2),
        fc_grad,
        fc_bias_grad,
        proj_grad.T,
        own(3),
    )


def solution(mesh):
    n_x, n_ctx, n_y = (mesh.shape[axis] for axis in ("dp", "context", "tensor"))
    inner = Mesh(mesh.devices.reshape(n_x, n_ctx // 4, 2, 2, n_y), ("x", "h", "l", "c", "y"))
    tokens = P("x", ROW, None)
    shard = P(SHARD)
    shard_rows = P(SHARD, None)
    return jax.shard_map(
        functools.partial(on_device, (n_x, n_ctx, n_y)),
        mesh=inner,
        in_specs=(
            tokens, P("x", None), P("x", None), shard, shard, shard_rows, shard, shard_rows, shard, shard, shard,
            P(SHARD, "y"), P("y"), P("y", SHARD), shard, tokens,
        ),
        out_specs=(
            tokens, tokens, shard_rows, shard, shard_rows, shard, shard, shard, shard, shard,
            P(SHARD, "y"), P("y"), P("y", SHARD), shard,
        ),
        check_vma=False,
    )
```
